32 devices in a mesh: tile: 4 (over y, x), sub: 8 (over z, core).
Axes of the slice: x: 2, y: 2, z: 4, core: 2. Of those that a mesh axis runs over, the one named last changes fastest.
Arguments:
- seeds: float32 [4, 6, 16, 256, 128], P('tile', None, 'sub'), may hold values from -6 to 6
- material: int32 [4, 16, 256, 128], P('tile', 'sub'), may hold values from 0 to 3
- decay: float32 [4], replicated, may hold values from 0.5 to 1
- coupling: float32 [4], replicated, may hold values from 0.1 to 0.6
Outputs:
- gradient: float32 [4, 6, 16, 256, 128], P('tile', None, 'sub')
The draws below stay inside these ranges and needn't reach their ends.
All inputs are finite; a program needn't handle non-finite values.
Results may differ from the reference program's by a relative error of at most 0.0003.
Values sent between devices are 32-bit elements; how exact they have to be, the bound alone decides.
No kernel may reach another device: no remote copies, remote signals or barrier semaphores. Data moves between devices by JAX's collectives and lax.ppermute only.
A program may use at most 64 MiB of HBM per device.

```python
import math
import jax
import jax.numpy as jnp
from jax import lax

TX = 256
TY = 128
BAND = 32
STEPS = 2
MATERIALS = 4
TILES = 4
Z = 16
N_TILE = 4


def touch_ends(values, rng, least, largest):
    longest = values.shape.index(max(values.shape))
    spots = []
    for shift in (0, 1):
        where = [jax.random.randint(jax.random.fold_in(rng, axis), (), 0, length) for axis, length in enumerate(values.shape)]
        where[longest] = (where[longest] + shift) % values.shape[longest]
        spots.append(tuple(where))
    return values.at[spots[0]].set(least).at[spots[1]].set(largest)


def shard_levels(key, dims, cuts, least, largest):
    level, own = 1.0, jax.random.fold_in(key, 6)
    for dim, shards_of in cuts:
        heights = jnp.exp(jax.random.uniform(jax.random.fold_in(own, dim), (shards_of,), jnp.float32, least / len(cuts), largest / len(cuts)))
        level = level * jnp.repeat(heights, dims[dim] // shards_of).reshape([-1 if axis == dim else 1 for axis in range(len(dims))])
    return level


def bell_draw(key, shape, scale, reach, split=(), kind=jnp.bfloat16):
    array = scale * jax.random.normal(key, shape, jnp.float32)
    if split:
        array = array * shard_levels(key, shape, split, -0.22, 0.18)
    return jnp.clip(array, -reach, reach).astype(kind)


def setup_inputs(seed: int = 0) -> dict:
    arg_keys = jax.random.split(jax.random.key(seed), 5)
    seeds = bell_draw(arg_keys[0], (TILES, 6, Z, TX, TY), 1.0, 6.0, ((0, 4), (2, 8)), jnp.float32)
    material = touch_ends(jax.random.randint(arg_keys[1], (TILES, Z, TX, TY), 0, MATERIALS), jax.random.fold_in(arg_keys[1], 1), 0, MATERIALS - 1).astype(jnp.int32)
    decay = jnp.clip(jax.random.uniform(arg_keys[2], (MATERIALS,), jnp.float32, 0.5, 1.0), 0.5, 1.0)
    coupling = jnp.clip(jnp.exp(jax.random.uniform(arg_keys[3], (MATERIALS,), jnp.float32, math.log(0.1), math.log(0.6))), 0.1, 0.6)
    return {"seeds": seeds, "material": material, "decay": decay, "coupling": coupling}


magnetic_coeff = 0.5

def lookup_table(material, table):
    labels = jnp.arange(table.shape[0], dtype=jnp.int32)[:, None, None, None]
    return lax.optimization_barrier(jnp.sum(jnp.where(material[None] == labels, table[:, None, None, None], 0.0), axis=0))

def plus_diff(values, axis_pos):
    width = values.shape[axis_pos]
    later = lax.slice_in_dim(values, 1, width, axis=axis_pos)
    padding = [(0, 0)] * values.ndim
    padding[axis_pos] = (0, 1)
    return jnp.pad(later, padding) - values

def minus_diff(values, axis_pos):
    width = values.shape[axis_pos]
    earlier = lax.slice_in_dim(values, 0, width - 1, axis=axis_pos)
    padding = [(0, 0)] * values.ndim
    padding[axis_pos] = (1, 0)
    return values - jnp.pad(earlier, padding)

def plus_depth(values, after_plane):
    return jnp.concatenate([values[1:], after_plane[None]], axis=0) - values

def minus_depth(values, before_plane):
    return values - jnp.concatenate([before_plane[None], values[:-1]], axis=0)

def curl_forward(fields, after):
    curl_x = plus_diff(fields[2], 2) - plus_depth(fields[1], after[1])
    curl_y = plus_depth(fields[0], after[0]) - plus_diff(fields[2], 1)
    curl_z = plus_diff(fields[1], 1) - plus_diff(fields[0], 2)
    return jnp.stack([curl_x, curl_y, curl_z])

def curl_backward(fields, before):
    curl_x = minus_diff(fields[2], 2) - minus_depth(fields[1], before[1])
    curl_y = minus_depth(fields[0], before[0]) - minus_diff(fields[2], 1)
    curl_z = minus_diff(fields[1], 1) - minus_diff(fields[0], 2)
    return jnp.stack([curl_x, curl_y, curl_z])

def ramp(count):
    position = jnp.arange(count).astype(jnp.float32) + 0.5
    low_part = position / BAND
    high_part = (count - position) / BAND
    return jnp.where(position < BAND, low_part, jnp.where(position > count - BAND, high_part, 1.0))

def reference(seeds, material, decay, coupling):
    side = math.isqrt(N_TILE)

    def run_tile(inputs):
        seed_tile, material_tile = inputs
        decay_map = lookup_table(material_tile, decay)
        coupling_map = lookup_table(material_tile, coupling)
        field_e = seed_tile[:3]
        field_h = seed_tile[3:]
        zero_planes = jnp.zeros((2, TX, TY), seed_tile.dtype)
        for turn_index in range(STEPS):
            scaled = coupling_map * field_e
            field_h = field_h + curl_forward(scaled, zero_planes)
            field_e = decay_map * field_e - magnetic_coeff * curl_backward(field_h, zero_planes)
        return jnp.concatenate([field_e, field_h], axis=0)
    adjoint = lax.map(run_tile, (seeds, material))
    weight = ramp(TX)[:, None] * ramp(TY)[None, :]
    weighted = adjoint * weight
    high_bands = weighted[:, :, :, TX - BAND:, :]
    low_bands = weighted[:, :, :, :BAND, :]
    from_prev = jnp.roll(high_bands, 1, axis=0)
    from_next = jnp.roll(low_bands, -1, axis=0)
    combined = weighted.at[:, :, :, :BAND, :].add(from_prev)
    combined = combined.at[:, :, :, TX - BAND:, :].add(from_next)
    top_slab = combined[..., TY - BAND:]
    bottom_slab = combined[..., :BAND]
    from_below = jnp.roll(top_slab, side, axis=0)
    from_above = jnp.roll(bottom_slab, -side, axis=0)
    result = combined.at[..., :BAND].add(from_below)
    result = result.at[..., TY - BAND:].add(from_above)
    return result
```

```python
import functools
import math

import jax
import jax.numpy as jnp
from jax import lax
from jax.experimental import pallas as pl
from jax.experimental.pallas import tpu as pltpu
from jax.sharding import PartitionSpec as P

BAND = 32
STEPS = 2
HALO = 8
PLANES = 5

magnetic_coeff = 0.5


def lane_of(shape):
    return lax.broadcasted_iota(jnp.int32, shape, 1)


def row_of(shape):
    return lax.broadcasted_iota(jnp.int32, shape, 0)


def next_x(v):
    rows = v.shape[0]
    return jnp.where(row_of(v.shape) == rows - 1, 0.0, pltpu.roll(v, rows - 1, 0))


def prev_x(v):
    return jnp.where(row_of(v.shape) == 0, 0.0, pltpu.roll(v, 1, 0))


def next_y(v):
    lanes = v.shape[1]
    return jnp.where(lane_of(v.shape) == lanes - 1, 0.0, pltpu.roll(v, lanes - 1, 1))


def prev_y(v):
    return jnp.where(lane_of(v.shape) == 0, 0.0, pltpu.roll(v, 1, 1))


def plus_x(v):
    return next_x(v) - v


def plus_y(v):
    return next_y(v) - v


def minus_x(v):
    return v - prev_x(v)


def minus_y(v):
    return v - prev_y(v)


def looked_up(labels, table):
    value = jnp.full(labels.shape, table[0], jnp.float32)
    for m in range(1, table.shape[0]):
        value = jnp.where(labels == m, table[m], value)
    return value


def update_h(h, v, v_after):
    depth = len(v[0])
    new = [[], [], []]
    for p in range(depth):
        vx, vy, vz = v[0][p], v[1][p], v[2][p]
        up_x, up_y = (v[0][p + 1], v[1][p + 1]) if p + 1 < depth else v_after
        dz_x = up_x - vx if up_x is not None else -vx
        dz_y = up_y - vy if up_y is not None else -vy
        new[0].append(h[0][p] + (plus_y(vz) - dz_y))
        new[1].append(h[1][p] + (dz_x - plus_x(vz)))
        new[2].append(h[2][p] + (plus_x(vy) - plus_y(vx)))
    return new


def update_e(e, ca, h, h_before):
    depth = len(h[0])
    new = [[], [], []]
    for p in range(depth):
        hx, hy, hz = h[0][p], h[1][p], h[2][p]
        low_x, low_y = (h[0][p - 1], h[1][p - 1]) if p > 0 else h_before
        dz_x = hx - low_x if low_x is not None else hx
        dz_y = hy - low_y if low_y is not None else hy
        new[0].append(ca[p] * e[0][p] - magnetic_coeff * (minus_y(hz) - dz_y))
        new[1].append(ca[p] * e[1][p] - magnetic_coeff * (dz_x - minus_x(hz)))
        new[2].append(ca[p] * e[2][p] - magnetic_coeff * (minus_x(hy) - minus_y(hx)))
    return new


def scaled(cb, e):
    return [[cb[p] * e[c][p] for p in range(len(cb))] for c in range(3)]


def loaded(seeds, material, decay, coupling, lo, hi):
    depth = seeds.shape[2]
    e = [[seeds[0, c, p, lo:hi] for p in range(depth)] for c in range(3)]
    h = [[seeds[0, 3 + c, p, lo:hi] for p in range(depth)] for c in range(3)]
    labels = [material[0, p, lo:hi] for p in range(depth)]
    ca = [looked_up(m, decay) for m in labels]
    cb = [looked_up(m, coupling) for m in labels]
    return e, h, ca, cb


NONE = (None, None)


def halo_kernel(spans, sub, decay, coupling, seeds, material, near, far):
    odd = lax.rem(lax.axis_index(sub), 2) == 1
    at = 0
    for lo, hi in spans:
        e, h, ca, cb = loaded(seeds, material, decay, coupling, lo, hi)
        v1 = scaled(cb, e)
        h1 = update_h(h, v1, NONE)
        e1 = update_e(e, ca, h1, NONE)
        v2 = scaled(cb, e1)
        h2 = update_h(h1, v2, NONE)
        up = (h1[0][-1], h1[1][-1], h2[0][-1], h2[1][-1], cb[-1])
        down = (v1[0][0], v1[1][0], v2[0][0], v2[1][0], cb[0])
        for k in range(PLANES):
            near[k, at : at + hi - lo] = jnp.where(odd, down[k], up[k])
            far[k, at : at + hi - lo] = jnp.where(odd, up[k], down[k])
        at += hi - lo


def ramp(position, count):
    position = position.astype(jnp.float32) + 0.5
    return jnp.where(
        position < BAND,
        position / BAND,
        jnp.where(position > count - BAND, (count - position) / BAND, 1.0),
    )


def final_fields(fields, near, far, at, rows, sub, sub_size):
    e, h, ca, cb = fields
    index = lax.axis_index(sub)
    odd = lax.rem(index, 2) == 1
    below, above = index > 0, index < sub_size - 1
    a = [near[k, at : at + rows] for k in range(PLANES)]
    b = [far[k, at : at + rows] for k in range(PLANES)]
    from_below = [jnp.where(odd, a[k], b[k]) for k in range(PLANES)]
    from_above = [jnp.where(above, jnp.where(odd, b[k], a[k]), 0.0) for k in range(PLANES)]
    part_h1x, part_h1y, part_h2x, part_h2y, cb_low = from_below
    v1x_up, v1y_up, part_v2x, part_v2y, cb_up = from_above

    v1 = scaled(cb, e)
    h1 = update_h(h, v1, (v1x_up, v1y_up))
    dh1x, dh1y = -v1[1][0], v1[0][0]
    h1_low = (jnp.where(below, part_h1x + dh1x, 0.0), jnp.where(below, part_h1y + dh1y, 0.0))
    e1 = update_e(e, ca, h1, h1_low)
    v2 = scaled(cb, e1)
    v2_up = (
        part_v2x - cb_up * (magnetic_coeff * h1[1][-1]),
        part_v2y + cb_up * (magnetic_coeff * h1[0][-1]),
    )
    h2 = update_h(h1, v2, v2_up)
    dv2x = cb_low * (magnetic_coeff * dh1y)
    dv2y = cb_low * (-magnetic_coeff * dh1x)
    dv2z = cb_low * (-magnetic_coeff * (minus_x(dh1y) - minus_y(dh1x)))
    h2x_low = part_h2x + (dh1x + (plus_y(dv2z) - (v2[1][0] - dv2y)))
    h2y_low = part_h2y + (dh1y + ((v2[0][0] - dv2x) - plus_x(dv2z)))
    h2_low = (jnp.where(below, h2x_low, 0.0), jnp.where(below, h2y_low, 0.0))
    e2 = update_e(e1, ca, h2, h2_low)
    return e2 + h2


def middle_out(block):
    return pltpu.roll(block, block.shape[1] // 2, 1)


def y_packed(first, second):
    lane = lane_of(first.shape)
    lanes = first.shape[1]
    middle = (lane >= BAND) & (lane < lanes - BAND)
    return jnp.where(middle, pltpu.roll(second, lanes // 2, 1), first)


def y_unpacked(block):
    lane = lane_of(block.shape)
    lanes = block.shape[1]
    a, b = pltpu.roll(block, BAND, 1), pltpu.roll(block, lanes - BAND, 1)
    middle = (lane >= BAND) & (lane < lanes - BAND)
    first = jnp.where(middle, 0.0, jnp.where(lane < BAND, a, b))
    second = jnp.where(middle, 0.0, jnp.where(lane < BAND, b, a))
    return first, second


def weighted_planes(seeds, material, decay, coupling, near, far, at, lo, hi, keep, sub, sub_size):
    fields = loaded(seeds, material, decay, coupling, lo, hi)
    planes = final_fields(fields, near, far, at, hi - lo, sub, sub_size)
    start, stop = keep
    size_x, size_y = seeds.shape[3:]
    shape = (stop - start, size_y)
    weight = ramp(row_of(shape) + start, size_x) * ramp(lane_of(shape), size_y)
    return [[plane[start - lo : stop - lo] * weight for plane in part] for part in planes]


def edge_kernel(spans, sub, sub_size, tile, decay, coupling, seeds, material, near, far, edge, corner, strip):
    at = 0
    parts = []
    size_x = seeds.shape[3]
    for (lo, hi), keep in zip(spans, ((0, BAND), (size_x - BAND, size_x))):
        parts.append(weighted_planes(seeds, material, decay, coupling, near, far, at, lo, hi, keep, sub, sub_size))
        at += hi - lo
    odd = lax.rem(lax.axis_index(tile), 2) == 1
    low, high = parts
    half = BAND // 2
    for c in range(6):
        for p in range(seeds.shape[2]):
            edge[c, p, :BAND] = low[c][p]
            edge[c, p, BAND:] = high[c][p]
            corner[c, p] = y_packed(low[c][p], high[c][p])
            away = jnp.where(odd, high[c][p], low[c][p])
            strip[c, p] = y_packed(middle_out(away[:half]), middle_out(away[half:]))


def middle_kernel(spans, sub, sub_size, decay, coupling, seeds, material, near, far, mid, bands):
    (lo, hi), = spans
    size_x = seeds.shape[3]
    keep = (BAND, size_x - BAND)
    planes = weighted_planes(seeds, material, decay, coupling, near, far, 0, lo, hi, keep, sub, sub_size)
    half = (keep[1] - keep[0]) // 2
    for c in range(6):
        for p in range(seeds.shape[2]):
            mid[c, p] = planes[c][p]
            bands[c, p] = y_packed(planes[c][p][:half], planes[c][p][half:])


def whole_kernel(spans, sub, sub_size, decay, coupling, seeds, material, near, far, out):
    (lo, hi), = spans
    planes = weighted_planes(seeds, material, decay, coupling, near, far, 0, lo, hi, (lo, hi), sub, sub_size)
    for c in range(6):
        for p in range(seeds.shape[2]):
            out[c, p] = planes[c][p]


def corner_kernel(tile, edge, corner, summed, send):
    odd = lax.rem(lax.axis_index(tile), 2) == 1
    half = BAND // 2
    for c in range(edge.shape[0]):
        for p in range(edge.shape[1]):
            first, second = y_unpacked(corner[c, p])
            low = edge[c, p, :BAND] + first
            high = edge[c, p, BAND:] + second
            summed[c, p, :BAND] = low
            summed[c, p, BAND:] = high
            by, away = jnp.where(odd, low, high), jnp.where(odd, high, low)
            send[c, p, :BAND] = by
            send[c, p, BAND:] = y_packed(away[:half], away[half:])


def seam_kernel(tile, summed, got, strip, out):
    odd = lax.rem(lax.axis_index(tile), 2) == 1
    half = BAND // 2
    for c in range(summed.shape[0]):
        for p in range(summed.shape[1]):
            by = got[c, p, :BAND]
            corners = y_unpacked(got[c, p, BAND:])
            block = strip[c, p]
            lane = lane_of(block.shape)
            middle = (lane >= BAND) & (lane < block.shape[1] - BAND)
            first = jnp.where(middle, middle_out(block), corners[0])
            second = jnp.where(middle, block, corners[1])
            away = jnp.concatenate([first, second], axis=0)
            out[c, p, :BAND] = summed[c, p, :BAND] + jnp.where(odd, by, away)
            out[c, p, BAND:] = summed[c, p, BAND:] + jnp.where(odd, away, by)


def last_kernel(edge, mid, bands, out):
    for p in range(mid.shape[1]):
        half = bands.shape[2]
        size_x = out.shape[3]
        first, second = y_unpacked(bands[0, p])
        out[0, 0, p, :BAND] = edge[0, p, :BAND]
        out[0, 0, p, BAND : BAND + half] = mid[0, p, :half] + first
        out[0, 0, p, BAND + half : size_x - BAND] = mid[0, p, half:] + second
        out[0, 0, p, size_x - BAND :] = edge[0, p, BAND:]


SMEM = pl.BlockSpec(memory_space=pltpu.SMEM)
VMEM = pl.BlockSpec(memory_space=pltpu.VMEM)
PARAMS = pltpu.CompilerParams(vmem_limit_bytes=32 * 1024 * 1024)


def called(kernel, shapes, in_specs, *operands):
    outs = [jax.ShapeDtypeStruct(shape, jnp.float32) for shape in shapes]
    return pl.pallas_call(
        kernel,
        out_shape=outs,
        in_specs=in_specs,
        out_specs=[VMEM] * len(outs),
        compiler_params=PARAMS,
    )(*operands)


def depth_exchange(near, far, sub_size, tile_size):
    near = lax.ppermute(near, "sub", [(i, i ^ 1) for i in range(sub_size)])
    pairs = []
    for t in range(tile_size):
        for i in range(sub_size):
            other = (i + 1) ^ 1
            j = other - 1
            if 0 <= j < sub_size:
                pairs.append((t * sub_size + i, t * sub_size + j))
            else:
                pairs.append((t * sub_size + i, (t ^ 1) * sub_size + i))
    far = lax.ppermute(far, ("tile", "sub"), pairs)
    return near, far


def swapped(value, bits, tile_size):
    return lax.ppermute(value, "tile", [(t, t ^ bits) for t in range(tile_size)])


def from_behind(value, steps, count):
    return lax.ppermute(value, "tile", [(t, (t + steps) % count) for t in range(count)])


def two_by_two(seeds, material, decay, coupling, sub_size, tile_size):
    depth, size_x, size_y = seeds.shape[2:]
    edges = ((0, BAND + HALO), (size_x - BAND - HALO, size_x))
    inner = ((BAND - HALO, size_x - BAND + HALO),)
    tables = [SMEM, SMEM, VMEM, VMEM]

    def halos(spans):
        shape = (PLANES, sum(hi - lo for lo, hi in spans), size_y)
        kernel = functools.partial(halo_kernel, spans, "sub")
        return called(kernel, [shape, shape], tables, decay, coupling, seeds, material)

    edge_near, edge_far = depth_exchange(*halos(edges), sub_size, tile_size)
    inner_near, inner_far = depth_exchange(*halos(inner), sub_size, tile_size)

    edge, corner, strip = called(
        functools.partial(edge_kernel, edges, "sub", sub_size, "tile"),
        [(6, depth, 2 * BAND, size_y), (6, depth, BAND, size_y), (6, depth, BAND // 2, size_y)],
        tables + [VMEM, VMEM], decay, coupling, seeds, material, edge_near, edge_far,
    )
    corner = swapped(corner, 2, tile_size)
    strip = swapped(strip, 3, tile_size)
    rows = size_x - 2 * BAND
    mid, bands = called(
        functools.partial(middle_kernel, inner, "sub", sub_size),
        [(6, depth, rows, size_y), (6, depth, rows // 2, size_y)],
        tables + [VMEM, VMEM], decay, coupling, seeds, material, inner_near, inner_far,
    )
    bands = swapped(bands, 2, tile_size)
    summed, send = called(
        functools.partial(corner_kernel, "tile"),
        [(6, depth, 2 * BAND, size_y), (6, depth, BAND + BAND // 2, size_y)],
        [VMEM, VMEM], edge, corner,
    )
    got = swapped(send, 1, tile_size)
    edge, = called(
        functools.partial(seam_kernel, "tile"), [(6, depth, 2 * BAND, size_y)],
        [VMEM, VMEM, VMEM], summed, got, strip,
    )
    block = lambda n: pl.BlockSpec((1, depth, n, size_y), lambda c: (c, 0, 0, 0))
    return pl.pallas_call(
        last_kernel,
        grid=(6,),
        out_shape=jax.ShapeDtypeStruct(seeds.shape, jnp.float32),
        in_specs=[block(2 * BAND), block(rows), block(rows // 2)],
        out_specs=pl.BlockSpec((1, 1, depth, size_x, size_y), lambda c: (0, c, 0, 0, 0)),
        compiler_params=PARAMS,
    )(edge, mid, bands)


def any_lattice(seeds, material, decay, coupling, sub_size, tile_size):
    depth, size_x, size_y = seeds.shape[2:]
    spans = ((0, size_x),)
    tables = [SMEM, SMEM, VMEM, VMEM]
    shape = (PLANES, size_x, size_y)
    near, far = called(
        functools.partial(halo_kernel, spans, "sub"), [shape, shape], tables, decay, coupling, seeds, material
    )
    near, far = depth_exchange(near, far, sub_size, tile_size)
    weighted, = called(
        functools.partial(whole_kernel, spans, "sub", sub_size), [(6, depth, size_x, size_y)],
        tables + [VMEM, VMEM], decay, coupling, seeds, material, near, far,
    )
    side = math.isqrt(tile_size)
    prev_band = from_behind(weighted[:, :, size_x - BAND :, :], 1, tile_size)
    next_band = from_behind(weighted[:, :, :BAND, :], -1, tile_size)
    combined = weighted.at[:, :, :BAND, :].add(prev_band)
    combined = combined.at[:, :, size_x - BAND :, :].add(next_band)
    flat = (6, depth, size_x * BAND // size_y, size_y)
    thin = (6, depth, size_x, BAND)
    top_slab = combined[..., size_y - BAND :].reshape(flat)
    bottom_slab = combined[..., :BAND].reshape(flat)
    result = combined.at[..., :BAND].add(from_behind(top_slab, side, tile_size).reshape(thin))
    result = result.at[..., size_y - BAND :].add(from_behind(bottom_slab, -side, tile_size).reshape(thin))
    return result[None]


def solution(mesh):
    sub_size, tile_size = mesh.shape["sub"], mesh.shape["tile"]
    body = two_by_two if tile_size == 4 else any_lattice

    def on_device(seeds, material, decay, coupling):
        return body(seeds, material, decay, coupling, sub_size, tile_size)

    placed = (P("tile", None, "sub", None, None), P("tile", "sub", None, None), P(), P())
    return jax.shard_map(
        on_device,
        mesh=mesh,
        in_specs=placed,
        out_specs=P("tile", None, "sub", None, None),
        check_vma=False,
    )
```

```python
import functools
import math

import jax
import jax.numpy as jnp
from jax import lax
from jax.experimental import pallas as pl
from jax.experimental.pallas import tpu as pltpu
from jax.sharding import PartitionSpec as P

BAND = 32
STEPS = 2
HALO = 8
PLANES = 5

magnetic_coeff = 0.5


def lane_of(shape):
    return lax.broadcasted_iota(jnp.int32, shape, 1)


def row_of(shape):
    return lax.broadcasted_iota(jnp.int32, shape, 0)


def next_x(v):
    rows = v.shape[0]
    return jnp.where(row_of(v.shape) == rows - 1, 0.0, pltpu.roll(v, rows - 1, 0))


def prev_x(v):
    return jnp.where(row_of(v.shape) == 0, 0.0, pltpu.roll(v, 1, 0))


def next_y(v):
    lanes = v.shape[1]
    return jnp.where(lane_of(v.shape) == lanes - 1, 0.0, pltpu.roll(v, lanes - 1, 1))


def prev_y(v):
    return jnp.where(lane_of(v.shape) == 0, 0.0, pltpu.roll(v, 1, 1))


def plus_x(v):
    return next_x(v) - v


def plus_y(v):
    return next_y(v) - v


def minus_x(v):
    return v - prev_x(v)


def minus_y(v):
    return v - prev_y(v)


def looked_up(labels, entries):
    value = jnp.broadcast_to(entries[0], labels.shape)
    for m in range(1, len(entries)):
        value = jnp.where(labels == m, entries[m], value)
    return value


def update_h(h, v, v_after):
    depth = len(v[0])
    new = [[], [], []]
    for p in range(depth):
        vx, vy, vz = v[0][p], v[1][p], v[2][p]
        up_x, up_y = (v[0][p + 1], v[1][p + 1]) if p + 1 < depth else v_after
        dz_x = up_x - vx if up_x is not None else -vx
        dz_y = up_y - vy if up_y is not None else -vy
        new[0].append(h[0][p] + (plus_y(vz) - dz_y))
        new[1].append(h[1][p] + (dz_x - plus_x(vz)))
        new[2].append(h[2][p] + (plus_x(vy) - plus_y(vx)))
    return new


def update_e(e, ca, h, h_before):
    depth = len(h[0])
    new = [[], [], []]
    for p in range(depth):
        hx, hy, hz = h[0][p], h[1][p], h[2][p]
        low_x, low_y = (h[0][p - 1], h[1][p - 1]) if p > 0 else h_before
        dz_x = hx - low_x if low_x is not None else hx
        dz_y = hy - low_y if low_y is not None else hy
        new[0].append(ca[p] * e[0][p] - magnetic_coeff * (minus_y(hz) - dz_y))
        new[1].append(ca[p] * e[1][p] - magnetic_coeff * (dz_x - minus_x(hz)))
        new[2].append(ca[p] * e[2][p] - magnetic_coeff * (minus_x(hy) - minus_y(hx)))
    return new


def scaled(cb, e):
    return [[cb[p] * e[c][p] for p in range(len(cb))] for c in range(3)]


def joined(ref, index, spans):
    return jnp.concatenate([ref[*index, lo:hi] for lo, hi in spans], axis=0)


def prepared(e, h, labels, tables):
    ca = [looked_up(m, tables[0]) for m in labels]
    cb = [looked_up(m, tables[1]) for m in labels]
    return e, h, ca, cb


def loaded(seeds, material, table, spans):
    depth = seeds.shape[2]
    count = table.shape[0] // 2
    e = [[joined(seeds, (0, c, p), spans) for p in range(depth)] for c in range(3)]
    h = [[joined(seeds, (0, 3 + c, p), spans) for p in range(depth)] for c in range(3)]
    labels = [joined(material, (0, p), spans) for p in range(depth)]
    rows = [table[m : m + 1] for m in range(2 * count)]
    return prepared(e, h, labels, (rows[:count], rows[count:]))


NONE = (None, None)


def send_halos(sub, fields, near, far):
    odd = lax.rem(lax.axis_index(sub), 2) == 1
    e, h, ca, cb = fields
    v1 = scaled(cb, e)
    h1 = update_h(h, v1, NONE)
    e1 = update_e(e, ca, h1, NONE)
    v2 = scaled(cb, e1)
    h2 = update_h(h1, v2, NONE)
    up = (h1[0][-1], h1[1][-1], h2[0][-1], h2[1][-1], cb[-1])
    down = (v1[0][0], v1[1][0], v2[0][0], v2[1][0], cb[0])
    for k in range(PLANES):
        near[k] = jnp.where(odd, down[k], up[k])
        far[k] = jnp.where(odd, up[k], down[k])


def halo_kernel(spans, sub, table, seeds, material, near, far):
    send_halos(sub, loaded(seeds, material, table, spans), near, far)


def first_halo_kernel(spans, sub, decay, coupling, seeds, material, near, far, held, labels, tables, sems):
    copies = [
        pltpu.make_async_copy(decay, tables.at[0], sems.at[0]),
        pltpu.make_async_copy(coupling, tables.at[1], sems.at[1]),
    ]
    at = 0
    for lo, hi in spans:
        rows, here = pl.ds(lo, hi - lo), pl.ds(at, hi - lo)
        copies.append(pltpu.make_async_copy(seeds.at[0, :, :, rows], held.at[:, :, here], sems.at[len(copies)]))
        copies.append(pltpu.make_async_copy(material.at[0, :, rows], labels.at[:, here], sems.at[len(copies)]))
        at += hi - lo
    for copy in copies:
        copy.start()
    for copy in copies:
        copy.wait()
    depth = held.shape[1]
    e = [[held[c, p] for p in range(depth)] for c in range(3)]
    h = [[held[3 + c, p] for p in range(depth)] for c in range(3)]
    entries = [[tables[k, m] for m in range(tables.shape[1])] for k in range(2)]
    fields = prepared(e, h, [labels[p] for p in range(depth)], entries)
    send_halos(sub, fields, near, far)


def ramp(position, count):
    position = position.astype(jnp.float32) + 0.5
    return jnp.where(
        position < BAND,
        position / BAND,
        jnp.where(position > count - BAND, (count - position) / BAND, 1.0),
    )


def final_fields(fields, near, far, sub, sub_size):
    e, h, ca, cb = fields
    index = lax.axis_index(sub)
    odd = lax.rem(index, 2) == 1
    below, above = index > 0, index < sub_size - 1
    a = [near[k] for k in range(PLANES)]
    b = [far[k] for k in range(PLANES)]
    from_below = [jnp.where(odd, a[k], b[k]) for k in range(PLANES)]
    from_above = [jnp.where(above, jnp.where(odd, b[k], a[k]), 0.0) for k in range(PLANES)]
    part_h1x, part_h1y, part_h2x, part_h2y, cb_low = from_below
    v1x_up, v1y_up, part_v2x, part_v2y, cb_up = from_above

    v1 = scaled(cb, e)
    h1 = update_h(h, v1, (v1x_up, v1y_up))
    dh1x, dh1y = -v1[1][0], v1[0][0]
    h1_low = (jnp.where(below, part_h1x + dh1x, 0.0), jnp.where(below, part_h1y + dh1y, 0.0))
    e1 = update_e(e, ca, h1, h1_low)
    v2 = scaled(cb, e1)
    v2_up = (
        part_v2x - cb_up * (magnetic_coeff * h1[1][-1]),
        part_v2y + cb_up * (magnetic_coeff * h1[0][-1]),
    )
    h2 = update_h(h1, v2, v2_up)
    dv2x = cb_low * (magnetic_coeff * dh1y)
    dv2y = cb_low * (-magnetic_coeff * dh1x)
    dv2z = cb_low * (-magnetic_coeff * (minus_x(dh1y) - minus_y(dh1x)))
    h2x_low = part_h2x + (dh1x + (plus_y(dv2z) - (v2[1][0] - dv2y)))
    h2y_low = part_h2y + (dh1y + ((v2[0][0] - dv2x) - plus_x(dv2z)))
    h2_low = (jnp.where(below, h2x_low, 0.0), jnp.where(below, h2y_low, 0.0))
    e2 = update_e(e1, ca, h2, h2_low)
    return e2 + h2


def middle_out(block):
    return pltpu.roll(block, block.shape[1] // 2, 1)


def y_packed(first, second):
    lane = lane_of(first.shape)
    lanes = first.shape[1]
    middle = (lane >= BAND) & (lane < lanes - BAND)
    return jnp.where(middle, pltpu.roll(second, lanes // 2, 1), first)


def y_unpacked(block):
    lane = lane_of(block.shape)
    lanes = block.shape[1]
    a, b = pltpu.roll(block, BAND, 1), pltpu.roll(block, lanes - BAND, 1)
    middle = (lane >= BAND) & (lane < lanes - BAND)
    first = jnp.where(middle, 0.0, jnp.where(lane < BAND, a, b))
    second = jnp.where(middle, 0.0, jnp.where(lane < BAND, b, a))
    return first, second


def weighted_planes(seeds, material, table, near, far, spans, keeps, sub, sub_size):
    planes = final_fields(loaded(seeds, material, table, spans), near, far, sub, sub_size)
    size_x, size_y = seeds.shape[3:]
    at, results = 0, []
    for (lo, hi), (start, stop) in zip(spans, keeps):
        shape = (stop - start, size_y)
        weight = ramp(row_of(shape) + start, size_x) * ramp(lane_of(shape), size_y)
        first = at + start - lo
        results.append([[plane[first : first + stop - start] * weight for plane in part] for part in planes])
        at += hi - lo
    return results


def edge_kernel(spans, sub, sub_size, tile, table, seeds, material, near, far, edge, corner, strip):
    size_x = seeds.shape[3]
    keeps = ((0, BAND), (size_x - BAND, size_x))
    low, high = weighted_planes(seeds, material, table, near, far, spans, keeps, sub, sub_size)
    odd = lax.rem(lax.axis_index(tile), 2) == 1
    half = BAND // 2
    for c in range(6):
        for p in range(seeds.shape[2]):
            edge[c, p, :BAND] = low[c][p]
            edge[c, p, BAND:] = high[c][p]
            corner[c, p] = y_packed(low[c][p], high[c][p])
            away = jnp.where(odd, high[c][p], low[c][p])
            strip[c, p] = y_packed(middle_out(away[:half]), middle_out(away[half:]))


def middle_kernel(spans, sub, sub_size, table, seeds, material, near, far, mid, bands):
    size_x = seeds.shape[3]
    keep = (BAND, size_x - BAND)
    planes, = weighted_planes(seeds, material, table, near, far, spans, (keep,), sub, sub_size)
    half = (keep[1] - keep[0]) // 2
    for c in range(6):
        for p in range(seeds.shape[2]):
            mid[c, p] = planes[c][p]
            bands[c, p] = y_packed(planes[c][p][:half], planes[c][p][half:])


def whole_kernel(spans, sub, sub_size, table, seeds, material, near, far, out):
    planes, = weighted_planes(seeds, material, table, near, far, spans, spans, sub, sub_size)
    for c in range(6):
        for p in range(seeds.shape[2]):
            out[c, p] = planes[c][p]


def corner_kernel(tile, edge, corner, summed, send):
    odd = lax.rem(lax.axis_index(tile), 2) == 1
    half = BAND // 2
    for c in range(edge.shape[0]):
        for p in range(edge.shape[1]):
            first, second = y_unpacked(corner[c, p])
            low = edge[c, p, :BAND] + first
            high = edge[c, p, BAND:] + second
            summed[c, p, :BAND] = low
            summed[c, p, BAND:] = high
            by, away = jnp.where(odd, low, high), jnp.where(odd, high, low)
            send[c, p, :BAND] = by
            send[c, p, BAND:] = y_packed(away[:half], away[half:])


def seam_kernel(tile, summed, got, strip, out):
    odd = lax.rem(lax.axis_index(tile), 2) == 1
    half = BAND // 2
    for c in range(summed.shape[0]):
        for p in range(summed.shape[1]):
            by = got[c, p, :BAND]
            corners = y_unpacked(got[c, p, BAND:])
            block = strip[c, p]
            lane = lane_of(block.shape)
            middle = (lane >= BAND) & (lane < block.shape[1] - BAND)
            first = jnp.where(middle, middle_out(block), corners[0])
            second = jnp.where(middle, block, corners[1])
            away = jnp.concatenate([first, second], axis=0)
            out[c, p, :BAND] = summed[c, p, :BAND] + jnp.where(odd, by, away)
            out[c, p, BAND:] = summed[c, p, BAND:] + jnp.where(odd, away, by)


def last_kernel(edge, mid, bands, out, whole, sems):
    half = bands.shape[2]
    size_x = out.shape[3]
    copies = []
    for c in range(mid.shape[0]):
        for p in range(mid.shape[1]):
            first, second = y_unpacked(bands[c, p])
            whole[c, p, :BAND] = edge[c, p, :BAND]
            whole[c, p, BAND : BAND + half] = mid[c, p, :half] + first
            whole[c, p, BAND + half : size_x - BAND] = mid[c, p, half:] + second
            whole[c, p, size_x - BAND :] = edge[c, p, BAND:]
        copies.append(pltpu.make_async_copy(whole.at[c], out.at[0, c], sems.at[c]))
        copies[-1].start()
    for copy in copies:
        copy.wait()


HBM = pl.BlockSpec(memory_space=pltpu.HBM)
VMEM = pl.BlockSpec(memory_space=pltpu.VMEM)
PARAMS = pltpu.CompilerParams(vmem_limit_bytes=32 * 1024 * 1024)


def called(kernel, shapes, *operands):
    outs = [jax.ShapeDtypeStruct(shape, jnp.float32) for shape in shapes]
    return pl.pallas_call(
        kernel,
        out_shape=outs,
        in_specs=[VMEM] * len(operands),
        out_specs=[VMEM] * len(outs),
        compiler_params=PARAMS,
    )(*operands)


def after(first, *values):
    return lax.optimization_barrier((first, *values))


def depth_exchange(near, far, sub_size, tile_size):
    near = lax.ppermute(near, "sub", [(i, i ^ 1) for i in range(sub_size)])
    pairs = []
    for t in range(tile_size):
        for i in range(sub_size):
            other = (i + 1) ^ 1
            j = other - 1
            if 0 <= j < sub_size:
                pairs.append((t * sub_size + i, t * sub_size + j))
            else:
                pairs.append((t * sub_size + i, (t ^ 1) * sub_size + i))
    far = lax.ppermute(far, ("tile", "sub"), pairs)
    return near, far


def swapped(value, bits, tile_size):
    return lax.ppermute(value, "tile", [(t, t ^ bits) for t in range(tile_size)])


def from_behind(value, steps, count):
    return lax.ppermute(value, "tile", [(t, (t + steps) % count) for t in range(count)])


def table_rows(decay, coupling, size_y):
    entries = jnp.concatenate([decay, coupling])
    return jnp.broadcast_to(entries[:, None], (entries.shape[0], size_y))


def two_by_two(seeds, material, decay, coupling, sub_size, tile_size):
    depth, size_x, size_y = seeds.shape[2:]
    edges = ((0, BAND + HALO), (size_x - BAND - HALO, size_x))
    inner = ((BAND - HALO, size_x - BAND + HALO),)
    rows = size_x - 2 * BAND
    count = sum(hi - lo for lo, hi in edges)

    shape = jax.ShapeDtypeStruct((PLANES, count, size_y), jnp.float32)
    near, far = pl.pallas_call(
        functools.partial(first_halo_kernel, edges, "sub"),
        out_shape=[shape, shape],
        in_specs=[HBM] * 4,
        out_specs=[VMEM] * 2,
        scratch_shapes=[
            pltpu.VMEM((6, depth, count, size_y), jnp.float32),
            pltpu.VMEM((depth, count, size_y), jnp.int32),
            pltpu.SMEM((2, *decay.shape), jnp.float32),
            pltpu.SemaphoreType.DMA((2 + 2 * len(edges),)),
        ],
        compiler_params=PARAMS,
    )(*(pltpu.with_memory_space_constraint(x, pltpu.HBM) for x in (decay, coupling, seeds, material)))
    table = table_rows(decay, coupling, size_y)
    edge_near, edge_far = depth_exchange(near, far, sub_size, tile_size)
    edge_near, table = after(edge_near, table)

    shape = (PLANES, rows + 2 * HALO, size_y)
    near, far = called(functools.partial(halo_kernel, inner, "sub"), [shape, shape], table, seeds, material)
    edge_far, near, far = after(edge_far, near, far)
    inner_near, inner_far = depth_exchange(near, far, sub_size, tile_size)

    edge, corner, strip = called(
        functools.partial(edge_kernel, edges, "sub", sub_size, "tile"),
        [(6, depth, 2 * BAND, size_y), (6, depth, BAND, size_y), (6, depth, BAND // 2, size_y)],
        table, seeds, material, edge_near, edge_far,
    )
    corner = swapped(corner, 2, tile_size)
    strip = swapped(strip, 3, tile_size)
    mid, bands = called(
        functools.partial(middle_kernel, inner, "sub", sub_size),
        [(6, depth, rows, size_y), (6, depth, rows // 2, size_y)],
        table, seeds, material, inner_near, inner_far,
    )
    corner, bands = after(corner, bands)
    bands = swapped(bands, 2, tile_size)
    summed, send = called(
        functools.partial(corner_kernel, "tile"),
        [(6, depth, 2 * BAND, size_y), (6, depth, BAND + BAND // 2, size_y)],
        edge, corner,
    )
    got = swapped(send, 1, tile_size)
    edge, = called(
        functools.partial(seam_kernel, "tile"), [(6, depth, 2 * BAND, size_y)], summed, got, strip
    )
    return pl.pallas_call(
        last_kernel,
        out_shape=jax.ShapeDtypeStruct(seeds.shape, jnp.float32),
        in_specs=[VMEM] * 3,
        out_specs=HBM,
        scratch_shapes=[pltpu.VMEM(seeds.shape[1:], jnp.float32), pltpu.SemaphoreType.DMA((6,))],
        compiler_params=PARAMS,
    )(edge, mid, bands)


def any_lattice(seeds, material, decay, coupling, sub_size, tile_size):
    depth, size_x, size_y = seeds.shape[2:]
    spans = ((0, size_x),)
    table = table_rows(decay, coupling, size_y)
    shape = (PLANES, size_x, size_y)
    near, far = called(functools.partial(halo_kernel, spans, "sub"), [shape, shape], table, seeds, material)
    near, far = depth_exchange(near, far, sub_size, tile_size)
    weighted, = called(
        functools.partial(whole_kernel, spans, "sub", sub_size), [(6, depth, size_x, size_y)],
        table, seeds, material, near, far,
    )
    side = math.isqrt(tile_size)
    prev_band = from_behind(weighted[:, :, size_x - BAND :, :], 1, tile_size)
    next_band = from_behind(weighted[:, :, :BAND, :], -1, tile_size)
    combined = weighted.at[:, :, :BAND, :].add(prev_band)
    combined = combined.at[:, :, size_x - BAND :, :].add(next_band)
    flat = (6, depth, size_x * BAND // size_y, size_y)
    thin = (6, depth, size_x, BAND)
    top_slab = combined[..., size_y - BAND :].reshape(flat)
    bottom_slab = combined[..., :BAND].reshape(flat)
    result = combined.at[..., :BAND].add(from_behind(top_slab, side, tile_size).reshape(thin))
    result = result.at[..., size_y - BAND :].add(from_behind(bottom_slab, -side, tile_size).reshape(thin))
    return result[None]


def solution(mesh):
    sub_size, tile_size = mesh.shape["sub"], mesh.shape["tile"]
    body = two_by_two if tile_size == 4 else any_lattice

    def on_device(seeds, material, decay, coupling):
        return body(seeds, material, decay, coupling, sub_size, tile_size)

    placed = (P("tile", None, "sub", None, None), P("tile", "sub", None, None), P(), P())
    return jax.shard_map(
        on_device,
        mesh=mesh,
        in_specs=placed,
        out_specs=P("tile", None, "sub", None, None),
        check_vma=False,
    )
```

```python
import functools
import math

import jax
import jax.numpy as jnp
from jax import lax
from jax.experimental import pallas as pl
from jax.experimental.pallas import tpu as pltpu
from jax.sharding import PartitionSpec as P

BAND = 32
STEPS = 2
HALO = 8
PLANES = 5
REACH = 4

magnetic_coeff = 0.5


def lane_of(shape):
    return lax.broadcasted_iota(jnp.int32, shape, 1)


def row_of(shape):
    return lax.broadcasted_iota(jnp.int32, shape, 0)


def next_x(v):
    rows = v.shape[0]
    return jnp.where(row_of(v.shape) == rows - 1, 0.0, pltpu.roll(v, rows - 1, 0))


def prev_x(v):
    return jnp.where(row_of(v.shape) == 0, 0.0, pltpu.roll(v, 1, 0))


def next_y(v):
    lanes = v.shape[1]
    return jnp.where(lane_of(v.shape) == lanes - 1, 0.0, pltpu.roll(v, lanes - 1, 1))


def prev_y(v):
    return jnp.where(lane_of(v.shape) == 0, 0.0, pltpu.roll(v, 1, 1))


def plus_x(v):
    return next_x(v) - v


def plus_y(v):
    return next_y(v) - v


def minus_x(v):
    return v - prev_x(v)


def minus_y(v):
    return v - prev_y(v)


def looked_up(labels, entries):
    value = jnp.broadcast_to(entries[0], labels.shape)
    for m in range(1, len(entries)):
        value = jnp.where(labels == m, entries[m], value)
    return value


def update_h(h, v, v_after):
    depth = len(v[0])
    new = [[], [], []]
    for p in range(depth):
        vx, vy, vz = v[0][p], v[1][p], v[2][p]
        up_x, up_y = (v[0][p + 1], v[1][p + 1]) if p + 1 < depth else v_after
        dz_x = up_x - vx if up_x is not None else -vx
        dz_y = up_y - vy if up_y is not None else -vy
        new[0].append(h[0][p] + (plus_y(vz) - dz_y))
        new[1].append(h[1][p] + (dz_x - plus_x(vz)))
        new[2].append(h[2][p] + (plus_x(vy) - plus_y(vx)))
    return new


def update_e(e, ca, h, h_before):
    depth = len(h[0])
    new = [[], [], []]
    for p in range(depth):
        hx, hy, hz = h[0][p], h[1][p], h[2][p]
        low_x, low_y = (h[0][p - 1], h[1][p - 1]) if p > 0 else h_before
        dz_x = hx - low_x if low_x is not None else hx
        dz_y = hy - low_y if low_y is not None else hy
        new[0].append(ca[p] * e[0][p] - magnetic_coeff * (minus_y(hz) - dz_y))
        new[1].append(ca[p] * e[1][p] - magnetic_coeff * (dz_x - minus_x(hz)))
        new[2].append(ca[p] * e[2][p] - magnetic_coeff * (minus_x(hy) - minus_y(hx)))
    return new


def scaled(cb, e):
    return [[cb[p] * e[c][p] for p in range(len(cb))] for c in range(3)]


def joined(ref, index, spans):
    return jnp.concatenate([ref[*index, lo:hi] for lo, hi in spans], axis=0)


def prepared(e, h, labels, tables):
    ca = [looked_up(m, tables[0]) for m in labels]
    cb = [looked_up(m, tables[1]) for m in labels]
    return e, h, ca, cb


def loaded(seeds, material, table, spans):
    depth = seeds.shape[2]
    count = table.shape[0] // 2
    e = [[joined(seeds, (0, c, p), spans) for p in range(depth)] for c in range(3)]
    h = [[joined(seeds, (0, 3 + c, p), spans) for p in range(depth)] for c in range(3)]
    labels = [joined(material, (0, p), spans) for p in range(depth)]
    rows = [table[m : m + 1] for m in range(2 * count)]
    return prepared(e, h, labels, (rows[:count], rows[count:]))


NONE = (None, None)


def send_halos(sub, fields, near, far, packed=lambda block: block):
    odd = lax.rem(lax.axis_index(sub), 2) == 1
    e, h, ca, cb = fields
    v1 = scaled(cb, e)
    h1 = update_h(h, v1, NONE)
    e1 = update_e(e, ca, h1, NONE)
    v2 = scaled(cb, e1)
    h2 = update_h(h1, v2, NONE)
    up = (h1[0][-1], h1[1][-1], h2[0][-1], h2[1][-1], cb[-1])
    down = (v1[0][0], v1[1][0], v2[0][0], v2[1][0], cb[0])
    for k in range(PLANES):
        near[k] = packed(jnp.where(odd, down[k], up[k]))
        far[k] = packed(jnp.where(odd, up[k], down[k]))


def halo_kernel(spans, sub, table, seeds, material, near, far):
    send_halos(sub, loaded(seeds, material, table, spans), near, far)


def first_halo_kernel(spans, sub, decay, coupling, seeds, material, near, far, held, labels, tables, sems):
    copies = [
        pltpu.make_async_copy(decay, tables.at[0], sems.at[0]),
        pltpu.make_async_copy(coupling, tables.at[1], sems.at[1]),
    ]
    at = 0
    for lo, hi in spans:
        rows, here = pl.ds(lo, hi - lo), pl.ds(at, hi - lo)
        copies.append(pltpu.make_async_copy(seeds.at[0, :, :, rows], held.at[:, :, here], sems.at[len(copies)]))
        copies.append(pltpu.make_async_copy(material.at[0, :, rows], labels.at[:, here], sems.at[len(copies)]))
        at += hi - lo
    for copy in copies:
        copy.start()
    for copy in copies:
        copy.wait()
    depth = held.shape[1]
    e = [[held[c, p] for p in range(depth)] for c in range(3)]
    h = [[held[3 + c, p] for p in range(depth)] for c in range(3)]
    entries = [[tables[k, m] for m in range(tables.shape[1])] for k in range(2)]
    fields = prepared(e, h, [labels[p] for p in range(depth)], entries)
    send_halos(sub, fields, near, far)


def ramp(position, count):
    position = position.astype(jnp.float32) + 0.5
    return jnp.where(
        position < BAND,
        position / BAND,
        jnp.where(position > count - BAND, (count - position) / BAND, 1.0),
    )


def final_fields(fields, near, far, sub, sub_size, unpacked=lambda block: block):
    e, h, ca, cb = fields
    index = lax.axis_index(sub)
    odd = lax.rem(index, 2) == 1
    below, above = index > 0, index < sub_size - 1
    a = [unpacked(near[k]) for k in range(PLANES)]
    b = [unpacked(far[k]) for k in range(PLANES)]
    from_below = [jnp.where(odd, a[k], b[k]) for k in range(PLANES)]
    from_above = [jnp.where(above, jnp.where(odd, b[k], a[k]), 0.0) for k in range(PLANES)]
    part_h1x, part_h1y, part_h2x, part_h2y, cb_low = from_below
    v1x_up, v1y_up, part_v2x, part_v2y, cb_up = from_above

    v1 = scaled(cb, e)
    h1 = update_h(h, v1, (v1x_up, v1y_up))
    dh1x, dh1y = -v1[1][0], v1[0][0]
    h1_low = (jnp.where(below, part_h1x + dh1x, 0.0), jnp.where(below, part_h1y + dh1y, 0.0))
    e1 = update_e(e, ca, h1, h1_low)
    v2 = scaled(cb, e1)
    v2_up = (
        part_v2x - cb_up * (magnetic_coeff * h1[1][-1]),
        part_v2y + cb_up * (magnetic_coeff * h1[0][-1]),
    )
    h2 = update_h(h1, v2, v2_up)
    dv2x = cb_low * (magnetic_coeff * dh1y)
    dv2y = cb_low * (-magnetic_coeff * dh1x)
    dv2z = cb_low * (-magnetic_coeff * (minus_x(dh1y) - minus_y(dh1x)))
    h2x_low = part_h2x + (dh1x + (plus_y(dv2z) - (v2[1][0] - dv2y)))
    h2y_low = part_h2y + (dh1y + ((v2[0][0] - dv2x) - plus_x(dv2z)))
    h2_low = (jnp.where(below, h2x_low, 0.0), jnp.where(below, h2y_low, 0.0))
    e2 = update_e(e1, ca, h2, h2_low)
    return e2 + h2


def middle_out(block):
    return pltpu.roll(block, block.shape[1] // 2, 1)


def y_packed(first, second):
    lane = lane_of(first.shape)
    lanes = first.shape[1]
    middle = (lane >= BAND) & (lane < lanes - BAND)
    return jnp.where(middle, pltpu.roll(second, lanes // 2, 1), first)


def y_unpacked(block):
    lane = lane_of(block.shape)
    lanes = block.shape[1]
    a, b = pltpu.roll(block, BAND, 1), pltpu.roll(block, lanes - BAND, 1)
    middle = (lane >= BAND) & (lane < lanes - BAND)
    first = jnp.where(middle, 0.0, jnp.where(lane < BAND, a, b))
    second = jnp.where(middle, 0.0, jnp.where(lane < BAND, b, a))
    return first, second


def bands_packed(block):
    rows, lanes = block.shape
    half = rows // 2
    side = jnp.zeros((8, lanes), block.dtype)
    lane = lane_of(side.shape)
    for g in range(rows // 8):
        piece = block[8 * g : 8 * g + 8]
        at = 2 * REACH * g
        low = pltpu.roll(piece, (at - BAND) % lanes, 1)
        high = pltpu.roll(piece, (at + 2 * REACH - lanes + BAND) % lanes, 1)
        side = jnp.where((lane >= at) & (lane < at + REACH), low, side)
        side = jnp.where((lane >= at + REACH) & (lane < at + 2 * REACH), high, side)
    return jnp.concatenate([y_packed(block[:half], block[half:]), side], axis=0)


def bands_unpacked(packed):
    half, lanes = packed.shape[0] - 8, packed.shape[1]
    main, side = packed[:half], packed[half:]
    lane = lane_of(main.shape)
    middle = (lane >= BAND) & (lane < lanes - BAND)
    block = jnp.concatenate([jnp.where(middle, 0.0, main), jnp.where(middle, 0.0, middle_out(main))], axis=0)
    lane = lane_of(side.shape)
    pieces = []
    for g in range(2 * half // 8):
        at = 2 * REACH * g
        low = pltpu.roll(side, (BAND - at) % lanes, 1)
        high = pltpu.roll(side, (lanes - BAND - 2 * REACH - at) % lanes, 1)
        piece = block[8 * g : 8 * g + 8]
        piece = jnp.where((lane >= BAND) & (lane < BAND + REACH), low, piece)
        pieces.append(jnp.where((lane >= lanes - BAND - REACH) & (lane < lanes - BAND), high, piece))
    return jnp.concatenate(pieces, axis=0)


def share_kernel(spans, seeds, material, shared):
    depth = seeds.shape[2]
    for c in range(6):
        for p in range(depth):
            shared[depth * c + p] = bands_packed(joined(seeds, (0, c, p), spans))
    for p in range(depth):
        shared[6 * depth + p] = bands_packed(joined(material, (0, p), spans).astype(jnp.float32))


def shared_fields(table, shared):
    depth = shared.shape[0] // 7
    count = table.shape[0] // 2
    planes = [bands_unpacked(shared[k]) for k in range(7 * depth)]
    f = [planes[depth * c : depth * (c + 1)] for c in range(7)]
    rows = [table[m : m + 1] for m in range(2 * count)]
    return prepared(f[:3], f[3:6], f[6], (rows[:count], rows[count:]))


def shared_halo_kernel(sub, table, shared, near, far):
    send_halos(sub, shared_fields(table, shared), near, far, bands_packed)


def weighted_planes(seeds, material, table, near, far, spans, keeps, sub, sub_size):
    planes = final_fields(loaded(seeds, material, table, spans), near, far, sub, sub_size)
    return weighted(planes, spans, keeps, *seeds.shape[3:])


def weighted(planes, spans, keeps, size_x, size_y):
    at, results = 0, []
    for (lo, hi), (start, stop) in zip(spans, keeps):
        shape = (stop - start, size_y)
        weight = ramp(row_of(shape) + start, size_x) * ramp(lane_of(shape), size_y)
        first = at + start - lo
        results.append([[plane[first : first + stop - start] * weight for plane in part] for part in planes])
        at += hi - lo
    return results


def edge_keeps(size_x):
    return ((0, BAND), (size_x - BAND, size_x))


def edge_kernel(spans, sub, sub_size, tile, table, seeds, material, near, far, edge, strip):
    keeps = edge_keeps(seeds.shape[3])
    low, high = weighted_planes(seeds, material, table, near, far, spans, keeps, sub, sub_size)
    odd = lax.rem(lax.axis_index(tile), 2) == 1
    half = BAND // 2
    for c in range(6):
        for p in range(seeds.shape[2]):
            edge[c, p, :BAND] = low[c][p]
            edge[c, p, BAND:] = high[c][p]
            away = jnp.where(odd, high[c][p], low[c][p])
            strip[c, p] = y_packed(middle_out(away[:half]), middle_out(away[half:]))


def middle_kernel(spans, sub, sub_size, table, seeds, material, near, far, mid, bands):
    size_x = seeds.shape[3]
    keep = (BAND, size_x - BAND)
    planes, = weighted_planes(seeds, material, table, near, far, spans, (keep,), sub, sub_size)
    half = (keep[1] - keep[0]) // 2
    for c in range(6):
        for p in range(seeds.shape[2]):
            mid[c, p] = planes[c][p]
            bands[c, p] = y_packed(planes[c][p][:half], planes[c][p][half:])


def whole_kernel(spans, sub, sub_size, table, seeds, material, near, far, out):
    planes, = weighted_planes(seeds, material, table, near, far, spans, spans, sub, sub_size)
    for c in range(6):
        for p in range(seeds.shape[2]):
            out[c, p] = planes[c][p]


def y_swapped(block):
    lane = lane_of(block.shape)
    lanes = block.shape[1]
    a, b = pltpu.roll(block, BAND, 1), pltpu.roll(block, lanes - BAND, 1)
    middle = (lane >= BAND) & (lane < lanes - BAND)
    return jnp.where(middle, 0.0, jnp.where(lane < BAND, a, b))


def corner_kernel(spans, size_x, sub, sub_size, tile, table, shared, near, far, edge, summed, send):
    planes = final_fields(shared_fields(table, shared), near, far, sub, sub_size, bands_unpacked)
    low_part, high_part = weighted(planes, spans, edge_keeps(size_x), size_x, edge.shape[3])
    odd = lax.rem(lax.axis_index(tile), 2) == 1
    half = BAND // 2
    for c in range(edge.shape[0]):
        for p in range(edge.shape[1]):
            low = edge[c, p, :BAND] + y_swapped(low_part[c][p])
            high = edge[c, p, BAND:] + y_swapped(high_part[c][p])
            summed[c, p, :BAND] = low
            summed[c, p, BAND:] = high
            by, away = jnp.where(odd, low, high), jnp.where(odd, high, low)
            send[c, p, :BAND] = by
            send[c, p, BAND:] = y_packed(away[:half], away[half:])


def seam_kernel(tile, summed, got, strip, out):
    odd = lax.rem(lax.axis_index(tile), 2) == 1
    half = BAND // 2
    for c in range(summed.shape[0]):
        for p in range(summed.shape[1]):
            by = got[c, p, :BAND]
            corners = y_unpacked(got[c, p, BAND:])
            block = strip[c, p]
            lane = lane_of(block.shape)
            middle = (lane >= BAND) & (lane < block.shape[1] - BAND)
            first = jnp.where(middle, middle_out(block), corners[0])
            second = jnp.where(middle, block, corners[1])
            away = jnp.concatenate([first, second], axis=0)
            out[c, p, :BAND] = summed[c, p, :BAND] + jnp.where(odd, by, away)
            out[c, p, BAND:] = summed[c, p, BAND:] + jnp.where(odd, away, by)


def last_kernel(edge, mid, bands, out, whole, sems):
    half = bands.shape[2]
    size_x = out.shape[3]
    copies = []
    for c in range(mid.shape[0]):
        for p in range(mid.shape[1]):
            first, second = y_unpacked(bands[c, p])
            whole[c, p, :BAND] = edge[c, p, :BAND]
            whole[c, p, BAND : BAND + half] = mid[c, p, :half] + first
            whole[c, p, BAND + half : size_x - BAND] = mid[c, p, half:] + second
            whole[c, p, size_x - BAND :] = edge[c, p, BAND:]
        copies.append(pltpu.make_async_copy(whole.at[c], out.at[0, c], sems.at[c]))
        copies[-1].start()
    for copy in copies:
        copy.wait()


HBM = pl.BlockSpec(memory_space=pltpu.HBM)
VMEM = pl.BlockSpec(memory_space=pltpu.VMEM)
PARAMS = pltpu.CompilerParams(vmem_limit_bytes=32 * 1024 * 1024)


def called(kernel, shapes, *operands):
    outs = [jax.ShapeDtypeStruct(shape, jnp.float32) for shape in shapes]
    return pl.pallas_call(
        kernel,
        out_shape=outs,
        in_specs=[VMEM] * len(operands),
        out_specs=[VMEM] * len(outs),
        compiler_params=PARAMS,
    )(*operands)


def after(first, *values):
    return lax.optimization_barrier((first, *values))


def depth_exchange(near, far, sub_size, tile_size):
    near = lax.ppermute(near, "sub", [(i, i ^ 1) for i in range(sub_size)])
    pairs = []
    for t in range(tile_size):
        for i in range(sub_size):
            other = (i + 1) ^ 1
            j = other - 1
            if 0 <= j < sub_size:
                pairs.append((t * sub_size + i, t * sub_size + j))
            else:
                pairs.append((t * sub_size + i, (t ^ 1) * sub_size + i))
    far = lax.ppermute(far, ("tile", "sub"), pairs)
    return near, far


def swapped(value, bits, tile_size):
    return lax.ppermute(value, "tile", [(t, t ^ bits) for t in range(tile_size)])


def from_behind(value, steps, count):
    return lax.ppermute(value, "tile", [(t, (t + steps) % count) for t in range(count)])


def table_rows(decay, coupling, size_y):
    entries = jnp.concatenate([decay, coupling])
    return jnp.broadcast_to(entries[:, None], (entries.shape[0], size_y))


def two_by_two(seeds, material, decay, coupling, sub_size, tile_size):
    depth, size_x, size_y = seeds.shape[2:]
    edges = ((0, BAND + HALO), (size_x - BAND - HALO, size_x))
    inner = ((BAND - HALO, size_x - BAND + HALO),)
    rows = size_x - 2 * BAND
    edge_rows, inner_rows = 2 * (BAND + HALO), rows + 2 * HALO
    packed_rows = edge_rows // 2 + 8

    shape = jax.ShapeDtypeStruct((PLANES, inner_rows, size_y), jnp.float32)
    near, far = pl.pallas_call(
        functools.partial(first_halo_kernel, inner, "sub"),
        out_shape=[shape, shape],
        in_specs=[HBM] * 4,
        out_specs=[VMEM] * 2,
        scratch_shapes=[
            pltpu.VMEM((6, depth, inner_rows, size_y), jnp.float32),
            pltpu.VMEM((depth, inner_rows, size_y), jnp.int32),
            pltpu.SMEM((2, *decay.shape), jnp.float32),
            pltpu.SemaphoreType.DMA((2 + 2 * len(inner),)),
        ],
        compiler_params=PARAMS,
    )(*(pltpu.with_memory_space_constraint(x, pltpu.HBM) for x in (decay, coupling, seeds, material)))
    near, seeds, material = after(near, seeds, material)
    inner_near, inner_far = depth_exchange(near, far, sub_size, tile_size)
    shared, = called(
        functools.partial(share_kernel, edges), [(7 * depth, packed_rows, size_y)], seeds, material
    )
    shared = swapped(shared, 2, tile_size)

    inner_near, table = after(inner_near, table_rows(decay, coupling, size_y))
    shape = (PLANES, edge_rows, size_y)
    near, far = called(functools.partial(halo_kernel, edges, "sub"), [shape, shape], table, seeds, material)
    inner_far, near, far = after(inner_far, near, far)
    edge_near, edge_far = depth_exchange(near, far, sub_size, tile_size)

    mid, bands = called(
        functools.partial(middle_kernel, inner, "sub", sub_size),
        [(6, depth, rows, size_y), (6, depth, rows // 2, size_y)],
        table, seeds, material, inner_near, inner_far,
    )
    bands = swapped(bands, 2, tile_size)

    shape = (PLANES, packed_rows, size_y)
    near, far = called(functools.partial(shared_halo_kernel, "sub"), [shape, shape], table, shared)
    near, far = depth_exchange(near, far, sub_size, tile_size)

    edge, strip = called(
        functools.partial(edge_kernel, edges, "sub", sub_size, "tile"),
        [(6, depth, 2 * BAND, size_y), (6, depth, BAND // 2, size_y)],
        table, seeds, material, edge_near, edge_far,
    )
    strip = swapped(strip, 3, tile_size)
    summed, send = called(
        functools.partial(corner_kernel, edges, size_x, "sub", sub_size, "tile"),
        [(6, depth, 2 * BAND, size_y), (6, depth, BAND + BAND // 2, size_y)],
        table, shared, near, far, edge,
    )
    got = swapped(send, 1, tile_size)
    edge, = called(
        functools.partial(seam_kernel, "tile"), [(6, depth, 2 * BAND, size_y)], summed, got, strip
    )
    return pl.pallas_call(
        last_kernel,
        out_shape=jax.ShapeDtypeStruct(seeds.shape, jnp.float32),
        in_specs=[VMEM] * 3,
        out_specs=HBM,
        scratch_shapes=[pltpu.VMEM(seeds.shape[1:], jnp.float32), pltpu.SemaphoreType.DMA((6,))],
        compiler_params=PARAMS,
    )(edge, mid, bands)


def any_lattice(seeds, material, decay, coupling, sub_size, tile_size):
    depth, size_x, size_y = seeds.shape[2:]
    spans = ((0, size_x),)
    table = table_rows(decay, coupling, size_y)
    shape = (PLANES, size_x, size_y)
    near, far = called(functools.partial(halo_kernel, spans, "sub"), [shape, shape], table, seeds, material)
    near, far = depth_exchange(near, far, sub_size, tile_size)
    weighted, = called(
        functools.partial(whole_kernel, spans, "sub", sub_size), [(6, depth, size_x, size_y)],
        table, seeds, material, near, far,
    )
    side = math.isqrt(tile_size)
    prev_band = from_behind(weighted[:, :, size_x - BAND :, :], 1, tile_size)
    next_band = from_behind(weighted[:, :, :BAND, :], -1, tile_size)
    combined = weighted.at[:, :, :BAND, :].add(prev_band)
    combined = combined.at[:, :, size_x - BAND :, :].add(next_band)
    flat = (6, depth, size_x * BAND // size_y, size_y)
    thin = (6, depth, size_x, BAND)
    top_slab = combined[..., size_y - BAND :].reshape(flat)
    bottom_slab = combined[..., :BAND].reshape(flat)
    result = combined.at[..., :BAND].add(from_behind(top_slab, side, tile_size).reshape(thin))
    result = result.at[..., size_y - BAND :].add(from_behind(bottom_slab, -side, tile_size).reshape(thin))
    return result[None]


def solution(mesh):
    sub_size, tile_size = mesh.shape["sub"], mesh.shape["tile"]
    body = two_by_two if tile_size == 4 else any_lattice

    def on_device(seeds, material, decay, coupling):
        return body(seeds, material, decay, coupling, sub_size, tile_size)

    placed = (P("tile", None, "sub", None, None), P("tile", "sub", None, None), P(), P())
    return jax.shard_map(
        on_device,
        mesh=mesh,
        in_specs=placed,
        out_specs=P("tile", None, "sub", None, None),
        check_vma=False,
    )
```

```python
import functools
import math

import jax
import jax.numpy as jnp
from jax import lax
from jax.experimental import pallas as pl
from jax.experimental.pallas import tpu as pltpu
from jax.sharding import PartitionSpec as P

BAND = 32
STEPS = 2
HALO = 8
PLANES = 5
REACH = 4
SHARED = 64
LARGE, SMALL = 10**10, 6 * 10**8

magnetic_coeff = 0.5


def lane_of(shape):
    return lax.broadcasted_iota(jnp.int32, shape, 1)


def row_of(shape):
    return lax.broadcasted_iota(jnp.int32, shape, 0)


def next_x(v):
    rows = v.shape[0]
    return jnp.where(row_of(v.shape) == rows - 1, 0.0, pltpu.roll(v, rows - 1, 0))


def prev_x(v):
    return jnp.where(row_of(v.shape) == 0, 0.0, pltpu.roll(v, 1, 0))


def next_y(v):
    lanes = v.shape[1]
    return jnp.where(lane_of(v.shape) == lanes - 1, 0.0, pltpu.roll(v, lanes - 1, 1))


def prev_y(v):
    return jnp.where(lane_of(v.shape) == 0, 0.0, pltpu.roll(v, 1, 1))


def plus_x(v):
    return next_x(v) - v


def plus_y(v):
    return next_y(v) - v


def minus_x(v):
    return v - prev_x(v)


def minus_y(v):
    return v - prev_y(v)


def looked_up(labels, entries):
    value = jnp.broadcast_to(entries[0], labels.shape)
    for m in range(1, len(entries)):
        value = jnp.where(labels == m, entries[m], value)
    return value


def update_h(h, v, v_after):
    depth = len(v[0])
    new = [[], [], []]
    for p in range(depth):
        vx, vy, vz = v[0][p], v[1][p], v[2][p]
        up_x, up_y = (v[0][p + 1], v[1][p + 1]) if p + 1 < depth else v_after
        dz_x = up_x - vx if up_x is not None else -vx
        dz_y = up_y - vy if up_y is not None else -vy
        new[0].append(h[0][p] + (plus_y(vz) - dz_y))
        new[1].append(h[1][p] + (dz_x - plus_x(vz)))
        new[2].append(h[2][p] + (plus_x(vy) - plus_y(vx)))
    return new


def update_e(e, ca, h, h_before):
    depth = len(h[0])
    new = [[], [], []]
    for p in range(depth):
        hx, hy, hz = h[0][p], h[1][p], h[2][p]
        low_x, low_y = (h[0][p - 1], h[1][p - 1]) if p > 0 else h_before
        dz_x = hx - low_x if low_x is not None else hx
        dz_y = hy - low_y if low_y is not None else hy
        new[0].append(ca[p] * e[0][p] - magnetic_coeff * (minus_y(hz) - dz_y))
        new[1].append(ca[p] * e[1][p] - magnetic_coeff * (dz_x - minus_x(hz)))
        new[2].append(ca[p] * e[2][p] - magnetic_coeff * (minus_x(hy) - minus_y(hx)))
    return new


def scaled(cb, e):
    return [[cb[p] * e[c][p] for p in range(len(cb))] for c in range(3)]


def joined(ref, index, spans):
    return jnp.concatenate([ref[*index, lo:hi] for lo, hi in spans], axis=0)


def prepared(e, h, labels, tables):
    ca = [looked_up(m, tables[0]) for m in labels]
    cb = [looked_up(m, tables[1]) for m in labels]
    return e, h, ca, cb


def raw(seeds, material, spans):
    depth = seeds.shape[2]
    e = [[joined(seeds, (0, c, p), spans) for p in range(depth)] for c in range(3)]
    h = [[joined(seeds, (0, 3 + c, p), spans) for p in range(depth)] for c in range(3)]
    return e, h, [joined(material, (0, p), spans) for p in range(depth)]


def table_entries(table):
    count = table.shape[0] // 2
    rows = [table[m : m + 1] for m in range(2 * count)]
    return rows[:count], rows[count:]


def loaded(seeds, material, table, spans):
    return prepared(*raw(seeds, material, spans), table_entries(table))


NONE = (None, None)


def send_halos(sub, fields, near, far, packed=lambda block: block):
    odd = lax.rem(lax.axis_index(sub), 2) == 1
    e, h, ca, cb = fields
    v1 = scaled(cb, e)
    h1 = update_h(h, v1, NONE)
    e1 = update_e(e, ca, h1, NONE)
    v2 = scaled(cb, e1)
    h2 = update_h(h1, v2, NONE)
    up = (h1[0][-1], h1[1][-1], h2[0][-1], h2[1][-1], cb[-1])
    down = (v1[0][0], v1[1][0], v2[0][0], v2[1][0], cb[0])
    for k in range(PLANES):
        near[k] = packed(jnp.where(odd, down[k], up[k]))
        far[k] = packed(jnp.where(odd, up[k], down[k]))


def halo_kernel(spans, sub, table, seeds, material, near, far):
    send_halos(sub, loaded(seeds, material, table, spans), near, far)


def ramp(position, count):
    position = position.astype(jnp.float32) + 0.5
    return jnp.where(
        position < BAND,
        position / BAND,
        jnp.where(position > count - BAND, (count - position) / BAND, 1.0),
    )


def final_fields(fields, near, far, sub, sub_size, unpacked=lambda block: block):
    e, h, ca, cb = fields
    index = lax.axis_index(sub)
    odd = lax.rem(index, 2) == 1
    below, above = index > 0, index < sub_size - 1
    a = [unpacked(near[k]) for k in range(PLANES)]
    b = [unpacked(far[k]) for k in range(PLANES)]
    from_below = [jnp.where(odd, a[k], b[k]) for k in range(PLANES)]
    from_above = [jnp.where(above, jnp.where(odd, b[k], a[k]), 0.0) for k in range(PLANES)]
    part_h1x, part_h1y, part_h2x, part_h2y, cb_low = from_below
    v1x_up, v1y_up, part_v2x, part_v2y, cb_up = from_above

    v1 = scaled(cb, e)
    h1 = update_h(h, v1, (v1x_up, v1y_up))
    dh1x, dh1y = -v1[1][0], v1[0][0]
    h1_low = (jnp.where(below, part_h1x + dh1x, 0.0), jnp.where(below, part_h1y + dh1y, 0.0))
    e1 = update_e(e, ca, h1, h1_low)
    v2 = scaled(cb, e1)
    v2_up = (
        part_v2x - cb_up * (magnetic_coeff * h1[1][-1]),
        part_v2y + cb_up * (magnetic_coeff * h1[0][-1]),
    )
    h2 = update_h(h1, v2, v2_up)
    dv2x = cb_low * (magnetic_coeff * dh1y)
    dv2y = cb_low * (-magnetic_coeff * dh1x)
    dv2z = cb_low * (-magnetic_coeff * (minus_x(dh1y) - minus_y(dh1x)))
    h2x_low = part_h2x + (dh1x + (plus_y(dv2z) - (v2[1][0] - dv2y)))
    h2y_low = part_h2y + (dh1y + ((v2[0][0] - dv2x) - plus_x(dv2z)))
    h2_low = (jnp.where(below, h2x_low, 0.0), jnp.where(below, h2y_low, 0.0))
    e2 = update_e(e1, ca, h2, h2_low)
    return e2 + h2


def middle_out(block):
    return pltpu.roll(block, block.shape[1] // 2, 1)


def y_packed(first, second):
    lane = lane_of(first.shape)
    lanes = first.shape[1]
    middle = (lane >= BAND) & (lane < lanes - BAND)
    return jnp.where(middle, pltpu.roll(second, lanes // 2, 1), first)


def y_unpacked(block):
    lane = lane_of(block.shape)
    lanes = block.shape[1]
    a, b = pltpu.roll(block, BAND, 1), pltpu.roll(block, lanes - BAND, 1)
    middle = (lane >= BAND) & (lane < lanes - BAND)
    first = jnp.where(middle, 0.0, jnp.where(lane < BAND, a, b))
    second = jnp.where(middle, 0.0, jnp.where(lane < BAND, b, a))
    return first, second


def bands_packed(block):
    rows, lanes = block.shape
    half = rows // 2
    lane = lane_of((8, lanes))
    side = jnp.zeros((8, lanes), block.dtype)
    for g in range(rows // 8):
        piece = pltpu.roll(block[8 * g : 8 * g + 8], (REACH * g - BAND) % lanes, 1)
        side = jnp.where(side_lanes(lane, g, lanes), piece, side)
    return jnp.concatenate([y_packed(block[:half], block[half:]), side], axis=0)


def side_lanes(lane, g, lanes):
    low, high = REACH * g, REACH * g + lanes - 2 * BAND - REACH
    return ((lane >= low) & (lane < low + REACH)) | ((lane >= high) & (lane < high + REACH))


def bands_unpacked(packed):
    half, lanes = packed.shape[0] - 8, packed.shape[1]
    main, side = packed[:half], packed[half:]
    lane = lane_of(main.shape)
    middle = (lane >= BAND) & (lane < lanes - BAND)
    block = jnp.concatenate([jnp.where(middle, 0.0, main), jnp.where(middle, 0.0, middle_out(main))], axis=0)
    lane = lane_of(side.shape)
    beside = ((lane >= BAND) & (lane < BAND + REACH)) | ((lane >= lanes - BAND - REACH) & (lane < lanes - BAND))
    pieces = []
    for g in range(2 * half // 8):
        moved = pltpu.roll(side, (BAND - REACH * g) % lanes, 1)
        pieces.append(jnp.where(beside, moved, block[8 * g : 8 * g + 8]))
    return jnp.concatenate(pieces, axis=0)


def first_kernel(edges, inner, span, sub, decay, coupling, seeds, material, *rest):
    near_edge, far_edge, near, far, shared, held, labels, tables, sems = rest
    copies = [
        pltpu.make_async_copy(seeds.at[0], held.at[0], sems.at[0]),
        pltpu.make_async_copy(material, labels, sems.at[1]),
        pltpu.make_async_copy(decay, tables.at[0], sems.at[2]),
        pltpu.make_async_copy(coupling, tables.at[1], sems.at[3]),
    ]
    for copy in copies:
        copy.start()
    for copy in copies:
        copy.wait()
    depth = held.shape[2]
    for c in range(6):
        for p in range(depth):
            shared[depth * c + p] = bands_packed(joined(held, (0, c, p), (span,)))
    for p in range(depth):
        shared[6 * depth + p] = bands_packed(joined(labels, (0, p), (span,)).astype(jnp.float32))
    entries = [[tables[k, m] for m in range(tables.shape[1])] for k in range(2)]
    send_halos(sub, prepared(*raw(held, labels, edges), entries), near_edge, far_edge)
    send_halos(sub, prepared(*raw(held, labels, inner), entries), near, far)


def shared_fields(table, shared):
    depth = shared.shape[0] // 7
    planes = [bands_unpacked(shared[k]) for k in range(7 * depth)]
    f = [planes[depth * c : depth * (c + 1)] for c in range(7)]
    return prepared(f[:3], f[3:6], f[6], table_entries(table))


def shared_halo_kernel(sub, table, shared, near, far):
    send_halos(sub, shared_fields(table, shared), near, far, bands_packed)


def weighted_planes(seeds, material, table, near, far, spans, keeps, sub, sub_size):
    planes = final_fields(loaded(seeds, material, table, spans), near, far, sub, sub_size)
    return weighted(planes, spans, keeps, *seeds.shape[3:])


def weighted(planes, spans, keeps, size_x, size_y):
    at, results = 0, []
    for (lo, hi), (start, stop) in zip(spans, keeps):
        shape = (stop - start, size_y)
        weight = ramp(row_of(shape) + start, size_x) * ramp(lane_of(shape), size_y)
        first = at + start - lo
        results.append([[plane[first : first + stop - start] * weight for plane in part] for part in planes])
        at += hi - lo
    return results


def edge_kernel(spans, sub, sub_size, tile, table, seeds, material, near, far, edge, corner, strip):
    size_x = seeds.shape[3]
    keeps = ((0, BAND), (size_x - BAND, size_x))
    low, high = weighted_planes(seeds, material, table, near, far, spans, keeps, sub, sub_size)
    odd = lax.rem(lax.axis_index(tile), 2) == 1
    half = BAND // 2
    for c in range(6):
        for p in range(seeds.shape[2]):
            edge[c, p, :BAND] = low[c][p]
            edge[c, p, BAND:] = high[c][p]
            corner[c, p] = y_packed(low[c][p], high[c][p])
            away = jnp.where(odd, high[c][p], low[c][p])
            strip[c, p] = y_packed(middle_out(away[:half]), middle_out(away[half:]))


def middle_kernel(spans, shared, sub, sub_size, table, seeds, material, near, far, mid, bands):
    size_x = seeds.shape[3]
    keep = (BAND, size_x - BAND)
    planes, = weighted_planes(seeds, material, table, near, far, spans, (keep,), sub, sub_size)
    half = bands.shape[2]
    for c in range(6):
        for p in range(seeds.shape[2]):
            mid[c, p] = planes[c][p]
            bands[c, p] = y_packed(planes[c][p][:half], planes[c][p][-half:])


def whole_kernel(spans, sub, sub_size, table, seeds, material, near, far, out):
    planes, = weighted_planes(seeds, material, table, near, far, spans, spans, sub, sub_size)
    for c in range(6):
        for p in range(seeds.shape[2]):
            out[c, p] = planes[c][p]


def y_swapped(block):
    lane = lane_of(block.shape)
    lanes = block.shape[1]
    a, b = pltpu.roll(block, BAND, 1), pltpu.roll(block, lanes - BAND, 1)
    middle = (lane >= BAND) & (lane < lanes - BAND)
    return jnp.where(middle, 0.0, jnp.where(lane < BAND, a, b))


def shared_kernel(span, keep, size_x, sub, sub_size, table, shared, near, far, part):
    planes = final_fields(shared_fields(table, shared), near, far, sub, sub_size, bands_unpacked)
    found, = weighted(planes, (span,), (keep,), size_x, part.shape[3])
    for c in range(part.shape[0]):
        for p in range(part.shape[1]):
            part[c, p] = y_swapped(found[c][p])


def corner_kernel(tile, edge, corner, summed, send):
    odd = lax.rem(lax.axis_index(tile), 2) == 1
    half = BAND // 2
    for c in range(edge.shape[0]):
        for p in range(edge.shape[1]):
            first, second = y_unpacked(corner[c, p])
            low = edge[c, p, :BAND] + first
            high = edge[c, p, BAND:] + second
            summed[c, p, :BAND] = low
            summed[c, p, BAND:] = high
            by, away = jnp.where(odd, low, high), jnp.where(odd, high, low)
            send[c, p, :BAND] = by
            send[c, p, BAND:] = y_packed(away[:half], away[half:])


def seam_kernel(tile, summed, got, strip, out):
    odd = lax.rem(lax.axis_index(tile), 2) == 1
    half = BAND // 2
    for c in range(summed.shape[0]):
        for p in range(summed.shape[1]):
            by = got[c, p, :BAND]
            corners = y_unpacked(got[c, p, BAND:])
            block = strip[c, p]
            lane = lane_of(block.shape)
            middle = (lane >= BAND) & (lane < block.shape[1] - BAND)
            first = jnp.where(middle, middle_out(block), corners[0])
            second = jnp.where(middle, block, corners[1])
            away = jnp.concatenate([first, second], axis=0)
            out[c, p, :BAND] = summed[c, p, :BAND] + jnp.where(odd, by, away)
            out[c, p, BAND:] = summed[c, p, BAND:] + jnp.where(odd, away, by)


def last_kernel(edge, mid, bands, part, out, whole, sems):
    half = bands.shape[2]
    size_x = out.shape[3]
    copies = []
    for c in range(mid.shape[0]):
        for p in range(mid.shape[1]):
            first, second = y_unpacked(bands[c, p])
            whole[c, p, :BAND] = edge[c, p, :BAND]
            whole[c, p, BAND : BAND + half] = mid[c, p, :half] + first
            whole[c, p, BAND + half : size_x - BAND - half] = mid[c, p, half:-half] + part[c, p]
            whole[c, p, size_x - BAND - half : size_x - BAND] = mid[c, p, -half:] + second
            whole[c, p, size_x - BAND :] = edge[c, p, BAND:]
        copies.append(pltpu.make_async_copy(whole.at[c], out.at[0, c], sems.at[c]))
        copies[-1].start()
    for copy in copies:
        copy.wait()


HBM = pl.BlockSpec(memory_space=pltpu.HBM)
VMEM = pl.BlockSpec(memory_space=pltpu.VMEM)
PARAMS = pltpu.CompilerParams(vmem_limit_bytes=32 * 1024 * 1024)


def cost(flops):
    return pl.CostEstimate(flops=flops, bytes_accessed=0, transcendentals=0)


def called(kernel, shapes, *operands, flops=0):
    outs = [jax.ShapeDtypeStruct(shape, jnp.float32) for shape in shapes]
    return pl.pallas_call(
        kernel,
        out_shape=outs,
        in_specs=[VMEM] * len(operands),
        out_specs=[VMEM] * len(outs),
        compiler_params=PARAMS,
        cost_estimate=cost(flops),
    )(*operands)


def after(first, *values):
    return lax.optimization_barrier((first, *values))


def depth_exchange(near, far, sub_size, tile_size):
    near = lax.ppermute(near, "sub", [(i, i ^ 1) for i in range(sub_size)])
    pairs = []
    for t in range(tile_size):
        for i in range(sub_size):
            other = (i + 1) ^ 1
            j = other - 1
            if 0 <= j < sub_size:
                pairs.append((t * sub_size + i, t * sub_size + j))
            else:
                pairs.append((t * sub_size + i, (t ^ 1) * sub_size + i))
    far = lax.ppermute(far, ("tile", "sub"), pairs)
    return near, far


def swapped(value, bits, tile_size):
    return lax.ppermute(value, "tile", [(t, t ^ bits) for t in range(tile_size)])


def from_behind(value, steps, count):
    return lax.ppermute(value, "tile", [(t, (t + steps) % count) for t in range(count)])


def table_rows(decay, coupling, size_y):
    entries = jnp.concatenate([decay, coupling])
    return jnp.broadcast_to(entries[:, None], (entries.shape[0], size_y))


def two_by_two(seeds, material, decay, coupling, sub_size, tile_size):
    depth, size_x, size_y = seeds.shape[2:]
    edges = ((0, BAND + HALO), (size_x - BAND - HALO, size_x))
    inner = ((BAND - HALO, size_x - BAND + HALO),)
    keep = ((size_x - SHARED) // 2, (size_x + SHARED) // 2)
    span = (keep[0] - HALO, keep[1] + HALO)
    rows = size_x - 2 * BAND
    edge_rows, inner_rows, span_rows = 2 * (BAND + HALO), rows + 2 * HALO, SHARED + 2 * HALO
    packed_rows = span_rows // 2 + 8

    edge_shape = (PLANES, edge_rows, size_y)
    inner_shape = (PLANES, inner_rows, size_y)
    shapes = [edge_shape, edge_shape, inner_shape, inner_shape, (7 * depth, packed_rows, size_y)]
    edge_near, edge_far, near, far, shared = pl.pallas_call(
        functools.partial(first_kernel, edges, inner, span, "sub"),
        out_shape=[jax.ShapeDtypeStruct(shape, jnp.float32) for shape in shapes],
        in_specs=[HBM] * 4,
        out_specs=[VMEM] * 5,
        scratch_shapes=[
            pltpu.VMEM(seeds.shape, jnp.float32),
            pltpu.VMEM(material.shape, jnp.int32),
            pltpu.SMEM((2, *decay.shape), jnp.float32),
            pltpu.SemaphoreType.DMA((4,)),
        ],
        compiler_params=PARAMS,
    )(*(pltpu.with_memory_space_constraint(x, pltpu.HBM) for x in (decay, coupling, seeds, material)))
    shared = swapped(shared, 2, tile_size)
    edge_near, edge_far = depth_exchange(edge_near, edge_far, sub_size, tile_size)
    inner_near, inner_far = depth_exchange(near, far, sub_size, tile_size)
    table = table_rows(decay, coupling, size_y)

    edge, corner, strip = called(
        functools.partial(edge_kernel, edges, "sub", sub_size, "tile"),
        [(6, depth, 2 * BAND, size_y), (6, depth, BAND, size_y), (6, depth, BAND // 2, size_y)],
        table, seeds, material, edge_near, edge_far,
    )
    corner = swapped(corner, 2, tile_size)
    strip = swapped(strip, 3, tile_size)

    shape = (PLANES, packed_rows, size_y)
    near, far = called(
        functools.partial(shared_halo_kernel, "sub"), [shape, shape], table, shared, flops=LARGE
    )
    near, inner_far = after(near, inner_far)
    near, far = depth_exchange(near, far, sub_size, tile_size)

    mid, bands = called(
        functools.partial(middle_kernel, inner, keep, "sub", sub_size),
        [(6, depth, rows, size_y), (6, depth, (rows - SHARED) // 2, size_y)],
        table, seeds, material, inner_near, inner_far,
    )
    bands = swapped(bands, 2, tile_size)

    corner, strip = after(corner, strip)
    summed, send = called(
        functools.partial(corner_kernel, "tile"),
        [(6, depth, 2 * BAND, size_y), (6, depth, BAND + BAND // 2, size_y)],
        edge, corner, flops=SMALL,
    )
    got = swapped(send, 1, tile_size)
    part, = called(
        functools.partial(shared_kernel, span, keep, size_x, "sub", sub_size), [(6, depth, SHARED, size_y)],
        table, shared, near, far,
    )
    edge, = called(
        functools.partial(seam_kernel, "tile"), [(6, depth, 2 * BAND, size_y)], summed, got, strip
    )
    return pl.pallas_call(
        last_kernel,
        out_shape=jax.ShapeDtypeStruct(seeds.shape, jnp.float32),
        in_specs=[VMEM] * 4,
        out_specs=HBM,
        scratch_shapes=[pltpu.VMEM(seeds.shape[1:], jnp.float32), pltpu.SemaphoreType.DMA((6,))],
        compiler_params=PARAMS,
    )(edge, mid, bands, part)


def any_lattice(seeds, material, decay, coupling, sub_size, tile_size):
    depth, size_x, size_y = seeds.shape[2:]
    spans = ((0, size_x),)
    table = table_rows(decay, coupling, size_y)
    shape = (PLANES, size_x, size_y)
    near, far = called(functools.partial(halo_kernel, spans, "sub"), [shape, shape], table, seeds, material)
    near, far = depth_exchange(near, far, sub_size, tile_size)
    weighted, = called(
        functools.partial(whole_kernel, spans, "sub", sub_size), [(6, depth, size_x, size_y)],
        table, seeds, material, near, far,
    )
    side = math.isqrt(tile_size)
    prev_band = from_behind(weighted[:, :, size_x - BAND :, :], 1, tile_size)
    next_band = from_behind(weighted[:, :, :BAND, :], -1, tile_size)
    combined = weighted.at[:, :, :BAND, :].add(prev_band)
    combined = combined.at[:, :, size_x - BAND :, :].add(next_band)
    flat = (6, depth, size_x * BAND // size_y, size_y)
    thin = (6, depth, size_x, BAND)
    top_slab = combined[..., size_y - BAND :].reshape(flat)
    bottom_slab = combined[..., :BAND].reshape(flat)
    result = combined.at[..., :BAND].add(from_behind(top_slab, side, tile_size).reshape(thin))
    result = result.at[..., size_y - BAND :].add(from_behind(bottom_slab, -side, tile_size).reshape(thin))
    return result[None]


def solution(mesh):
    sub_size, tile_size = mesh.shape["sub"], mesh.shape["tile"]
    body = two_by_two if tile_size == 4 else any_lattice

    def on_device(seeds, material, decay, coupling):
        return body(seeds, material, decay, coupling, sub_size, tile_size)

    placed = (P("tile", None, "sub", None, None), P("tile", "sub", None, None), P(), P())
    return jax.shard_map(
        on_device,
        mesh=mesh,
        in_specs=placed,
        out_specs=P("tile", None, "sub", None, None),
        check_vma=False,
    )
```

```python
import functools
import math

import jax
import jax.numpy as jnp
from jax import lax
from jax.experimental import pallas as pl
from jax.experimental.pallas import tpu as pltpu
from jax.sharding import PartitionSpec as P

BAND = 32
STEPS = 2
HALO = 8
PLANES = 5
REACH = 4
SHARED = 64
LARGE, SMALL = 10**10, 6 * 10**8

magnetic_coeff = 0.5


def lane_of(shape):
    return lax.broadcasted_iota(jnp.int32, shape, 1)


def row_of(shape):
    return lax.broadcasted_iota(jnp.int32, shape, 0)


def next_x(v):
    rows = v.shape[0]
    return jnp.where(row_of(v.shape) == rows - 1, 0.0, pltpu.roll(v, rows - 1, 0))


def prev_x(v):
    return jnp.where(row_of(v.shape) == 0, 0.0, pltpu.roll(v, 1, 0))


def next_y(v):
    lanes = v.shape[1]
    return jnp.where(lane_of(v.shape) == lanes - 1, 0.0, pltpu.roll(v, lanes - 1, 1))


def prev_y(v):
    return jnp.where(lane_of(v.shape) == 0, 0.0, pltpu.roll(v, 1, 1))


def plus_x(v):
    return next_x(v) - v


def plus_y(v):
    return next_y(v) - v


def minus_x(v):
    return v - prev_x(v)


def minus_y(v):
    return v - prev_y(v)


def looked_up(labels, entries):
    value = jnp.broadcast_to(entries[0], labels.shape)
    for m in range(1, len(entries)):
        value = jnp.where(labels == m, entries[m], value)
    return value


def update_h(h, v, v_after):
    depth = len(v[0])
    new = [[], [], []]
    for p in range(depth):
        vx, vy, vz = v[0][p], v[1][p], v[2][p]
        up_x, up_y = (v[0][p + 1], v[1][p + 1]) if p + 1 < depth else v_after
        dz_x = up_x - vx if up_x is not None else -vx
        dz_y = up_y - vy if up_y is not None else -vy
        new[0].append(h[0][p] + (plus_y(vz) - dz_y))
        new[1].append(h[1][p] + (dz_x - plus_x(vz)))
        new[2].append(h[2][p] + (plus_x(vy) - plus_y(vx)))
    return new


def update_e(e, ca, h, h_before):
    depth = len(h[0])
    new = [[], [], []]
    for p in range(depth):
        hx, hy, hz = h[0][p], h[1][p], h[2][p]
        low_x, low_y = (h[0][p - 1], h[1][p - 1]) if p > 0 else h_before
        dz_x = hx - low_x if low_x is not None else hx
        dz_y = hy - low_y if low_y is not None else hy
        new[0].append(ca[p] * e[0][p] - magnetic_coeff * (minus_y(hz) - dz_y))
        new[1].append(ca[p] * e[1][p] - magnetic_coeff * (dz_x - minus_x(hz)))
        new[2].append(ca[p] * e[2][p] - magnetic_coeff * (minus_x(hy) - minus_y(hx)))
    return new


def scaled(cb, e):
    return [[cb[p] * e[c][p] for p in range(len(cb))] for c in range(3)]


def joined(ref, index, spans):
    return jnp.concatenate([ref[*index, lo:hi] for lo, hi in spans], axis=0)


def prepared(e, h, labels, tables):
    ca = [looked_up(m, tables[0]) for m in labels]
    cb = [looked_up(m, tables[1]) for m in labels]
    return e, h, ca, cb


def raw(seeds, material, spans):
    depth = seeds.shape[2]
    e = [[joined(seeds, (0, c, p), spans) for p in range(depth)] for c in range(3)]
    h = [[joined(seeds, (0, 3 + c, p), spans) for p in range(depth)] for c in range(3)]
    return e, h, [joined(material, (0, p), spans) for p in range(depth)]


def table_entries(table):
    count = table.shape[0] // 2
    rows = [table[m : m + 1] for m in range(2 * count)]
    return rows[:count], rows[count:]


def loaded(seeds, material, table, spans):
    return prepared(*raw(seeds, material, spans), table_entries(table))


NONE = (None, None)


def send_halos(sub, fields, near, far, packed=lambda block: block):
    odd = lax.rem(lax.axis_index(sub), 2) == 1
    e, h, ca, cb = fields
    v1 = scaled(cb, e)
    h1 = update_h(h, v1, NONE)
    e1 = update_e(e, ca, h1, NONE)
    v2 = scaled(cb, e1)
    h2 = update_h(h1, v2, NONE)
    up = (h1[0][-1], h1[1][-1], h2[0][-1], h2[1][-1], cb[-1])
    down = (v1[0][0], v1[1][0], v2[0][0], v2[1][0], cb[0])
    for k in range(PLANES):
        near[k] = packed(jnp.where(odd, down[k], up[k]))
        far[k] = packed(jnp.where(odd, up[k], down[k]))


def halo_kernel(spans, sub, table, seeds, material, near, far):
    send_halos(sub, loaded(seeds, material, table, spans), near, far)


def ramp(position, count):
    position = position.astype(jnp.float32) + 0.5
    return jnp.where(
        position < BAND,
        position / BAND,
        jnp.where(position > count - BAND, (count - position) / BAND, 1.0),
    )


def final_fields(fields, near, far, sub, sub_size, unpacked=lambda block: block):
    e, h, ca, cb = fields
    index = lax.axis_index(sub)
    odd = lax.rem(index, 2) == 1
    below, above = index > 0, index < sub_size - 1
    a = [unpacked(near[k]) for k in range(PLANES)]
    b = [unpacked(far[k]) for k in range(PLANES)]
    from_below = [jnp.where(odd, a[k], b[k]) for k in range(PLANES)]
    from_above = [jnp.where(above, jnp.where(odd, b[k], a[k]), 0.0) for k in range(PLANES)]
    part_h1x, part_h1y, part_h2x, part_h2y, cb_low = from_below
    v1x_up, v1y_up, part_v2x, part_v2y, cb_up = from_above

    v1 = scaled(cb, e)
    h1 = update_h(h, v1, (v1x_up, v1y_up))
    dh1x, dh1y = -v1[1][0], v1[0][0]
    h1_low = (jnp.where(below, part_h1x + dh1x, 0.0), jnp.where(below, part_h1y + dh1y, 0.0))
    e1 = update_e(e, ca, h1, h1_low)
    v2 = scaled(cb, e1)
    v2_up = (
        part_v2x - cb_up * (magnetic_coeff * h1[1][-1]),
        part_v2y + cb_up * (magnetic_coeff * h1[0][-1]),
    )
    h2 = update_h(h1, v2, v2_up)
    dv2x = cb_low * (magnetic_coeff * dh1y)
    dv2y = cb_low * (-magnetic_coeff * dh1x)
    dv2z = cb_low * (-magnetic_coeff * (minus_x(dh1y) - minus_y(dh1x)))
    h2x_low = part_h2x + (dh1x + (plus_y(dv2z) - (v2[1][0] - dv2y)))
    h2y_low = part_h2y + (dh1y + ((v2[0][0] - dv2x) - plus_x(dv2z)))
    h2_low = (jnp.where(below, h2x_low, 0.0), jnp.where(below, h2y_low, 0.0))
    e2 = update_e(e1, ca, h2, h2_low)
    return e2 + h2


def middle_out(block):
    return pltpu.roll(block, block.shape[1] // 2, 1)


def y_packed(first, second):
    lane = lane_of(first.shape)
    lanes = first.shape[1]
    middle = (lane >= BAND) & (lane < lanes - BAND)
    return jnp.where(middle, pltpu.roll(second, lanes // 2, 1), first)


def y_unpacked(block):
    lane = lane_of(block.shape)
    lanes = block.shape[1]
    a, b = pltpu.roll(block, BAND, 1), pltpu.roll(block, lanes - BAND, 1)
    middle = (lane >= BAND) & (lane < lanes - BAND)
    first = jnp.where(middle, 0.0, jnp.where(lane < BAND, a, b))
    second = jnp.where(middle, 0.0, jnp.where(lane < BAND, b, a))
    return first, second


def bands_packed(block):
    rows, lanes = block.shape
    half = rows // 2
    lane = lane_of((8, lanes))
    side = jnp.zeros((8, lanes), block.dtype)
    for g in range(rows // 8):
        piece = pltpu.roll(block[8 * g : 8 * g + 8], (REACH * g - BAND) % lanes, 1)
        side = jnp.where(side_lanes(lane, g, lanes), piece, side)
    return jnp.concatenate([y_packed(block[:half], block[half:]), side], axis=0)


def side_lanes(lane, g, lanes):
    low, high = REACH * g, REACH * g + lanes - 2 * BAND - REACH
    return ((lane >= low) & (lane < low + REACH)) | ((lane >= high) & (lane < high + REACH))


def bands_unpacked(packed):
    half, lanes = packed.shape[0] - 8, packed.shape[1]
    main, side = packed[:half], packed[half:]
    lane = lane_of(main.shape)
    middle = (lane >= BAND) & (lane < lanes - BAND)
    block = jnp.concatenate([jnp.where(middle, 0.0, main), jnp.where(middle, 0.0, middle_out(main))], axis=0)
    lane = lane_of(side.shape)
    beside = ((lane >= BAND) & (lane < BAND + REACH)) | ((lane >= lanes - BAND - REACH) & (lane < lanes - BAND))
    pieces = []
    for g in range(2 * half // 8):
        moved = pltpu.roll(side, (BAND - REACH * g) % lanes, 1)
        pieces.append(jnp.where(beside, moved, block[8 * g : 8 * g + 8]))
    return jnp.concatenate(pieces, axis=0)


def share_kernel(span, seeds, material, shared, held, labels, sems):
    rows = pl.ds(span[0], span[1] - span[0])
    depth = held.shape[1]
    copies = [pltpu.make_async_copy(material.at[0, :, rows], labels, sems.at[6])]
    copies += [pltpu.make_async_copy(seeds.at[0, c, :, rows], held.at[c], sems.at[c]) for c in range(6)]
    for copy in copies:
        copy.start()
    copies[0].wait()
    for p in range(depth):
        shared[6 * depth + p] = bands_packed(labels[p].astype(jnp.float32))
    for c in range(6):
        copies[1 + c].wait()
        for p in range(depth):
            shared[depth * c + p] = bands_packed(held[c, p])


def halo_pair_kernel(edges, inner, sub, table, seeds, material, near_edge, far_edge, near, far):
    send_halos(sub, loaded(seeds, material, table, edges), near_edge, far_edge)
    send_halos(sub, loaded(seeds, material, table, inner), near, far)


def shared_fields(table, shared):
    depth = shared.shape[0] // 7
    planes = [bands_unpacked(shared[k]) for k in range(7 * depth)]
    f = [planes[depth * c : depth * (c + 1)] for c in range(7)]
    return prepared(f[:3], f[3:6], f[6], table_entries(table))


def shared_halo_kernel(sub, table, shared, near, far):
    send_halos(sub, shared_fields(table, shared), near, far, bands_packed)


def weighted_planes(seeds, material, table, near, far, spans, keeps, sub, sub_size):
    planes = final_fields(loaded(seeds, material, table, spans), near, far, sub, sub_size)
    return weighted(planes, spans, keeps, *seeds.shape[3:])


def weighted(planes, spans, keeps, size_x, size_y):
    at, results = 0, []
    for (lo, hi), (start, stop) in zip(spans, keeps):
        shape = (stop - start, size_y)
        weight = ramp(row_of(shape) + start, size_x) * ramp(lane_of(shape), size_y)
        first = at + start - lo
        results.append([[plane[first : first + stop - start] * weight for plane in part] for part in planes])
        at += hi - lo
    return results


def edge_kernel(spans, sub, sub_size, tile, table, seeds, material, near, far, edge, corner, strip):
    size_x = seeds.shape[3]
    keeps = ((0, BAND), (size_x - BAND, size_x))
    low, high = weighted_planes(seeds, material, table, near, far, spans, keeps, sub, sub_size)
    odd = lax.rem(lax.axis_index(tile), 2) == 1
    half = BAND // 2
    for c in range(6):
        for p in range(seeds.shape[2]):
            edge[c, p, :BAND] = low[c][p]
            edge[c, p, BAND:] = high[c][p]
            corner[c, p] = y_packed(low[c][p], high[c][p])
            away = jnp.where(odd, high[c][p], low[c][p])
            strip[c, p] = y_packed(middle_out(away[:half]), middle_out(away[half:]))


def middle_kernel(spans, shared, sub, sub_size, table, seeds, material, near, far, mid, bands):
    size_x = seeds.shape[3]
    keep = (BAND, size_x - BAND)
    planes, = weighted_planes(seeds, material, table, near, far, spans, (keep,), sub, sub_size)
    half = bands.shape[2]
    for c in range(6):
        for p in range(seeds.shape[2]):
            mid[c, p] = planes[c][p]
            bands[c, p] = y_packed(planes[c][p][:half], planes[c][p][-half:])


def whole_kernel(spans, sub, sub_size, table, seeds, material, near, far, out):
    planes, = weighted_planes(seeds, material, table, near, far, spans, spans, sub, sub_size)
    for c in range(6):
        for p in range(seeds.shape[2]):
            out[c, p] = planes[c][p]


def y_swapped(block):
    lane = lane_of(block.shape)
    lanes = block.shape[1]
    a, b = pltpu.roll(block, BAND, 1), pltpu.roll(block, lanes - BAND, 1)
    middle = (lane >= BAND) & (lane < lanes - BAND)
    return jnp.where(middle, 0.0, jnp.where(lane < BAND, a, b))


def shared_kernel(span, keep, size_x, sub, sub_size, table, shared, near, far, part):
    planes = final_fields(shared_fields(table, shared), near, far, sub, sub_size, bands_unpacked)
    found, = weighted(planes, (span,), (keep,), size_x, part.shape[3])
    for c in range(part.shape[0]):
        for p in range(part.shape[1]):
            part[c, p] = y_swapped(found[c][p])


def corner_kernel(tile, edge, corner, summed, send):
    odd = lax.rem(lax.axis_index(tile), 2) == 1
    half = BAND // 2
    for c in range(edge.shape[0]):
        for p in range(edge.shape[1]):
            first, second = y_unpacked(corner[c, p])
            low = edge[c, p, :BAND] + first
            high = edge[c, p, BAND:] + second
            summed[c, p, :BAND] = low
            summed[c, p, BAND:] = high
            by, away = jnp.where(odd, low, high), jnp.where(odd, high, low)
            send[c, p, :BAND] = by
            send[c, p, BAND:] = y_packed(away[:half], away[half:])


def seam_kernel(tile, summed, got, strip, out):
    odd = lax.rem(lax.axis_index(tile), 2) == 1
    half = BAND // 2
    for c in range(summed.shape[0]):
        for p in range(summed.shape[1]):
            by = got[c, p, :BAND]
            corners = y_unpacked(got[c, p, BAND:])
            block = strip[c, p]
            lane = lane_of(block.shape)
            middle = (lane >= BAND) & (lane < block.shape[1] - BAND)
            first = jnp.where(middle, middle_out(block), corners[0])
            second = jnp.where(middle, block, corners[1])
            away = jnp.concatenate([first, second], axis=0)
            out[c, p, :BAND] = summed[c, p, :BAND] + jnp.where(odd, by, away)
            out[c, p, BAND:] = summed[c, p, BAND:] + jnp.where(odd, away, by)


def last_kernel(edge, mid, bands, part, out, whole, sems):
    half = bands.shape[2]
    size_x = out.shape[3]
    copies = []
    for c in range(mid.shape[0]):
        for p in range(mid.shape[1]):
            first, second = y_unpacked(bands[c, p])
            whole[c, p, :BAND] = edge[c, p, :BAND]
            whole[c, p, BAND : BAND + half] = mid[c, p, :half] + first
            whole[c, p, BAND + half : size_x - BAND - half] = mid[c, p, half:-half] + part[c, p]
            whole[c, p, size_x - BAND - half : size_x - BAND] = mid[c, p, -half:] + second
            whole[c, p, size_x - BAND :] = edge[c, p, BAND:]
        copies.append(pltpu.make_async_copy(whole.at[c], out.at[0, c], sems.at[c]))
        copies[-1].start()
    for copy in copies:
        copy.wait()


HBM = pl.BlockSpec(memory_space=pltpu.HBM)
VMEM = pl.BlockSpec(memory_space=pltpu.VMEM)
PARAMS = pltpu.CompilerParams(vmem_limit_bytes=32 * 1024 * 1024)


def cost(flops):
    return pl.CostEstimate(flops=flops, bytes_accessed=0, transcendentals=0)


def called(kernel, shapes, *operands, flops=0):
    outs = [jax.ShapeDtypeStruct(shape, jnp.float32) for shape in shapes]
    return pl.pallas_call(
        kernel,
        out_shape=outs,
        in_specs=[VMEM] * len(operands),
        out_specs=[VMEM] * len(outs),
        compiler_params=PARAMS,
        cost_estimate=cost(flops),
    )(*operands)


def after(first, *values):
    return lax.optimization_barrier((first, *values))


def near_exchange(near, sub_size):
    return lax.ppermute(near, "sub", [(i, i ^ 1) for i in range(sub_size)])


def far_exchange(far, sub_size, tile_size, ends_by_tile=True):
    pairs = []
    for t in range(tile_size):
        for i in range(sub_size):
            j = ((i + 1) ^ 1) - 1
            if 0 <= j < sub_size:
                other = (t, j)
            elif ends_by_tile:
                other = (t ^ 1, i)
            else:
                other = (t, sub_size - 1 - i)
            pairs.append((t * sub_size + i, other[0] * sub_size + other[1]))
    return lax.ppermute(far, ("tile", "sub"), pairs)


def swapped(value, bits, tile_size):
    return lax.ppermute(value, "tile", [(t, t ^ bits) for t in range(tile_size)])


def from_behind(value, steps, count):
    return lax.ppermute(value, "tile", [(t, (t + steps) % count) for t in range(count)])


def table_rows(decay, coupling, size_y):
    entries = jnp.concatenate([decay, coupling])
    return jnp.broadcast_to(entries[:, None], (entries.shape[0], size_y))


def two_by_two(seeds, material, decay, coupling, sub_size, tile_size):
    depth, size_x, size_y = seeds.shape[2:]
    edges = ((0, BAND + HALO), (size_x - BAND - HALO, size_x))
    inner = ((BAND - HALO, size_x - BAND + HALO),)
    keep = ((size_x - SHARED) // 2, (size_x + SHARED) // 2)
    span = (keep[0] - HALO, keep[1] + HALO)
    rows = size_x - 2 * BAND
    edge_rows, inner_rows, span_rows = 2 * (BAND + HALO), rows + 2 * HALO, SHARED + 2 * HALO
    packed_rows = span_rows // 2 + 8

    shared = pl.pallas_call(
        functools.partial(share_kernel, span),
        out_shape=jax.ShapeDtypeStruct((7 * depth, packed_rows, size_y), jnp.float32),
        in_specs=[HBM] * 2,
        out_specs=VMEM,
        scratch_shapes=[
            pltpu.VMEM((6, depth, span_rows, size_y), jnp.float32),
            pltpu.VMEM((depth, span_rows, size_y), jnp.int32),
            pltpu.SemaphoreType.DMA((7,)),
        ],
        compiler_params=PARAMS,
        cost_estimate=cost(0),
    )(*(pltpu.with_memory_space_constraint(x, pltpu.HBM) for x in (seeds, material)))
    table = table_rows(decay, coupling, size_y)
    shared, table = after(shared, table)
    shared = swapped(shared, 2, tile_size)
    edge_near, edge_far, inner_near, inner_far = called(
        functools.partial(halo_pair_kernel, edges, inner, "sub"),
        [(PLANES, edge_rows, size_y)] * 2 + [(PLANES, inner_rows, size_y)] * 2, table, seeds, material,
    )
    edge_near, inner_near = near_exchange(edge_near, sub_size), near_exchange(inner_near, sub_size)
    edge_far = far_exchange(edge_far, sub_size, tile_size)
    inner_far = far_exchange(inner_far, sub_size, tile_size)

    edge, corner, strip = called(
        functools.partial(edge_kernel, edges, "sub", sub_size, "tile"),
        [(6, depth, 2 * BAND, size_y), (6, depth, BAND, size_y), (6, depth, BAND // 2, size_y)],
        table, seeds, material, edge_near, edge_far,
    )
    corner = swapped(corner, 2, tile_size)
    strip = swapped(strip, 3, tile_size)

    shape = (PLANES, packed_rows, size_y)
    shared_near, shared_far = called(
        functools.partial(shared_halo_kernel, "sub"), [shape, shape], table, shared, flops=LARGE
    )
    shared_near, inner_far = after(shared_near, inner_far)
    shared_near = near_exchange(shared_near, sub_size)
    shared_far = far_exchange(shared_far, sub_size, tile_size, ends_by_tile=False)

    mid, bands = called(
        functools.partial(middle_kernel, inner, keep, "sub", sub_size),
        [(6, depth, rows, size_y), (6, depth, (rows - SHARED) // 2, size_y)],
        table, seeds, material, inner_near, inner_far,
    )
    bands = swapped(bands, 2, tile_size)

    corner, strip = after(corner, strip)
    summed, send = called(
        functools.partial(corner_kernel, "tile"),
        [(6, depth, 2 * BAND, size_y), (6, depth, BAND + BAND // 2, size_y)],
        edge, corner, flops=SMALL,
    )
    got = swapped(send, 1, tile_size)
    part, = called(
        functools.partial(shared_kernel, span, keep, size_x, "sub", sub_size), [(6, depth, SHARED, size_y)],
        table, shared, shared_near, shared_far,
    )
    edge, = called(
        functools.partial(seam_kernel, "tile"), [(6, depth, 2 * BAND, size_y)], summed, got, strip
    )
    return pl.pallas_call(
        last_kernel,
        out_shape=jax.ShapeDtypeStruct(seeds.shape, jnp.float32),
        in_specs=[VMEM] * 4,
        out_specs=HBM,
        scratch_shapes=[pltpu.VMEM(seeds.shape[1:], jnp.float32), pltpu.SemaphoreType.DMA((6,))],
        compiler_params=PARAMS,
    )(edge, mid, bands, part)


def any_lattice(seeds, material, decay, coupling, sub_size, tile_size):
    depth, size_x, size_y = seeds.shape[2:]
    spans = ((0, size_x),)
    table = table_rows(decay, coupling, size_y)
    shape = (PLANES, size_x, size_y)
    near, far = called(functools.partial(halo_kernel, spans, "sub"), [shape, shape], table, seeds, material)
    near = near_exchange(near, sub_size)
    far = far_exchange(far, sub_size, tile_size)
    weighted, = called(
        functools.partial(whole_kernel, spans, "sub", sub_size), [(6, depth, size_x, size_y)],
        table, seeds, material, near, far,
    )
    side = math.isqrt(tile_size)
    prev_band = from_behind(weighted[:, :, size_x - BAND :, :], 1, tile_size)
    next_band = from_behind(weighted[:, :, :BAND, :], -1, tile_size)
    combined = weighted.at[:, :, :BAND, :].add(prev_band)
    combined = combined.at[:, :, size_x - BAND :, :].add(next_band)
    flat = (6, depth, size_x * BAND // size_y, size_y)
    thin = (6, depth, size_x, BAND)
    top_slab = combined[..., size_y - BAND :].reshape(flat)
    bottom_slab = combined[..., :BAND].reshape(flat)
    result = combined.at[..., :BAND].add(from_behind(top_slab, side, tile_size).reshape(thin))
    result = result.at[..., size_y - BAND :].add(from_behind(bottom_slab, -side, tile_size).reshape(thin))
    return result[None]


def solution(mesh):
    sub_size, tile_size = mesh.shape["sub"], mesh.shape["tile"]
    body = two_by_two if tile_size == 4 else any_lattice

    def on_device(seeds, material, decay, coupling):
        return body(seeds, material, decay, coupling, sub_size, tile_size)

    placed = (P("tile", None, "sub", None, None), P("tile", "sub", None, None), P(), P())
    return jax.shard_map(
        on_device,
        mesh=mesh,
        in_specs=placed,
        out_specs=P("tile", None, "sub", None, None),
        check_vma=False,
    )
```

```python
import functools
import math

import jax
import jax.numpy as jnp
from jax import lax
from jax.experimental import pallas as pl
from jax.experimental.pallas import tpu as pltpu
from jax.sharding import PartitionSpec as P

BAND = 32
STEPS = 2
HALO = 8
PLANES = 5
REACH = 2
SHARED = 80
LARGE, SMALL = 10**10, 6 * 10**8

magnetic_coeff = 0.5


def lane_of(shape):
    return lax.broadcasted_iota(jnp.int32, shape, 1)


def row_of(shape):
    return lax.broadcasted_iota(jnp.int32, shape, 0)


def next_x(v):
    rows = v.shape[0]
    return jnp.where(row_of(v.shape) == rows - 1, 0.0, pltpu.roll(v, rows - 1, 0))


def prev_x(v):
    return jnp.where(row_of(v.shape) == 0, 0.0, pltpu.roll(v, 1, 0))


def next_y(v):
    lanes = v.shape[1]
    return jnp.where(lane_of(v.shape) == lanes - 1, 0.0, pltpu.roll(v, lanes - 1, 1))


def prev_y(v):
    return jnp.where(lane_of(v.shape) == 0, 0.0, pltpu.roll(v, 1, 1))


def plus_x(v):
    return next_x(v) - v


def plus_y(v):
    return next_y(v) - v


def minus_x(v):
    return v - prev_x(v)


def minus_y(v):
    return v - prev_y(v)


def looked_up(labels, entries):
    value = jnp.broadcast_to(entries[0], labels.shape)
    for m in range(1, len(entries)):
        value = jnp.where(labels == m, entries[m], value)
    return value


def update_h(h, v, v_after):
    depth = len(v[0])
    new = [[], [], []]
    for p in range(depth):
        vx, vy, vz = v[0][p], v[1][p], v[2][p]
        up_x, up_y = (v[0][p + 1], v[1][p + 1]) if p + 1 < depth else v_after
        dz_x = up_x - vx if up_x is not None else -vx
        dz_y = up_y - vy if up_y is not None else -vy
        new[0].append(h[0][p] + (plus_y(vz) - dz_y))
        new[1].append(h[1][p] + (dz_x - plus_x(vz)))
        new[2].append(h[2][p] + (plus_x(vy) - plus_y(vx)))
    return new


def update_e(e, ca, h, h_before):
    depth = len(h[0])
    new = [[], [], []]
    for p in range(depth):
        hx, hy, hz = h[0][p], h[1][p], h[2][p]
        low_x, low_y = (h[0][p - 1], h[1][p - 1]) if p > 0 else h_before
        dz_x = hx - low_x if low_x is not None else hx
        dz_y = hy - low_y if low_y is not None else hy
        new[0].append(ca[p] * e[0][p] - magnetic_coeff * (minus_y(hz) - dz_y))
        new[1].append(ca[p] * e[1][p] - magnetic_coeff * (dz_x - minus_x(hz)))
        new[2].append(ca[p] * e[2][p] - magnetic_coeff * (minus_x(hy) - minus_y(hx)))
    return new


def scaled(cb, e):
    return [[cb[p] * e[c][p] for p in range(len(cb))] for c in range(3)]


def joined(ref, index, spans):
    return jnp.concatenate([ref[*index, lo:hi] for lo, hi in spans], axis=0)


def prepared(e, h, labels, tables):
    ca = [looked_up(m, tables[0]) for m in labels]
    cb = [looked_up(m, tables[1]) for m in labels]
    return e, h, ca, cb


def raw(seeds, material, spans):
    depth = seeds.shape[2]
    e = [[joined(seeds, (0, c, p), spans) for p in range(depth)] for c in range(3)]
    h = [[joined(seeds, (0, 3 + c, p), spans) for p in range(depth)] for c in range(3)]
    return e, h, [joined(material, (0, p), spans) for p in range(depth)]


def table_entries(table):
    count = table.shape[0] // 2
    rows = [table[m : m + 1] for m in range(2 * count)]
    return rows[:count], rows[count:]


def loaded(seeds, material, table, spans):
    return prepared(*raw(seeds, material, spans), table_entries(table))


NONE = (None, None)


def send_halos(sub, fields, near, far, packed=lambda block: block):
    odd = lax.rem(lax.axis_index(sub), 2) == 1
    e, h, ca, cb = fields
    v1 = scaled(cb, e)
    h1 = update_h(h, v1, NONE)
    e1 = update_e(e, ca, h1, NONE)
    v2 = scaled(cb, e1)
    h2 = update_h(h1, v2, NONE)
    up = (h1[0][-1], h1[1][-1], h2[0][-1], h2[1][-1], cb[-1])
    down = (v1[0][0], v1[1][0], v2[0][0], v2[1][0], cb[0])
    for k in range(PLANES):
        near[k] = packed(jnp.where(odd, down[k], up[k]))
        far[k] = packed(jnp.where(odd, up[k], down[k]))


def halo_kernel(spans, sub, table, seeds, material, near, far):
    send_halos(sub, loaded(seeds, material, table, spans), near, far)


def ramp(position, count):
    position = position.astype(jnp.float32) + 0.5
    return jnp.where(
        position < BAND,
        position / BAND,
        jnp.where(position > count - BAND, (count - position) / BAND, 1.0),
    )


def final_fields(fields, near, far, sub, sub_size, unpacked=lambda block: block):
    e, h, ca, cb = fields
    index = lax.axis_index(sub)
    odd = lax.rem(index, 2) == 1
    below, above = index > 0, index < sub_size - 1
    a = [unpacked(near[k]) for k in range(PLANES)]
    b = [unpacked(far[k]) for k in range(PLANES)]
    from_below = [jnp.where(odd, a[k], b[k]) for k in range(PLANES)]
    from_above = [jnp.where(above, jnp.where(odd, b[k], a[k]), 0.0) for k in range(PLANES)]
    part_h1x, part_h1y, part_h2x, part_h2y, cb_low = from_below
    v1x_up, v1y_up, part_v2x, part_v2y, cb_up = from_above

    v1 = scaled(cb, e)
    h1 = update_h(h, v1, (v1x_up, v1y_up))
    dh1x, dh1y = -v1[1][0], v1[0][0]
    h1_low = (jnp.where(below, part_h1x + dh1x, 0.0), jnp.where(below, part_h1y + dh1y, 0.0))
    e1 = update_e(e, ca, h1, h1_low)
    v2 = scaled(cb, e1)
    v2_up = (
        part_v2x - cb_up * (magnetic_coeff * h1[1][-1]),
        part_v2y + cb_up * (magnetic_coeff * h1[0][-1]),
    )
    h2 = update_h(h1, v2, v2_up)
    dv2x = cb_low * (magnetic_coeff * dh1y)
    dv2y = cb_low * (-magnetic_coeff * dh1x)
    dv2z = cb_low * (-magnetic_coeff * (minus_x(dh1y) - minus_y(dh1x)))
    h2x_low = part_h2x + (dh1x + (plus_y(dv2z) - (v2[1][0] - dv2y)))
    h2y_low = part_h2y + (dh1y + ((v2[0][0] - dv2x) - plus_x(dv2z)))
    h2_low = (jnp.where(below, h2x_low, 0.0), jnp.where(below, h2y_low, 0.0))
    e2 = update_e(e1, ca, h2, h2_low)
    return e2 + h2


def middle_out(block):
    return pltpu.roll(block, block.shape[1] // 2, 1)


def y_packed(first, second):
    lane = lane_of(first.shape)
    lanes = first.shape[1]
    middle = (lane >= BAND) & (lane < lanes - BAND)
    return jnp.where(middle, pltpu.roll(second, lanes // 2, 1), first)


def y_unpacked(block):
    lane = lane_of(block.shape)
    lanes = block.shape[1]
    a, b = pltpu.roll(block, BAND, 1), pltpu.roll(block, lanes - BAND, 1)
    middle = (lane >= BAND) & (lane < lanes - BAND)
    first = jnp.where(middle, 0.0, jnp.where(lane < BAND, a, b))
    second = jnp.where(middle, 0.0, jnp.where(lane < BAND, b, a))
    return first, second


def side_lanes(shape, groups, apart):
    lane = lane_of(shape)
    width = REACH * groups
    return (lane < width) | ((lane >= apart) & (lane < apart + width))


def bands_packed(block):
    rows, lanes = block.shape
    half, groups, apart = rows // 2, rows // 8, lanes - 2 * BAND - REACH
    side = jnp.zeros((8, lanes), block.dtype)
    for g in range(groups):
        piece = pltpu.roll(block[8 * g : 8 * g + 8], (REACH * g - BAND) % lanes, 1)
        side = jnp.where(side_lanes(side.shape, g, apart), side, piece)
    upper, lower = side[:4], pltpu.roll(side[4:], REACH * groups, 1)
    side = jnp.where(side_lanes(upper.shape, groups, apart), upper, lower)
    return jnp.concatenate([y_packed(block[:half], block[half:]), side], axis=0)


def bands_unpacked(packed):
    half, lanes = packed.shape[0] - 4, packed.shape[1]
    groups = half // 4
    main, side = packed[:half], packed[half:]
    lane = lane_of(main.shape)
    middle = (lane >= BAND) & (lane < lanes - BAND)
    block = jnp.concatenate([jnp.where(middle, 0.0, main), jnp.where(middle, 0.0, middle_out(main))], axis=0)
    side = jnp.concatenate([side, pltpu.roll(side, lanes - REACH * groups, 1)], axis=0)
    lane = lane_of(side.shape)
    beside = ((lane >= BAND) & (lane < BAND + REACH)) | ((lane >= lanes - BAND - REACH) & (lane < lanes - BAND))
    pieces = []
    for g in range(groups):
        moved = pltpu.roll(side, (BAND - REACH * g) % lanes, 1)
        pieces.append(jnp.where(beside, moved, block[8 * g : 8 * g + 8]))
    return jnp.concatenate(pieces, axis=0)


def share_kernel(span, skip, seeds, material, shared, held, labels, sems):
    rows = pl.ds(span[0], span[1] - span[0])
    depth = held.shape[1]
    stop = span[1] - span[0] - skip
    copies = [pltpu.make_async_copy(material.at[0, :, rows], labels, sems.at[6])]
    copies += [pltpu.make_async_copy(seeds.at[0, c, :, rows], held.at[c], sems.at[c]) for c in range(6)]
    for copy in copies:
        copy.start()
    copies[0].wait()
    for p in range(depth):
        shared[6 * depth + p] = bands_packed(labels[p, skip:stop].astype(jnp.float32))
    for c in range(6):
        copies[1 + c].wait()
        for p in range(depth):
            shared[depth * c + p] = bands_packed(held[c, p, skip:stop])


def halo_pair_kernel(edges, inner, sub, table, seeds, material, near_edge, far_edge, near, far):
    send_halos(sub, loaded(seeds, material, table, edges), near_edge, far_edge)
    send_halos(sub, loaded(seeds, material, table, inner), near, far)


def shared_fields(table, shared):
    depth = shared.shape[0] // 7
    planes = [bands_unpacked(shared[k]) for k in range(7 * depth)]
    f = [planes[depth * c : depth * (c + 1)] for c in range(7)]
    return prepared(f[:3], f[3:6], f[6], table_entries(table))


def shared_halo_kernel(sub, table, shared, near, far):
    send_halos(sub, shared_fields(table, shared), near, far, bands_packed)


def weighted_planes(seeds, material, table, near, far, spans, keeps, sub, sub_size):
    planes = final_fields(loaded(seeds, material, table, spans), near, far, sub, sub_size)
    return weighted(planes, spans, keeps, *seeds.shape[3:])


def weighted(planes, spans, keeps, size_x, size_y):
    at, results = 0, []
    for (lo, hi), (start, stop) in zip(spans, keeps):
        shape = (stop - start, size_y)
        weight = ramp(row_of(shape) + start, size_x) * ramp(lane_of(shape), size_y)
        first = at + start - lo
        results.append([[plane[first : first + stop - start] * weight for plane in part] for part in planes])
        at += hi - lo
    return results


def edge_kernel(spans, sub, sub_size, tile, table, seeds, material, near, far, edge, corner, strip):
    size_x = seeds.shape[3]
    keeps = ((0, BAND), (size_x - BAND, size_x))
    low, high = weighted_planes(seeds, material, table, near, far, spans, keeps, sub, sub_size)
    odd = lax.rem(lax.axis_index(tile), 2) == 1
    half = BAND // 2
    for c in range(6):
        for p in range(seeds.shape[2]):
            edge[c, p, :BAND] = low[c][p]
            edge[c, p, BAND:] = high[c][p]
            corner[c, p] = y_packed(low[c][p], high[c][p])
            away = jnp.where(odd, high[c][p], low[c][p])
            strip[c, p] = y_packed(middle_out(away[:half]), middle_out(away[half:]))


def middle_kernel(spans, shared, sub, sub_size, table, seeds, material, near, far, mid, bands):
    size_x = seeds.shape[3]
    keep = (BAND, size_x - BAND)
    planes, = weighted_planes(seeds, material, table, near, far, spans, (keep,), sub, sub_size)
    half = bands.shape[2]
    for c in range(6):
        for p in range(seeds.shape[2]):
            mid[c, p] = planes[c][p]
            bands[c, p] = y_packed(planes[c][p][:half], planes[c][p][-half:])


def whole_kernel(spans, sub, sub_size, table, seeds, material, near, far, out):
    planes, = weighted_planes(seeds, material, table, near, far, spans, spans, sub, sub_size)
    for c in range(6):
        for p in range(seeds.shape[2]):
            out[c, p] = planes[c][p]


def y_swapped(block):
    lane = lane_of(block.shape)
    lanes = block.shape[1]
    a, b = pltpu.roll(block, BAND, 1), pltpu.roll(block, lanes - BAND, 1)
    middle = (lane >= BAND) & (lane < lanes - BAND)
    return jnp.where(middle, 0.0, jnp.where(lane < BAND, a, b))


def shared_kernel(span, keep, size_x, sub, sub_size, table, shared, near, far, part):
    planes = final_fields(shared_fields(table, shared), near, far, sub, sub_size, bands_unpacked)
    found, = weighted(planes, (span,), (keep,), size_x, part.shape[3])
    for c in range(part.shape[0]):
        for p in range(part.shape[1]):
            part[c, p] = y_swapped(found[c][p])


def corner_kernel(tile, edge, corner, summed, send):
    odd = lax.rem(lax.axis_index(tile), 2) == 1
    half = BAND // 2
    for c in range(edge.shape[0]):
        for p in range(edge.shape[1]):
            first, second = y_unpacked(corner[c, p])
            low = edge[c, p, :BAND] + first
            high = edge[c, p, BAND:] + second
            summed[c, p, :BAND] = low
            summed[c, p, BAND:] = high
            by, away = jnp.where(odd, low, high), jnp.where(odd, high, low)
            send[c, p, :BAND] = by
            send[c, p, BAND:] = y_packed(away[:half], away[half:])


def seam_kernel(tile, summed, got, strip, out):
    odd = lax.rem(lax.axis_index(tile), 2) == 1
    half = BAND // 2
    for c in range(summed.shape[0]):
        for p in range(summed.shape[1]):
            by = got[c, p, :BAND]
            corners = y_unpacked(got[c, p, BAND:])
            block = strip[c, p]
            lane = lane_of(block.shape)
            middle = (lane >= BAND) & (lane < block.shape[1] - BAND)
            first = jnp.where(middle, middle_out(block), corners[0])
            second = jnp.where(middle, block, corners[1])
            away = jnp.concatenate([first, second], axis=0)
            out[c, p, :BAND] = summed[c, p, :BAND] + jnp.where(odd, by, away)
            out[c, p, BAND:] = summed[c, p, BAND:] + jnp.where(odd, away, by)


def early_kernel(edge, mid, part, out, whole, sems):
    size_x = out.shape[3]
    start = (size_x - part.shape[2]) // 2
    rows = pl.ds(start, part.shape[2])
    low, high = pl.ds(0, BAND), pl.ds(size_x - BAND, BAND)
    for c in range(mid.shape[0]):
        for p in range(mid.shape[1]):
            whole[c, p] = mid[c, p, start - BAND : start - BAND + part.shape[2]] + part[c, p]
    copies = [
        pltpu.make_async_copy(whole, out.at[0, :, :, rows], sems.at[0]),
        pltpu.make_async_copy(edge.at[:, :, pl.ds(0, BAND)], out.at[0, :, :, low], sems.at[1]),
        pltpu.make_async_copy(edge.at[:, :, pl.ds(BAND, BAND)], out.at[0, :, :, high], sems.at[2]),
    ]
    for copy in copies:
        copy.start()
    for copy in copies:
        copy.wait()


def last_kernel(mid, bands, _, out, low, high, sems):
    half = bands.shape[2]
    size_x = out.shape[3]
    copies = []
    for c in range(mid.shape[0]):
        for p in range(mid.shape[1]):
            first, second = y_unpacked(bands[c, p])
            low[c, p] = mid[c, p, :half] + first
            high[c, p] = mid[c, p, -half:] + second
        for k, (rows, start) in enumerate(((low, BAND), (high, size_x - BAND - half))):
            copies.append(pltpu.make_async_copy(rows.at[c], out.at[0, c, :, pl.ds(start, half)], sems.at[2 * c + k]))
            copies[-1].start()
    for copy in copies:
        copy.wait()


HBM = pl.BlockSpec(memory_space=pltpu.HBM)
VMEM = pl.BlockSpec(memory_space=pltpu.VMEM)
PARAMS = pltpu.CompilerParams(vmem_limit_bytes=32 * 1024 * 1024)


def cost(flops):
    return pl.CostEstimate(flops=flops, bytes_accessed=0, transcendentals=0)


def called(kernel, shapes, *operands, flops=0):
    outs = [jax.ShapeDtypeStruct(shape, jnp.float32) for shape in shapes]
    return pl.pallas_call(
        kernel,
        out_shape=outs,
        in_specs=[VMEM] * len(operands),
        out_specs=[VMEM] * len(outs),
        compiler_params=PARAMS,
        cost_estimate=cost(flops),
    )(*operands)


def after(first, *values):
    return lax.optimization_barrier((first, *values))


def near_exchange(near, sub_size):
    return lax.ppermute(near, "sub", [(i, i ^ 1) for i in range(sub_size)])


def far_exchange(far, sub_size, tile_size, ends_by_tile=True):
    pairs = []
    for t in range(tile_size):
        for i in range(sub_size):
            j = ((i + 1) ^ 1) - 1
            if 0 <= j < sub_size:
                other = (t, j)
            elif ends_by_tile:
                other = (t ^ 1, i)
            else:
                other = (t, sub_size - 1 - i)
            pairs.append((t * sub_size + i, other[0] * sub_size + other[1]))
    return lax.ppermute(far, ("tile", "sub"), pairs)


def swapped(value, bits, tile_size):
    return lax.ppermute(value, "tile", [(t, t ^ bits) for t in range(tile_size)])


def from_behind(value, steps, count):
    return lax.ppermute(value, "tile", [(t, (t + steps) % count) for t in range(count)])


def table_rows(decay, coupling, size_y):
    entries = jnp.concatenate([decay, coupling])
    return jnp.broadcast_to(entries[:, None], (entries.shape[0], size_y))


def two_by_two(seeds, material, decay, coupling, sub_size, tile_size):
    depth, size_x, size_y = seeds.shape[2:]
    edges = ((0, BAND + HALO), (size_x - BAND - HALO, size_x))
    inner = ((BAND - HALO, size_x - BAND + HALO),)
    keep = ((size_x - SHARED) // 2, (size_x + SHARED) // 2)
    span = (keep[0] - HALO // 2, keep[1] + HALO // 2)
    fetched = (keep[0] - HALO, keep[1] + HALO)
    rows = size_x - 2 * BAND
    edge_rows, inner_rows, span_rows = 2 * (BAND + HALO), rows + 2 * HALO, SHARED + 2 * HALO
    packed_rows = (SHARED + HALO) // 2 + 4

    shared = pl.pallas_call(
        functools.partial(share_kernel, fetched, HALO // 2),
        out_shape=jax.ShapeDtypeStruct((7 * depth, packed_rows, size_y), jnp.float32),
        in_specs=[HBM] * 2,
        out_specs=VMEM,
        scratch_shapes=[
            pltpu.VMEM((6, depth, span_rows, size_y), jnp.float32),
            pltpu.VMEM((depth, span_rows, size_y), jnp.int32),
            pltpu.SemaphoreType.DMA((7,)),
        ],
        compiler_params=PARAMS,
        cost_estimate=cost(0),
    )(*(pltpu.with_memory_space_constraint(x, pltpu.HBM) for x in (seeds, material)))
    shared, decay, coupling = after(shared, decay, coupling)
    table = table_rows(decay, coupling, size_y)
    shared = swapped(shared, 2, tile_size)
    edge_near, edge_far, inner_near, inner_far = called(
        functools.partial(halo_pair_kernel, edges, inner, "sub"),
        [(PLANES, edge_rows, size_y)] * 2 + [(PLANES, inner_rows, size_y)] * 2, table, seeds, material,
    )
    edge_near, inner_near = near_exchange(edge_near, sub_size), near_exchange(inner_near, sub_size)
    edge_far = far_exchange(edge_far, sub_size, tile_size)
    inner_far = far_exchange(inner_far, sub_size, tile_size)

    edge_far, decay, coupling = after(edge_far, decay, coupling)
    edge, corner, strip = called(
        functools.partial(edge_kernel, edges, "sub", sub_size, "tile"),
        [(6, depth, 2 * BAND, size_y), (6, depth, BAND, size_y), (6, depth, BAND // 2, size_y)],
        table_rows(decay, coupling, size_y), seeds, material, edge_near, edge_far,
    )
    corner = swapped(corner, 2, tile_size)
    strip = swapped(strip, 3, tile_size)

    shape = (PLANES, packed_rows, size_y)
    shared_near, shared_far = called(
        functools.partial(shared_halo_kernel, "sub"), [shape, shape], table, shared, flops=LARGE
    )
    shared_near, inner_far = after(shared_near, inner_far)
    shared_near = near_exchange(shared_near, sub_size)
    shared_far = far_exchange(shared_far, sub_size, tile_size, ends_by_tile=False)

    mid, bands = called(
        functools.partial(middle_kernel, inner, keep, "sub", sub_size),
        [(6, depth, rows, size_y), (6, depth, (rows - SHARED) // 2, size_y)],
        table, seeds, material, inner_near, inner_far,
    )
    bands = swapped(bands, 2, tile_size)

    corner, strip, shared_near, shared_far = after(corner, strip, shared_near, shared_far)
    summed, send = called(
        functools.partial(corner_kernel, "tile"),
        [(6, depth, 2 * BAND, size_y), (6, depth, BAND + BAND // 2, size_y)],
        edge, corner, flops=SMALL,
    )
    got = swapped(send, 1, tile_size)
    part, = called(
        functools.partial(shared_kernel, span, keep, size_x, "sub", sub_size), [(6, depth, SHARED, size_y)],
        table, shared, shared_near, shared_far,
    )
    edge, = called(
        functools.partial(seam_kernel, "tile"), [(6, depth, 2 * BAND, size_y)], summed, got, strip
    )
    half = (rows - SHARED) // 2
    whole = jax.ShapeDtypeStruct(seeds.shape, jnp.float32)
    early = pl.pallas_call(
        early_kernel,
        out_shape=whole,
        in_specs=[VMEM] * 3,
        out_specs=HBM,
        scratch_shapes=[pltpu.VMEM((6, depth, SHARED, size_y), jnp.float32), pltpu.SemaphoreType.DMA((3,))],
        compiler_params=PARAMS,
        cost_estimate=cost(0),
    )(edge, mid, part)
    return pl.pallas_call(
        last_kernel,
        out_shape=whole,
        in_specs=[VMEM, VMEM, HBM],
        out_specs=HBM,
        scratch_shapes=[pltpu.VMEM((6, depth, half, size_y), jnp.float32)] * 2 + [pltpu.SemaphoreType.DMA((12,))],
        input_output_aliases={2: 0},
        compiler_params=PARAMS,
        cost_estimate=cost(0),
    )(mid, bands, early)


def any_lattice(seeds, material, decay, coupling, sub_size, tile_size):
    depth, size_x, size_y = seeds.shape[2:]
    spans = ((0, size_x),)
    table = table_rows(decay, coupling, size_y)
    shape = (PLANES, size_x, size_y)
    near, far = called(functools.partial(halo_kernel, spans, "sub"), [shape, shape], table, seeds, material)
    near = near_exchange(near, sub_size)
    far = far_exchange(far, sub_size, tile_size)
    weighted, = called(
        functools.partial(whole_kernel, spans, "sub", sub_size), [(6, depth, size_x, size_y)],
        table, seeds, material, near, far,
    )
    side = math.isqrt(tile_size)
    prev_band = from_behind(weighted[:, :, size_x - BAND :, :], 1, tile_size)
    next_band = from_behind(weighted[:, :, :BAND, :], -1, tile_size)
    combined = weighted.at[:, :, :BAND, :].add(prev_band)
    combined = combined.at[:, :, size_x - BAND :, :].add(next_band)
    flat = (6, depth, size_x * BAND // size_y, size_y)
    thin = (6, depth, size_x, BAND)
    top_slab = combined[..., size_y - BAND :].reshape(flat)
    bottom_slab = combined[..., :BAND].reshape(flat)
    result = combined.at[..., :BAND].add(from_behind(top_slab, side, tile_size).reshape(thin))
    result = result.at[..., size_y - BAND :].add(from_behind(bottom_slab, -side, tile_size).reshape(thin))
    return result[None]


def solution(mesh):
    sub_size, tile_size = mesh.shape["sub"], mesh.shape["tile"]
    body = two_by_two if tile_size == 4 else any_lattice

    def on_device(seeds, material, decay, coupling):
        return body(seeds, material, decay, coupling, sub_size, tile_size)

    placed = (P("tile", None, "sub", None, None), P("tile", "sub", None, None), P(), P())
    return jax.shard_map(
        on_device,
        mesh=mesh,
        in_specs=placed,
        out_specs=P("tile", None, "sub", None, None),
        check_vma=False,
    )
```

```python
import functools
import math

import jax
import jax.numpy as jnp
from jax import lax
from jax.experimental import pallas as pl
from jax.experimental.pallas import tpu as pltpu
from jax.sharding import PartitionSpec as P

BAND = 32
STEPS = 2
HALO = 8
PLANES = 5
REACH = 2
SHARED = 80
LARGE, MEDIUM, SMALL = 10**10, 3 * 10**9, 2 * 10**8

magnetic_coeff = 0.5


def lane_of(shape):
    return lax.broadcasted_iota(jnp.int32, shape, 1)


def row_of(shape):
    return lax.broadcasted_iota(jnp.int32, shape, 0)


def next_x(v):
    rows = v.shape[0]
    return jnp.where(row_of(v.shape) == rows - 1, 0.0, pltpu.roll(v, rows - 1, 0))


def prev_x(v):
    return jnp.where(row_of(v.shape) == 0, 0.0, pltpu.roll(v, 1, 0))


def next_y(v):
    lanes = v.shape[1]
    return jnp.where(lane_of(v.shape) == lanes - 1, 0.0, pltpu.roll(v, lanes - 1, 1))


def prev_y(v):
    return jnp.where(lane_of(v.shape) == 0, 0.0, pltpu.roll(v, 1, 1))


def plus_x(v):
    return next_x(v) - v


def plus_y(v):
    return next_y(v) - v


def minus_x(v):
    return v - prev_x(v)


def minus_y(v):
    return v - prev_y(v)


def looked_up(labels, entries):
    value = jnp.broadcast_to(entries[0], labels.shape)
    for m in range(1, len(entries)):
        value = jnp.where(labels == m, entries[m], value)
    return value


def update_h(h, v, v_after):
    depth = len(v[0])
    new = [[], [], []]
    for p in range(depth):
        vx, vy, vz = v[0][p], v[1][p], v[2][p]
        up_x, up_y = (v[0][p + 1], v[1][p + 1]) if p + 1 < depth else v_after
        dz_x = up_x - vx if up_x is not None else -vx
        dz_y = up_y - vy if up_y is not None else -vy
        new[0].append(h[0][p] + (plus_y(vz) - dz_y))
        new[1].append(h[1][p] + (dz_x - plus_x(vz)))
        new[2].append(h[2][p] + (plus_x(vy) - plus_y(vx)))
    return new


def update_e(e, ca, h, h_before):
    depth = len(h[0])
    new = [[], [], []]
    for p in range(depth):
        hx, hy, hz = h[0][p], h[1][p], h[2][p]
        low_x, low_y = (h[0][p - 1], h[1][p - 1]) if p > 0 else h_before
        dz_x = hx - low_x if low_x is not None else hx
        dz_y = hy - low_y if low_y is not None else hy
        new[0].append(ca[p] * e[0][p] - magnetic_coeff * (minus_y(hz) - dz_y))
        new[1].append(ca[p] * e[1][p] - magnetic_coeff * (dz_x - minus_x(hz)))
        new[2].append(ca[p] * e[2][p] - magnetic_coeff * (minus_x(hy) - minus_y(hx)))
    return new


def scaled(cb, e):
    return [[cb[p] * e[c][p] for p in range(len(cb))] for c in range(3)]


def joined(ref, index, spans):
    return jnp.concatenate([ref[*index, lo:hi] for lo, hi in spans], axis=0)


def prepared(e, h, labels, tables):
    ca = [looked_up(m, tables[0]) for m in labels]
    cb = [looked_up(m, tables[1]) for m in labels]
    return e, h, ca, cb


def raw(seeds, material, spans):
    depth = seeds.shape[2]
    e = [[joined(seeds, (0, c, p), spans) for p in range(depth)] for c in range(3)]
    h = [[joined(seeds, (0, 3 + c, p), spans) for p in range(depth)] for c in range(3)]
    return e, h, [joined(material, (0, p), spans) for p in range(depth)]


def table_entries(table):
    count = table.shape[0] // 2
    rows = [table[m : m + 1] for m in range(2 * count)]
    return rows[:count], rows[count:]


def loaded(seeds, material, table, spans):
    return prepared(*raw(seeds, material, spans), table_entries(table))


NONE = (None, None)


def send_halos(sub, fields, near, far, packed=lambda block: block):
    odd = lax.rem(lax.axis_index(sub), 2) == 1
    e, h, ca, cb = fields
    v1 = scaled(cb, e)
    h1 = update_h(h, v1, NONE)
    e1 = update_e(e, ca, h1, NONE)
    v2 = scaled(cb, e1)
    h2 = update_h(h1, v2, NONE)
    up = (h1[0][-1], h1[1][-1], h2[0][-1], h2[1][-1], cb[-1])
    down = (v1[0][0], v1[1][0], v2[0][0], v2[1][0], cb[0])
    for k in range(PLANES):
        near[k] = packed(jnp.where(odd, down[k], up[k]))
        far[k] = packed(jnp.where(odd, up[k], down[k]))


def halo_kernel(spans, sub, table, seeds, material, near, far):
    send_halos(sub, loaded(seeds, material, table, spans), near, far)


def ramp(position, count):
    position = position.astype(jnp.float32) + 0.5
    return jnp.where(
        position < BAND,
        position / BAND,
        jnp.where(position > count - BAND, (count - position) / BAND, 1.0),
    )


def final_fields(fields, near, far, sub, sub_size, unpacked=lambda block: block):
    e, h, ca, cb = fields
    index = lax.axis_index(sub)
    odd = lax.rem(index, 2) == 1
    below, above = index > 0, index < sub_size - 1
    a = [unpacked(near[k]) for k in range(PLANES)]
    b = [unpacked(far[k]) for k in range(PLANES)]
    from_below = [jnp.where(odd, a[k], b[k]) for k in range(PLANES)]
    from_above = [jnp.where(above, jnp.where(odd, b[k], a[k]), 0.0) for k in range(PLANES)]
    part_h1x, part_h1y, part_h2x, part_h2y, cb_low = from_below
    v1x_up, v1y_up, part_v2x, part_v2y, cb_up = from_above

    v1 = scaled(cb, e)
    h1 = update_h(h, v1, (v1x_up, v1y_up))
    dh1x, dh1y = -v1[1][0], v1[0][0]
    h1_low = (jnp.where(below, part_h1x + dh1x, 0.0), jnp.where(below, part_h1y + dh1y, 0.0))
    e1 = update_e(e, ca, h1, h1_low)
    v2 = scaled(cb, e1)
    v2_up = (
        part_v2x - cb_up * (magnetic_coeff * h1[1][-1]),
        part_v2y + cb_up * (magnetic_coeff * h1[0][-1]),
    )
    h2 = update_h(h1, v2, v2_up)
    dv2x = cb_low * (magnetic_coeff * dh1y)
    dv2y = cb_low * (-magnetic_coeff * dh1x)
    dv2z = cb_low * (-magnetic_coeff * (minus_x(dh1y) - minus_y(dh1x)))
    h2x_low = part_h2x + (dh1x + (plus_y(dv2z) - (v2[1][0] - dv2y)))
    h2y_low = part_h2y + (dh1y + ((v2[0][0] - dv2x) - plus_x(dv2z)))
    h2_low = (jnp.where(below, h2x_low, 0.0), jnp.where(below, h2y_low, 0.0))
    e2 = update_e(e1, ca, h2, h2_low)
    return e2 + h2


def middle_out(block):
    return pltpu.roll(block, block.shape[1] // 2, 1)


def y_packed(first, second):
    lane = lane_of(first.shape)
    lanes = first.shape[1]
    middle = (lane >= BAND) & (lane < lanes - BAND)
    return jnp.where(middle, pltpu.roll(second, lanes // 2, 1), first)


def y_unpacked(block):
    lane = lane_of(block.shape)
    lanes = block.shape[1]
    a, b = pltpu.roll(block, BAND, 1), pltpu.roll(block, lanes - BAND, 1)
    middle = (lane >= BAND) & (lane < lanes - BAND)
    first = jnp.where(middle, 0.0, jnp.where(lane < BAND, a, b))
    second = jnp.where(middle, 0.0, jnp.where(lane < BAND, b, a))
    return first, second


def low_rows(shape):
    return row_of(shape) < 4


def bands_packed(block):
    rows, lanes = block.shape
    count = rows // 2 + 4
    width = REACH * (rows // 8)
    side = jnp.zeros((8, lanes), block.dtype)
    lane = lane_of(side.shape)
    high = lanes - BAND
    for g in range(rows // 8):
        at = BAND + REACH * (g + 1)
        piece = pltpu.roll(block[8 * g : 8 * g + 8], REACH * (g + 1), 1)
        here = ((lane >= at) & (lane < at + REACH)) | (
            (lane >= at + high - BAND - REACH) & (lane < at + high - BAND)
        )
        side = jnp.where(here, piece, side)
    other = pltpu.roll(pltpu.roll(side, 4, 0), width + REACH, 1)
    own = ((lane >= BAND) & (lane < BAND + REACH + width)) | ((lane >= high) & (lane < high + width))
    side = jnp.where(own, side, other)
    middle = (lane >= BAND) & (lane < high)
    packed = y_packed(block[:count], block[rows - count :])
    first = jnp.where(low_rows(side.shape) & middle, side, packed[:8])
    last = jnp.where(low_rows(side.shape) | middle, packed[count - 8 :], side)
    return jnp.concatenate([first, packed[8 : count - 8], last], axis=0)


def bands_unpacked(packed):
    count, lanes = packed.shape
    rows = 2 * count - 8
    width = REACH * (rows // 8)
    high = lanes - BAND
    first, last = packed[:8], packed[count - 8 :]
    low = low_rows(first.shape)
    lane = lane_of(first.shape)
    middle = (lane >= BAND) & (lane < high)
    side = jnp.where(low, first, last)
    other = pltpu.roll(pltpu.roll(side, 4, 0), lanes - width - REACH, 1)
    side = jnp.where(low == middle, side, other)
    beside = ((lane >= BAND) & (lane < BAND + REACH)) | ((lane >= high - REACH) & (lane < high))
    moved = [pltpu.roll(packed[at : at + 8], lanes // 2, 1) for at in range(0, count, 8)]
    pieces = [packed[at : at + 8] for at in range(0, count - 8, 8)] + [jnp.where(low, last, moved[0])] + moved[1:]
    result = []
    for g, piece in enumerate(pieces):
        near_by = pltpu.roll(side, lanes - REACH * (g + 1), 1)
        result.append(jnp.where(middle, jnp.where(beside, near_by, 0.0), piece))
    return jnp.concatenate(result, axis=0)


def share_kernel(span, skip, seeds, material, shared, held, labels, sems):
    rows = pl.ds(span[0], span[1] - span[0])
    depth = held.shape[1]
    stop = span[1] - span[0] - skip
    copies = [pltpu.make_async_copy(material.at[0, :, rows], labels, sems.at[6])]
    copies += [pltpu.make_async_copy(seeds.at[0, c, :, rows], held.at[c], sems.at[c]) for c in range(6)]
    for copy in copies:
        copy.start()
    copies[0].wait()
    for p in range(depth):
        shared[6 * depth + p] = bands_packed(labels[p, skip:stop].astype(jnp.float32))
    for c in range(6):
        copies[1 + c].wait()
        for p in range(depth):
            shared[depth * c + p] = bands_packed(held[c, p, skip:stop])


def halo_pair_kernel(edges, inner, sub, table, seeds, material, near_edge, far_edge, near, far):
    send_halos(sub, loaded(seeds, material, table, edges), near_edge, far_edge)
    send_halos(sub, loaded(seeds, material, table, inner), near, far)


def shared_fields(table, shared):
    depth = shared.shape[0] // 7
    planes = [bands_unpacked(shared[k]) for k in range(7 * depth)]
    f = [planes[depth * c : depth * (c + 1)] for c in range(7)]
    return prepared(f[:3], f[3:6], f[6], table_entries(table))


def shared_halo_kernel(sub, table, shared, near, far):
    send_halos(sub, shared_fields(table, shared), near, far, bands_packed)


def weighted_planes(seeds, material, table, near, far, spans, keeps, sub, sub_size):
    planes = final_fields(loaded(seeds, material, table, spans), near, far, sub, sub_size)
    return weighted(planes, spans, keeps, *seeds.shape[3:])


def weighted(planes, spans, keeps, size_x, size_y):
    at, results = 0, []
    for (lo, hi), (start, stop) in zip(spans, keeps):
        shape = (stop - start, size_y)
        weight = ramp(row_of(shape) + start, size_x) * ramp(lane_of(shape), size_y)
        first = at + start - lo
        results.append([[plane[first : first + stop - start] * weight for plane in part] for part in planes])
        at += hi - lo
    return results


def edge_kernel(spans, sub, sub_size, tile, table, seeds, material, near, far, edge, corner, strip):
    size_x = seeds.shape[3]
    keeps = ((0, BAND), (size_x - BAND, size_x))
    low, high = weighted_planes(seeds, material, table, near, far, spans, keeps, sub, sub_size)
    odd = lax.rem(lax.axis_index(tile), 2) == 1
    half = BAND // 2
    for c in range(6):
        for p in range(seeds.shape[2]):
            edge[c, p, :BAND] = low[c][p]
            edge[c, p, BAND:] = high[c][p]
            corner[c, p] = y_packed(low[c][p], high[c][p])
            away = jnp.where(odd, high[c][p], low[c][p])
            strip[c, p] = y_packed(middle_out(away[:half]), middle_out(away[half:]))


def middle_kernel(spans, shared, sub, sub_size, table, seeds, material, near, far, mid, bands):
    size_x = seeds.shape[3]
    keep = (BAND, size_x - BAND)
    planes, = weighted_planes(seeds, material, table, near, far, spans, (keep,), sub, sub_size)
    half = bands.shape[2]
    for c in range(6):
        for p in range(seeds.shape[2]):
            mid[c, p] = planes[c][p]
            bands[c, p] = y_packed(planes[c][p][:half], planes[c][p][-half:])


def whole_kernel(spans, sub, sub_size, table, seeds, material, near, far, out):
    planes, = weighted_planes(seeds, material, table, near, far, spans, spans, sub, sub_size)
    for c in range(6):
        for p in range(seeds.shape[2]):
            out[c, p] = planes[c][p]


def y_swapped(block):
    lane = lane_of(block.shape)
    lanes = block.shape[1]
    a, b = pltpu.roll(block, BAND, 1), pltpu.roll(block, lanes - BAND, 1)
    middle = (lane >= BAND) & (lane < lanes - BAND)
    return jnp.where(middle, 0.0, jnp.where(lane < BAND, a, b))


def shared_kernel(span, size_x, sub, sub_size, table, shared, near, far, part):
    planes = final_fields(shared_fields(table, shared), near, far, sub, sub_size, bands_unpacked)
    found, = weighted(planes, (span,), (span,), size_x, part.shape[3])
    for c in range(part.shape[0]):
        for p in range(part.shape[1]):
            part[c, p] = y_swapped(found[c][p])


def corner_kernel(tile, edge, corner, summed, send):
    odd = lax.rem(lax.axis_index(tile), 2) == 1
    half = BAND // 2
    for c in range(edge.shape[0]):
        for p in range(edge.shape[1]):
            first, second = y_unpacked(corner[c, p])
            low = edge[c, p, :BAND] + first
            high = edge[c, p, BAND:] + second
            summed[c, p, :BAND] = low
            summed[c, p, BAND:] = high
            by, away = jnp.where(odd, low, high), jnp.where(odd, high, low)
            send[c, p, :BAND] = by
            send[c, p, BAND:] = y_packed(away[:half], away[half:])


def seam_kernel(tile, summed, got, strip, out):
    odd = lax.rem(lax.axis_index(tile), 2) == 1
    half = BAND // 2
    for c in range(summed.shape[0]):
        for p in range(summed.shape[1]):
            by = got[c, p, :BAND]
            corners = y_unpacked(got[c, p, BAND:])
            block = strip[c, p]
            lane = lane_of(block.shape)
            middle = (lane >= BAND) & (lane < block.shape[1] - BAND)
            first = jnp.where(middle, middle_out(block), corners[0])
            second = jnp.where(middle, block, corners[1])
            away = jnp.concatenate([first, second], axis=0)
            out[c, p, :BAND] = summed[c, p, :BAND] + jnp.where(odd, by, away)
            out[c, p, BAND:] = summed[c, p, BAND:] + jnp.where(odd, away, by)


def early_kernel(edge, mid, part, out, whole, sems):
    size_x = out.shape[3]
    skip = HALO // 2
    count = part.shape[2] - 2 * skip
    start = (size_x - count) // 2
    rows = pl.ds(start, count)
    low, high = pl.ds(0, BAND), pl.ds(size_x - BAND, BAND)
    for c in range(mid.shape[0]):
        for p in range(mid.shape[1]):
            whole[c, p] = mid[c, p, start - BAND : start - BAND + count] + part[c, p, skip : skip + count]
    copies = [
        pltpu.make_async_copy(whole, out.at[0, :, :, rows], sems.at[0]),
        pltpu.make_async_copy(edge.at[:, :, pl.ds(0, BAND)], out.at[0, :, :, low], sems.at[1]),
        pltpu.make_async_copy(edge.at[:, :, pl.ds(BAND, BAND)], out.at[0, :, :, high], sems.at[2]),
    ]
    for copy in copies:
        copy.start()
    for copy in copies:
        copy.wait()


def last_kernel(mid, bands, _, out, low, high, sems):
    half = bands.shape[2]
    size_x = out.shape[3]
    copies = []
    for c in range(mid.shape[0]):
        for p in range(mid.shape[1]):
            first, second = y_unpacked(bands[c, p])
            low[c, p] = mid[c, p, :half] + first
            high[c, p] = mid[c, p, -half:] + second
        for k, (rows, start) in enumerate(((low, BAND), (high, size_x - BAND - half))):
            copies.append(pltpu.make_async_copy(rows.at[c], out.at[0, c, :, pl.ds(start, half)], sems.at[2 * c + k]))
            copies[-1].start()
    for copy in copies:
        copy.wait()


HBM = pl.BlockSpec(memory_space=pltpu.HBM)
VMEM = pl.BlockSpec(memory_space=pltpu.VMEM)
PARAMS = pltpu.CompilerParams(vmem_limit_bytes=32 * 1024 * 1024)


def cost(flops):
    return pl.CostEstimate(flops=flops, bytes_accessed=0, transcendentals=0)


def called(kernel, shapes, *operands, flops=0):
    outs = [jax.ShapeDtypeStruct(shape, jnp.float32) for shape in shapes]
    return pl.pallas_call(
        kernel,
        out_shape=outs,
        in_specs=[VMEM] * len(operands),
        out_specs=[VMEM] * len(outs),
        compiler_params=PARAMS,
        cost_estimate=cost(flops),
    )(*operands)


def after(first, *values):
    return lax.optimization_barrier((first, *values))


def near_exchange(near, sub_size):
    return lax.ppermute(near, "sub", [(i, i ^ 1) for i in range(sub_size)])


def far_exchange(far, sub_size, tile_size, ends_by_tile=True):
    pairs = []
    for t in range(tile_size):
        for i in range(sub_size):
            j = ((i + 1) ^ 1) - 1
            if 0 <= j < sub_size:
                other = (t, j)
            elif ends_by_tile:
                other = (t ^ 1, i)
            else:
                other = (t, sub_size - 1 - i)
            pairs.append((t * sub_size + i, other[0] * sub_size + other[1]))
    return lax.ppermute(far, ("tile", "sub"), pairs)


def swapped(value, bits, tile_size):
    return lax.ppermute(value, "tile", [(t, t ^ bits) for t in range(tile_size)])


def from_behind(value, steps, count):
    return lax.ppermute(value, "tile", [(t, (t + steps) % count) for t in range(count)])


def table_rows(decay, coupling, size_y):
    entries = jnp.concatenate([decay, coupling])
    return jnp.broadcast_to(entries[:, None], (entries.shape[0], size_y))


def two_by_two(seeds, material, decay, coupling, sub_size, tile_size):
    depth, size_x, size_y = seeds.shape[2:]
    edges = ((0, BAND + HALO), (size_x - BAND - HALO, size_x))
    inner = ((BAND - HALO, size_x - BAND + HALO),)
    keep = ((size_x - SHARED) // 2, (size_x + SHARED) // 2)
    span = (keep[0] - HALO // 2, keep[1] + HALO // 2)
    fetched = (keep[0] - HALO, keep[1] + HALO)
    rows = size_x - 2 * BAND
    edge_rows, inner_rows, span_rows = 2 * (BAND + HALO), rows + 2 * HALO, SHARED + 2 * HALO
    packed_rows = (SHARED + HALO) // 2 + 4

    shared = pl.pallas_call(
        functools.partial(share_kernel, fetched, HALO // 2),
        out_shape=jax.ShapeDtypeStruct((7 * depth, packed_rows, size_y), jnp.float32),
        in_specs=[HBM] * 2,
        out_specs=VMEM,
        scratch_shapes=[
            pltpu.VMEM((6, depth, span_rows, size_y), jnp.float32),
            pltpu.VMEM((depth, span_rows, size_y), jnp.int32),
            pltpu.SemaphoreType.DMA((7,)),
        ],
        compiler_params=PARAMS,
        cost_estimate=cost(0),
    )(*(pltpu.with_memory_space_constraint(x, pltpu.HBM) for x in (seeds, material)))
    shared, decay, coupling = after(shared, decay, coupling)
    table = table_rows(decay, coupling, size_y)
    shared = swapped(shared, 2, tile_size)
    edge_near, edge_far, inner_near, inner_far = called(
        functools.partial(halo_pair_kernel, edges, inner, "sub"),
        [(PLANES, edge_rows, size_y)] * 2 + [(PLANES, inner_rows, size_y)] * 2, table, seeds, material,
    )
    edge_near, inner_near = near_exchange(edge_near, sub_size), near_exchange(inner_near, sub_size)
    edge_far = far_exchange(edge_far, sub_size, tile_size)
    inner_far = far_exchange(inner_far, sub_size, tile_size)

    edge_far, decay, coupling = after(edge_far, decay, coupling)
    edge, corner, strip = called(
        functools.partial(edge_kernel, edges, "sub", sub_size, "tile"),
        [(6, depth, 2 * BAND, size_y), (6, depth, BAND, size_y), (6, depth, BAND // 2, size_y)],
        table_rows(decay, coupling, size_y), seeds, material, edge_near, edge_far,
    )
    corner = swapped(corner, 2, tile_size)
    strip = swapped(strip, 3, tile_size)

    shape = (PLANES, packed_rows, size_y)
    shared_near, shared_far = called(
        functools.partial(shared_halo_kernel, "sub"), [shape, shape], table, shared, flops=LARGE
    )
    shared_near, inner_far = after(shared_near, inner_far)
    shared_near = near_exchange(shared_near, sub_size)
    shared_far = far_exchange(shared_far, sub_size, tile_size, ends_by_tile=False)

    mid, bands = called(
        functools.partial(middle_kernel, inner, keep, "sub", sub_size),
        [(6, depth, rows, size_y), (6, depth, (rows - SHARED) // 2, size_y)],
        table, seeds, material, inner_near, inner_far,
    )
    bands = swapped(bands, 2, tile_size)

    corner, strip, mid = after(corner, strip, mid)
    summed, send = called(
        functools.partial(corner_kernel, "tile"),
        [(6, depth, 2 * BAND, size_y), (6, depth, BAND + BAND // 2, size_y)],
        edge, corner, flops=SMALL,
    )
    got = swapped(send, 1, tile_size)
    part, = called(
        functools.partial(shared_kernel, span, size_x, "sub", sub_size),
        [(6, depth, SHARED + HALO, size_y)], table, shared, shared_near, shared_far, flops=MEDIUM,
    )
    edge, = called(
        functools.partial(seam_kernel, "tile"), [(6, depth, 2 * BAND, size_y)], summed, got, strip
    )
    half = (rows - SHARED) // 2
    whole = jax.ShapeDtypeStruct(seeds.shape, jnp.float32)
    early = pl.pallas_call(
        early_kernel,
        out_shape=whole,
        in_specs=[VMEM] * 3,
        out_specs=HBM,
        scratch_shapes=[pltpu.VMEM((6, depth, SHARED, size_y), jnp.float32), pltpu.SemaphoreType.DMA((3,))],
        compiler_params=PARAMS,
        cost_estimate=cost(0),
    )(edge, mid, part)
    return pl.pallas_call(
        last_kernel,
        out_shape=whole,
        in_specs=[VMEM, VMEM, HBM],
        out_specs=HBM,
        scratch_shapes=[pltpu.VMEM((6, depth, half, size_y), jnp.float32)] * 2 + [pltpu.SemaphoreType.DMA((12,))],
        input_output_aliases={2: 0},
        compiler_params=PARAMS,
        cost_estimate=cost(0),
    )(mid, bands, early)


def any_lattice(seeds, material, decay, coupling, sub_size, tile_size):
    depth, size_x, size_y = seeds.shape[2:]
    spans = ((0, size_x),)
    table = table_rows(decay, coupling, size_y)
    shape = (PLANES, size_x, size_y)
    near, far = called(functools.partial(halo_kernel, spans, "sub"), [shape, shape], table, seeds, material)
    near = near_exchange(near, sub_size)
    far = far_exchange(far, sub_size, tile_size)
    weighted, = called(
        functools.partial(whole_kernel, spans, "sub", sub_size), [(6, depth, size_x, size_y)],
        table, seeds, material, near, far,
    )
    side = math.isqrt(tile_size)
    prev_band = from_behind(weighted[:, :, size_x - BAND :, :], 1, tile_size)
    next_band = from_behind(weighted[:, :, :BAND, :], -1, tile_size)
    combined = weighted.at[:, :, :BAND, :].add(prev_band)
    combined = combined.at[:, :, size_x - BAND :, :].add(next_band)
    flat = (6, depth, size_x * BAND // size_y, size_y)
    thin = (6, depth, size_x, BAND)
    top_slab = combined[..., size_y - BAND :].reshape(flat)
    bottom_slab = combined[..., :BAND].reshape(flat)
    result = combined.at[..., :BAND].add(from_behind(top_slab, side, tile_size).reshape(thin))
    result = result.at[..., size_y - BAND :].add(from_behind(bottom_slab, -side, tile_size).reshape(thin))
    return result[None]


def solution(mesh):
    sub_size, tile_size = mesh.shape["sub"], mesh.shape["tile"]
    body = two_by_two if tile_size == 4 else any_lattice

    def on_device(seeds, material, decay, coupling):
        return body(seeds, material, decay, coupling, sub_size, tile_size)

    placed = (P("tile", None, "sub", None, None), P("tile", "sub", None, None), P(), P())
    return jax.shard_map(
        on_device,
        mesh=mesh,
        in_specs=placed,
        out_specs=P("tile", None, "sub", None, None),
        check_vma=False,
    )
```

```python
import functools
import math

import jax
import jax.numpy as jnp
from jax import lax
from jax.experimental import pallas as pl
from jax.experimental.pallas import tpu as pltpu
from jax.sharding import PartitionSpec as P

BAND = 32
STEPS = 2
HALO = 8
PLANES = 5
REACH = 2
SHARED = 80
LARGE, MEDIUM, SMALL = 10**10, 3 * 10**9, 2 * 10**8

magnetic_coeff = 0.5


def lane_of(shape):
    return lax.broadcasted_iota(jnp.int32, shape, len(shape) - 1)


def row_of(shape):
    return lax.broadcasted_iota(jnp.int32, shape, len(shape) - 2)


def rolled(v, shift):
    return pltpu.roll(v, shift % v.shape[-1], v.ndim - 1)


def next_x(v):
    rows = v.shape[0]
    return jnp.where(row_of(v.shape) == rows - 1, 0.0, pltpu.roll(v, rows - 1, 0))


def prev_x(v):
    return jnp.where(row_of(v.shape) == 0, 0.0, pltpu.roll(v, 1, 0))


def next_y(v):
    lanes = v.shape[1]
    return jnp.where(lane_of(v.shape) == lanes - 1, 0.0, pltpu.roll(v, lanes - 1, 1))


def prev_y(v):
    return jnp.where(lane_of(v.shape) == 0, 0.0, pltpu.roll(v, 1, 1))


def plus_x(v):
    return next_x(v) - v


def plus_y(v):
    return next_y(v) - v


def minus_x(v):
    return v - prev_x(v)


def minus_y(v):
    return v - prev_y(v)


def looked_up(labels, entries):
    value = jnp.broadcast_to(entries[0], labels.shape)
    for m in range(1, len(entries)):
        value = jnp.where(labels == m, entries[m], value)
    return value


def update_h(h, v, v_after):
    depth = len(v[0])
    new = [[], [], []]
    for p in range(depth):
        vx, vy, vz = v[0][p], v[1][p], v[2][p]
        up_x, up_y = (v[0][p + 1], v[1][p + 1]) if p + 1 < depth else v_after
        dz_x = up_x - vx if up_x is not None else -vx
        dz_y = up_y - vy if up_y is not None else -vy
        new[0].append(h[0][p] + (plus_y(vz) - dz_y))
        new[1].append(h[1][p] + (dz_x - plus_x(vz)))
        new[2].append(h[2][p] + (plus_x(vy) - plus_y(vx)))
    return new


def update_e(e, ca, h, h_before):
    depth = len(h[0])
    new = [[], [], []]
    for p in range(depth):
        hx, hy, hz = h[0][p], h[1][p], h[2][p]
        low_x, low_y = (h[0][p - 1], h[1][p - 1]) if p > 0 else h_before
        dz_x = hx - low_x if low_x is not None else hx
        dz_y = hy - low_y if low_y is not None else hy
        new[0].append(ca[p] * e[0][p] - magnetic_coeff * (minus_y(hz) - dz_y))
        new[1].append(ca[p] * e[1][p] - magnetic_coeff * (dz_x - minus_x(hz)))
        new[2].append(ca[p] * e[2][p] - magnetic_coeff * (minus_x(hy) - minus_y(hx)))
    return new


def scaled(cb, e):
    return [[cb[p] * e[c][p] for p in range(len(cb))] for c in range(3)]


def joined(ref, index, spans):
    return jnp.concatenate([ref[*index, lo:hi] for lo, hi in spans], axis=0)


def prepared(e, h, labels, tables):
    ca = [looked_up(m, tables[0]) for m in labels]
    cb = [looked_up(m, tables[1]) for m in labels]
    return e, h, ca, cb


def raw(seeds, material, spans):
    depth = seeds.shape[2]
    e = [[joined(seeds, (0, c, p), spans) for p in range(depth)] for c in range(3)]
    h = [[joined(seeds, (0, 3 + c, p), spans) for p in range(depth)] for c in range(3)]
    return e, h, [joined(material, (0, p), spans) for p in range(depth)]


def table_entries(table):
    count = table.shape[0] // 2
    rows = [table[m : m + 1] for m in range(2 * count)]
    return rows[:count], rows[count:]


def loaded(seeds, material, table, spans):
    return prepared(*raw(seeds, material, spans), table_entries(table))


NONE = (None, None)


def send_halos(sub, fields, near, far, packed=lambda planes: planes):
    odd = lax.rem(lax.axis_index(sub), 2) == 1
    e, h, ca, cb = fields
    v1 = scaled(cb, e)
    h1 = update_h(h, v1, NONE)
    e1 = update_e(e, ca, h1, NONE)
    v2 = scaled(cb, e1)
    h2 = update_h(h1, v2, NONE)
    up = (h1[0][-1], h1[1][-1], h2[0][-1], h2[1][-1], cb[-1])
    down = (v1[0][0], v1[1][0], v2[0][0], v2[1][0], cb[0])
    up, down = packed(jnp.stack(up)), packed(jnp.stack(down))
    near[...] = jnp.where(odd, down, up)
    far[...] = jnp.where(odd, up, down)


def halo_kernel(spans, sub, table, seeds, material, near, far):
    send_halos(sub, loaded(seeds, material, table, spans), near, far)


def ramp(position, count):
    position = position.astype(jnp.float32) + 0.5
    return jnp.where(
        position < BAND,
        position / BAND,
        jnp.where(position > count - BAND, (count - position) / BAND, 1.0),
    )


def final_fields(fields, near, far, sub, sub_size, unpacked=lambda planes: planes):
    e, h, ca, cb = fields
    index = lax.axis_index(sub)
    odd = lax.rem(index, 2) == 1
    below, above = index > 0, index < sub_size - 1
    a, b = near[...], far[...]
    from_below = unpacked(jnp.where(odd, a, b))
    from_above = unpacked(jnp.where(above, jnp.where(odd, b, a), 0.0))
    part_h1x, part_h1y, part_h2x, part_h2y, cb_low = from_below
    v1x_up, v1y_up, part_v2x, part_v2y, cb_up = from_above

    v1 = scaled(cb, e)
    h1 = update_h(h, v1, (v1x_up, v1y_up))
    dh1x, dh1y = -v1[1][0], v1[0][0]
    h1_low = (jnp.where(below, part_h1x + dh1x, 0.0), jnp.where(below, part_h1y + dh1y, 0.0))
    e1 = update_e(e, ca, h1, h1_low)
    v2 = scaled(cb, e1)
    v2_up = (
        part_v2x - cb_up * (magnetic_coeff * h1[1][-1]),
        part_v2y + cb_up * (magnetic_coeff * h1[0][-1]),
    )
    h2 = update_h(h1, v2, v2_up)
    dv2x = cb_low * (magnetic_coeff * dh1y)
    dv2y = cb_low * (-magnetic_coeff * dh1x)
    dv2z = cb_low * (-magnetic_coeff * (minus_x(dh1y) - minus_y(dh1x)))
    h2x_low = part_h2x + (dh1x + (plus_y(dv2z) - (v2[1][0] - dv2y)))
    h2y_low = part_h2y + (dh1y + ((v2[0][0] - dv2x) - plus_x(dv2z)))
    h2_low = (jnp.where(below, h2x_low, 0.0), jnp.where(below, h2y_low, 0.0))
    e2 = update_e(e1, ca, h2, h2_low)
    return e2 + h2


def middle_out(block):
    return rolled(block, block.shape[-1] // 2)


def y_packed(first, second):
    lane = lane_of(first.shape)
    middle = (lane >= BAND) & (lane < first.shape[-1] - BAND)
    return jnp.where(middle, middle_out(second), first)


def y_unpacked(block):
    lane = lane_of(block.shape)
    lanes = block.shape[1]
    a, b = pltpu.roll(block, BAND, 1), pltpu.roll(block, lanes - BAND, 1)
    middle = (lane >= BAND) & (lane < lanes - BAND)
    first = jnp.where(middle, 0.0, jnp.where(lane < BAND, a, b))
    second = jnp.where(middle, 0.0, jnp.where(lane < BAND, b, a))
    return first, second


def low_rows(shape):
    return row_of(shape) < 4


def bands_packed(block):
    rows, lanes = block.shape[1:]
    count, width, high = rows // 2 + 4, REACH * (rows // 8), lanes - BAND
    shape = (block.shape[0], 8, lanes)
    lane = lane_of(shape)
    low = low_rows(shape)
    side = jnp.zeros(shape, block.dtype)
    for g in range(rows // 8):
        at = BAND + REACH * (g + 1)
        piece = rolled(block[:, 8 * g : 8 * g + 8], REACH * (g + 1))
        here = ((lane >= at) & (lane < at + REACH)) | (
            (lane >= at + high - BAND - REACH) & (lane < at + high - BAND)
        )
        side = jnp.where(here, piece, side)
    other = rolled(pltpu.roll(side, 4, 1), width + REACH)
    own = ((lane >= BAND) & (lane < BAND + REACH + width)) | ((lane >= high) & (lane < high + width))
    side = jnp.where(own, side, other)
    middle = (lane >= BAND) & (lane < high)
    packed = y_packed(block[:, :count], block[:, rows - count :])
    first = jnp.where(low & middle, side, packed[:, :8])
    last = jnp.where(low | middle, packed[:, count - 8 :], side)
    return jnp.concatenate([first, packed[:, 8 : count - 8], last], axis=1)


def bands_unpacked(packed):
    count, lanes = packed.shape[1:]
    rows = 2 * count - 8
    width, high = REACH * (rows // 8), lanes - BAND
    first, last = packed[:, :8], packed[:, count - 8 :]
    low = low_rows(first.shape)
    lane = lane_of(first.shape)
    middle = (lane >= BAND) & (lane < high)
    side = jnp.where(low, first, last)
    other = rolled(pltpu.roll(side, 4, 1), -width - REACH)
    side = jnp.where(low == middle, side, other)
    beside = ((lane >= BAND) & (lane < BAND + REACH)) | ((lane >= high - REACH) & (lane < high))
    moved = [rolled(packed[:, at : at + 8], lanes // 2) for at in range(0, count, 8)]
    pieces = [packed[:, at : at + 8] for at in range(0, count - 8, 8)]
    pieces += [jnp.where(low, last, moved[0])] + moved[1:]
    result = []
    for g, piece in enumerate(pieces):
        result.append(jnp.where(middle, jnp.where(beside, rolled(side, -REACH * (g + 1)), 0.0), piece))
    return jnp.concatenate(result, axis=1)


def share_kernel(span, skip, seeds, material, shared, held, labels, sems):
    rows = pl.ds(span[0], span[1] - span[0])
    depth = held.shape[1]
    stop = span[1] - span[0] - skip
    copies = [pltpu.make_async_copy(material.at[0, :, rows], labels, sems.at[6])]
    copies += [pltpu.make_async_copy(seeds.at[0, c, :, rows], held.at[c], sems.at[c]) for c in range(6)]
    for copy in copies:
        copy.start()
    copies[0].wait()
    shared[6 * depth :] = bands_packed(labels[:, skip:stop].astype(jnp.float32))
    for c in range(6):
        copies[1 + c].wait()
    shared[: 6 * depth] = bands_packed(jnp.concatenate([held[c, :, skip:stop] for c in range(6)], axis=0))


def halo_pair_kernel(edges, inner, sub, table, seeds, material, near_edge, far_edge, near, far):
    send_halos(sub, loaded(seeds, material, table, edges), near_edge, far_edge)
    send_halos(sub, loaded(seeds, material, table, inner), near, far)


def shared_fields(table, shared):
    depth = shared.shape[0] // 7
    planes = bands_unpacked(shared[...])
    f = [planes[depth * c : depth * (c + 1)] for c in range(7)]
    return prepared(f[:3], f[3:6], f[6], table_entries(table))


def shared_halo_kernel(sub, table, shared, near, far):
    send_halos(sub, shared_fields(table, shared), near, far, bands_packed)


def weighted_planes(seeds, material, table, near, far, spans, keeps, sub, sub_size):
    planes = final_fields(loaded(seeds, material, table, spans), near, far, sub, sub_size)
    return weighted(planes, spans, keeps, *seeds.shape[3:])


def weighted(planes, spans, keeps, size_x, size_y):
    at, results = 0, []
    for (lo, hi), (start, stop) in zip(spans, keeps):
        shape = (stop - start, size_y)
        weight = ramp(row_of(shape) + start, size_x) * ramp(lane_of(shape), size_y)
        first = at + start - lo
        results.append([[plane[first : first + stop - start] * weight for plane in part] for part in planes])
        at += hi - lo
    return results


def edge_kernel(spans, sub, sub_size, tile, table, seeds, material, near, far, edge, corner, strip):
    size_x = seeds.shape[3]
    keeps = ((0, BAND), (size_x - BAND, size_x))
    low, high = weighted_planes(seeds, material, table, near, far, spans, keeps, sub, sub_size)
    odd = lax.rem(lax.axis_index(tile), 2) == 1
    half = BAND // 2
    for c in range(6):
        for p in range(seeds.shape[2]):
            edge[c, p, :BAND] = low[c][p]
            edge[c, p, BAND:] = high[c][p]
            corner[c, p] = y_packed(low[c][p], high[c][p])
            away = jnp.where(odd, high[c][p], low[c][p])
            strip[c, p] = y_packed(middle_out(away[:half]), middle_out(away[half:]))


def middle_kernel(spans, shared, sub, sub_size, table, seeds, material, near, far, mid, bands):
    size_x = seeds.shape[3]
    keep = (BAND, size_x - BAND)
    planes, = weighted_planes(seeds, material, table, near, far, spans, (keep,), sub, sub_size)
    half = bands.shape[2]
    for c in range(6):
        for p in range(seeds.shape[2]):
            mid[c, p] = planes[c][p]
            bands[c, p] = y_packed(planes[c][p][:half], planes[c][p][-half:])


def whole_kernel(spans, sub, sub_size, table, seeds, material, near, far, out):
    planes, = weighted_planes(seeds, material, table, near, far, spans, spans, sub, sub_size)
    for c in range(6):
        for p in range(seeds.shape[2]):
            out[c, p] = planes[c][p]


def y_swapped(block):
    lane = lane_of(block.shape)
    lanes = block.shape[1]
    a, b = pltpu.roll(block, BAND, 1), pltpu.roll(block, lanes - BAND, 1)
    middle = (lane >= BAND) & (lane < lanes - BAND)
    return jnp.where(middle, 0.0, jnp.where(lane < BAND, a, b))


def shared_kernel(span, size_x, sub, sub_size, table, shared, near, far, part):
    planes = final_fields(shared_fields(table, shared), near, far, sub, sub_size, bands_unpacked)
    found, = weighted(planes, (span,), (span,), size_x, part.shape[3])
    for c in range(part.shape[0]):
        for p in range(part.shape[1]):
            part[c, p] = y_swapped(found[c][p])


def corner_kernel(tile, edge, corner, summed, send):
    odd = lax.rem(lax.axis_index(tile), 2) == 1
    half = BAND // 2
    for c in range(edge.shape[0]):
        for p in range(edge.shape[1]):
            first, second = y_unpacked(corner[c, p])
            low = edge[c, p, :BAND] + first
            high = edge[c, p, BAND:] + second
            summed[c, p, :BAND] = low
            summed[c, p, BAND:] = high
            by, away = jnp.where(odd, low, high), jnp.where(odd, high, low)
            send[c, p, :BAND] = by
            send[c, p, BAND:] = y_packed(away[:half], away[half:])


def seam_kernel(tile, summed, got, strip, out):
    odd = lax.rem(lax.axis_index(tile), 2) == 1
    half = BAND // 2
    for c in range(summed.shape[0]):
        for p in range(summed.shape[1]):
            by = got[c, p, :BAND]
            corners = y_unpacked(got[c, p, BAND:])
            block = strip[c, p]
            lane = lane_of(block.shape)
            middle = (lane >= BAND) & (lane < block.shape[1] - BAND)
            first = jnp.where(middle, middle_out(block), corners[0])
            second = jnp.where(middle, block, corners[1])
            away = jnp.concatenate([first, second], axis=0)
            out[c, p, :BAND] = summed[c, p, :BAND] + jnp.where(odd, by, away)
            out[c, p, BAND:] = summed[c, p, BAND:] + jnp.where(odd, away, by)


def early_kernel(edge, mid, part, out, whole, sems):
    size_x = out.shape[3]
    skip = HALO // 2
    count = part.shape[2] - 2 * skip
    start = (size_x - count) // 2
    rows = pl.ds(start, count)
    low, high = pl.ds(0, BAND), pl.ds(size_x - BAND, BAND)
    for c in range(mid.shape[0]):
        for p in range(mid.shape[1]):
            whole[c, p] = mid[c, p, start - BAND : start - BAND + count] + part[c, p, skip : skip + count]
    copies = [
        pltpu.make_async_copy(whole, out.at[0, :, :, rows], sems.at[0]),
        pltpu.make_async_copy(edge.at[:, :, pl.ds(0, BAND)], out.at[0, :, :, low], sems.at[1]),
        pltpu.make_async_copy(edge.at[:, :, pl.ds(BAND, BAND)], out.at[0, :, :, high], sems.at[2]),
    ]
    for copy in copies:
        copy.start()
    for copy in copies:
        copy.wait()


def last_kernel(mid, bands, _, out, low, high, sems):
    half = bands.shape[2]
    size_x = out.shape[3]
    copies = []
    for c in range(mid.shape[0]):
        for p in range(mid.shape[1]):
            first, second = y_unpacked(bands[c, p])
            low[c, p] = mid[c, p, :half] + first
            high[c, p] = mid[c, p, -half:] + second
        for k, (rows, start) in enumerate(((low, BAND), (high, size_x - BAND - half))):
            copies.append(pltpu.make_async_copy(rows.at[c], out.at[0, c, :, pl.ds(start, half)], sems.at[2 * c + k]))
            copies[-1].start()
    for copy in copies:
        copy.wait()


HBM = pl.BlockSpec(memory_space=pltpu.HBM)
VMEM = pl.BlockSpec(memory_space=pltpu.VMEM)
PARAMS = pltpu.CompilerParams(vmem_limit_bytes=32 * 1024 * 1024)


def cost(flops):
    return pl.CostEstimate(flops=flops, bytes_accessed=0, transcendentals=0)


def called(kernel, shapes, *operands, flops=0):
    outs = [jax.ShapeDtypeStruct(shape, jnp.float32) for shape in shapes]
    return pl.pallas_call(
        kernel,
        out_shape=outs,
        in_specs=[VMEM] * len(operands),
        out_specs=[VMEM] * len(outs),
        compiler_params=PARAMS,
        cost_estimate=cost(flops),
    )(*operands)


def after(first, *values):
    return lax.optimization_barrier((first, *values))


def near_exchange(near, sub_size):
    return lax.ppermute(near, "sub", [(i, i ^ 1) for i in range(sub_size)])


def far_exchange(far, sub_size, tile_size, ends_by_tile=True):
    pairs = []
    for t in range(tile_size):
        for i in range(sub_size):
            j = ((i + 1) ^ 1) - 1
            if 0 <= j < sub_size:
                other = (t, j)
            elif ends_by_tile:
                other = (t ^ 1, i)
            else:
                other = (t, sub_size - 1 - i)
            pairs.append((t * sub_size + i, other[0] * sub_size + other[1]))
    return lax.ppermute(far, ("tile", "sub"), pairs)


def swapped(value, bits, tile_size):
    return lax.ppermute(value, "tile", [(t, t ^ bits) for t in range(tile_size)])


def from_behind(value, steps, count):
    return lax.ppermute(value, "tile", [(t, (t + steps) % count) for t in range(count)])


def table_rows(decay, coupling, size_y):
    entries = jnp.concatenate([decay, coupling])
    return jnp.broadcast_to(entries[:, None], (entries.shape[0], size_y))


def two_by_two(seeds, material, decay, coupling, sub_size, tile_size):
    depth, size_x, size_y = seeds.shape[2:]
    edges = ((0, BAND + HALO), (size_x - BAND - HALO, size_x))
    inner = ((BAND - HALO, size_x - BAND + HALO),)
    keep = ((size_x - SHARED) // 2, (size_x + SHARED) // 2)
    span = (keep[0] - HALO // 2, keep[1] + HALO // 2)
    fetched = (keep[0] - HALO, keep[1] + HALO)
    rows = size_x - 2 * BAND
    edge_rows, inner_rows, span_rows = 2 * (BAND + HALO), rows + 2 * HALO, SHARED + 2 * HALO
    packed_rows = (SHARED + HALO) // 2 + 4

    shared = pl.pallas_call(
        functools.partial(share_kernel, fetched, HALO // 2),
        out_shape=jax.ShapeDtypeStruct((7 * depth, packed_rows, size_y), jnp.float32),
        in_specs=[HBM] * 2,
        out_specs=VMEM,
        scratch_shapes=[
            pltpu.VMEM((6, depth, span_rows, size_y), jnp.float32),
            pltpu.VMEM((depth, span_rows, size_y), jnp.int32),
            pltpu.SemaphoreType.DMA((7,)),
        ],
        compiler_params=PARAMS,
        cost_estimate=cost(0),
    )(*(pltpu.with_memory_space_constraint(x, pltpu.HBM) for x in (seeds, material)))
    shared, decay, coupling = after(shared, decay, coupling)
    table = table_rows(decay, coupling, size_y)
    shared = swapped(shared, 2, tile_size)
    edge_near, edge_far, inner_near, inner_far = called(
        functools.partial(halo_pair_kernel, edges, inner, "sub"),
        [(PLANES, edge_rows, size_y)] * 2 + [(PLANES, inner_rows, size_y)] * 2, table, seeds, material,
    )
    edge_near, inner_near = near_exchange(edge_near, sub_size), near_exchange(inner_near, sub_size)
    edge_far = far_exchange(edge_far, sub_size, tile_size)
    inner_far = far_exchange(inner_far, sub_size, tile_size)

    edge_far, decay, coupling = after(edge_far, decay, coupling)
    edge, corner, strip = called(
        functools.partial(edge_kernel, edges, "sub", sub_size, "tile"),
        [(6, depth, 2 * BAND, size_y), (6, depth, BAND, size_y), (6, depth, BAND // 2, size_y)],
        table_rows(decay, coupling, size_y), seeds, material, edge_near, edge_far,
    )
    corner = swapped(corner, 2, tile_size)
    strip = swapped(strip, 3, tile_size)

    shape = (PLANES, packed_rows, size_y)
    shared_near, shared_far = called(
        functools.partial(shared_halo_kernel, "sub"), [shape, shape], table, shared, flops=LARGE
    )
    shared_near, inner_far = after(shared_near, inner_far)
    shared_near = near_exchange(shared_near, sub_size)
    shared_far = far_exchange(shared_far, sub_size, tile_size, ends_by_tile=False)

    mid, bands = called(
        functools.partial(middle_kernel, inner, keep, "sub", sub_size),
        [(6, depth, rows, size_y), (6, depth, (rows - SHARED) // 2, size_y)],
        table, seeds, material, inner_near, inner_far,
    )
    bands = swapped(bands, 2, tile_size)

    corner, strip, mid = after(corner, strip, mid)
    summed, send = called(
        functools.partial(corner_kernel, "tile"),
        [(6, depth, 2 * BAND, size_y), (6, depth, BAND + BAND // 2, size_y)],
        edge, corner, flops=SMALL,
    )
    got = swapped(send, 1, tile_size)
    part, = called(
        functools.partial(shared_kernel, span, size_x, "sub", sub_size),
        [(6, depth, SHARED + HALO, size_y)], table, shared, shared_near, shared_far, flops=MEDIUM,
    )
    edge, = called(
        functools.partial(seam_kernel, "tile"), [(6, depth, 2 * BAND, size_y)], summed, got, strip
    )
    half = (rows - SHARED) // 2
    whole = jax.ShapeDtypeStruct(seeds.shape, jnp.float32)
    early = pl.pallas_call(
        early_kernel,
        out_shape=whole,
        in_specs=[VMEM] * 3,
        out_specs=HBM,
        scratch_shapes=[pltpu.VMEM((6, depth, SHARED, size_y), jnp.float32), pltpu.SemaphoreType.DMA((3,))],
        compiler_params=PARAMS,
        cost_estimate=cost(0),
    )(edge, mid, part)
    return pl.pallas_call(
        last_kernel,
        out_shape=whole,
        in_specs=[VMEM, VMEM, HBM],
        out_specs=HBM,
        scratch_shapes=[pltpu.VMEM((6, depth, half, size_y), jnp.float32)] * 2 + [pltpu.SemaphoreType.DMA((12,))],
        input_output_aliases={2: 0},
        compiler_params=PARAMS,
        cost_estimate=cost(0),
    )(mid, bands, early)


def any_lattice(seeds, material, decay, coupling, sub_size, tile_size):
    depth, size_x, size_y = seeds.shape[2:]
    spans = ((0, size_x),)
    table = table_rows(decay, coupling, size_y)
    shape = (PLANES, size_x, size_y)
    near, far = called(functools.partial(halo_kernel, spans, "sub"), [shape, shape], table, seeds, material)
    near = near_exchange(near, sub_size)
    far = far_exchange(far, sub_size, tile_size)
    weighted, = called(
        functools.partial(whole_kernel, spans, "sub", sub_size), [(6, depth, size_x, size_y)],
        table, seeds, material, near, far,
    )
    side = math.isqrt(tile_size)
    prev_band = from_behind(weighted[:, :, size_x - BAND :, :], 1, tile_size)
    next_band = from_behind(weighted[:, :, :BAND, :], -1, tile_size)
    combined = weighted.at[:, :, :BAND, :].add(prev_band)
    combined = combined.at[:, :, size_x - BAND :, :].add(next_band)
    flat = (6, depth, size_x * BAND // size_y, size_y)
    thin = (6, depth, size_x, BAND)
    top_slab = combined[..., size_y - BAND :].reshape(flat)
    bottom_slab = combined[..., :BAND].reshape(flat)
    result = combined.at[..., :BAND].add(from_behind(top_slab, side, tile_size).reshape(thin))
    result = result.at[..., size_y - BAND :].add(from_behind(bottom_slab, -side, tile_size).reshape(thin))
    return result[None]


def solution(mesh):
    sub_size, tile_size = mesh.shape["sub"], mesh.shape["tile"]
    body = two_by_two if tile_size == 4 else any_lattice

    def on_device(seeds, material, decay, coupling):
        return body(seeds, material, decay, coupling, sub_size, tile_size)

    placed = (P("tile", None, "sub", None, None), P("tile", "sub", None, None), P(), P())
    return jax.shard_map(
        on_device,
        mesh=mesh,
        in_specs=placed,
        out_specs=P("tile", None, "sub", None, None),
        check_vma=False,
    )
```

```python
import functools
import math

import jax
import jax.numpy as jnp
from jax import lax
from jax.experimental import pallas as pl
from jax.experimental.pallas import tpu as pltpu
from jax.sharding import PartitionSpec as P

BAND = 32
STEPS = 2
HALO = 8
PLANES = 5
REACH = 2
SHARED = 80
LARGE, MEDIUM, SMALL = 10**10, 3 * 10**9, 0

magnetic_coeff = 0.5


def lane_of(shape):
    return lax.broadcasted_iota(jnp.int32, shape, len(shape) - 1)


def row_of(shape):
    return lax.broadcasted_iota(jnp.int32, shape, len(shape) - 2)


def rolled(v, shift):
    return pltpu.roll(v, shift % v.shape[-1], v.ndim - 1)


def next_x(v):
    rows = v.shape[0]
    return jnp.where(row_of(v.shape) == rows - 1, 0.0, pltpu.roll(v, rows - 1, 0))


def prev_x(v):
    return jnp.where(row_of(v.shape) == 0, 0.0, pltpu.roll(v, 1, 0))


def next_y(v):
    lanes = v.shape[1]
    return jnp.where(lane_of(v.shape) == lanes - 1, 0.0, pltpu.roll(v, lanes - 1, 1))


def prev_y(v):
    return jnp.where(lane_of(v.shape) == 0, 0.0, pltpu.roll(v, 1, 1))


def plus_x(v):
    return next_x(v) - v


def plus_y(v):
    return next_y(v) - v


def minus_x(v):
    return v - prev_x(v)


def minus_y(v):
    return v - prev_y(v)


def looked_up(labels, entries):
    value = jnp.broadcast_to(entries[0], labels.shape)
    for m in range(1, len(entries)):
        value = jnp.where(labels == m, entries[m], value)
    return value


def update_h(h, v, v_after):
    depth = len(v[0])
    new = [[], [], []]
    for p in range(depth):
        vx, vy, vz = v[0][p], v[1][p], v[2][p]
        up_x, up_y = (v[0][p + 1], v[1][p + 1]) if p + 1 < depth else v_after
        dz_x = up_x - vx if up_x is not None else -vx
        dz_y = up_y - vy if up_y is not None else -vy
        new[0].append(h[0][p] + (plus_y(vz) - dz_y))
        new[1].append(h[1][p] + (dz_x - plus_x(vz)))
        new[2].append(h[2][p] + (plus_x(vy) - plus_y(vx)))
    return new


def update_e(e, ca, h, h_before):
    depth = len(h[0])
    new = [[], [], []]
    for p in range(depth):
        hx, hy, hz = h[0][p], h[1][p], h[2][p]
        low_x, low_y = (h[0][p - 1], h[1][p - 1]) if p > 0 else h_before
        dz_x = hx - low_x if low_x is not None else hx
        dz_y = hy - low_y if low_y is not None else hy
        new[0].append(ca[p] * e[0][p] - magnetic_coeff * (minus_y(hz) - dz_y))
        new[1].append(ca[p] * e[1][p] - magnetic_coeff * (dz_x - minus_x(hz)))
        new[2].append(ca[p] * e[2][p] - magnetic_coeff * (minus_x(hy) - minus_y(hx)))
    return new


def scaled(cb, e):
    return [[cb[p] * e[c][p] for p in range(len(cb))] for c in range(3)]


def joined(ref, index, spans):
    return jnp.concatenate([ref[*index, lo:hi] for lo, hi in spans], axis=0)


def prepared(e, h, labels, tables):
    ca = [looked_up(m, tables[0]) for m in labels]
    cb = [looked_up(m, tables[1]) for m in labels]
    return e, h, ca, cb


def raw(seeds, material, spans):
    depth = seeds.shape[2]
    e = [[joined(seeds, (0, c, p), spans) for p in range(depth)] for c in range(3)]
    h = [[joined(seeds, (0, 3 + c, p), spans) for p in range(depth)] for c in range(3)]
    return e, h, [joined(material, (0, p), spans) for p in range(depth)]


def table_entries(table):
    count = table.shape[0] // 2
    rows = [table[m : m + 1] for m in range(2 * count)]
    return rows[:count], rows[count:]


def loaded(seeds, material, table, spans):
    return prepared(*raw(seeds, material, spans), table_entries(table))


NONE = (None, None)


def send_halos(sub, fields, near, far, packed=lambda planes: planes):
    odd = lax.rem(lax.axis_index(sub), 2) == 1
    e, h, ca, cb = fields
    v1 = scaled(cb, e)
    h1 = update_h(h, v1, NONE)
    e1 = update_e(e, ca, h1, NONE)
    v2 = scaled(cb, e1)
    h2 = update_h(h1, v2, NONE)
    up = (h1[0][-1], h1[1][-1], h2[0][-1], h2[1][-1], cb[-1])
    down = (v1[0][0], v1[1][0], v2[0][0], v2[1][0], cb[0])
    up, down = packed(jnp.stack(up)), packed(jnp.stack(down))
    near[...] = jnp.where(odd, down, up)
    far[...] = jnp.where(odd, up, down)


def halo_kernel(spans, sub, table, seeds, material, near, far):
    send_halos(sub, loaded(seeds, material, table, spans), near, far)


def ramp(position, count):
    position = position.astype(jnp.float32) + 0.5
    return jnp.where(
        position < BAND,
        position / BAND,
        jnp.where(position > count - BAND, (count - position) / BAND, 1.0),
    )


def final_fields(fields, near, far, sub, sub_size, unpacked=lambda planes: planes):
    e, h, ca, cb = fields
    index = lax.axis_index(sub)
    odd = lax.rem(index, 2) == 1
    below, above = index > 0, index < sub_size - 1
    a, b = near[...], far[...]
    from_below = unpacked(jnp.where(odd, a, b))
    from_above = unpacked(jnp.where(above, jnp.where(odd, b, a), 0.0))
    part_h1x, part_h1y, part_h2x, part_h2y, cb_low = from_below
    v1x_up, v1y_up, part_v2x, part_v2y, cb_up = from_above

    v1 = scaled(cb, e)
    h1 = update_h(h, v1, (v1x_up, v1y_up))
    dh1x, dh1y = -v1[1][0], v1[0][0]
    h1_low = (jnp.where(below, part_h1x + dh1x, 0.0), jnp.where(below, part_h1y + dh1y, 0.0))
    e1 = update_e(e, ca, h1, h1_low)
    v2 = scaled(cb, e1)
    v2_up = (
        part_v2x - cb_up * (magnetic_coeff * h1[1][-1]),
        part_v2y + cb_up * (magnetic_coeff * h1[0][-1]),
    )
    h2 = update_h(h1, v2, v2_up)
    dv2x = cb_low * (magnetic_coeff * dh1y)
    dv2y = cb_low * (-magnetic_coeff * dh1x)
    dv2z = cb_low * (-magnetic_coeff * (minus_x(dh1y) - minus_y(dh1x)))
    h2x_low = part_h2x + (dh1x + (plus_y(dv2z) - (v2[1][0] - dv2y)))
    h2y_low = part_h2y + (dh1y + ((v2[0][0] - dv2x) - plus_x(dv2z)))
    h2_low = (jnp.where(below, h2x_low, 0.0), jnp.where(below, h2y_low, 0.0))
    e2 = update_e(e1, ca, h2, h2_low)
    return e2 + h2


def middle_out(block):
    return rolled(block, block.shape[-1] // 2)


def y_packed(first, second):
    lane = lane_of(first.shape)
    middle = (lane >= BAND) & (lane < first.shape[-1] - BAND)
    return jnp.where(middle, middle_out(second), first)


def y_unpacked(block):
    lane = lane_of(block.shape)
    lanes = block.shape[1]
    a, b = pltpu.roll(block, BAND, 1), pltpu.roll(block, lanes - BAND, 1)
    middle = (lane >= BAND) & (lane < lanes - BAND)
    first = jnp.where(middle, 0.0, jnp.where(lane < BAND, a, b))
    second = jnp.where(middle, 0.0, jnp.where(lane < BAND, b, a))
    return first, second


def low_rows(shape):
    return row_of(shape) < 4


def bands_packed(block):
    rows, lanes = block.shape[1:]
    count, width, high = rows // 2 + 4, REACH * (rows // 8), lanes - BAND
    shape = (block.shape[0], 8, lanes)
    lane = lane_of(shape)
    low = low_rows(shape)
    side = jnp.zeros(shape, block.dtype)
    for g in range(rows // 8):
        at = BAND + REACH * (g + 1)
        piece = rolled(block[:, 8 * g : 8 * g + 8], REACH * (g + 1))
        here = ((lane >= at) & (lane < at + REACH)) | (
            (lane >= at + high - BAND - REACH) & (lane < at + high - BAND)
        )
        side = jnp.where(here, piece, side)
    other = rolled(pltpu.roll(side, 4, 1), width + REACH)
    own = ((lane >= BAND) & (lane < BAND + REACH + width)) | ((lane >= high) & (lane < high + width))
    side = jnp.where(own, side, other)
    middle = (lane >= BAND) & (lane < high)
    packed = y_packed(block[:, :count], block[:, rows - count :])
    first = jnp.where(low & middle, side, packed[:, :8])
    last = jnp.where(low | middle, packed[:, count - 8 :], side)
    return jnp.concatenate([first, packed[:, 8 : count - 8], last], axis=1)


def bands_unpacked(packed):
    count, lanes = packed.shape[1:]
    rows = 2 * count - 8
    width, high = REACH * (rows // 8), lanes - BAND
    first, last = packed[:, :8], packed[:, count - 8 :]
    low = low_rows(first.shape)
    lane = lane_of(first.shape)
    middle = (lane >= BAND) & (lane < high)
    side = jnp.where(low, first, last)
    other = rolled(pltpu.roll(side, 4, 1), -width - REACH)
    side = jnp.where(low == middle, side, other)
    beside = ((lane >= BAND) & (lane < BAND + REACH)) | ((lane >= high - REACH) & (lane < high))
    moved = [rolled(packed[:, at : at + 8], lanes // 2) for at in range(0, count, 8)]
    pieces = [packed[:, at : at + 8] for at in range(0, count - 8, 8)]
    pieces += [jnp.where(low, last, moved[0])] + moved[1:]
    result = []
    for g, piece in enumerate(pieces):
        result.append(jnp.where(middle, jnp.where(beside, rolled(side, -REACH * (g + 1)), 0.0), piece))
    return jnp.concatenate(result, axis=1)


def share_kernel(span, skip, seeds, material, shared, held, labels, sems):
    rows = pl.ds(span[0], span[1] - span[0])
    depth = held.shape[1]
    stop = span[1] - span[0] - skip
    copies = [pltpu.make_async_copy(material.at[0, :, rows], labels, sems.at[6])]
    copies += [pltpu.make_async_copy(seeds.at[0, c, :, rows], held.at[c], sems.at[c]) for c in range(6)]
    for copy in copies:
        copy.start()
    copies[0].wait()
    shared[6 * depth :] = bands_packed(labels[:, skip:stop].astype(jnp.float32))
    for c in range(6):
        copies[1 + c].wait()
    shared[: 6 * depth] = bands_packed(jnp.concatenate([held[c, :, skip:stop] for c in range(6)], axis=0))


def halo_pair_kernel(edges, inner, sub, table, seeds, material, near_edge, far_edge, near, far):
    send_halos(sub, loaded(seeds, material, table, edges), near_edge, far_edge)
    send_halos(sub, loaded(seeds, material, table, inner), near, far)


def shared_fields(table, shared):
    depth = shared.shape[0] // 7
    planes = bands_unpacked(shared[...])
    f = [planes[depth * c : depth * (c + 1)] for c in range(7)]
    return prepared(f[:3], f[3:6], f[6], table_entries(table))


def shared_halo_kernel(sub, table, shared, near, far):
    send_halos(sub, shared_fields(table, shared), near, far, bands_packed)


def weighted_planes(seeds, material, table, near, far, spans, keeps, sub, sub_size):
    planes = final_fields(loaded(seeds, material, table, spans), near, far, sub, sub_size)
    return weighted(planes, spans, keeps, *seeds.shape[3:])


def weighted(planes, spans, keeps, size_x, size_y):
    at, results = 0, []
    for (lo, hi), (start, stop) in zip(spans, keeps):
        shape = (stop - start, size_y)
        weight = ramp(row_of(shape) + start, size_x) * ramp(lane_of(shape), size_y)
        first = at + start - lo
        results.append([[plane[first : first + stop - start] * weight for plane in part] for part in planes])
        at += hi - lo
    return results


def edge_kernel(spans, sub, sub_size, tile, table, seeds, material, near, far, edge, corner, strip):
    size_x = seeds.shape[3]
    keeps = ((0, BAND), (size_x - BAND, size_x))
    low, high = weighted_planes(seeds, material, table, near, far, spans, keeps, sub, sub_size)
    odd = lax.rem(lax.axis_index(tile), 2) == 1
    half = BAND // 2
    for c in range(6):
        for p in range(seeds.shape[2]):
            edge[c, p, :BAND] = low[c][p]
            edge[c, p, BAND:] = high[c][p]
            corner[c, p] = y_packed(low[c][p], high[c][p])
            away = jnp.where(odd, high[c][p], low[c][p])
            strip[c, p] = y_packed(middle_out(away[:half]), middle_out(away[half:]))


def middle_kernel(spans, shared, sub, sub_size, table, seeds, material, near, far, mid, bands):
    size_x = seeds.shape[3]
    keep = (BAND, size_x - BAND)
    planes, = weighted_planes(seeds, material, table, near, far, spans, (keep,), sub, sub_size)
    half = bands.shape[2]
    for c in range(6):
        for p in range(seeds.shape[2]):
            mid[c, p] = planes[c][p]
            bands[c, p] = y_packed(planes[c][p][:half], planes[c][p][-half:])


def whole_kernel(spans, sub, sub_size, table, seeds, material, near, far, out):
    planes, = weighted_planes(seeds, material, table, near, far, spans, spans, sub, sub_size)
    for c in range(6):
        for p in range(seeds.shape[2]):
            out[c, p] = planes[c][p]


def y_swapped(block):
    lane = lane_of(block.shape)
    lanes = block.shape[1]
    a, b = pltpu.roll(block, BAND, 1), pltpu.roll(block, lanes - BAND, 1)
    middle = (lane >= BAND) & (lane < lanes - BAND)
    return jnp.where(middle, 0.0, jnp.where(lane < BAND, a, b))


def shared_kernel(span, size_x, sub, sub_size, table, shared, near, far, part):
    planes = final_fields(shared_fields(table, shared), near, far, sub, sub_size, bands_unpacked)
    found, = weighted(planes, (span,), (span,), size_x, part.shape[3])
    for c in range(part.shape[0]):
        for p in range(part.shape[1]):
            part[c, p] = y_swapped(found[c][p])


def corner_kernel(tile, edge, corner, summed, send):
    odd = lax.rem(lax.axis_index(tile), 2) == 1
    half = BAND // 2
    for c in range(edge.shape[0]):
        for p in range(edge.shape[1]):
            first, second = y_unpacked(corner[c, p])
            low = edge[c, p, :BAND] + first
            high = edge[c, p, BAND:] + second
            summed[c, p, :BAND] = low
            summed[c, p, BAND:] = high
            by, away = jnp.where(odd, low, high), jnp.where(odd, high, low)
            send[c, p, :BAND] = by
            send[c, p, BAND:] = y_packed(away[:half], away[half:])


def seam_kernel(tile, summed, got, strip, out):
    odd = lax.rem(lax.axis_index(tile), 2) == 1
    half = BAND // 2
    for c in range(summed.shape[0]):
        for p in range(summed.shape[1]):
            by = got[c, p, :BAND]
            corners = y_unpacked(got[c, p, BAND:])
            block = strip[c, p]
            lane = lane_of(block.shape)
            middle = (lane >= BAND) & (lane < block.shape[1] - BAND)
            first = jnp.where(middle, middle_out(block), corners[0])
            second = jnp.where(middle, block, corners[1])
            away = jnp.concatenate([first, second], axis=0)
            out[c, p, :BAND] = summed[c, p, :BAND] + jnp.where(odd, by, away)
            out[c, p, BAND:] = summed[c, p, BAND:] + jnp.where(odd, away, by)


def early_kernel(edge, mid, part, out, whole, sems):
    size_x = out.shape[3]
    skip = HALO // 2
    count = part.shape[2] - 2 * skip
    start = (size_x - count) // 2
    rows = pl.ds(start, count)
    low, high = pl.ds(0, BAND), pl.ds(size_x - BAND, BAND)
    for c in range(mid.shape[0]):
        for p in range(mid.shape[1]):
            whole[c, p] = mid[c, p, start - BAND : start - BAND + count] + part[c, p, skip : skip + count]
    copies = [
        pltpu.make_async_copy(whole, out.at[0, :, :, rows], sems.at[0]),
        pltpu.make_async_copy(edge.at[:, :, pl.ds(0, BAND)], out.at[0, :, :, low], sems.at[1]),
        pltpu.make_async_copy(edge.at[:, :, pl.ds(BAND, BAND)], out.at[0, :, :, high], sems.at[2]),
    ]
    for copy in copies:
        copy.start()
    for copy in copies:
        copy.wait()


def last_kernel(mid, bands, _, out, low, high, sems):
    half = bands.shape[2]
    size_x = out.shape[3]
    copies = []
    for c in range(mid.shape[0]):
        for p in range(mid.shape[1]):
            first, second = y_unpacked(bands[c, p])
            low[c, p] = mid[c, p, :half] + first
            high[c, p] = mid[c, p, -half:] + second
        for k, (rows, start) in enumerate(((low, BAND), (high, size_x - BAND - half))):
            copies.append(pltpu.make_async_copy(rows.at[c], out.at[0, c, :, pl.ds(start, half)], sems.at[2 * c + k]))
            copies[-1].start()
    for copy in copies:
        copy.wait()


HBM = pl.BlockSpec(memory_space=pltpu.HBM)
VMEM = pl.BlockSpec(memory_space=pltpu.VMEM)
PARAMS = pltpu.CompilerParams(vmem_limit_bytes=32 * 1024 * 1024)


def cost(flops):
    return pl.CostEstimate(flops=flops, bytes_accessed=0, transcendentals=0)


def called(kernel, shapes, *operands, flops=0):
    outs = [jax.ShapeDtypeStruct(shape, jnp.float32) for shape in shapes]
    return pl.pallas_call(
        kernel,
        out_shape=outs,
        in_specs=[VMEM] * len(operands),
        out_specs=[VMEM] * len(outs),
        compiler_params=PARAMS,
        cost_estimate=cost(flops),
    )(*operands)


def after(first, *values):
    return lax.optimization_barrier((first, *values))


def near_exchange(near, sub_size):
    return lax.ppermute(near, "sub", [(i, i ^ 1) for i in range(sub_size)])


def far_exchange(far, sub_size, tile_size, ends_by_tile=True):
    pairs = []
    for t in range(tile_size):
        for i in range(sub_size):
            j = ((i + 1) ^ 1) - 1
            if 0 <= j < sub_size:
                other = (t, j)
            elif ends_by_tile:
                other = (t ^ 1, i)
            else:
                other = (t, sub_size - 1 - i)
            pairs.append((t * sub_size + i, other[0] * sub_size + other[1]))
    return lax.ppermute(far, ("tile", "sub"), pairs)


def swapped(value, bits, tile_size):
    return lax.ppermute(value, "tile", [(t, t ^ bits) for t in range(tile_size)])


def from_behind(value, steps, count):
    return lax.ppermute(value, "tile", [(t, (t + steps) % count) for t in range(count)])


def table_rows(decay, coupling, size_y):
    entries = jnp.concatenate([decay, coupling])
    return jnp.broadcast_to(entries[:, None], (entries.shape[0], size_y))


def two_by_two(seeds, material, decay, coupling, sub_size, tile_size):
    depth, size_x, size_y = seeds.shape[2:]
    edges = ((0, BAND + HALO), (size_x - BAND - HALO, size_x))
    inner = ((BAND - HALO, size_x - BAND + HALO),)
    keep = ((size_x - SHARED) // 2, (size_x + SHARED) // 2)
    span = (keep[0] - HALO // 2, keep[1] + HALO // 2)
    fetched = (keep[0] - HALO, keep[1] + HALO)
    rows = size_x - 2 * BAND
    edge_rows, inner_rows, span_rows = 2 * (BAND + HALO), rows + 2 * HALO, SHARED + 2 * HALO
    packed_rows = (SHARED + HALO) // 2 + 4

    shared = pl.pallas_call(
        functools.partial(share_kernel, fetched, HALO // 2),
        out_shape=jax.ShapeDtypeStruct((7 * depth, packed_rows, size_y), jnp.float32),
        in_specs=[HBM] * 2,
        out_specs=VMEM,
        scratch_shapes=[
            pltpu.VMEM((6, depth, span_rows, size_y), jnp.float32),
            pltpu.VMEM((depth, span_rows, size_y), jnp.int32),
            pltpu.SemaphoreType.DMA((7,)),
        ],
        compiler_params=PARAMS,
        cost_estimate=cost(0),
    )(*(pltpu.with_memory_space_constraint(x, pltpu.HBM) for x in (seeds, material)))
    shared, decay, coupling = after(shared, decay, coupling)
    table = table_rows(decay, coupling, size_y)
    shared = swapped(shared, 2, tile_size)
    edge_near, edge_far, inner_near, inner_far = called(
        functools.partial(halo_pair_kernel, edges, inner, "sub"),
        [(PLANES, edge_rows, size_y)] * 2 + [(PLANES, inner_rows, size_y)] * 2, table, seeds, material,
    )
    edge_near, inner_near = near_exchange(edge_near, sub_size), near_exchange(inner_near, sub_size)
    edge_far = far_exchange(edge_far, sub_size, tile_size)
    inner_far = far_exchange(inner_far, sub_size, tile_size)

    edge_far, decay, coupling = after(edge_far, decay, coupling)
    edge, corner, strip = called(
        functools.partial(edge_kernel, edges, "sub", sub_size, "tile"),
        [(6, depth, 2 * BAND, size_y), (6, depth, BAND, size_y), (6, depth, BAND // 2, size_y)],
        table_rows(decay, coupling, size_y), seeds, material, edge_near, edge_far,
    )
    corner = swapped(corner, 2, tile_size)
    strip = swapped(strip, 3, tile_size)

    shape = (PLANES, packed_rows, size_y)
    shared_near, shared_far = called(
        functools.partial(shared_halo_kernel, "sub"), [shape, shape], table, shared, flops=LARGE
    )
    shared_near, inner_far = after(shared_near, inner_far)
    shared_near = near_exchange(shared_near, sub_size)
    shared_far = far_exchange(shared_far, sub_size, tile_size, ends_by_tile=False)

    mid, bands = called(
        functools.partial(middle_kernel, inner, keep, "sub", sub_size),
        [(6, depth, rows, size_y), (6, depth, (rows - SHARED) // 2, size_y)],
        table, seeds, material, inner_near, inner_far,
    )
    bands = swapped(bands, 2, tile_size)

    corner, strip, mid = after(corner, strip, mid)
    summed, send = called(
        functools.partial(corner_kernel, "tile"),
        [(6, depth, 2 * BAND, size_y), (6, depth, BAND + BAND // 2, size_y)],
        edge, corner, flops=SMALL,
    )
    got = swapped(send, 1, tile_size)
    part, = called(
        functools.partial(shared_kernel, span, size_x, "sub", sub_size),
        [(6, depth, SHARED + HALO, size_y)], table, shared, shared_near, shared_far, flops=MEDIUM,
    )
    edge, = called(
        functools.partial(seam_kernel, "tile"), [(6, depth, 2 * BAND, size_y)], summed, got, strip
    )
    half = (rows - SHARED) // 2
    whole = jax.ShapeDtypeStruct(seeds.shape, jnp.float32)
    early = pl.pallas_call(
        early_kernel,
        out_shape=whole,
        in_specs=[VMEM] * 3,
        out_specs=HBM,
        scratch_shapes=[pltpu.VMEM((6, depth, SHARED, size_y), jnp.float32), pltpu.SemaphoreType.DMA((3,))],
        compiler_params=PARAMS,
        cost_estimate=cost(0),
    )(edge, mid, part)
    return pl.pallas_call(
        last_kernel,
        out_shape=whole,
        in_specs=[VMEM, VMEM, HBM],
        out_specs=HBM,
        scratch_shapes=[pltpu.VMEM((6, depth, half, size_y), jnp.float32)] * 2 + [pltpu.SemaphoreType.DMA((12,))],
        input_output_aliases={2: 0},
        compiler_params=PARAMS,
        cost_estimate=cost(0),
    )(mid, bands, early)


def any_lattice(seeds, material, decay, coupling, sub_size, tile_size):
    depth, size_x, size_y = seeds.shape[2:]
    spans = ((0, size_x),)
    table = table_rows(decay, coupling, size_y)
    shape = (PLANES, size_x, size_y)
    near, far = called(functools.partial(halo_kernel, spans, "sub"), [shape, shape], table, seeds, material)
    near = near_exchange(near, sub_size)
    far = far_exchange(far, sub_size, tile_size)
    weighted, = called(
        functools.partial(whole_kernel, spans, "sub", sub_size), [(6, depth, size_x, size_y)],
        table, seeds, material, near, far,
    )
    side = math.isqrt(tile_size)
    prev_band = from_behind(weighted[:, :, size_x - BAND :, :], 1, tile_size)
    next_band = from_behind(weighted[:, :, :BAND, :], -1, tile_size)
    combined = weighted.at[:, :, :BAND, :].add(prev_band)
    combined = combined.at[:, :, size_x - BAND :, :].add(next_band)
    flat = (6, depth, size_x * BAND // size_y, size_y)
    thin = (6, depth, size_x, BAND)
    top_slab = combined[..., size_y - BAND :].reshape(flat)
    bottom_slab = combined[..., :BAND].reshape(flat)
    result = combined.at[..., :BAND].add(from_behind(top_slab, side, tile_size).reshape(thin))
    result = result.at[..., size_y - BAND :].add(from_behind(bottom_slab, -side, tile_size).reshape(thin))
    return result[None]


def solution(mesh):
    sub_size, tile_size = mesh.shape["sub"], mesh.shape["tile"]
    body = two_by_two if tile_size == 4 else any_lattice

    def on_device(seeds, material, decay, coupling):
        return body(seeds, material, decay, coupling, sub_size, tile_size)

    placed = (P("tile", None, "sub", None, None), P("tile", "sub", None, None), P(), P())
    return jax.shard_map(
        on_device,
        mesh=mesh,
        in_specs=placed,
        out_specs=P("tile", None, "sub", None, None),
        check_vma=False,
    )
```

```python
import functools
import math

import jax
import jax.numpy as jnp
from jax import lax
from jax.experimental import pallas as pl
from jax.experimental.pallas import tpu as pltpu
from jax.sharding import PartitionSpec as P

BAND = 32
STEPS = 2
HALO = 8
PLANES = 5
REACH = 2
SHARED = 80
LARGE, MEDIUM, SMALL = 10**10, 25 * 10**8, 0

magnetic_coeff = 0.5


def lane_of(shape):
    return lax.broadcasted_iota(jnp.int32, shape, len(shape) - 1)


def row_of(shape):
    return lax.broadcasted_iota(jnp.int32, shape, len(shape) - 2)


def rolled(v, shift):
    return pltpu.roll(v, shift % v.shape[-1], v.ndim - 1)


def next_x(v):
    rows = v.shape[0]
    return jnp.where(row_of(v.shape) == rows - 1, 0.0, pltpu.roll(v, rows - 1, 0))


def prev_x(v):
    return jnp.where(row_of(v.shape) == 0, 0.0, pltpu.roll(v, 1, 0))


def next_y(v):
    lanes = v.shape[1]
    return jnp.where(lane_of(v.shape) == lanes - 1, 0.0, pltpu.roll(v, lanes - 1, 1))


def prev_y(v):
    return jnp.where(lane_of(v.shape) == 0, 0.0, pltpu.roll(v, 1, 1))


def plus_x(v):
    return next_x(v) - v


def plus_y(v):
    return next_y(v) - v


def minus_x(v):
    return v - prev_x(v)


def minus_y(v):
    return v - prev_y(v)


def looked_up(labels, entries):
    value = jnp.broadcast_to(entries[0], labels.shape)
    for m in range(1, len(entries)):
        value = jnp.where(labels == m, entries[m], value)
    return value


def update_h(h, v, v_after):
    depth = len(v[0])
    new = [[], [], []]
    for p in range(depth):
        vx, vy, vz = v[0][p], v[1][p], v[2][p]
        up_x, up_y = (v[0][p + 1], v[1][p + 1]) if p + 1 < depth else v_after
        dz_x = up_x - vx if up_x is not None else -vx
        dz_y = up_y - vy if up_y is not None else -vy
        new[0].append(h[0][p] + (plus_y(vz) - dz_y))
        new[1].append(h[1][p] + (dz_x - plus_x(vz)))
        new[2].append(h[2][p] + (plus_x(vy) - plus_y(vx)))
    return new


def update_e(e, ca, h, h_before):
    depth = len(h[0])
    new = [[], [], []]
    for p in range(depth):
        hx, hy, hz = h[0][p], h[1][p], h[2][p]
        low_x, low_y = (h[0][p - 1], h[1][p - 1]) if p > 0 else h_before
        dz_x = hx - low_x if low_x is not None else hx
        dz_y = hy - low_y if low_y is not None else hy
        new[0].append(ca[p] * e[0][p] - magnetic_coeff * (minus_y(hz) - dz_y))
        new[1].append(ca[p] * e[1][p] - magnetic_coeff * (dz_x - minus_x(hz)))
        new[2].append(ca[p] * e[2][p] - magnetic_coeff * (minus_x(hy) - minus_y(hx)))
    return new


def scaled(cb, e):
    return [[cb[p] * e[c][p] for p in range(len(cb))] for c in range(3)]


def joined(ref, index, spans):
    return jnp.concatenate([ref[*index, lo:hi] for lo, hi in spans], axis=0)


def prepared(e, h, labels, tables):
    ca = [looked_up(m, tables[0]) for m in labels]
    cb = [looked_up(m, tables[1]) for m in labels]
    return e, h, ca, cb


def raw(seeds, material, spans):
    depth = seeds.shape[2]
    e = [[joined(seeds, (0, c, p), spans) for p in range(depth)] for c in range(3)]
    h = [[joined(seeds, (0, 3 + c, p), spans) for p in range(depth)] for c in range(3)]
    return e, h, [joined(material, (0, p), spans) for p in range(depth)]


def table_entries(table):
    count = table.shape[0] // 2
    rows = [table[m : m + 1] for m in range(2 * count)]
    return rows[:count], rows[count:]


def loaded(seeds, material, table, spans):
    return prepared(*raw(seeds, material, spans), table_entries(table))


NONE = (None, None)


def send_halos(sub, fields, near, far, packed=lambda planes: planes):
    odd = lax.rem(lax.axis_index(sub), 2) == 1
    e, h, ca, cb = fields
    v1 = scaled(cb, e)
    h1 = update_h(h, v1, NONE)
    e1 = update_e(e, ca, h1, NONE)
    v2 = scaled(cb, e1)
    h2 = update_h(h1, v2, NONE)
    up = (h1[0][-1], h1[1][-1], h2[0][-1], h2[1][-1], cb[-1])
    down = (v1[0][0], v1[1][0], v2[0][0], v2[1][0], cb[0])
    up, down = packed(jnp.stack(up)), packed(jnp.stack(down))
    near[...] = jnp.where(odd, down, up)
    far[...] = jnp.where(odd, up, down)


def halo_kernel(spans, sub, table, seeds, material, near, far):
    send_halos(sub, loaded(seeds, material, table, spans), near, far)


def ramp(position, count):
    position = position.astype(jnp.float32) + 0.5
    return jnp.where(
        position < BAND,
        position / BAND,
        jnp.where(position > count - BAND, (count - position) / BAND, 1.0),
    )


def final_fields(fields, near, far, sub, sub_size, unpacked=lambda planes: planes):
    e, h, ca, cb = fields
    index = lax.axis_index(sub)
    odd = lax.rem(index, 2) == 1
    below, above = index > 0, index < sub_size - 1
    a, b = near[...], far[...]
    from_below = unpacked(jnp.where(odd, a, b))
    from_above = unpacked(jnp.where(above, jnp.where(odd, b, a), 0.0))
    part_h1x, part_h1y, part_h2x, part_h2y, cb_low = from_below
    v1x_up, v1y_up, part_v2x, part_v2y, cb_up = from_above

    v1 = scaled(cb, e)
    h1 = update_h(h, v1, (v1x_up, v1y_up))
    dh1x, dh1y = -v1[1][0], v1[0][0]
    h1_low = (jnp.where(below, part_h1x + dh1x, 0.0), jnp.where(below, part_h1y + dh1y, 0.0))
    e1 = update_e(e, ca, h1, h1_low)
    v2 = scaled(cb, e1)
    v2_up = (
        part_v2x - cb_up * (magnetic_coeff * h1[1][-1]),
        part_v2y + cb_up * (magnetic_coeff * h1[0][-1]),
    )
    h2 = update_h(h1, v2, v2_up)
    dv2x = cb_low * (magnetic_coeff * dh1y)
    dv2y = cb_low * (-magnetic_coeff * dh1x)
    dv2z = cb_low * (-magnetic_coeff * (minus_x(dh1y) - minus_y(dh1x)))
    h2x_low = part_h2x + (dh1x + (plus_y(dv2z) - (v2[1][0] - dv2y)))
    h2y_low = part_h2y + (dh1y + ((v2[0][0] - dv2x) - plus_x(dv2z)))
    h2_low = (jnp.where(below, h2x_low, 0.0), jnp.where(below, h2y_low, 0.0))
    e2 = update_e(e1, ca, h2, h2_low)
    return e2 + h2


def middle_out(block):
    return rolled(block, block.shape[-1] // 2)


def y_packed(first, second):
    lane = lane_of(first.shape)
    middle = (lane >= BAND) & (lane < first.shape[-1] - BAND)
    return jnp.where(middle, middle_out(second), first)


def y_unpacked(block):
    lane = lane_of(block.shape)
    lanes = block.shape[1]
    a, b = pltpu.roll(block, BAND, 1), pltpu.roll(block, lanes - BAND, 1)
    middle = (lane >= BAND) & (lane < lanes - BAND)
    first = jnp.where(middle, 0.0, jnp.where(lane < BAND, a, b))
    second = jnp.where(middle, 0.0, jnp.where(lane < BAND, b, a))
    return first, second


def low_rows(shape):
    return row_of(shape) < 4


def bands_packed(block):
    rows, lanes = block.shape[1:]
    count, width, high = rows // 2 + 4, REACH * (rows // 8), lanes - BAND
    shape = (block.shape[0], 8, lanes)
    lane = lane_of(shape)
    low = low_rows(shape)
    side = jnp.zeros(shape, block.dtype)
    for g in range(rows // 8):
        at = BAND + REACH * (g + 1)
        piece = rolled(block[:, 8 * g : 8 * g + 8], REACH * (g + 1))
        here = ((lane >= at) & (lane < at + REACH)) | (
            (lane >= at + high - BAND - REACH) & (lane < at + high - BAND)
        )
        side = jnp.where(here, piece, side)
    other = rolled(pltpu.roll(side, 4, 1), width + REACH)
    own = ((lane >= BAND) & (lane < BAND + REACH + width)) | ((lane >= high) & (lane < high + width))
    side = jnp.where(own, side, other)
    middle = (lane >= BAND) & (lane < high)
    packed = y_packed(block[:, :count], block[:, rows - count :])
    first = jnp.where(low & middle, side, packed[:, :8])
    last = jnp.where(low | middle, packed[:, count - 8 :], side)
    return jnp.concatenate([first, packed[:, 8 : count - 8], last], axis=1)


def bands_unpacked(packed):
    count, lanes = packed.shape[1:]
    rows = 2 * count - 8
    width, high = REACH * (rows // 8), lanes - BAND
    first, last = packed[:, :8], packed[:, count - 8 :]
    low = low_rows(first.shape)
    lane = lane_of(first.shape)
    middle = (lane >= BAND) & (lane < high)
    side = jnp.where(low, first, last)
    other = rolled(pltpu.roll(side, 4, 1), -width - REACH)
    side = jnp.where(low == middle, side, other)
    beside = ((lane >= BAND) & (lane < BAND + REACH)) | ((lane >= high - REACH) & (lane < high))
    moved = [rolled(packed[:, at : at + 8], lanes // 2) for at in range(0, count, 8)]
    pieces = [packed[:, at : at + 8] for at in range(0, count - 8, 8)]
    pieces += [jnp.where(low, last, moved[0])] + moved[1:]
    result = []
    for g, piece in enumerate(pieces):
        result.append(jnp.where(middle, jnp.where(beside, rolled(side, -REACH * (g + 1)), 0.0), piece))
    return jnp.concatenate(result, axis=1)


def share_kernel(span, skip, seeds, material, shared, held, labels, sems):
    rows = pl.ds(span[0], span[1] - span[0])
    depth = held.shape[1]
    stop = span[1] - span[0] - skip
    copies = [pltpu.make_async_copy(material.at[0, :, rows], labels, sems.at[6])]
    copies += [pltpu.make_async_copy(seeds.at[0, c, :, rows], held.at[c], sems.at[c]) for c in range(6)]
    for copy in copies:
        copy.start()
    copies[0].wait()
    shared[6 * depth :] = bands_packed(labels[:, skip:stop].astype(jnp.float32))
    for c in range(6):
        copies[1 + c].wait()
    shared[: 6 * depth] = bands_packed(jnp.concatenate([held[c, :, skip:stop] for c in range(6)], axis=0))


def halo_pair_kernel(edges, inner, sub, table, seeds, material, near_edge, far_edge, near, far):
    send_halos(sub, loaded(seeds, material, table, edges), near_edge, far_edge)
    send_halos(sub, loaded(seeds, material, table, inner), near, far)


def shared_fields(table, shared):
    depth = shared.shape[0] // 7
    planes = bands_unpacked(shared[...])
    f = [planes[depth * c : depth * (c + 1)] for c in range(7)]
    return prepared(f[:3], f[3:6], f[6], table_entries(table))


def shared_halo_kernel(sub, table, shared, near, far, done):
    done[...] = jnp.zeros(done.shape, done.dtype)
    send_halos(sub, shared_fields(table, shared), near, far, bands_packed)


def weighted_planes(seeds, material, table, near, far, spans, keeps, sub, sub_size):
    planes = final_fields(loaded(seeds, material, table, spans), near, far, sub, sub_size)
    return weighted(planes, spans, keeps, *seeds.shape[3:])


def weighted(planes, spans, keeps, size_x, size_y):
    at, results = 0, []
    for (lo, hi), (start, stop) in zip(spans, keeps):
        shape = (stop - start, size_y)
        weight = ramp(row_of(shape) + start, size_x) * ramp(lane_of(shape), size_y)
        first = at + start - lo
        results.append([[plane[first : first + stop - start] * weight for plane in part] for part in planes])
        at += hi - lo
    return results


def edge_kernel(spans, sub, sub_size, tile, table, seeds, material, near, far, edge, corner, strip):
    size_x = seeds.shape[3]
    keeps = ((0, BAND), (size_x - BAND, size_x))
    low, high = weighted_planes(seeds, material, table, near, far, spans, keeps, sub, sub_size)
    odd = lax.rem(lax.axis_index(tile), 2) == 1
    half = BAND // 2
    for c in range(6):
        for p in range(seeds.shape[2]):
            edge[c, p, :BAND] = low[c][p]
            edge[c, p, BAND:] = high[c][p]
            corner[c, p] = y_packed(low[c][p], high[c][p])
            away = jnp.where(odd, high[c][p], low[c][p])
            strip[c, p] = y_packed(middle_out(away[:half]), middle_out(away[half:]))


def middle_kernel(
    spans, sub, sub_size, tile, table, seeds, material, near, far, edge, _, mid, bands, beside
):
    size_x = seeds.shape[3]
    keep = (BAND, size_x - BAND)
    planes, = weighted_planes(seeds, material, table, near, far, spans, (keep,), sub, sub_size)
    odd = lax.rem(lax.axis_index(tile), 2) == 1
    half, quarter = bands.shape[2], BAND // 2
    for c in range(6):
        for p in range(seeds.shape[2]):
            mid[c, p] = planes[c][p]
            bands[c, p] = y_packed(planes[c][p][:half], planes[c][p][-half:])
            by = jnp.where(odd, edge[c, p, :BAND], edge[c, p, BAND:])
            beside[c, p] = y_packed(middle_out(by[:quarter]), middle_out(by[quarter:]))


def whole_kernel(spans, sub, sub_size, table, seeds, material, near, far, out):
    planes, = weighted_planes(seeds, material, table, near, far, spans, spans, sub, sub_size)
    for c in range(6):
        for p in range(seeds.shape[2]):
            out[c, p] = planes[c][p]


def y_swapped(block):
    lane = lane_of(block.shape)
    lanes = block.shape[1]
    a, b = pltpu.roll(block, BAND, 1), pltpu.roll(block, lanes - BAND, 1)
    middle = (lane >= BAND) & (lane < lanes - BAND)
    return jnp.where(middle, 0.0, jnp.where(lane < BAND, a, b))


def shared_kernel(span, size_x, sub, sub_size, table, shared, near, far, part):
    planes = final_fields(shared_fields(table, shared), near, far, sub, sub_size, bands_unpacked)
    found, = weighted(planes, (span,), (span,), size_x, part.shape[3])
    for c in range(part.shape[0]):
        for p in range(part.shape[1]):
            part[c, p] = y_swapped(found[c][p])


def corner_kernel(tile, edge, corner, summed, send):
    odd = lax.rem(lax.axis_index(tile), 2) == 1
    half = BAND // 2
    for c in range(edge.shape[0]):
        for p in range(edge.shape[1]):
            first, second = y_unpacked(corner[c, p])
            low = edge[c, p, :BAND] + first
            high = edge[c, p, BAND:] + second
            summed[c, p, :BAND] = low
            summed[c, p, BAND:] = high
            by, away = jnp.where(odd, low, high), jnp.where(odd, high, low)
            send[c, p, :half] = y_packed(by[:half], by[half:])
            send[c, p, half:] = y_packed(away[:half], away[half:])


def strip_of(corners, block):
    lane = lane_of(block.shape)
    middle = (lane >= BAND) & (lane < block.shape[-1] - BAND)
    first = jnp.where(middle, middle_out(block), corners[0])
    second = jnp.where(middle, block, corners[1])
    return jnp.concatenate([first, second], axis=0)


def early_kernel(mid, part, out, whole, sem):
    size_x = out.shape[3]
    skip = HALO // 2
    count = part.shape[2] - 2 * skip
    start = (size_x - count) // 2
    for c in range(mid.shape[0]):
        for p in range(mid.shape[1]):
            whole[c, p] = mid[c, p, start - BAND : start - BAND + count] + part[c, p, skip : skip + count]
    copy = pltpu.make_async_copy(whole, out.at[0, :, :, pl.ds(start, count)], sem)
    copy.start()
    copy.wait()


def last_kernel(tile, mid, bands, summed, got, strip, beside, _, out, low, high, sems):
    odd = lax.rem(lax.axis_index(tile), 2) == 1
    half, count = bands.shape[2], low.shape[2]
    quarter = BAND // 2
    size_x = out.shape[3]
    copies = []
    for c in range(mid.shape[0]):
        for p in range(mid.shape[1]):
            first, second = y_unpacked(bands[c, p])
            low[c, p, BAND:] = mid[c, p, :half] + first
            high[c, p, :half] = mid[c, p, -half:] + second
            straight = got[c, p, :quarter]
            by = strip_of((straight, middle_out(straight)), beside[c, p])
            away = strip_of(y_unpacked(got[c, p, quarter:]), strip[c, p])
            low[c, p, :BAND] = summed[c, p, :BAND] + jnp.where(odd, by, away)
            high[c, p, half:] = summed[c, p, BAND:] + jnp.where(odd, away, by)
        for k, (rows, start) in enumerate(((low, 0), (high, size_x - count))):
            copies.append(pltpu.make_async_copy(rows.at[c], out.at[0, c, :, pl.ds(start, count)], sems.at[2 * c + k]))
            copies[-1].start()
    for copy in copies:
        copy.wait()


HBM = pl.BlockSpec(memory_space=pltpu.HBM)
VMEM = pl.BlockSpec(memory_space=pltpu.VMEM)
PARAMS = pltpu.CompilerParams(vmem_limit_bytes=32 * 1024 * 1024)


def cost(flops):
    return pl.CostEstimate(flops=flops, bytes_accessed=0, transcendentals=0)


def called(kernel, shapes, *operands, flops=0):
    outs = [jax.ShapeDtypeStruct(shape, jnp.float32) for shape in shapes]
    return pl.pallas_call(
        kernel,
        out_shape=outs,
        in_specs=[VMEM] * len(operands),
        out_specs=[VMEM] * len(outs),
        compiler_params=PARAMS,
        cost_estimate=cost(flops),
    )(*operands)


def after(first, *values):
    return lax.optimization_barrier((first, *values))


def near_exchange(near, sub_size):
    return lax.ppermute(near, "sub", [(i, i ^ 1) for i in range(sub_size)])


def far_exchange(far, sub_size, tile_size, ends_by_tile=True):
    pairs = []
    for t in range(tile_size):
        for i in range(sub_size):
            j = ((i + 1) ^ 1) - 1
            if 0 <= j < sub_size:
                other = (t, j)
            elif ends_by_tile:
                other = (t ^ 1, i)
            else:
                other = (t, sub_size - 1 - i)
            pairs.append((t * sub_size + i, other[0] * sub_size + other[1]))
    return lax.ppermute(far, ("tile", "sub"), pairs)


def swapped(value, bits, tile_size):
    return lax.ppermute(value, "tile", [(t, t ^ bits) for t in range(tile_size)])


def from_behind(value, steps, count):
    return lax.ppermute(value, "tile", [(t, (t + steps) % count) for t in range(count)])


def table_rows(decay, coupling, size_y):
    entries = jnp.concatenate([decay, coupling])
    return jnp.broadcast_to(entries[:, None], (entries.shape[0], size_y))


def two_by_two(seeds, material, decay, coupling, sub_size, tile_size):
    depth, size_x, size_y = seeds.shape[2:]
    edges = ((0, BAND + HALO), (size_x - BAND - HALO, size_x))
    inner = ((BAND - HALO, size_x - BAND + HALO),)
    keep = ((size_x - SHARED) // 2, (size_x + SHARED) // 2)
    span = (keep[0] - HALO // 2, keep[1] + HALO // 2)
    fetched = (keep[0] - HALO, keep[1] + HALO)
    rows = size_x - 2 * BAND
    edge_rows, inner_rows, span_rows = 2 * (BAND + HALO), rows + 2 * HALO, SHARED + 2 * HALO
    packed_rows = (SHARED + HALO) // 2 + 4

    shared = pl.pallas_call(
        functools.partial(share_kernel, fetched, HALO // 2),
        out_shape=jax.ShapeDtypeStruct((7 * depth, packed_rows, size_y), jnp.float32),
        in_specs=[HBM] * 2,
        out_specs=VMEM,
        scratch_shapes=[
            pltpu.VMEM((6, depth, span_rows, size_y), jnp.float32),
            pltpu.VMEM((depth, span_rows, size_y), jnp.int32),
            pltpu.SemaphoreType.DMA((7,)),
        ],
        compiler_params=PARAMS,
        cost_estimate=cost(0),
    )(*(pltpu.with_memory_space_constraint(x, pltpu.HBM) for x in (seeds, material)))
    shared, decay, coupling = after(shared, decay, coupling)
    table = table_rows(decay, coupling, size_y)
    shared = swapped(shared, 2, tile_size)
    edge_near, edge_far, inner_near, inner_far = called(
        functools.partial(halo_pair_kernel, edges, inner, "sub"),
        [(PLANES, edge_rows, size_y)] * 2 + [(PLANES, inner_rows, size_y)] * 2, table, seeds, material,
    )
    edge_near, inner_near = near_exchange(edge_near, sub_size), near_exchange(inner_near, sub_size)
    edge_far = far_exchange(edge_far, sub_size, tile_size)
    inner_far = far_exchange(inner_far, sub_size, tile_size)

    edge_far, decay, coupling = after(edge_far, decay, coupling)
    edge, corner, strip = called(
        functools.partial(edge_kernel, edges, "sub", sub_size, "tile"),
        [(6, depth, 2 * BAND, size_y), (6, depth, BAND, size_y), (6, depth, BAND // 2, size_y)],
        table_rows(decay, coupling, size_y), seeds, material, edge_near, edge_far,
    )
    corner = swapped(corner, 2, tile_size)
    strip = swapped(strip, 3, tile_size)

    shape = (PLANES, packed_rows, size_y)
    shared_near, shared_far, done = called(
        functools.partial(shared_halo_kernel, "sub"), [shape, shape, (8, size_y)], table, shared, flops=LARGE
    )
    shared_near = near_exchange(shared_near, sub_size)
    shared_far = far_exchange(shared_far, sub_size, tile_size, ends_by_tile=False)

    mid, bands, beside = called(
        functools.partial(middle_kernel, inner, "sub", sub_size, "tile"),
        [(6, depth, rows, size_y), (6, depth, (rows - SHARED) // 2, size_y), (6, depth, BAND // 2, size_y)],
        table, seeds, material, inner_near, inner_far, edge, done,
    )
    bands = swapped(bands, 2, tile_size)
    beside = swapped(beside, 1, tile_size)

    corner, strip, mid = after(corner, strip, mid)
    summed, send = called(
        functools.partial(corner_kernel, "tile"),
        [(6, depth, 2 * BAND, size_y), (6, depth, BAND, size_y)],
        edge, corner, flops=SMALL,
    )
    got = swapped(send, 1, tile_size)
    beside, shared_near = after(beside, shared_near)
    part, = called(
        functools.partial(shared_kernel, span, size_x, "sub", sub_size),
        [(6, depth, SHARED + HALO, size_y)], table, shared, shared_near, shared_far, flops=MEDIUM,
    )
    whole = jax.ShapeDtypeStruct(seeds.shape, jnp.float32)
    early = pl.pallas_call(
        early_kernel,
        out_shape=whole,
        in_specs=[VMEM] * 2,
        out_specs=HBM,
        scratch_shapes=[pltpu.VMEM((6, depth, SHARED, size_y), jnp.float32), pltpu.SemaphoreType.DMA],
        compiler_params=PARAMS,
        cost_estimate=cost(0),
    )(mid, part)
    return pl.pallas_call(
        functools.partial(last_kernel, "tile"),
        out_shape=whole,
        in_specs=[VMEM] * 6 + [HBM],
        out_specs=HBM,
        scratch_shapes=[pltpu.VMEM((6, depth, (size_x - SHARED) // 2, size_y), jnp.float32)] * 2
        + [pltpu.SemaphoreType.DMA((12,))],
        input_output_aliases={6: 0},
        compiler_params=PARAMS,
        cost_estimate=cost(0),
    )(mid, bands, summed, got, strip, beside, early)


def any_lattice(seeds, material, decay, coupling, sub_size, tile_size):
    depth, size_x, size_y = seeds.shape[2:]
    spans = ((0, size_x),)
    table = table_rows(decay, coupling, size_y)
    shape = (PLANES, size_x, size_y)
    near, far = called(functools.partial(halo_kernel, spans, "sub"), [shape, shape], table, seeds, material)
    near = near_exchange(near, sub_size)
    far = far_exchange(far, sub_size, tile_size)
    weighted, = called(
        functools.partial(whole_kernel, spans, "sub", sub_size), [(6, depth, size_x, size_y)],
        table, seeds, material, near, far,
    )
    side = math.isqrt(tile_size)
    prev_band = from_behind(weighted[:, :, size_x - BAND :, :], 1, tile_size)
    next_band = from_behind(weighted[:, :, :BAND, :], -1, tile_size)
    combined = weighted.at[:, :, :BAND, :].add(prev_band)
    combined = combined.at[:, :, size_x - BAND :, :].add(next_band)
    flat = (6, depth, size_x * BAND // size_y, size_y)
    thin = (6, depth, size_x, BAND)
    top_slab = combined[..., size_y - BAND :].reshape(flat)
    bottom_slab = combined[..., :BAND].reshape(flat)
    result = combined.at[..., :BAND].add(from_behind(top_slab, side, tile_size).reshape(thin))
    result = result.at[..., size_y - BAND :].add(from_behind(bottom_slab, -side, tile_size).reshape(thin))
    return result[None]


def solution(mesh):
    sub_size, tile_size = mesh.shape["sub"], mesh.shape["tile"]
    body = two_by_two if tile_size == 4 else any_lattice

    def on_device(seeds, material, decay, coupling):
        return body(seeds, material, decay, coupling, sub_size, tile_size)

    placed = (P("tile", None, "sub", None, None), P("tile", "sub", None, None), P(), P())
    return jax.shard_map(
        on_device,
        mesh=mesh,
        in_specs=placed,
        out_specs=P("tile", None, "sub", None, None),
        check_vma=False,
    )
```

```python
import functools
import math

import jax
import jax.numpy as jnp
from jax import lax
from jax.experimental import pallas as pl
from jax.experimental.pallas import tpu as pltpu
from jax.sharding import PartitionSpec as P

BAND = 32
STEPS = 2
HALO = 8
PLANES = 5
REACH = 2
SHARED = 96
LARGE, MEDIUM, SMALL = 10**10, 2 * 10**9, 0

magnetic_coeff = 0.5


def lane_of(shape):
    return lax.broadcasted_iota(jnp.int32, shape, len(shape) - 1)


def row_of(shape):
    return lax.broadcasted_iota(jnp.int32, shape, len(shape) - 2)


def rolled(v, shift):
    return pltpu.roll(v, shift % v.shape[-1], v.ndim - 1)


def next_x(v):
    rows = v.shape[0]
    return jnp.where(row_of(v.shape) == rows - 1, 0.0, pltpu.roll(v, rows - 1, 0))


def prev_x(v):
    return jnp.where(row_of(v.shape) == 0, 0.0, pltpu.roll(v, 1, 0))


def next_y(v):
    lanes = v.shape[1]
    return jnp.where(lane_of(v.shape) == lanes - 1, 0.0, pltpu.roll(v, lanes - 1, 1))


def prev_y(v):
    return jnp.where(lane_of(v.shape) == 0, 0.0, pltpu.roll(v, 1, 1))


def plus_x(v):
    return next_x(v) - v


def plus_y(v):
    return next_y(v) - v


def minus_x(v):
    return v - prev_x(v)


def minus_y(v):
    return v - prev_y(v)


def looked_up(labels, entries):
    value = jnp.broadcast_to(entries[0], labels.shape)
    for m in range(1, len(entries)):
        value = jnp.where(labels == m, entries[m], value)
    return value


def update_h(h, v, v_after):
    depth = len(v[0])
    new = [[], [], []]
    for p in range(depth):
        vx, vy, vz = v[0][p], v[1][p], v[2][p]
        up_x, up_y = (v[0][p + 1], v[1][p + 1]) if p + 1 < depth else v_after
        dz_x = up_x - vx if up_x is not None else -vx
        dz_y = up_y - vy if up_y is not None else -vy
        new[0].append(h[0][p] + (plus_y(vz) - dz_y))
        new[1].append(h[1][p] + (dz_x - plus_x(vz)))
        new[2].append(h[2][p] + (plus_x(vy) - plus_y(vx)))
    return new


def update_e(e, ca, h, h_before):
    depth = len(h[0])
    new = [[], [], []]
    for p in range(depth):
        hx, hy, hz = h[0][p], h[1][p], h[2][p]
        low_x, low_y = (h[0][p - 1], h[1][p - 1]) if p > 0 else h_before
        dz_x = hx - low_x if low_x is not None else hx
        dz_y = hy - low_y if low_y is not None else hy
        new[0].append(ca[p] * e[0][p] - magnetic_coeff * (minus_y(hz) - dz_y))
        new[1].append(ca[p] * e[1][p] - magnetic_coeff * (dz_x - minus_x(hz)))
        new[2].append(ca[p] * e[2][p] - magnetic_coeff * (minus_x(hy) - minus_y(hx)))
    return new


def scaled(cb, e):
    return [[cb[p] * e[c][p] for p in range(len(cb))] for c in range(3)]


def joined(ref, index, spans):
    return jnp.concatenate([ref[*index, lo:hi] for lo, hi in spans], axis=0)


def prepared(e, h, labels, tables):
    ca = [looked_up(m, tables[0]) for m in labels]
    cb = [looked_up(m, tables[1]) for m in labels]
    return e, h, ca, cb


def raw(seeds, material, spans):
    depth = seeds.shape[2]
    e = [[joined(seeds, (0, c, p), spans) for p in range(depth)] for c in range(3)]
    h = [[joined(seeds, (0, 3 + c, p), spans) for p in range(depth)] for c in range(3)]
    return e, h, [joined(material, (0, p), spans) for p in range(depth)]


def table_entries(table):
    count = table.shape[0] // 2
    rows = [table[m : m + 1] for m in range(2 * count)]
    return rows[:count], rows[count:]


def loaded(seeds, material, table, spans):
    return prepared(*raw(seeds, material, spans), table_entries(table))


NONE = (None, None)


def send_halos(sub, fields, near, far, packed=lambda planes: planes):
    odd = lax.rem(lax.axis_index(sub), 2) == 1
    e, h, ca, cb = fields
    v1 = scaled(cb, e)
    h1 = update_h(h, v1, NONE)
    e1 = update_e(e, ca, h1, NONE)
    v2 = scaled(cb, e1)
    h2 = update_h(h1, v2, NONE)
    up = (h1[0][-1], h1[1][-1], h2[0][-1], h2[1][-1], cb[-1])
    down = (v1[0][0], v1[1][0], v2[0][0], v2[1][0], cb[0])
    up, down = packed(jnp.stack(up)), packed(jnp.stack(down))
    near[...] = jnp.where(odd, down, up)
    far[...] = jnp.where(odd, up, down)


def halo_kernel(spans, sub, table, seeds, material, near, far):
    send_halos(sub, loaded(seeds, material, table, spans), near, far)


def ramp(position, count):
    position = position.astype(jnp.float32) + 0.5
    return jnp.where(
        position < BAND,
        position / BAND,
        jnp.where(position > count - BAND, (count - position) / BAND, 1.0),
    )


def final_fields(fields, near, far, sub, sub_size, unpacked=lambda planes: planes):
    e, h, ca, cb = fields
    index = lax.axis_index(sub)
    odd = lax.rem(index, 2) == 1
    below, above = index > 0, index < sub_size - 1
    a, b = near[...], far[...]
    from_below = unpacked(jnp.where(odd, a, b))
    from_above = unpacked(jnp.where(above, jnp.where(odd, b, a), 0.0))
    part_h1x, part_h1y, part_h2x, part_h2y, cb_low = from_below
    v1x_up, v1y_up, part_v2x, part_v2y, cb_up = from_above

    v1 = scaled(cb, e)
    h1 = update_h(h, v1, (v1x_up, v1y_up))
    dh1x, dh1y = -v1[1][0], v1[0][0]
    h1_low = (jnp.where(below, part_h1x + dh1x, 0.0), jnp.where(below, part_h1y + dh1y, 0.0))
    e1 = update_e(e, ca, h1, h1_low)
    v2 = scaled(cb, e1)
    v2_up = (
        part_v2x - cb_up * (magnetic_coeff * h1[1][-1]),
        part_v2y + cb_up * (magnetic_coeff * h1[0][-1]),
    )
    h2 = update_h(h1, v2, v2_up)
    dv2x = cb_low * (magnetic_coeff * dh1y)
    dv2y = cb_low * (-magnetic_coeff * dh1x)
    dv2z = cb_low * (-magnetic_coeff * (minus_x(dh1y) - minus_y(dh1x)))
    h2x_low = part_h2x + (dh1x + (plus_y(dv2z) - (v2[1][0] - dv2y)))
    h2y_low = part_h2y + (dh1y + ((v2[0][0] - dv2x) - plus_x(dv2z)))
    h2_low = (jnp.where(below, h2x_low, 0.0), jnp.where(below, h2y_low, 0.0))
    e2 = update_e(e1, ca, h2, h2_low)
    return e2 + h2


def middle_out(block):
    return rolled(block, block.shape[-1] // 2)


def y_packed(first, second):
    lane = lane_of(first.shape)
    middle = (lane >= BAND) & (lane < first.shape[-1] - BAND)
    return jnp.where(middle, middle_out(second), first)


def y_unpacked(block):
    lane = lane_of(block.shape)
    lanes = block.shape[1]
    a, b = pltpu.roll(block, BAND, 1), pltpu.roll(block, lanes - BAND, 1)
    middle = (lane >= BAND) & (lane < lanes - BAND)
    first = jnp.where(middle, 0.0, jnp.where(lane < BAND, a, b))
    second = jnp.where(middle, 0.0, jnp.where(lane < BAND, b, a))
    return first, second


def low_rows(shape):
    return row_of(shape) < 4


def bands_packed(block):
    rows, lanes = block.shape[1:]
    count, width, high = rows // 2 + 4, REACH * (rows // 8), lanes - BAND
    shape = (block.shape[0], 8, lanes)
    lane = lane_of(shape)
    low = low_rows(shape)
    side = jnp.zeros(shape, block.dtype)
    for g in range(rows // 8):
        at = BAND + REACH * (g + 1)
        piece = rolled(block[:, 8 * g : 8 * g + 8], REACH * (g + 1))
        here = ((lane >= at) & (lane < at + REACH)) | (
            (lane >= at + high - BAND - REACH) & (lane < at + high - BAND)
        )
        side = jnp.where(here, piece, side)
    other = rolled(pltpu.roll(side, 4, 1), width + REACH)
    own = ((lane >= BAND) & (lane < BAND + REACH + width)) | ((lane >= high) & (lane < high + width))
    side = jnp.where(own, side, other)
    middle = (lane >= BAND) & (lane < high)
    packed = y_packed(block[:, :count], block[:, rows - count :])
    first = jnp.where(low & middle, side, packed[:, :8])
    last = jnp.where(low | middle, packed[:, count - 8 :], side)
    return jnp.concatenate([first, packed[:, 8 : count - 8], last], axis=1)


def bands_unpacked(packed):
    count, lanes = packed.shape[1:]
    rows = 2 * count - 8
    width, high = REACH * (rows // 8), lanes - BAND
    first, last = packed[:, :8], packed[:, count - 8 :]
    low = low_rows(first.shape)
    lane = lane_of(first.shape)
    middle = (lane >= BAND) & (lane < high)
    side = jnp.where(low, first, last)
    other = rolled(pltpu.roll(side, 4, 1), -width - REACH)
    side = jnp.where(low == middle, side, other)
    beside = ((lane >= BAND) & (lane < BAND + REACH)) | ((lane >= high - REACH) & (lane < high))
    moved = [rolled(packed[:, at : at + 8], lanes // 2) for at in range(0, count, 8)]
    pieces = [packed[:, at : at + 8] for at in range(0, count - 8, 8)]
    pieces += [jnp.where(low, last, moved[0])] + moved[1:]
    result = []
    for g, piece in enumerate(pieces):
        result.append(jnp.where(middle, jnp.where(beside, rolled(side, -REACH * (g + 1)), 0.0), piece))
    return jnp.concatenate(result, axis=1)


def share_kernel(span, skip, seeds, material, shared, held, labels, sems):
    rows = pl.ds(span[0], span[1] - span[0])
    depth = held.shape[1]
    stop = span[1] - span[0] - skip
    copies = [pltpu.make_async_copy(material.at[0, :, rows], labels, sems.at[6])]
    copies += [pltpu.make_async_copy(seeds.at[0, c, :, rows], held.at[c], sems.at[c]) for c in range(6)]
    for copy in copies:
        copy.start()
    copies[0].wait()
    shared[6 * depth :] = bands_packed(labels[:, skip:stop].astype(jnp.float32))
    for c in range(6):
        copies[1 + c].wait()
    shared[: 6 * depth] = bands_packed(jnp.concatenate([held[c, :, skip:stop] for c in range(6)], axis=0))


def halo_pair_kernel(edges, inner, sub, table, seeds, material, near_edge, far_edge, near, far):
    send_halos(sub, loaded(seeds, material, table, edges), near_edge, far_edge)
    send_halos(sub, loaded(seeds, material, table, inner), near, far)


def shared_fields(table, shared):
    depth = shared.shape[0] // 7
    planes = bands_unpacked(shared[...])
    f = [planes[depth * c : depth * (c + 1)] for c in range(7)]
    return prepared(f[:3], f[3:6], f[6], table_entries(table))


def shared_halo_kernel(sub, table, shared, near, far, done):
    done[...] = jnp.zeros(done.shape, done.dtype)
    send_halos(sub, shared_fields(table, shared), near, far, bands_packed)


def weighted_planes(seeds, material, table, near, far, spans, keeps, sub, sub_size):
    planes = final_fields(loaded(seeds, material, table, spans), near, far, sub, sub_size)
    return weighted(planes, spans, keeps, *seeds.shape[3:])


def weighted(planes, spans, keeps, size_x, size_y):
    at, results = 0, []
    for (lo, hi), (start, stop) in zip(spans, keeps):
        shape = (stop - start, size_y)
        weight = ramp(row_of(shape) + start, size_x) * ramp(lane_of(shape), size_y)
        first = at + start - lo
        results.append([[plane[first : first + stop - start] * weight for plane in part] for part in planes])
        at += hi - lo
    return results


def edge_kernel(spans, sub, sub_size, tile, table, seeds, material, near, far, edge, corner, strip):
    size_x = seeds.shape[3]
    keeps = ((0, BAND), (size_x - BAND, size_x))
    low, high = weighted_planes(seeds, material, table, near, far, spans, keeps, sub, sub_size)
    odd = lax.rem(lax.axis_index(tile), 2) == 1
    half = BAND // 2
    for c in range(6):
        for p in range(seeds.shape[2]):
            edge[c, p, :BAND] = low[c][p]
            edge[c, p, BAND:] = high[c][p]
            corner[c, p] = y_packed(low[c][p], high[c][p])
            away = jnp.where(odd, high[c][p], low[c][p])
            strip[c, p] = y_packed(middle_out(away[:half]), middle_out(away[half:]))


def middle_kernel(
    spans, sub, sub_size, tile, table, seeds, material, near, far, edge, _, mid, bands, beside
):
    size_x = seeds.shape[3]
    keep = (BAND, size_x - BAND)
    planes, = weighted_planes(seeds, material, table, near, far, spans, (keep,), sub, sub_size)
    odd = lax.rem(lax.axis_index(tile), 2) == 1
    half, quarter = bands.shape[2], BAND // 2
    for c in range(6):
        for p in range(seeds.shape[2]):
            mid[c, p] = planes[c][p]
            bands[c, p] = y_packed(planes[c][p][:half], planes[c][p][-half:])
            by = jnp.where(odd, edge[c, p, :BAND], edge[c, p, BAND:])
            beside[c, p] = y_packed(middle_out(by[:quarter]), middle_out(by[quarter:]))


def whole_kernel(spans, sub, sub_size, table, seeds, material, near, far, out):
    planes, = weighted_planes(seeds, material, table, near, far, spans, spans, sub, sub_size)
    for c in range(6):
        for p in range(seeds.shape[2]):
            out[c, p] = planes[c][p]


def y_swapped(block):
    lane = lane_of(block.shape)
    lanes = block.shape[1]
    a, b = pltpu.roll(block, BAND, 1), pltpu.roll(block, lanes - BAND, 1)
    middle = (lane >= BAND) & (lane < lanes - BAND)
    return jnp.where(middle, 0.0, jnp.where(lane < BAND, a, b))


def shared_kernel(span, size_x, sub, sub_size, table, shared, near, far, part):
    planes = final_fields(shared_fields(table, shared), near, far, sub, sub_size, bands_unpacked)
    found, = weighted(planes, (span,), (span,), size_x, part.shape[3])
    for c in range(part.shape[0]):
        for p in range(part.shape[1]):
            part[c, p] = y_swapped(found[c][p])


def corner_kernel(tile, edge, corner, summed, send):
    odd = lax.rem(lax.axis_index(tile), 2) == 1
    half = BAND // 2
    for c in range(edge.shape[0]):
        for p in range(edge.shape[1]):
            first, second = y_unpacked(corner[c, p])
            low = edge[c, p, :BAND] + first
            high = edge[c, p, BAND:] + second
            summed[c, p, :BAND] = low
            summed[c, p, BAND:] = high
            by, away = jnp.where(odd, low, high), jnp.where(odd, high, low)
            send[c, p, :half] = y_packed(by[:half], by[half:])
            send[c, p, half:] = y_packed(away[:half], away[half:])


def strip_of(corners, block):
    lane = lane_of(block.shape)
    middle = (lane >= BAND) & (lane < block.shape[-1] - BAND)
    first = jnp.where(middle, middle_out(block), corners[0])
    second = jnp.where(middle, block, corners[1])
    return jnp.concatenate([first, second], axis=0)


def early_kernel(mid, part, out, whole, sem):
    size_x = out.shape[3]
    skip = HALO // 2
    count = part.shape[2] - 2 * skip
    start = (size_x - count) // 2
    for c in range(mid.shape[0]):
        for p in range(mid.shape[1]):
            whole[c, p] = mid[c, p, start - BAND : start - BAND + count] + part[c, p, skip : skip + count]
    copy = pltpu.make_async_copy(whole, out.at[0, :, :, pl.ds(start, count)], sem)
    copy.start()
    copy.wait()


def last_kernel(tile, mid, bands, summed, got, strip, beside, _, out, low, high, sems):
    odd = lax.rem(lax.axis_index(tile), 2) == 1
    half, count = bands.shape[2], low.shape[2]
    quarter = BAND // 2
    size_x = out.shape[3]
    copies = []
    for c in range(mid.shape[0]):
        for p in range(mid.shape[1]):
            first, second = y_unpacked(bands[c, p])
            low[c, p, BAND:] = mid[c, p, :half] + first
            high[c, p, :half] = mid[c, p, -half:] + second
            straight = got[c, p, :quarter]
            by = strip_of((straight, middle_out(straight)), beside[c, p])
            away = strip_of(y_unpacked(got[c, p, quarter:]), strip[c, p])
            low[c, p, :BAND] = summed[c, p, :BAND] + jnp.where(odd, by, away)
            high[c, p, half:] = summed[c, p, BAND:] + jnp.where(odd, away, by)
        for k, (rows, start) in enumerate(((low, 0), (high, size_x - count))):
            copies.append(pltpu.make_async_copy(rows.at[c], out.at[0, c, :, pl.ds(start, count)], sems.at[2 * c + k]))
            copies[-1].start()
    for copy in copies:
        copy.wait()


HBM = pl.BlockSpec(memory_space=pltpu.HBM)
VMEM = pl.BlockSpec(memory_space=pltpu.VMEM)
PARAMS = pltpu.CompilerParams(vmem_limit_bytes=32 * 1024 * 1024)


def cost(flops):
    return pl.CostEstimate(flops=flops, bytes_accessed=0, transcendentals=0)


def called(kernel, shapes, *operands, flops=0):
    outs = [jax.ShapeDtypeStruct(shape, jnp.float32) for shape in shapes]
    return pl.pallas_call(
        kernel,
        out_shape=outs,
        in_specs=[VMEM] * len(operands),
        out_specs=[VMEM] * len(outs),
        compiler_params=PARAMS,
        cost_estimate=cost(flops),
    )(*operands)


def after(first, *values):
    return lax.optimization_barrier((first, *values))


def near_exchange(near, sub_size):
    return lax.ppermute(near, "sub", [(i, i ^ 1) for i in range(sub_size)])


def far_exchange(far, sub_size, tile_size):
    pairs = []
    for t in range(tile_size):
        for i in range(sub_size):
            j = ((i + 1) ^ 1) - 1
            other = (t, j) if 0 <= j < sub_size else (t ^ 1, i)
            pairs.append((t * sub_size + i, other[0] * sub_size + other[1]))
    return lax.ppermute(far, ("tile", "sub"), pairs)


def swapped(value, bits, tile_size):
    return lax.ppermute(value, "tile", [(t, t ^ bits) for t in range(tile_size)])


def from_behind(value, steps, count):
    return lax.ppermute(value, "tile", [(t, (t + steps) % count) for t in range(count)])


def table_rows(decay, coupling, size_y):
    entries = jnp.concatenate([decay, coupling])
    return jnp.broadcast_to(entries[:, None], (entries.shape[0], size_y))


def two_by_two(seeds, material, decay, coupling, sub_size, tile_size):
    depth, size_x, size_y = seeds.shape[2:]
    edges = ((0, BAND + HALO), (size_x - BAND - HALO, size_x))
    inner = ((BAND - HALO, size_x - BAND + HALO),)
    keep = ((size_x - SHARED) // 2, (size_x + SHARED) // 2)
    span = (keep[0] - HALO // 2, keep[1] + HALO // 2)
    fetched = (keep[0] - HALO, keep[1] + HALO)
    rows = size_x - 2 * BAND
    edge_rows, inner_rows, span_rows = 2 * (BAND + HALO), rows + 2 * HALO, SHARED + 2 * HALO
    packed_rows = (SHARED + HALO) // 2 + 4

    shared = pl.pallas_call(
        functools.partial(share_kernel, fetched, HALO // 2),
        out_shape=jax.ShapeDtypeStruct((7 * depth, packed_rows, size_y), jnp.float32),
        in_specs=[HBM] * 2,
        out_specs=VMEM,
        scratch_shapes=[
            pltpu.VMEM((6, depth, span_rows, size_y), jnp.float32),
            pltpu.VMEM((depth, span_rows, size_y), jnp.int32),
            pltpu.SemaphoreType.DMA((7,)),
        ],
        compiler_params=PARAMS,
        cost_estimate=cost(0),
    )(*(pltpu.with_memory_space_constraint(x, pltpu.HBM) for x in (seeds, material)))
    shared, decay, coupling = after(shared, decay, coupling)
    table = table_rows(decay, coupling, size_y)
    shared = swapped(shared, 2, tile_size)
    edge_near, edge_far, inner_near, inner_far = called(
        functools.partial(halo_pair_kernel, edges, inner, "sub"),
        [(PLANES, edge_rows, size_y)] * 2 + [(PLANES, inner_rows, size_y)] * 2, table, seeds, material,
    )
    edge_near, inner_near = near_exchange(edge_near, sub_size), near_exchange(inner_near, sub_size)
    edge_far = far_exchange(edge_far, sub_size, tile_size)
    inner_far = far_exchange(inner_far, sub_size, tile_size)

    edge_far, decay, coupling = after(edge_far, decay, coupling)
    edge, corner, strip = called(
        functools.partial(edge_kernel, edges, "sub", sub_size, "tile"),
        [(6, depth, 2 * BAND, size_y), (6, depth, BAND, size_y), (6, depth, BAND // 2, size_y)],
        table_rows(decay, coupling, size_y), seeds, material, edge_near, edge_far,
    )
    corner = swapped(corner, 2, tile_size)
    strip = swapped(strip, 3, tile_size)

    shape = (PLANES, packed_rows, size_y)
    shared_near, shared_far, done = called(
        functools.partial(shared_halo_kernel, "sub"), [shape, shape, (8, size_y)], table, shared, flops=LARGE
    )
    shared_near = near_exchange(shared_near, sub_size)
    shared_far = far_exchange(shared_far, sub_size, tile_size)

    mid, bands, beside = called(
        functools.partial(middle_kernel, inner, "sub", sub_size, "tile"),
        [(6, depth, rows, size_y), (6, depth, (rows - SHARED) // 2, size_y), (6, depth, BAND // 2, size_y)],
        table, seeds, material, inner_near, inner_far, edge, done,
    )
    bands = swapped(bands, 2, tile_size)
    beside = swapped(beside, 1, tile_size)

    corner, strip, mid = after(corner, strip, mid)
    summed, send = called(
        functools.partial(corner_kernel, "tile"),
        [(6, depth, 2 * BAND, size_y), (6, depth, BAND, size_y)],
        edge, corner, flops=SMALL,
    )
    got = swapped(send, 1, tile_size)
    beside, shared_near = after(beside, shared_near)
    part, = called(
        functools.partial(shared_kernel, span, size_x, "sub", sub_size),
        [(6, depth, SHARED + HALO, size_y)], table, shared, shared_near, shared_far, flops=MEDIUM,
    )
    whole = jax.ShapeDtypeStruct(seeds.shape, jnp.float32)
    early = pl.pallas_call(
        early_kernel,
        out_shape=whole,
        in_specs=[VMEM] * 2,
        out_specs=HBM,
        scratch_shapes=[pltpu.VMEM((6, depth, SHARED, size_y), jnp.float32), pltpu.SemaphoreType.DMA],
        compiler_params=PARAMS,
        cost_estimate=cost(0),
    )(mid, part)
    return pl.pallas_call(
        functools.partial(last_kernel, "tile"),
        out_shape=whole,
        in_specs=[VMEM] * 6 + [HBM],
        out_specs=HBM,
        scratch_shapes=[pltpu.VMEM((6, depth, (size_x - SHARED) // 2, size_y), jnp.float32)] * 2
        + [pltpu.SemaphoreType.DMA((12,))],
        input_output_aliases={6: 0},
        compiler_params=PARAMS,
        cost_estimate=cost(0),
    )(mid, bands, summed, got, strip, beside, early)


def any_lattice(seeds, material, decay, coupling, sub_size, tile_size):
    depth, size_x, size_y = seeds.shape[2:]
    spans = ((0, size_x),)
    table = table_rows(decay, coupling, size_y)
    shape = (PLANES, size_x, size_y)
    near, far = called(functools.partial(halo_kernel, spans, "sub"), [shape, shape], table, seeds, material)
    near = near_exchange(near, sub_size)
    far = far_exchange(far, sub_size, tile_size)
    weighted, = called(
        functools.partial(whole_kernel, spans, "sub", sub_size), [(6, depth, size_x, size_y)],
        table, seeds, material, near, far,
    )
    side = math.isqrt(tile_size)
    prev_band = from_behind(weighted[:, :, size_x - BAND :, :], 1, tile_size)
    next_band = from_behind(weighted[:, :, :BAND, :], -1, tile_size)
    combined = weighted.at[:, :, :BAND, :].add(prev_band)
    combined = combined.at[:, :, size_x - BAND :, :].add(next_band)
    flat = (6, depth, size_x * BAND // size_y, size_y)
    thin = (6, depth, size_x, BAND)
    top_slab = combined[..., size_y - BAND :].reshape(flat)
    bottom_slab = combined[..., :BAND].reshape(flat)
    result = combined.at[..., :BAND].add(from_behind(top_slab, side, tile_size).reshape(thin))
    result = result.at[..., size_y - BAND :].add(from_behind(bottom_slab, -side, tile_size).reshape(thin))
    return result[None]


def solution(mesh):
    sub_size, tile_size = mesh.shape["sub"], mesh.shape["tile"]
    body = two_by_two if tile_size == 4 else any_lattice

    def on_device(seeds, material, decay, coupling):
        return body(seeds, material, decay, coupling, sub_size, tile_size)

    placed = (P("tile", None, "sub", None, None), P("tile", "sub", None, None), P(), P())
    return jax.shard_map(
        on_device,
        mesh=mesh,
        in_specs=placed,
        out_specs=P("tile", None, "sub", None, None),
        check_vma=False,
    )
```

```python
import functools
import math

import jax
import jax.numpy as jnp
from jax import lax
from jax.experimental import pallas as pl
from jax.experimental.pallas import tpu as pltpu
from jax.sharding import PartitionSpec as P

BAND = 32
HALO = 8
PLANES = 5
REACH = 2
SHARED = 96
LARGE, MEDIUM, SMALL = 10**10, 2 * 10**9, 0

magnetic_coeff = 0.5


def lane_of(shape):
    return lax.broadcasted_iota(jnp.int32, shape, len(shape) - 1)


def row_of(shape):
    return lax.broadcasted_iota(jnp.int32, shape, len(shape) - 2)


def rolled(v, shift):
    return pltpu.roll(v, shift % v.shape[-1], v.ndim - 1)


def next_x(v):
    rows = v.shape[0]
    return jnp.where(row_of(v.shape) == rows - 1, 0.0, pltpu.roll(v, rows - 1, 0))


def prev_x(v):
    return jnp.where(row_of(v.shape) == 0, 0.0, pltpu.roll(v, 1, 0))


def next_y(v):
    lanes = v.shape[1]
    return jnp.where(lane_of(v.shape) == lanes - 1, 0.0, pltpu.roll(v, lanes - 1, 1))


def prev_y(v):
    return jnp.where(lane_of(v.shape) == 0, 0.0, pltpu.roll(v, 1, 1))


def plus_x(v):
    return next_x(v) - v


def plus_y(v):
    return next_y(v) - v


def minus_x(v):
    return v - prev_x(v)


def minus_y(v):
    return v - prev_y(v)


def looked_up(labels, entries):
    value = jnp.broadcast_to(entries[0], labels.shape)
    for m in range(1, len(entries)):
        value = jnp.where(labels == m, entries[m], value)
    return value


def update_h(h, v, v_after):
    depth = len(v[0])
    new = [[], [], []]
    for p in range(depth):
        vx, vy, vz = v[0][p], v[1][p], v[2][p]
        up_x, up_y = (v[0][p + 1], v[1][p + 1]) if p + 1 < depth else v_after
        dz_x = up_x - vx if up_x is not None else -vx
        dz_y = up_y - vy if up_y is not None else -vy
        new[0].append(h[0][p] + (plus_y(vz) - dz_y))
        new[1].append(h[1][p] + (dz_x - plus_x(vz)))
        new[2].append(h[2][p] + (plus_x(vy) - plus_y(vx)))
    return new


def update_e(e, ca, h, h_before):
    depth = len(h[0])
    new = [[], [], []]
    for p in range(depth):
        hx, hy, hz = h[0][p], h[1][p], h[2][p]
        low_x, low_y = (h[0][p - 1], h[1][p - 1]) if p > 0 else h_before
        dz_x = hx - low_x if low_x is not None else hx
        dz_y = hy - low_y if low_y is not None else hy
        new[0].append(ca[p] * e[0][p] - magnetic_coeff * (minus_y(hz) - dz_y))
        new[1].append(ca[p] * e[1][p] - magnetic_coeff * (dz_x - minus_x(hz)))
        new[2].append(ca[p] * e[2][p] - magnetic_coeff * (minus_x(hy) - minus_y(hx)))
    return new


def scaled(cb, e):
    return [[cb[p] * e[c][p] for p in range(len(cb))] for c in range(3)]


def joined(ref, index, spans):
    return jnp.concatenate([ref[*index, lo:hi] for lo, hi in spans], axis=0)


def prepared(e, h, labels, tables):
    ca = [looked_up(m, tables[0]) for m in labels]
    cb = [looked_up(m, tables[1]) for m in labels]
    return e, h, ca, cb


def raw(seeds, material, spans):
    depth = seeds.shape[1]
    e = [[joined(seeds, (c, p), spans) for p in range(depth)] for c in range(3)]
    h = [[joined(seeds, (3 + c, p), spans) for p in range(depth)] for c in range(3)]
    return e, h, [joined(material, (p,), spans) for p in range(depth)]


def table_entries(table):
    count = table.shape[0] // 2
    rows = [table[m : m + 1] for m in range(2 * count)]
    return rows[:count], rows[count:]


def loaded(seeds, material, table, spans):
    return prepared(*raw(seeds, material, spans), table_entries(table))


NONE = (None, None)


def send_halos(sub, fields, near, far, packed=lambda planes: planes):
    odd = lax.rem(lax.axis_index(sub), 2) == 1
    e, h, ca, cb = fields
    v1 = scaled(cb, e)
    h1 = update_h(h, v1, NONE)
    e1 = update_e(e, ca, h1, NONE)
    v2 = scaled(cb, e1)
    h2 = update_h(h1, v2, NONE)
    up = (h1[0][-1], h1[1][-1], h2[0][-1], h2[1][-1], cb[-1])
    down = (v1[0][0], v1[1][0], v2[0][0], v2[1][0], cb[0])
    up, down = packed(jnp.stack(up)), packed(jnp.stack(down))
    near[...] = jnp.where(odd, down, up)
    far[...] = jnp.where(odd, up, down)


def halo_kernel(spans, sub, table, seeds, material, near, far):
    send_halos(sub, loaded(seeds, material, table, spans), near, far)


def ramp(position, count):
    position = position.astype(jnp.float32) + 0.5
    return jnp.where(
        position < BAND,
        position / BAND,
        jnp.where(position > count - BAND, (count - position) / BAND, 1.0),
    )


def final_fields(fields, near, far, sub, sub_size, unpacked=lambda planes: planes):
    e, h, ca, cb = fields
    index = lax.axis_index(sub)
    odd = lax.rem(index, 2) == 1
    below, above = index > 0, index < sub_size - 1
    a, b = near[...], far[...]
    from_below = unpacked(jnp.where(odd, a, b))
    from_above = unpacked(jnp.where(above, jnp.where(odd, b, a), 0.0))
    part_h1x, part_h1y, part_h2x, part_h2y, cb_low = from_below
    v1x_up, v1y_up, part_v2x, part_v2y, cb_up = from_above

    v1 = scaled(cb, e)
    h1 = update_h(h, v1, (v1x_up, v1y_up))
    dh1x, dh1y = -v1[1][0], v1[0][0]
    h1_low = (jnp.where(below, part_h1x + dh1x, 0.0), jnp.where(below, part_h1y + dh1y, 0.0))
    e1 = update_e(e, ca, h1, h1_low)
    v2 = scaled(cb, e1)
    v2_up = (
        part_v2x - cb_up * (magnetic_coeff * h1[1][-1]),
        part_v2y + cb_up * (magnetic_coeff * h1[0][-1]),
    )
    h2 = update_h(h1, v2, v2_up)
    dv2x = cb_low * (magnetic_coeff * dh1y)
    dv2y = cb_low * (-magnetic_coeff * dh1x)
    dv2z = cb_low * (-magnetic_coeff * (minus_x(dh1y) - minus_y(dh1x)))
    h2x_low = part_h2x + (dh1x + (plus_y(dv2z) - (v2[1][0] - dv2y)))
    h2y_low = part_h2y + (dh1y + ((v2[0][0] - dv2x) - plus_x(dv2z)))
    h2_low = (jnp.where(below, h2x_low, 0.0), jnp.where(below, h2y_low, 0.0))
    e2 = update_e(e1, ca, h2, h2_low)
    return e2 + h2


def middle_out(block):
    return rolled(block, block.shape[-1] // 2)


def y_packed(first, second):
    lane = lane_of(first.shape)
    middle = (lane >= BAND) & (lane < first.shape[-1] - BAND)
    return jnp.where(middle, middle_out(second), first)


def inner_lanes(shape):
    lane = lane_of(shape)
    return (lane >= BAND) & (lane < shape[-1] - BAND)


def y_unpacked(block):
    a, b = rolled(block, BAND), rolled(block, -BAND)
    middle = inner_lanes(block.shape)
    below = lane_of(block.shape) < BAND
    first = jnp.where(middle, 0.0, jnp.where(below, a, b))
    second = jnp.where(middle, 0.0, jnp.where(below, b, a))
    return first, second


def strip_packed(strip):
    half = strip.shape[1] // 2
    first, second = strip[:, :half], strip[:, half:]
    return jnp.where(inner_lanes(first.shape), second, middle_out(first))


def strip_of(corners, block):
    middle = inner_lanes(block.shape)
    first = jnp.where(middle, middle_out(block), corners[0])
    second = jnp.where(middle, block, corners[1])
    return jnp.concatenate([first, second], axis=1)


def low_rows(shape):
    return row_of(shape) < 4


def bands_packed(block):
    rows, lanes = block.shape[1:]
    count, width, high = rows // 2 + 4, REACH * (rows // 8), lanes - BAND
    shape = (block.shape[0], 8, lanes)
    lane = lane_of(shape)
    low = low_rows(shape)
    side = jnp.zeros(shape, block.dtype)
    for g in range(rows // 8):
        at = BAND + REACH * (g + 1)
        piece = rolled(block[:, 8 * g : 8 * g + 8], REACH * (g + 1))
        here = ((lane >= at) & (lane < at + REACH)) | (
            (lane >= at + high - BAND - REACH) & (lane < at + high - BAND)
        )
        side = jnp.where(here, piece, side)
    other = rolled(pltpu.roll(side, 4, 1), width + REACH)
    own = ((lane >= BAND) & (lane < BAND + REACH + width)) | ((lane >= high) & (lane < high + width))
    side = jnp.where(own, side, other)
    middle = (lane >= BAND) & (lane < high)
    packed = y_packed(block[:, :count], block[:, rows - count :])
    first = jnp.where(low & middle, side, packed[:, :8])
    last = jnp.where(low | middle, packed[:, count - 8 :], side)
    return jnp.concatenate([first, packed[:, 8 : count - 8], last], axis=1)


def bands_unpacked(packed):
    count, lanes = packed.shape[1:]
    rows = 2 * count - 8
    width, high = REACH * (rows // 8), lanes - BAND
    first, last = packed[:, :8], packed[:, count - 8 :]
    low = low_rows(first.shape)
    lane = lane_of(first.shape)
    middle = (lane >= BAND) & (lane < high)
    side = jnp.where(low, first, last)
    other = rolled(pltpu.roll(side, 4, 1), -width - REACH)
    side = jnp.where(low == middle, side, other)
    beside = ((lane >= BAND) & (lane < BAND + REACH)) | ((lane >= high - REACH) & (lane < high))
    moved = [rolled(packed[:, at : at + 8], lanes // 2) for at in range(0, count, 8)]
    pieces = [packed[:, at : at + 8] for at in range(0, count - 8, 8)]
    pieces += [jnp.where(low, last, moved[0])] + moved[1:]
    result = []
    for g, piece in enumerate(pieces):
        result.append(jnp.where(middle, jnp.where(beside, rolled(side, -REACH * (g + 1)), 0.0), piece))
    return jnp.concatenate(result, axis=1)


def first_kernel(span, skip, decay, coupling, seeds, material, shared, held, labels, table, entries, sems):
    size_x = held.shape[2]
    copies = []

    def fetch(source, target):
        copies.append(pltpu.make_async_copy(source, target, sems.at[len(copies)]))
        copies[-1].start()

    def fetch_rows(lo, hi):
        rows = pl.ds(lo, hi - lo)
        fetch(material.at[0, :, rows], labels.at[:, rows])
        for c in range(0, 6, 2):
            some = pl.ds(c, 2)
            fetch(seeds.at[0, some, :, rows], held.at[some, :, rows])

    fetch_rows(*span)
    early = len(copies)
    fetch(decay, entries.at[0])
    fetch(coupling, entries.at[1])
    fetch_rows(0, span[0])
    fetch_rows(span[1], size_x)
    rows = slice(span[0] + skip, span[1] - skip)
    for copy in copies[:early]:
        copy.wait()
    planes = [held[c, :, rows] for c in range(6)] + [labels[:, rows].astype(jnp.float32)]
    shared[...] = bands_packed(jnp.concatenate(planes, axis=0))
    for copy in copies[early:]:
        copy.wait()
    count = entries.shape[1]
    for k in range(2):
        for m in range(count):
            table[k * count + m : k * count + m + 1] = jnp.full((1, table.shape[1]), entries[k, m], jnp.float32)


def halo_pair_kernel(edges, inner, sub, table, seeds, material, near_edge, far_edge, near, far):
    send_halos(sub, loaded(seeds, material, table, edges), near_edge, far_edge)
    send_halos(sub, loaded(seeds, material, table, inner), near, far)


def shared_fields(table, shared):
    depth = shared.shape[0] // 7
    planes = bands_unpacked(shared[...])
    f = [planes[depth * c : depth * (c + 1)] for c in range(7)]
    return prepared(f[:3], f[3:6], f[6], table_entries(table))


def shared_halo_kernel(sub, table, shared, near, far, done):
    done[...] = jnp.zeros(done.shape, done.dtype)
    send_halos(sub, shared_fields(table, shared), near, far, bands_packed)


def weighted_planes(seeds, material, table, near, far, spans, keeps, sub, sub_size):
    planes = final_fields(loaded(seeds, material, table, spans), near, far, sub, sub_size)
    return weighted(planes, spans, keeps, *seeds.shape[2:])


def weighted(planes, spans, keeps, size_x, size_y):
    at, results = 0, []
    for (lo, hi), (start, stop) in zip(spans, keeps):
        shape = (stop - start, size_y)
        weight = ramp(row_of(shape) + start, size_x) * ramp(lane_of(shape), size_y)
        first = at + start - lo
        results.append(jnp.stack([plane[first : first + stop - start] * weight for part in planes for plane in part]))
        at += hi - lo
    return results


def edge_kernel(spans, sub, sub_size, tile, table, seeds, material, near, far, edge, corner, strip):
    size_x = seeds.shape[2]
    keeps = ((0, BAND), (size_x - BAND, size_x))
    low, high = weighted_planes(seeds, material, table, near, far, spans, keeps, sub, sub_size)
    odd = lax.rem(lax.axis_index(tile), 2) == 1
    edge[:, :BAND] = low
    edge[:, BAND:] = high
    corner[...] = y_packed(low, high)
    strip[...] = strip_packed(jnp.where(odd, high, low))


def middle_kernel(spans, sub, sub_size, tile, table, seeds, material, near, far, edge, _, mid, bands, beside):
    size_x = seeds.shape[2]
    keep = (BAND, size_x - BAND)
    odd = lax.rem(lax.axis_index(tile), 2) == 1
    beside[...] = strip_packed(jnp.where(odd, edge[:, :BAND], edge[:, BAND:]))
    planes, = weighted_planes(seeds, material, table, near, far, spans, (keep,), sub, sub_size)
    half = bands.shape[1]
    mid[...] = planes
    bands[...] = y_packed(planes[:, :half], planes[:, -half:])


def whole_kernel(spans, sub, sub_size, table, seeds, material, near, far, out):
    planes, = weighted_planes(seeds, material, table, near, far, spans, spans, sub, sub_size)
    out[...] = planes


def y_swapped(block):
    below = lane_of(block.shape) < BAND
    return jnp.where(inner_lanes(block.shape), 0.0, jnp.where(below, rolled(block, BAND), rolled(block, -BAND)))


def shared_kernel(span, size_x, sub, sub_size, table, shared, near, far, part):
    planes = final_fields(shared_fields(table, shared), near, far, sub, sub_size, bands_unpacked)
    found, = weighted(planes, (span,), (span,), size_x, part.shape[2])
    part[...] = y_swapped(found)


def corner_kernel(tile, edge, corner, summed, send):
    odd = lax.rem(lax.axis_index(tile), 2) == 1
    half = BAND // 2
    first, second = y_unpacked(corner[...])
    low = edge[:, :BAND] + first
    high = edge[:, BAND:] + second
    summed[:, :BAND] = low
    summed[:, BAND:] = high
    by, away = jnp.where(odd, low, high), jnp.where(odd, high, low)
    send[:, :half] = y_packed(by[:, :half], by[:, half:])
    send[:, half:] = y_packed(away[:, :half], away[:, half:])


def early_kernel(mid, part, out, whole, sem):
    size_x = out.shape[3]
    skip = HALO // 2
    count = part.shape[1] - 2 * skip
    start = (size_x - count) // 2
    found = mid[:, start - BAND : start - BAND + count] + part[:, skip : skip + count]
    whole[...] = found.reshape(whole.shape)
    copy = pltpu.make_async_copy(whole, out.at[0, :, :, pl.ds(start, count)], sem)
    copy.start()
    copy.wait()


def last_kernel(tile, mid, bands, summed, got, strip, beside, _, out, low, high, sems):
    odd = lax.rem(lax.axis_index(tile), 2) == 1
    half, count = bands.shape[1], low.shape[2]
    quarter = BAND // 2
    depth, size_x = out.shape[2:4]
    copies = []
    for c in range(6):
        at = slice(depth * c, depth * (c + 1))
        first, second = y_unpacked(bands[at])
        low[c, :, BAND:] = mid[at, :half] + first
        high[c, :, :half] = mid[at, -half:] + second
        straight = got[at, :quarter]
        by = strip_of((straight, middle_out(straight)), beside[at])
        away = strip_of(y_unpacked(got[at, quarter:]), strip[at])
        low[c, :, :BAND] = summed[at, :BAND] + jnp.where(odd, by, away)
        high[c, :, half:] = summed[at, BAND:] + jnp.where(odd, away, by)
        for k, (rows, start) in enumerate(((low, 0), (high, size_x - count))):
            copies.append(pltpu.make_async_copy(rows.at[c], out.at[0, c, :, pl.ds(start, count)], sems.at[2 * c + k]))
            copies[-1].start()
    for copy in copies:
        copy.wait()


HBM = pl.BlockSpec(memory_space=pltpu.HBM)
VMEM = pl.BlockSpec(memory_space=pltpu.VMEM)
PARAMS = pltpu.CompilerParams(vmem_limit_bytes=32 * 1024 * 1024)


def cost(flops):
    return pl.CostEstimate(flops=flops, bytes_accessed=0, transcendentals=0)


def called(kernel, shapes, *operands, flops=0):
    outs = [jax.ShapeDtypeStruct(shape, jnp.float32) for shape in shapes]
    return pl.pallas_call(
        kernel,
        out_shape=outs,
        in_specs=[VMEM] * len(operands),
        out_specs=[VMEM] * len(outs),
        compiler_params=PARAMS,
        cost_estimate=cost(flops),
    )(*operands)


def after(first, *values):
    return lax.optimization_barrier((first, *values))


def near_exchange(near, sub_size):
    return lax.ppermute(near, "sub", [(i, i ^ 1) for i in range(sub_size)])


def far_exchange(far, sub_size, tile_size):
    pairs = []
    for t in range(tile_size):
        for i in range(sub_size):
            j = ((i + 1) ^ 1) - 1
            other = (t, j) if 0 <= j < sub_size else (t ^ 1, i)
            pairs.append((t * sub_size + i, other[0] * sub_size + other[1]))
    return lax.ppermute(far, ("tile", "sub"), pairs)


def swapped(value, bits, tile_size):
    return lax.ppermute(value, "tile", [(t, t ^ bits) for t in range(tile_size)])


def from_behind(value, steps, count):
    return lax.ppermute(value, "tile", [(t, (t + steps) % count) for t in range(count)])


def table_rows(decay, coupling, size_y):
    entries = jnp.concatenate([decay, coupling])
    return jnp.broadcast_to(entries[:, None], (entries.shape[0], size_y))


def two_by_two(seeds, material, decay, coupling, sub_size, tile_size):
    depth, size_x, size_y = seeds.shape[2:]
    planes = 6 * depth
    edges = ((0, BAND + HALO), (size_x - BAND - HALO, size_x))
    inner = ((BAND - HALO, size_x - BAND + HALO),)
    keep = ((size_x - SHARED) // 2, (size_x + SHARED) // 2)
    span = (keep[0] - HALO // 2, keep[1] + HALO // 2)
    fetched = (keep[0] - HALO, keep[1] + HALO)
    rows = size_x - 2 * BAND
    edge_rows, inner_rows = 2 * (BAND + HALO), rows + 2 * HALO
    packed_rows = (SHARED + HALO) // 2 + 4
    whole = jax.ShapeDtypeStruct(seeds.shape, jnp.float32)

    shared, seeds, material, table = pl.pallas_call(
        functools.partial(first_kernel, fetched, HALO // 2),
        out_shape=[
            jax.ShapeDtypeStruct((7 * depth, packed_rows, size_y), jnp.float32),
            jax.ShapeDtypeStruct(seeds.shape[1:], jnp.float32),
            jax.ShapeDtypeStruct(material.shape[1:], jnp.int32),
            jax.ShapeDtypeStruct((2 * decay.shape[0], size_y), jnp.float32),
        ],
        in_specs=[HBM] * 4,
        out_specs=[VMEM] * 4,
        scratch_shapes=[pltpu.SMEM((2, *decay.shape), jnp.float32), pltpu.SemaphoreType.DMA((14,))],
        compiler_params=PARAMS,
        cost_estimate=cost(0),
    )(*(pltpu.with_memory_space_constraint(x, pltpu.HBM) for x in (decay, coupling, seeds, material)))
    shared = swapped(shared, 2, tile_size)
    edge_near, edge_far, inner_near, inner_far = called(
        functools.partial(halo_pair_kernel, edges, inner, "sub"),
        [(PLANES, edge_rows, size_y)] * 2 + [(PLANES, inner_rows, size_y)] * 2, table, seeds, material,
    )
    edge_near, inner_near = near_exchange(edge_near, sub_size), near_exchange(inner_near, sub_size)
    edge_far = far_exchange(edge_far, sub_size, tile_size)
    inner_far = far_exchange(inner_far, sub_size, tile_size)

    edge, corner, strip = called(
        functools.partial(edge_kernel, edges, "sub", sub_size, "tile"),
        [(planes, 2 * BAND, size_y), (planes, BAND, size_y), (planes, BAND // 2, size_y)],
        table, seeds, material, edge_near, edge_far,
    )
    corner = swapped(corner, 2, tile_size)
    strip = swapped(strip, 3, tile_size)

    shape = (PLANES, packed_rows, size_y)
    shared_near, shared_far, done = called(
        functools.partial(shared_halo_kernel, "sub"), [shape, shape, (8, size_y)], table, shared, flops=LARGE
    )
    shared_near = near_exchange(shared_near, sub_size)
    shared_far = far_exchange(shared_far, sub_size, tile_size)

    mid, bands, beside = called(
        functools.partial(middle_kernel, inner, "sub", sub_size, "tile"),
        [(planes, rows, size_y), (planes, (rows - SHARED) // 2, size_y), (planes, BAND // 2, size_y)],
        table, seeds, material, inner_near, inner_far, edge, done,
    )
    bands = swapped(bands, 2, tile_size)
    beside = swapped(beside, 1, tile_size)

    corner, strip, mid = after(corner, strip, mid)
    summed, send = called(
        functools.partial(corner_kernel, "tile"), [(planes, 2 * BAND, size_y), (planes, BAND, size_y)],
        edge, corner, flops=SMALL,
    )
    got = swapped(send, 1, tile_size)
    beside, shared_near = after(beside, shared_near)
    part, = called(
        functools.partial(shared_kernel, span, size_x, "sub", sub_size),
        [(planes, SHARED + HALO, size_y)], table, shared, shared_near, shared_far, flops=MEDIUM,
    )
    early = pl.pallas_call(
        early_kernel,
        out_shape=whole,
        in_specs=[VMEM] * 2,
        out_specs=HBM,
        scratch_shapes=[pltpu.VMEM((6, depth, SHARED, size_y), jnp.float32), pltpu.SemaphoreType.DMA],
        compiler_params=PARAMS,
        cost_estimate=cost(0),
    )(mid, part)
    return pl.pallas_call(
        functools.partial(last_kernel, "tile"),
        out_shape=whole,
        in_specs=[VMEM] * 6 + [HBM],
        out_specs=HBM,
        scratch_shapes=[pltpu.VMEM((6, depth, (size_x - SHARED) // 2, size_y), jnp.float32)] * 2
        + [pltpu.SemaphoreType.DMA((12,))],
        input_output_aliases={6: 0},
        compiler_params=PARAMS,
        cost_estimate=cost(0),
    )(mid, bands, summed, got, strip, beside, early)


def any_lattice(seeds, material, decay, coupling, sub_size, tile_size):
    depth, size_x, size_y = seeds.shape[2:]
    seeds, material = seeds[0], material[0]
    spans = ((0, size_x),)
    table = table_rows(decay, coupling, size_y)
    shape = (PLANES, size_x, size_y)
    near, far = called(functools.partial(halo_kernel, spans, "sub"), [shape, shape], table, seeds, material)
    near = near_exchange(near, sub_size)
    far = far_exchange(far, sub_size, tile_size)
    weighted, = called(
        functools.partial(whole_kernel, spans, "sub", sub_size), [(6 * depth, size_x, size_y)],
        table, seeds, material, near, far,
    )
    weighted = weighted.reshape(6, depth, size_x, size_y)
    side = math.isqrt(tile_size)
    prev_band = from_behind(weighted[:, :, size_x - BAND :, :], 1, tile_size)
    next_band = from_behind(weighted[:, :, :BAND, :], -1, tile_size)
    combined = weighted.at[:, :, :BAND, :].add(prev_band)
    combined = combined.at[:, :, size_x - BAND :, :].add(next_band)
    flat = (6, depth, size_x * BAND // size_y, size_y)
    thin = (6, depth, size_x, BAND)
    top_slab = combined[..., size_y - BAND :].reshape(flat)
    bottom_slab = combined[..., :BAND].reshape(flat)
    result = combined.at[..., :BAND].add(from_behind(top_slab, side, tile_size).reshape(thin))
    result = result.at[..., size_y - BAND :].add(from_behind(bottom_slab, -side, tile_size).reshape(thin))
    return result[None]


def solution(mesh):
    sub_size, tile_size = mesh.shape["sub"], mesh.shape["tile"]
    body = two_by_two if tile_size == 4 else any_lattice

    def on_device(seeds, material, decay, coupling):
        return body(seeds, material, decay, coupling, sub_size, tile_size)

    placed = (P("tile", None, "sub", None, None), P("tile", "sub", None, None), P(), P())
    return jax.shard_map(
        on_device,
        mesh=mesh,
        in_specs=placed,
        out_specs=P("tile", None, "sub", None, None),
        check_vma=False,
    )
```

```python
import functools
import math

import jax
import jax.numpy as jnp
from jax import lax
from jax.experimental import pallas as pl
from jax.experimental.pallas import tpu as pltpu
from jax.sharding import PartitionSpec as P

BAND = 32
HALO = 8
PLANES = 5
REACH = 2
SHARED = 96
CORNER, SHARE = 5 * 10**9, 15 * 10**8

magnetic_coeff = 0.5


def lane_of(shape):
    return lax.broadcasted_iota(jnp.int32, shape, len(shape) - 1)


def row_of(shape):
    return lax.broadcasted_iota(jnp.int32, shape, len(shape) - 2)


def rolled(v, shift):
    return pltpu.roll(v, shift % v.shape[-1], v.ndim - 1)


def next_x(v):
    rows = v.shape[0]
    return jnp.where(row_of(v.shape) == rows - 1, 0.0, pltpu.roll(v, rows - 1, 0))


def prev_x(v):
    return jnp.where(row_of(v.shape) == 0, 0.0, pltpu.roll(v, 1, 0))


def next_y(v):
    lanes = v.shape[1]
    return jnp.where(lane_of(v.shape) == lanes - 1, 0.0, pltpu.roll(v, lanes - 1, 1))


def prev_y(v):
    return jnp.where(lane_of(v.shape) == 0, 0.0, pltpu.roll(v, 1, 1))


def plus_x(v):
    return next_x(v) - v


def plus_y(v):
    return next_y(v) - v


def minus_x(v):
    return v - prev_x(v)


def minus_y(v):
    return v - prev_y(v)


def looked_up(labels, entries):
    value = jnp.broadcast_to(entries[0], labels.shape)
    for m in range(1, len(entries)):
        value = jnp.where(labels == m, entries[m], value)
    return value


def update_h(h, v, v_after):
    depth = len(v[0])
    new = [[], [], []]
    for p in range(depth):
        vx, vy, vz = v[0][p], v[1][p], v[2][p]
        up_x, up_y = (v[0][p + 1], v[1][p + 1]) if p + 1 < depth else v_after
        dz_x = up_x - vx if up_x is not None else -vx
        dz_y = up_y - vy if up_y is not None else -vy
        new[0].append(h[0][p] + (plus_y(vz) - dz_y))
        new[1].append(h[1][p] + (dz_x - plus_x(vz)))
        new[2].append(h[2][p] + (plus_x(vy) - plus_y(vx)))
    return new


def update_e(e, ca, h, h_before):
    depth = len(h[0])
    new = [[], [], []]
    for p in range(depth):
        hx, hy, hz = h[0][p], h[1][p], h[2][p]
        low_x, low_y = (h[0][p - 1], h[1][p - 1]) if p > 0 else h_before
        dz_x = hx - low_x if low_x is not None else hx
        dz_y = hy - low_y if low_y is not None else hy
        new[0].append(ca[p] * e[0][p] - magnetic_coeff * (minus_y(hz) - dz_y))
        new[1].append(ca[p] * e[1][p] - magnetic_coeff * (dz_x - minus_x(hz)))
        new[2].append(ca[p] * e[2][p] - magnetic_coeff * (minus_x(hy) - minus_y(hx)))
    return new


def scaled(cb, e):
    return [[cb[p] * e[c][p] for p in range(len(cb))] for c in range(3)]


def joined(ref, index, spans):
    return jnp.concatenate([ref[*index, lo:hi] for lo, hi in spans], axis=0)


def prepared(e, h, labels, tables):
    ca = [looked_up(m, tables[0]) for m in labels]
    cb = [looked_up(m, tables[1]) for m in labels]
    return e, h, ca, cb


def raw(seeds, material, spans):
    depth = seeds.shape[1]
    e = [[joined(seeds, (c, p), spans) for p in range(depth)] for c in range(3)]
    h = [[joined(seeds, (3 + c, p), spans) for p in range(depth)] for c in range(3)]
    return e, h, [joined(material, (p,), spans) for p in range(depth)]


def table_entries(table):
    count = table.shape[0] // 2
    rows = [table[m : m + 1] for m in range(2 * count)]
    return rows[:count], rows[count:]


def loaded(seeds, material, table, spans):
    return prepared(*raw(seeds, material, spans), table_entries(table))


NONE = (None, None)


def send_halos(sub, fields, near, far, packed=lambda planes: planes):
    odd = lax.rem(lax.axis_index(sub), 2) == 1
    e, h, ca, cb = fields
    v1 = scaled(cb, e)
    h1 = update_h(h, v1, NONE)
    e1 = update_e(e, ca, h1, NONE)
    v2 = scaled(cb, e1)
    h2 = update_h(h1, v2, NONE)
    up = (h1[0][-1], h1[1][-1], h2[0][-1], h2[1][-1], cb[-1])
    down = (v1[0][0], v1[1][0], v2[0][0], v2[1][0], cb[0])
    up, down = packed(jnp.stack(up)), packed(jnp.stack(down))
    near[...] = jnp.where(odd, down, up)
    far[...] = jnp.where(odd, up, down)


def halo_kernel(spans, sub, table, seeds, material, near, far):
    send_halos(sub, loaded(seeds, material, table, spans), near, far)


def ramp(position, count):
    position = position.astype(jnp.float32) + 0.5
    return jnp.where(
        position < BAND,
        position / BAND,
        jnp.where(position > count - BAND, (count - position) / BAND, 1.0),
    )


def final_fields(fields, near, far, sub, sub_size, unpacked=lambda planes: planes):
    e, h, ca, cb = fields
    index = lax.axis_index(sub)
    odd = lax.rem(index, 2) == 1
    below, above = index > 0, index < sub_size - 1
    a, b = near[...], far[...]
    from_below = unpacked(jnp.where(odd, a, b))
    from_above = unpacked(jnp.where(above, jnp.where(odd, b, a), 0.0))
    part_h1x, part_h1y, part_h2x, part_h2y, cb_low = from_below
    v1x_up, v1y_up, part_v2x, part_v2y, cb_up = from_above

    v1 = scaled(cb, e)
    h1 = update_h(h, v1, (v1x_up, v1y_up))
    dh1x, dh1y = -v1[1][0], v1[0][0]
    h1_low = (jnp.where(below, part_h1x + dh1x, 0.0), jnp.where(below, part_h1y + dh1y, 0.0))
    e1 = update_e(e, ca, h1, h1_low)
    v2 = scaled(cb, e1)
    v2_up = (
        part_v2x - cb_up * (magnetic_coeff * h1[1][-1]),
        part_v2y + cb_up * (magnetic_coeff * h1[0][-1]),
    )
    h2 = update_h(h1, v2, v2_up)
    dv2x = cb_low * (magnetic_coeff * dh1y)
    dv2y = cb_low * (-magnetic_coeff * dh1x)
    dv2z = cb_low * (-magnetic_coeff * (minus_x(dh1y) - minus_y(dh1x)))
    h2x_low = part_h2x + (dh1x + (plus_y(dv2z) - (v2[1][0] - dv2y)))
    h2y_low = part_h2y + (dh1y + ((v2[0][0] - dv2x) - plus_x(dv2z)))
    h2_low = (jnp.where(below, h2x_low, 0.0), jnp.where(below, h2y_low, 0.0))
    e2 = update_e(e1, ca, h2, h2_low)
    return e2 + h2


def middle_out(block):
    return rolled(block, block.shape[-1] // 2)


def y_packed(first, second):
    lane = lane_of(first.shape)
    middle = (lane >= BAND) & (lane < first.shape[-1] - BAND)
    return jnp.where(middle, middle_out(second), first)


def inner_lanes(shape):
    lane = lane_of(shape)
    return (lane >= BAND) & (lane < shape[-1] - BAND)


def y_unpacked(block):
    a, b = rolled(block, BAND), rolled(block, -BAND)
    middle = inner_lanes(block.shape)
    below = lane_of(block.shape) < BAND
    first = jnp.where(middle, 0.0, jnp.where(below, a, b))
    second = jnp.where(middle, 0.0, jnp.where(below, b, a))
    return first, second


def strip_packed(strip):
    half = strip.shape[1] // 2
    first, second = strip[:, :half], strip[:, half:]
    return jnp.where(inner_lanes(first.shape), second, middle_out(first))


def strip_of(corners, block):
    middle = inner_lanes(block.shape)
    first = jnp.where(middle, middle_out(block), corners[0])
    second = jnp.where(middle, block, corners[1])
    return jnp.concatenate([first, second], axis=1)


def low_rows(shape):
    return row_of(shape) < 4


def bands_packed(block):
    rows, lanes = block.shape[1:]
    count, width, high = rows // 2 + 4, REACH * (rows // 8), lanes - BAND
    shape = (block.shape[0], 8, lanes)
    lane = lane_of(shape)
    low = low_rows(shape)
    side = jnp.zeros(shape, block.dtype)
    for g in range(rows // 8):
        at = BAND + REACH * (g + 1)
        piece = rolled(block[:, 8 * g : 8 * g + 8], REACH * (g + 1))
        here = ((lane >= at) & (lane < at + REACH)) | (
            (lane >= at + high - BAND - REACH) & (lane < at + high - BAND)
        )
        side = jnp.where(here, piece, side)
    other = rolled(pltpu.roll(side, 4, 1), width + REACH)
    own = ((lane >= BAND) & (lane < BAND + REACH + width)) | ((lane >= high) & (lane < high + width))
    side = jnp.where(own, side, other)
    middle = (lane >= BAND) & (lane < high)
    packed = y_packed(block[:, :count], block[:, rows - count :])
    first = jnp.where(low & middle, side, packed[:, :8])
    last = jnp.where(low | middle, packed[:, count - 8 :], side)
    return jnp.concatenate([first, packed[:, 8 : count - 8], last], axis=1)


def bands_unpacked(packed):
    count, lanes = packed.shape[1:]
    rows = 2 * count - 8
    width, high = REACH * (rows // 8), lanes - BAND
    first, last = packed[:, :8], packed[:, count - 8 :]
    low = low_rows(first.shape)
    lane = lane_of(first.shape)
    middle = (lane >= BAND) & (lane < high)
    side = jnp.where(low, first, last)
    other = rolled(pltpu.roll(side, 4, 1), -width - REACH)
    side = jnp.where(low == middle, side, other)
    beside = ((lane >= BAND) & (lane < BAND + REACH)) | ((lane >= high - REACH) & (lane < high))
    moved = [rolled(packed[:, at : at + 8], lanes // 2) for at in range(0, count, 8)]
    pieces = [packed[:, at : at + 8] for at in range(0, count - 8, 8)]
    pieces += [jnp.where(low, last, moved[0])] + moved[1:]
    result = []
    for g, piece in enumerate(pieces):
        result.append(jnp.where(middle, jnp.where(beside, rolled(side, -REACH * (g + 1)), 0.0), piece))
    return jnp.concatenate(result, axis=1)


def first_kernel(span, skip, decay, coupling, seeds, material, shared, held, labels, table, entries, sems):
    size_x = held.shape[2]
    copies = []

    def fetch(source, target):
        copies.append(pltpu.make_async_copy(source, target, sems.at[len(copies)]))
        copies[-1].start()

    def fetch_rows(lo, hi):
        rows = pl.ds(lo, hi - lo)
        fetch(material.at[0, :, rows], labels.at[:, rows])
        for c in range(0, 6, 2):
            some = pl.ds(c, 2)
            fetch(seeds.at[0, some, :, rows], held.at[some, :, rows])

    fetch_rows(*span)
    early = len(copies)
    fetch(decay, entries.at[0])
    fetch(coupling, entries.at[1])
    fetch_rows(0, span[0])
    fetch_rows(span[1], size_x)
    rows = slice(span[0] + skip, span[1] - skip)
    for copy in copies[:early]:
        copy.wait()
    planes = [held[c, :, rows] for c in range(6)] + [labels[:, rows].astype(jnp.float32)]
    shared[...] = bands_packed(jnp.concatenate(planes, axis=0))
    for copy in copies[early:]:
        copy.wait()
    count = entries.shape[1]
    for k in range(2):
        for m in range(count):
            table[k * count + m : k * count + m + 1] = jnp.full((1, table.shape[1]), entries[k, m], jnp.float32)


def halo_pair_kernel(edges, inner, sub, table, seeds, material, near_edge, far_edge, near, far):
    send_halos(sub, loaded(seeds, material, table, edges), near_edge, far_edge)
    send_halos(sub, loaded(seeds, material, table, inner), near, far)


def shared_fields(table, shared):
    depth = shared.shape[0] // 7
    planes = bands_unpacked(shared[...])
    f = [planes[depth * c : depth * (c + 1)] for c in range(7)]
    return prepared(f[:3], f[3:6], f[6], table_entries(table))


def shared_halo_kernel(spans, sub, table, seeds, material, shared, _, near, far):
    other = shared.shape[1]
    own = pl.ds(other, near.shape[1] - other)
    send_halos(sub, loaded(seeds, material, table, spans), near.at[:, own], far.at[:, own])
    both = pl.ds(0, other)
    send_halos(sub, shared_fields(table, shared), near.at[:, both], far.at[:, both], bands_packed)


def weighted_planes(seeds, material, table, near, far, spans, keeps, sub, sub_size):
    planes = final_fields(loaded(seeds, material, table, spans), near, far, sub, sub_size)
    return weighted(planes, spans, keeps, *seeds.shape[2:])


def weighted(planes, spans, keeps, size_x, size_y):
    at, results = 0, []
    for (lo, hi), (start, stop) in zip(spans, keeps):
        shape = (stop - start, size_y)
        weight = ramp(row_of(shape) + start, size_x) * ramp(lane_of(shape), size_y)
        first = at + start - lo
        results.append(jnp.stack([plane[first : first + stop - start] * weight for part in planes for plane in part]))
        at += hi - lo
    return results


def edge_kernel(spans, sub, sub_size, tile, table, seeds, material, near, far, edge, corner, beside):
    size_x = seeds.shape[2]
    keeps = ((0, BAND), (size_x - BAND, size_x))
    low, high = weighted_planes(seeds, material, table, near, far, spans, keeps, sub, sub_size)
    odd = lax.rem(lax.axis_index(tile), 2) == 1
    edge[:, :BAND] = low
    edge[:, BAND:] = high
    corner[...] = y_packed(low, high)
    beside[...] = strip_packed(jnp.where(odd, low, high))


def late_kernel(spans, keeps, sub, sub_size, tile, table, seeds, material, near, far, edge, late, bands, strip):
    odd = lax.rem(lax.axis_index(tile), 2) == 1
    strip[...] = strip_packed(jnp.where(odd, edge[:, BAND:], edge[:, :BAND]))
    low, high = weighted_planes(seeds, material, table, near, far, spans, keeps, sub, sub_size)
    half = bands.shape[1]
    late[:, :half] = low
    late[:, half:] = high
    bands[...] = y_packed(low, high)


def whole_kernel(spans, sub, sub_size, table, seeds, material, near, far, out):
    planes, = weighted_planes(seeds, material, table, near, far, spans, spans, sub, sub_size)
    out[...] = planes


def y_swapped(block):
    below = lane_of(block.shape) < BAND
    return jnp.where(inner_lanes(block.shape), 0.0, jnp.where(below, rolled(block, BAND), rolled(block, -BAND)))


def shared_kernel(spans, span, keep, sub, sub_size, table, seeds, material, shared, near, far, out, whole, sem):
    other = shared.shape[1]
    own = pl.ds(other, near.shape[1] - other)
    size_x, size_y = seeds.shape[2:]
    mine, = weighted_planes(seeds, material, table, near.at[:, own], far.at[:, own], spans, (keep,), sub, sub_size)
    both = pl.ds(0, other)
    planes = final_fields(
        shared_fields(table, shared), near.at[:, both], far.at[:, both], sub, sub_size, bands_unpacked
    )
    found, = weighted(planes, (span,), (span,), size_x, size_y)
    found = y_swapped(found)
    start, stop = keep
    skip = start - span[0]
    whole[...] = (mine + found[:, skip : skip + stop - start]).reshape(whole.shape)
    copy = pltpu.make_async_copy(whole, out.at[0, :, :, pl.ds(start, stop - start)], sem)
    copy.start()
    copy.wait()


def corner_kernel(tile, edge, corner, _, summed, send):
    odd = lax.rem(lax.axis_index(tile), 2) == 1
    half = BAND // 2
    first, second = y_unpacked(corner[...])
    low = edge[:, :BAND] + first
    high = edge[:, BAND:] + second
    summed[:, :BAND] = low
    summed[:, BAND:] = high
    by, away = jnp.where(odd, low, high), jnp.where(odd, high, low)
    send[:, :half] = y_packed(by[:, :half], by[:, half:])
    send[:, half:] = y_packed(away[:, :half], away[:, half:])


def last_kernel(tile, late, bands, summed, got, strip, beside, _, out, low, high, sems):
    odd = lax.rem(lax.axis_index(tile), 2) == 1
    half, count = bands.shape[1], low.shape[2]
    quarter = BAND // 2
    depth, size_x = out.shape[2:4]
    copies = []
    for c in range(6):
        at = slice(depth * c, depth * (c + 1))
        first, second = y_unpacked(bands[at])
        low[c, :, BAND:] = late[at, :half] + first
        high[c, :, :half] = late[at, half:] + second
        straight = got[at, :quarter]
        by = strip_of((straight, middle_out(straight)), beside[at])
        away = strip_of(y_unpacked(got[at, quarter:]), strip[at])
        low[c, :, :BAND] = summed[at, :BAND] + jnp.where(odd, by, away)
        high[c, :, half:] = summed[at, BAND:] + jnp.where(odd, away, by)
        for k, (rows, start) in enumerate(((low, 0), (high, size_x - count))):
            copies.append(pltpu.make_async_copy(rows.at[c], out.at[0, c, :, pl.ds(start, count)], sems.at[2 * c + k]))
            copies[-1].start()
    for copy in copies:
        copy.wait()


HBM = pl.BlockSpec(memory_space=pltpu.HBM)
VMEM = pl.BlockSpec(memory_space=pltpu.VMEM)
PARAMS = pltpu.CompilerParams(vmem_limit_bytes=32 * 1024 * 1024)


def cost(flops):
    return pl.CostEstimate(flops=flops, bytes_accessed=0, transcendentals=0)


def called(kernel, shapes, *operands, flops=0):
    outs = [jax.ShapeDtypeStruct(shape, jnp.float32) for shape in shapes]
    return pl.pallas_call(
        kernel,
        out_shape=outs,
        in_specs=[VMEM] * len(operands),
        out_specs=[VMEM] * len(outs),
        compiler_params=PARAMS,
        cost_estimate=cost(flops),
    )(*operands)


def after(first, *values):
    return lax.optimization_barrier((first, *values))


def near_exchange(near, sub_size):
    return lax.ppermute(near, "sub", [(i, i ^ 1) for i in range(sub_size)])


def far_exchange(far, sub_size, tile_size):
    pairs = []
    for t in range(tile_size):
        for i in range(sub_size):
            j = ((i + 1) ^ 1) - 1
            other = (t, j) if 0 <= j < sub_size else (t ^ 1, i)
            pairs.append((t * sub_size + i, other[0] * sub_size + other[1]))
    return lax.ppermute(far, ("tile", "sub"), pairs)


def swapped(value, bits, tile_size):
    return lax.ppermute(value, "tile", [(t, t ^ bits) for t in range(tile_size)])


def from_behind(value, steps, count):
    return lax.ppermute(value, "tile", [(t, (t + steps) % count) for t in range(count)])


def table_rows(decay, coupling, size_y):
    entries = jnp.concatenate([decay, coupling])
    return jnp.broadcast_to(entries[:, None], (entries.shape[0], size_y))


def two_by_two(seeds, material, decay, coupling, sub_size, tile_size):
    depth, size_x, size_y = seeds.shape[2:]
    planes = 6 * depth
    keep = ((size_x - SHARED) // 2, (size_x + SHARED) // 2)
    span = (keep[0] - HALO // 2, keep[1] + HALO // 2)
    own = (keep[0] - HALO, keep[1] + HALO)
    late_keeps = ((BAND, keep[0]), (keep[1], size_x - BAND))
    late_spans = ((BAND - HALO, own[0] + 2 * HALO), (own[1] - 2 * HALO, size_x - BAND + HALO))
    edges = ((0, BAND + HALO), (size_x - BAND - HALO, size_x))
    edge_rows, late_rows = (sum(hi - lo for lo, hi in spans) for spans in (edges, late_spans))
    late = late_keeps[0][1] - late_keeps[0][0]
    packed_rows = (SHARED + HALO) // 2 + 4
    whole = jax.ShapeDtypeStruct(seeds.shape, jnp.float32)

    shared, seeds, material, table = pl.pallas_call(
        functools.partial(first_kernel, own, HALO // 2),
        out_shape=[
            jax.ShapeDtypeStruct((7 * depth, packed_rows, size_y), jnp.float32),
            jax.ShapeDtypeStruct(seeds.shape[1:], jnp.float32),
            jax.ShapeDtypeStruct(material.shape[1:], jnp.int32),
            jax.ShapeDtypeStruct((2 * decay.shape[0], size_y), jnp.float32),
        ],
        in_specs=[HBM] * 4,
        out_specs=[VMEM] * 4,
        scratch_shapes=[pltpu.SMEM((2, *decay.shape), jnp.float32), pltpu.SemaphoreType.DMA((14,))],
        compiler_params=PARAMS,
        cost_estimate=cost(0),
    )(*(pltpu.with_memory_space_constraint(x, pltpu.HBM) for x in (decay, coupling, seeds, material)))
    shared = swapped(shared, 2, tile_size)
    edge_near, edge_far, late_near, late_far = called(
        functools.partial(halo_pair_kernel, edges, late_spans, "sub"),
        [(PLANES, edge_rows, size_y)] * 2 + [(PLANES, late_rows, size_y)] * 2, table, seeds, material,
    )
    edge_near, late_near = near_exchange(edge_near, sub_size), near_exchange(late_near, sub_size)
    edge_far = far_exchange(edge_far, sub_size, tile_size)
    late_far = far_exchange(late_far, sub_size, tile_size)

    edge, corner, beside = called(
        functools.partial(edge_kernel, edges, "sub", sub_size, "tile"),
        [(planes, 2 * BAND, size_y), (planes, BAND, size_y), (planes, BAND // 2, size_y)],
        table, seeds, material, edge_near, edge_far,
    )
    corner = swapped(corner, 2, tile_size)
    beside = swapped(beside, 1, tile_size)

    late, bands, strip = called(
        functools.partial(late_kernel, late_spans, late_keeps, "sub", sub_size, "tile"),
        [(planes, 2 * late, size_y), (planes, late, size_y), (planes, BAND // 2, size_y)],
        table, seeds, material, late_near, late_far, edge,
    )
    bands = swapped(bands, 2, tile_size)
    strip = swapped(strip, 3, tile_size)

    shape = (PLANES, packed_rows + SHARED + 2 * HALO, size_y)
    shared_near, shared_far = called(
        functools.partial(shared_halo_kernel, (own,), "sub"), [shape, shape],
        table, seeds, material, shared, late,
    )
    shared_near = near_exchange(shared_near, sub_size)
    shared_far = far_exchange(shared_far, sub_size, tile_size)

    summed, send = called(
        functools.partial(corner_kernel, "tile"), [(planes, 2 * BAND, size_y), (planes, BAND, size_y)],
        edge, corner, beside, flops=CORNER,
    )
    got = swapped(send, 1, tile_size)
    early = pl.pallas_call(
        functools.partial(shared_kernel, (own,), span, keep, "sub", sub_size),
        out_shape=whole,
        in_specs=[VMEM] * 6,
        out_specs=HBM,
        scratch_shapes=[pltpu.VMEM((6, depth, SHARED, size_y), jnp.float32), pltpu.SemaphoreType.DMA],
        compiler_params=PARAMS,
        cost_estimate=cost(SHARE),
    )(table, seeds, material, shared, shared_near, shared_far)
    return pl.pallas_call(
        functools.partial(last_kernel, "tile"),
        out_shape=whole,
        in_specs=[VMEM] * 6 + [HBM],
        out_specs=HBM,
        scratch_shapes=[pltpu.VMEM((6, depth, (size_x - SHARED) // 2, size_y), jnp.float32)] * 2
        + [pltpu.SemaphoreType.DMA((12,))],
        input_output_aliases={6: 0},
        compiler_params=PARAMS,
        cost_estimate=cost(0),
    )(late, bands, summed, got, strip, beside, early)


def any_lattice(seeds, material, decay, coupling, sub_size, tile_size):
    depth, size_x, size_y = seeds.shape[2:]
    seeds, material = seeds[0], material[0]
    spans = ((0, size_x),)
    table = table_rows(decay, coupling, size_y)
    shape = (PLANES, size_x, size_y)
    near, far = called(functools.partial(halo_kernel, spans, "sub"), [shape, shape], table, seeds, material)
    near = near_exchange(near, sub_size)
    far = far_exchange(far, sub_size, tile_size)
    weighted, = called(
        functools.partial(whole_kernel, spans, "sub", sub_size), [(6 * depth, size_x, size_y)],
        table, seeds, material, near, far,
    )
    weighted = weighted.reshape(6, depth, size_x, size_y)
    side = math.isqrt(tile_size)
    prev_band = from_behind(weighted[:, :, size_x - BAND :, :], 1, tile_size)
    next_band = from_behind(weighted[:, :, :BAND, :], -1, tile_size)
    combined = weighted.at[:, :, :BAND, :].add(prev_band)
    combined = combined.at[:, :, size_x - BAND :, :].add(next_band)
    flat = (6, depth, size_x * BAND // size_y, size_y)
    thin = (6, depth, size_x, BAND)
    top_slab = combined[..., size_y - BAND :].reshape(flat)
    bottom_slab = combined[..., :BAND].reshape(flat)
    result = combined.at[..., :BAND].add(from_behind(top_slab, side, tile_size).reshape(thin))
    result = result.at[..., size_y - BAND :].add(from_behind(bottom_slab, -side, tile_size).reshape(thin))
    return result[None]


def solution(mesh):
    sub_size, tile_size = mesh.shape["sub"], mesh.shape["tile"]
    body = two_by_two if tile_size == 4 else any_lattice

    def on_device(seeds, material, decay, coupling):
        return body(seeds, material, decay, coupling, sub_size, tile_size)

    placed = (P("tile", None, "sub", None, None), P("tile", "sub", None, None), P(), P())
    return jax.shard_map(
        on_device,
        mesh=mesh,
        in_specs=placed,
        out_specs=P("tile", None, "sub", None, None),
        check_vma=False,
    )
```

```python
import functools
import math

import jax
import jax.numpy as jnp
from jax import lax
from jax.experimental import pallas as pl
from jax.experimental.pallas import tpu as pltpu
from jax.sharding import PartitionSpec as P

BAND = 32
HALO = 8
PLANES = 5
REACH = 2
SHARED = 96
LARGE, MEDIUM, SMALL = 10**10, 2 * 10**9, 5 * 10**8

magnetic_coeff = 0.5


def lane_of(shape):
    return lax.broadcasted_iota(jnp.int32, shape, len(shape) - 1)


def row_of(shape):
    return lax.broadcasted_iota(jnp.int32, shape, len(shape) - 2)


def rolled(v, shift):
    return pltpu.roll(v, shift % v.shape[-1], v.ndim - 1)


def next_x(v):
    rows = v.shape[0]
    return jnp.where(row_of(v.shape) == rows - 1, 0.0, pltpu.roll(v, rows - 1, 0))


def prev_x(v):
    return jnp.where(row_of(v.shape) == 0, 0.0, pltpu.roll(v, 1, 0))


def next_y(v):
    lanes = v.shape[1]
    return jnp.where(lane_of(v.shape) == lanes - 1, 0.0, pltpu.roll(v, lanes - 1, 1))


def prev_y(v):
    return jnp.where(lane_of(v.shape) == 0, 0.0, pltpu.roll(v, 1, 1))


def plus_x(v):
    return next_x(v) - v


def plus_y(v):
    return next_y(v) - v


def minus_x(v):
    return v - prev_x(v)


def minus_y(v):
    return v - prev_y(v)


def looked_up(labels, entries):
    value = jnp.broadcast_to(entries[0], labels.shape)
    for m in range(1, len(entries)):
        value = jnp.where(labels == m, entries[m], value)
    return value


def update_h(h, v, v_after):
    depth = len(v[0])
    new = [[], [], []]
    for p in range(depth):
        vx, vy, vz = v[0][p], v[1][p], v[2][p]
        up_x, up_y = (v[0][p + 1], v[1][p + 1]) if p + 1 < depth else v_after
        dz_x = up_x - vx if up_x is not None else -vx
        dz_y = up_y - vy if up_y is not None else -vy
        new[0].append(h[0][p] + (plus_y(vz) - dz_y))
        new[1].append(h[1][p] + (dz_x - plus_x(vz)))
        new[2].append(h[2][p] + (plus_x(vy) - plus_y(vx)))
    return new


def update_e(e, ca, h, h_before):
    depth = len(h[0])
    new = [[], [], []]
    for p in range(depth):
        hx, hy, hz = h[0][p], h[1][p], h[2][p]
        low_x, low_y = (h[0][p - 1], h[1][p - 1]) if p > 0 else h_before
        dz_x = hx - low_x if low_x is not None else hx
        dz_y = hy - low_y if low_y is not None else hy
        new[0].append(ca[p] * e[0][p] - magnetic_coeff * (minus_y(hz) - dz_y))
        new[1].append(ca[p] * e[1][p] - magnetic_coeff * (dz_x - minus_x(hz)))
        new[2].append(ca[p] * e[2][p] - magnetic_coeff * (minus_x(hy) - minus_y(hx)))
    return new


def scaled(cb, e):
    return [[cb[p] * e[c][p] for p in range(len(cb))] for c in range(3)]


def joined(ref, index, spans):
    return jnp.concatenate([ref[*index, lo:hi] for lo, hi in spans], axis=0)


def prepared(e, h, labels, tables):
    ca = [looked_up(m, tables[0]) for m in labels]
    cb = [looked_up(m, tables[1]) for m in labels]
    return e, h, ca, cb


def raw(seeds, material, spans):
    depth = seeds.shape[1]
    e = [[joined(seeds, (c, p), spans) for p in range(depth)] for c in range(3)]
    h = [[joined(seeds, (3 + c, p), spans) for p in range(depth)] for c in range(3)]
    return e, h, [joined(material, (p,), spans) for p in range(depth)]


def table_entries(table):
    count = table.shape[0] // 2
    rows = [table[m : m + 1] for m in range(2 * count)]
    return rows[:count], rows[count:]


def loaded(seeds, material, table, spans):
    return prepared(*raw(seeds, material, spans), table_entries(table))


NONE = (None, None)


def send_halos(sub, fields, near, far, packed=lambda planes: planes):
    odd = lax.rem(lax.axis_index(sub), 2) == 1
    e, h, ca, cb = fields
    v1 = scaled(cb, e)
    h1 = update_h(h, v1, NONE)
    e1 = update_e(e, ca, h1, NONE)
    v2 = scaled(cb, e1)
    h2 = update_h(h1, v2, NONE)
    up = (h1[0][-1], h1[1][-1], h2[0][-1], h2[1][-1], cb[-1])
    down = (v1[0][0], v1[1][0], v2[0][0], v2[1][0], cb[0])
    up, down = packed(jnp.stack(up)), packed(jnp.stack(down))
    near[...] = jnp.where(odd, down, up)
    far[...] = jnp.where(odd, up, down)


def halo_kernel(spans, sub, table, seeds, material, near, far):
    send_halos(sub, loaded(seeds, material, table, spans), near, far)


def ramp(position, count):
    position = position.astype(jnp.float32) + 0.5
    return jnp.where(
        position < BAND,
        position / BAND,
        jnp.where(position > count - BAND, (count - position) / BAND, 1.0),
    )


def final_fields(fields, near, far, sub, sub_size, unpacked=lambda planes: planes):
    e, h, ca, cb = fields
    index = lax.axis_index(sub)
    odd = lax.rem(index, 2) == 1
    below, above = index > 0, index < sub_size - 1
    a, b = near[...], far[...]
    from_below = unpacked(jnp.where(odd, a, b))
    from_above = unpacked(jnp.where(above, jnp.where(odd, b, a), 0.0))
    part_h1x, part_h1y, part_h2x, part_h2y, cb_low = from_below
    v1x_up, v1y_up, part_v2x, part_v2y, cb_up = from_above

    v1 = scaled(cb, e)
    h1 = update_h(h, v1, (v1x_up, v1y_up))
    dh1x, dh1y = -v1[1][0], v1[0][0]
    h1_low = (jnp.where(below, part_h1x + dh1x, 0.0), jnp.where(below, part_h1y + dh1y, 0.0))
    e1 = update_e(e, ca, h1, h1_low)
    v2 = scaled(cb, e1)
    v2_up = (
        part_v2x - cb_up * (magnetic_coeff * h1[1][-1]),
        part_v2y + cb_up * (magnetic_coeff * h1[0][-1]),
    )
    h2 = update_h(h1, v2, v2_up)
    dv2x = cb_low * (magnetic_coeff * dh1y)
    dv2y = cb_low * (-magnetic_coeff * dh1x)
    dv2z = cb_low * (-magnetic_coeff * (minus_x(dh1y) - minus_y(dh1x)))
    h2x_low = part_h2x + (dh1x + (plus_y(dv2z) - (v2[1][0] - dv2y)))
    h2y_low = part_h2y + (dh1y + ((v2[0][0] - dv2x) - plus_x(dv2z)))
    h2_low = (jnp.where(below, h2x_low, 0.0), jnp.where(below, h2y_low, 0.0))
    e2 = update_e(e1, ca, h2, h2_low)
    return e2 + h2


def middle_out(block):
    return rolled(block, block.shape[-1] // 2)


def y_packed(first, second):
    lane = lane_of(first.shape)
    middle = (lane >= BAND) & (lane < first.shape[-1] - BAND)
    return jnp.where(middle, middle_out(second), first)


def inner_lanes(shape):
    lane = lane_of(shape)
    return (lane >= BAND) & (lane < shape[-1] - BAND)


def y_unpacked(block):
    a, b = rolled(block, BAND), rolled(block, -BAND)
    middle = inner_lanes(block.shape)
    below = lane_of(block.shape) < BAND
    first = jnp.where(middle, 0.0, jnp.where(below, a, b))
    second = jnp.where(middle, 0.0, jnp.where(below, b, a))
    return first, second


def strip_packed(strip):
    half = strip.shape[1] // 2
    first, second = strip[:, :half], strip[:, half:]
    return jnp.where(inner_lanes(first.shape), second, middle_out(first))


def strip_of(corners, block):
    middle = inner_lanes(block.shape)
    first = jnp.where(middle, middle_out(block), corners[0])
    second = jnp.where(middle, block, corners[1])
    return jnp.concatenate([first, second], axis=1)


def low_rows(shape):
    return row_of(shape) < 4


def bands_packed(block):
    rows, lanes = block.shape[1:]
    count, width, high = rows // 2 + 4, REACH * (rows // 8), lanes - BAND
    shape = (block.shape[0], 8, lanes)
    lane = lane_of(shape)
    low = low_rows(shape)
    side = jnp.zeros(shape, block.dtype)
    for g in range(rows // 8):
        at = BAND + REACH * (g + 1)
        piece = rolled(block[:, 8 * g : 8 * g + 8], REACH * (g + 1))
        here = ((lane >= at) & (lane < at + REACH)) | (
            (lane >= at + high - BAND - REACH) & (lane < at + high - BAND)
        )
        side = jnp.where(here, piece, side)
    other = rolled(pltpu.roll(side, 4, 1), width + REACH)
    own = ((lane >= BAND) & (lane < BAND + REACH + width)) | ((lane >= high) & (lane < high + width))
    side = jnp.where(own, side, other)
    middle = (lane >= BAND) & (lane < high)
    packed = y_packed(block[:, :count], block[:, rows - count :])
    first = jnp.where(low & middle, side, packed[:, :8])
    last = jnp.where(low | middle, packed[:, count - 8 :], side)
    return jnp.concatenate([first, packed[:, 8 : count - 8], last], axis=1)


def bands_unpacked(packed):
    count, lanes = packed.shape[1:]
    rows = 2 * count - 8
    width, high = REACH * (rows // 8), lanes - BAND
    first, last = packed[:, :8], packed[:, count - 8 :]
    low = low_rows(first.shape)
    lane = lane_of(first.shape)
    middle = (lane >= BAND) & (lane < high)
    side = jnp.where(low, first, last)
    other = rolled(pltpu.roll(side, 4, 1), -width - REACH)
    side = jnp.where(low == middle, side, other)
    beside = ((lane >= BAND) & (lane < BAND + REACH)) | ((lane >= high - REACH) & (lane < high))
    moved = [rolled(packed[:, at : at + 8], lanes // 2) for at in range(0, count, 8)]
    pieces = [packed[:, at : at + 8] for at in range(0, count - 8, 8)]
    pieces += [jnp.where(low, last, moved[0])] + moved[1:]
    result = []
    for g, piece in enumerate(pieces):
        result.append(jnp.where(middle, jnp.where(beside, rolled(side, -REACH * (g + 1)), 0.0), piece))
    return jnp.concatenate(result, axis=1)


def first_kernel(span, skip, decay, coupling, seeds, material, shared, held, labels, table, entries, sems):
    size_x = held.shape[2]
    copies = []

    def fetch(source, target):
        copies.append(pltpu.make_async_copy(source, target, sems.at[len(copies)]))
        copies[-1].start()

    def fetch_rows(lo, hi):
        rows = pl.ds(lo, hi - lo)
        fetch(material.at[0, :, rows], labels.at[:, rows])
        for c in range(0, 6, 2):
            some = pl.ds(c, 2)
            fetch(seeds.at[0, some, :, rows], held.at[some, :, rows])

    fetch_rows(*span)
    early = len(copies)
    fetch(decay, entries.at[0])
    fetch(coupling, entries.at[1])
    fetch_rows(0, span[0])
    fetch_rows(span[1], size_x)
    rows = slice(span[0] + skip, span[1] - skip)
    for copy in copies[:early]:
        copy.wait()
    planes = [held[c, :, rows] for c in range(6)] + [labels[:, rows].astype(jnp.float32)]
    shared[...] = bands_packed(jnp.concatenate(planes, axis=0))
    for copy in copies[early:]:
        copy.wait()
    count = entries.shape[1]
    for k in range(2):
        for m in range(count):
            table[k * count + m : k * count + m + 1] = jnp.full((1, table.shape[1]), entries[k, m], jnp.float32)


def halo_pair_kernel(edges, inner, sub, table, seeds, material, near_edge, far_edge, near, far):
    send_halos(sub, loaded(seeds, material, table, edges), near_edge, far_edge)
    send_halos(sub, loaded(seeds, material, table, inner), near, far)


def shared_fields(table, shared):
    depth = shared.shape[0] // 7
    planes = bands_unpacked(shared[...])
    f = [planes[depth * c : depth * (c + 1)] for c in range(7)]
    return prepared(f[:3], f[3:6], f[6], table_entries(table))


def shared_halo_kernel(sub, table, shared, near, far, done):
    done[...] = jnp.zeros(done.shape, done.dtype)
    send_halos(sub, shared_fields(table, shared), near, far, bands_packed)


def weighted_planes(seeds, material, table, near, far, spans, keeps, sub, sub_size):
    planes = final_fields(loaded(seeds, material, table, spans), near, far, sub, sub_size)
    return weighted(planes, spans, keeps, *seeds.shape[2:])


def weighted(planes, spans, keeps, size_x, size_y):
    at, results = 0, []
    for (lo, hi), (start, stop) in zip(spans, keeps):
        shape = (stop - start, size_y)
        weight = ramp(row_of(shape) + start, size_x) * ramp(lane_of(shape), size_y)
        first = at + start - lo
        results.append(jnp.stack([plane[first : first + stop - start] * weight for part in planes for plane in part]))
        at += hi - lo
    return results


def edge_kernel(spans, sub, sub_size, tile, table, seeds, material, near, far, edge, corner, beside):
    size_x = seeds.shape[2]
    keeps = ((0, BAND), (size_x - BAND, size_x))
    low, high = weighted_planes(seeds, material, table, near, far, spans, keeps, sub, sub_size)
    odd = lax.rem(lax.axis_index(tile), 2) == 1
    edge[:, :BAND] = low
    edge[:, BAND:] = high
    corner[...] = y_packed(low, high)
    beside[...] = strip_packed(jnp.where(odd, low, high))


def middle_kernel(spans, sub, sub_size, tile, table, seeds, material, near, far, edge, _, mid, bands, strip):
    size_x = seeds.shape[2]
    keep = (BAND, size_x - BAND)
    odd = lax.rem(lax.axis_index(tile), 2) == 1
    strip[...] = strip_packed(jnp.where(odd, edge[:, BAND:], edge[:, :BAND]))
    planes, = weighted_planes(seeds, material, table, near, far, spans, (keep,), sub, sub_size)
    half = bands.shape[1]
    mid[...] = planes
    bands[...] = y_packed(planes[:, :half], planes[:, -half:])


def whole_kernel(spans, sub, sub_size, table, seeds, material, near, far, out):
    planes, = weighted_planes(seeds, material, table, near, far, spans, spans, sub, sub_size)
    out[...] = planes


def y_swapped(block):
    below = lane_of(block.shape) < BAND
    return jnp.where(inner_lanes(block.shape), 0.0, jnp.where(below, rolled(block, BAND), rolled(block, -BAND)))


def shared_kernel(span, size_x, sub, sub_size, table, shared, near, far, part):
    planes = final_fields(shared_fields(table, shared), near, far, sub, sub_size, bands_unpacked)
    found, = weighted(planes, (span,), (span,), size_x, part.shape[2])
    part[...] = y_swapped(found)


def corner_kernel(tile, edge, corner, _, summed, send):
    odd = lax.rem(lax.axis_index(tile), 2) == 1
    half = BAND // 2
    first, second = y_unpacked(corner[...])
    low = edge[:, :BAND] + first
    high = edge[:, BAND:] + second
    summed[:, :BAND] = low
    summed[:, BAND:] = high
    by, away = jnp.where(odd, low, high), jnp.where(odd, high, low)
    send[:, :half] = y_packed(by[:, :half], by[:, half:])
    send[:, half:] = y_packed(away[:, :half], away[:, half:])


def early_kernel(mid, part, out, whole, sem):
    size_x = out.shape[3]
    skip = HALO // 2
    count = part.shape[1] - 2 * skip
    start = (size_x - count) // 2
    found = mid[:, start - BAND : start - BAND + count] + part[:, skip : skip + count]
    whole[...] = found.reshape(whole.shape)
    copy = pltpu.make_async_copy(whole, out.at[0, :, :, pl.ds(start, count)], sem)
    copy.start()
    copy.wait()


def last_kernel(tile, mid, bands, summed, got, strip, beside, _, out, low, high, sems):
    odd = lax.rem(lax.axis_index(tile), 2) == 1
    half, count = bands.shape[1], low.shape[2]
    quarter = BAND // 2
    depth, size_x = out.shape[2:4]
    copies = []
    for c in range(6):
        at = slice(depth * c, depth * (c + 1))
        first, second = y_unpacked(bands[at])
        low[c, :, BAND:] = mid[at, :half] + first
        high[c, :, :half] = mid[at, -half:] + second
        straight = got[at, :quarter]
        by = strip_of((straight, middle_out(straight)), beside[at])
        away = strip_of(y_unpacked(got[at, quarter:]), strip[at])
        low[c, :, :BAND] = summed[at, :BAND] + jnp.where(odd, by, away)
        high[c, :, half:] = summed[at, BAND:] + jnp.where(odd, away, by)
        for k, (rows, start) in enumerate(((low, 0), (high, size_x - count))):
            copies.append(pltpu.make_async_copy(rows.at[c], out.at[0, c, :, pl.ds(start, count)], sems.at[2 * c + k]))
            copies[-1].start()
    for copy in copies:
        copy.wait()


HBM = pl.BlockSpec(memory_space=pltpu.HBM)
VMEM = pl.BlockSpec(memory_space=pltpu.VMEM)
PARAMS = pltpu.CompilerParams(vmem_limit_bytes=32 * 1024 * 1024)


def cost(flops):
    return pl.CostEstimate(flops=flops, bytes_accessed=0, transcendentals=0)


def called(kernel, shapes, *operands, flops=0):
    outs = [jax.ShapeDtypeStruct(shape, jnp.float32) for shape in shapes]
    return pl.pallas_call(
        kernel,
        out_shape=outs,
        in_specs=[VMEM] * len(operands),
        out_specs=[VMEM] * len(outs),
        compiler_params=PARAMS,
        cost_estimate=cost(flops),
    )(*operands)


def after(first, *values):
    return lax.optimization_barrier((first, *values))


def near_exchange(near, sub_size):
    return lax.ppermute(near, "sub", [(i, i ^ 1) for i in range(sub_size)])


def far_exchange(far, sub_size, tile_size):
    pairs = []
    for t in range(tile_size):
        for i in range(sub_size):
            j = ((i + 1) ^ 1) - 1
            other = (t, j) if 0 <= j < sub_size else (t ^ 1, i)
            pairs.append((t * sub_size + i, other[0] * sub_size + other[1]))
    return lax.ppermute(far, ("tile", "sub"), pairs)


def swapped(value, bits, tile_size):
    return lax.ppermute(value, "tile", [(t, t ^ bits) for t in range(tile_size)])


def from_behind(value, steps, count):
    return lax.ppermute(value, "tile", [(t, (t + steps) % count) for t in range(count)])


def table_rows(decay, coupling, size_y):
    entries = jnp.concatenate([decay, coupling])
    return jnp.broadcast_to(entries[:, None], (entries.shape[0], size_y))


def two_by_two(seeds, material, decay, coupling, sub_size, tile_size):
    depth, size_x, size_y = seeds.shape[2:]
    planes = 6 * depth
    edges = ((0, BAND + HALO), (size_x - BAND - HALO, size_x))
    inner = ((BAND - HALO, size_x - BAND + HALO),)
    keep = ((size_x - SHARED) // 2, (size_x + SHARED) // 2)
    span = (keep[0] - HALO // 2, keep[1] + HALO // 2)
    fetched = (keep[0] - HALO, keep[1] + HALO)
    rows = size_x - 2 * BAND
    edge_rows, inner_rows = 2 * (BAND + HALO), rows + 2 * HALO
    packed_rows = (SHARED + HALO) // 2 + 4
    whole = jax.ShapeDtypeStruct(seeds.shape, jnp.float32)

    shared, seeds, material, table = pl.pallas_call(
        functools.partial(first_kernel, fetched, HALO // 2),
        out_shape=[
            jax.ShapeDtypeStruct((7 * depth, packed_rows, size_y), jnp.float32),
            jax.ShapeDtypeStruct(seeds.shape[1:], jnp.float32),
            jax.ShapeDtypeStruct(material.shape[1:], jnp.int32),
            jax.ShapeDtypeStruct((2 * decay.shape[0], size_y), jnp.float32),
        ],
        in_specs=[HBM] * 4,
        out_specs=[VMEM] * 4,
        scratch_shapes=[pltpu.SMEM((2, *decay.shape), jnp.float32), pltpu.SemaphoreType.DMA((14,))],
        compiler_params=PARAMS,
        cost_estimate=cost(0),
    )(*(pltpu.with_memory_space_constraint(x, pltpu.HBM) for x in (decay, coupling, seeds, material)))
    shared = swapped(shared, 2, tile_size)
    edge_near, edge_far, inner_near, inner_far = called(
        functools.partial(halo_pair_kernel, edges, inner, "sub"),
        [(PLANES, edge_rows, size_y)] * 2 + [(PLANES, inner_rows, size_y)] * 2, table, seeds, material,
    )
    edge_near, inner_near = near_exchange(edge_near, sub_size), near_exchange(inner_near, sub_size)
    edge_far = far_exchange(edge_far, sub_size, tile_size)
    inner_far = far_exchange(inner_far, sub_size, tile_size)

    edge, corner, beside = called(
        functools.partial(edge_kernel, edges, "sub", sub_size, "tile"),
        [(planes, 2 * BAND, size_y), (planes, BAND, size_y), (planes, BAND // 2, size_y)],
        table, seeds, material, edge_near, edge_far,
    )
    corner = swapped(corner, 2, tile_size)
    beside = swapped(beside, 1, tile_size)

    shape = (PLANES, packed_rows, size_y)
    shared_near, shared_far, done = called(
        functools.partial(shared_halo_kernel, "sub"), [shape, shape, (8, size_y)], table, shared, flops=LARGE
    )
    shared_near = near_exchange(shared_near, sub_size)
    shared_far = far_exchange(shared_far, sub_size, tile_size)

    mid, bands, strip = called(
        functools.partial(middle_kernel, inner, "sub", sub_size, "tile"),
        [(planes, rows, size_y), (planes, (rows - SHARED) // 2, size_y), (planes, BAND // 2, size_y)],
        table, seeds, material, inner_near, inner_far, edge, done,
    )
    bands = swapped(bands, 2, tile_size)
    strip = swapped(strip, 3, tile_size)

    corner, mid = after(corner, mid)
    summed, send = called(
        functools.partial(corner_kernel, "tile"), [(planes, 2 * BAND, size_y), (planes, BAND, size_y)],
        edge, corner, beside, flops=SMALL,
    )
    got = swapped(send, 1, tile_size)
    part, = called(
        functools.partial(shared_kernel, span, size_x, "sub", sub_size),
        [(planes, SHARED + HALO, size_y)], table, shared, shared_near, shared_far, flops=MEDIUM,
    )
    early = pl.pallas_call(
        early_kernel,
        out_shape=whole,
        in_specs=[VMEM] * 2,
        out_specs=HBM,
        scratch_shapes=[pltpu.VMEM((6, depth, SHARED, size_y), jnp.float32), pltpu.SemaphoreType.DMA],
        compiler_params=PARAMS,
        cost_estimate=cost(0),
    )(mid, part)
    return pl.pallas_call(
        functools.partial(last_kernel, "tile"),
        out_shape=whole,
        in_specs=[VMEM] * 6 + [HBM],
        out_specs=HBM,
        scratch_shapes=[pltpu.VMEM((6, depth, (size_x - SHARED) // 2, size_y), jnp.float32)] * 2
        + [pltpu.SemaphoreType.DMA((12,))],
        input_output_aliases={6: 0},
        compiler_params=PARAMS,
        cost_estimate=cost(0),
    )(mid, bands, summed, got, strip, beside, early)


def any_lattice(seeds, material, decay, coupling, sub_size, tile_size):
    depth, size_x, size_y = seeds.shape[2:]
    seeds, material = seeds[0], material[0]
    spans = ((0, size_x),)
    table = table_rows(decay, coupling, size_y)
    shape = (PLANES, size_x, size_y)
    near, far = called(functools.partial(halo_kernel, spans, "sub"), [shape, shape], table, seeds, material)
    near = near_exchange(near, sub_size)
    far = far_exchange(far, sub_size, tile_size)
    weighted, = called(
        functools.partial(whole_kernel, spans, "sub", sub_size), [(6 * depth, size_x, size_y)],
        table, seeds, material, near, far,
    )
    weighted = weighted.reshape(6, depth, size_x, size_y)
    side = math.isqrt(tile_size)
    prev_band = from_behind(weighted[:, :, size_x - BAND :, :], 1, tile_size)
    next_band = from_behind(weighted[:, :, :BAND, :], -1, tile_size)
    combined = weighted.at[:, :, :BAND, :].add(prev_band)
    combined = combined.at[:, :, size_x - BAND :, :].add(next_band)
    flat = (6, depth, size_x * BAND // size_y, size_y)
    thin = (6, depth, size_x, BAND)
    top_slab = combined[..., size_y - BAND :].reshape(flat)
    bottom_slab = combined[..., :BAND].reshape(flat)
    result = combined.at[..., :BAND].add(from_behind(top_slab, side, tile_size).reshape(thin))
    result = result.at[..., size_y - BAND :].add(from_behind(bottom_slab, -side, tile_size).reshape(thin))
    return result[None]


def solution(mesh):
    sub_size, tile_size = mesh.shape["sub"], mesh.shape["tile"]
    body = two_by_two if tile_size == 4 else any_lattice

    def on_device(seeds, material, decay, coupling):
        return body(seeds, material, decay, coupling, sub_size, tile_size)

    placed = (P("tile", None, "sub", None, None), P("tile", "sub", None, None), P(), P())
    return jax.shard_map(
        on_device,
        mesh=mesh,
        in_specs=placed,
        out_specs=P("tile", None, "sub", None, None),
        check_vma=False,
    )
```

```python
import functools
import math

import jax
import jax.numpy as jnp
from jax import lax
from jax.experimental import pallas as pl
from jax.experimental.pallas import tpu as pltpu
from jax.sharding import PartitionSpec as P

BAND = 32
HALO = 8
PLANES = 5
REACH = 2
SHARED = 96
LARGE, MEDIUM, SMALL = 10**10, 15 * 10**8, 0

magnetic_coeff = 0.5


def lane_of(shape):
    return lax.broadcasted_iota(jnp.int32, shape, len(shape) - 1)


def row_of(shape):
    return lax.broadcasted_iota(jnp.int32, shape, len(shape) - 2)


def rolled(v, shift):
    return pltpu.roll(v, shift % v.shape[-1], v.ndim - 1)


def next_x(v):
    rows = v.shape[0]
    return jnp.where(row_of(v.shape) == rows - 1, 0.0, pltpu.roll(v, rows - 1, 0))


def prev_x(v):
    return jnp.where(row_of(v.shape) == 0, 0.0, pltpu.roll(v, 1, 0))


def next_y(v):
    lanes = v.shape[1]
    return jnp.where(lane_of(v.shape) == lanes - 1, 0.0, pltpu.roll(v, lanes - 1, 1))


def prev_y(v):
    return jnp.where(lane_of(v.shape) == 0, 0.0, pltpu.roll(v, 1, 1))


def plus_x(v):
    return next_x(v) - v


def plus_y(v):
    return next_y(v) - v


def minus_x(v):
    return v - prev_x(v)


def minus_y(v):
    return v - prev_y(v)


def looked_up(labels, entries):
    value = jnp.broadcast_to(entries[0], labels.shape)
    for m in range(1, len(entries)):
        value = jnp.where(labels == m, entries[m], value)
    return value


def update_h(h, v, v_after):
    depth = len(v[0])
    new = [[], [], []]
    for p in range(depth):
        vx, vy, vz = v[0][p], v[1][p], v[2][p]
        up_x, up_y = (v[0][p + 1], v[1][p + 1]) if p + 1 < depth else v_after
        dz_x = up_x - vx if up_x is not None else -vx
        dz_y = up_y - vy if up_y is not None else -vy
        new[0].append(h[0][p] + (plus_y(vz) - dz_y))
        new[1].append(h[1][p] + (dz_x - plus_x(vz)))
        new[2].append(h[2][p] + (plus_x(vy) - plus_y(vx)))
    return new


def update_e(e, ca, h, h_before):
    depth = len(h[0])
    new = [[], [], []]
    for p in range(depth):
        hx, hy, hz = h[0][p], h[1][p], h[2][p]
        low_x, low_y = (h[0][p - 1], h[1][p - 1]) if p > 0 else h_before
        dz_x = hx - low_x if low_x is not None else hx
        dz_y = hy - low_y if low_y is not None else hy
        new[0].append(ca[p] * e[0][p] - magnetic_coeff * (minus_y(hz) - dz_y))
        new[1].append(ca[p] * e[1][p] - magnetic_coeff * (dz_x - minus_x(hz)))
        new[2].append(ca[p] * e[2][p] - magnetic_coeff * (minus_x(hy) - minus_y(hx)))
    return new


def scaled(cb, e):
    return [[cb[p] * e[c][p] for p in range(len(cb))] for c in range(3)]


def joined(ref, index, spans):
    return jnp.concatenate([ref[*index, lo:hi] for lo, hi in spans], axis=0)


def prepared(e, h, labels, tables):
    ca = [looked_up(m, tables[0]) for m in labels]
    cb = [looked_up(m, tables[1]) for m in labels]
    return e, h, ca, cb


def raw(seeds, material, spans):
    depth = seeds.shape[1]
    e = [[joined(seeds, (c, p), spans) for p in range(depth)] for c in range(3)]
    h = [[joined(seeds, (3 + c, p), spans) for p in range(depth)] for c in range(3)]
    return e, h, [joined(material, (p,), spans) for p in range(depth)]


def table_entries(table):
    count = table.shape[0] // 2
    rows = [table[m : m + 1] for m in range(2 * count)]
    return rows[:count], rows[count:]


def loaded(seeds, material, table, spans):
    return prepared(*raw(seeds, material, spans), table_entries(table))


NONE = (None, None)


def send_halos(sub, fields, near, far, packed=lambda planes: planes):
    odd = lax.rem(lax.axis_index(sub), 2) == 1
    e, h, ca, cb = fields
    v1 = scaled(cb, e)
    h1 = update_h(h, v1, NONE)
    e1 = update_e(e, ca, h1, NONE)
    v2 = scaled(cb, e1)
    h2 = update_h(h1, v2, NONE)
    up = (h1[0][-1], h1[1][-1], h2[0][-1], h2[1][-1], cb[-1])
    down = (v1[0][0], v1[1][0], v2[0][0], v2[1][0], cb[0])
    up, down = packed(jnp.stack(up)), packed(jnp.stack(down))
    near[...] = jnp.where(odd, down, up)
    far[...] = jnp.where(odd, up, down)


def halo_kernel(spans, sub, table, seeds, material, near, far):
    send_halos(sub, loaded(seeds, material, table, spans), near, far)


def ramp(position, count):
    position = position.astype(jnp.float32) + 0.5
    return jnp.where(
        position < BAND,
        position / BAND,
        jnp.where(position > count - BAND, (count - position) / BAND, 1.0),
    )


def final_fields(fields, near, far, sub, sub_size, unpacked=lambda planes: planes):
    e, h, ca, cb = fields
    index = lax.axis_index(sub)
    odd = lax.rem(index, 2) == 1
    below, above = index > 0, index < sub_size - 1
    a, b = near[...], far[...]
    from_below = unpacked(jnp.where(odd, a, b))
    from_above = unpacked(jnp.where(above, jnp.where(odd, b, a), 0.0))
    part_h1x, part_h1y, part_h2x, part_h2y, cb_low = from_below
    v1x_up, v1y_up, part_v2x, part_v2y, cb_up = from_above

    v1 = scaled(cb, e)
    h1 = update_h(h, v1, (v1x_up, v1y_up))
    dh1x, dh1y = -v1[1][0], v1[0][0]
    h1_low = (jnp.where(below, part_h1x + dh1x, 0.0), jnp.where(below, part_h1y + dh1y, 0.0))
    e1 = update_e(e, ca, h1, h1_low)
    v2 = scaled(cb, e1)
    v2_up = (
        part_v2x - cb_up * (magnetic_coeff * h1[1][-1]),
        part_v2y + cb_up * (magnetic_coeff * h1[0][-1]),
    )
    h2 = update_h(h1, v2, v2_up)
    dv2x = cb_low * (magnetic_coeff * dh1y)
    dv2y = cb_low * (-magnetic_coeff * dh1x)
    dv2z = cb_low * (-magnetic_coeff * (minus_x(dh1y) - minus_y(dh1x)))
    h2x_low = part_h2x + (dh1x + (plus_y(dv2z) - (v2[1][0] - dv2y)))
    h2y_low = part_h2y + (dh1y + ((v2[0][0] - dv2x) - plus_x(dv2z)))
    h2_low = (jnp.where(below, h2x_low, 0.0), jnp.where(below, h2y_low, 0.0))
    e2 = update_e(e1, ca, h2, h2_low)
    return e2 + h2


def middle_out(block):
    return rolled(block, block.shape[-1] // 2)


def y_packed(first, second):
    lane = lane_of(first.shape)
    middle = (lane >= BAND) & (lane < first.shape[-1] - BAND)
    return jnp.where(middle, middle_out(second), first)


def inner_lanes(shape):
    lane = lane_of(shape)
    return (lane >= BAND) & (lane < shape[-1] - BAND)


def y_unpacked(block):
    a, b = rolled(block, BAND), rolled(block, -BAND)
    middle = inner_lanes(block.shape)
    below = lane_of(block.shape) < BAND
    first = jnp.where(middle, 0.0, jnp.where(below, a, b))
    second = jnp.where(middle, 0.0, jnp.where(below, b, a))
    return first, second


def strip_packed(strip):
    half = strip.shape[1] // 2
    first, second = strip[:, :half], strip[:, half:]
    return jnp.where(inner_lanes(first.shape), second, middle_out(first))


def strip_of(corners, block):
    middle = inner_lanes(block.shape)
    first = jnp.where(middle, middle_out(block), corners[0])
    second = jnp.where(middle, block, corners[1])
    return jnp.concatenate([first, second], axis=1)


def low_rows(shape):
    return row_of(shape) < 4


def bands_packed(block):
    rows, lanes = block.shape[1:]
    count, width, high = rows // 2 + 4, REACH * (rows // 8), lanes - BAND
    shape = (block.shape[0], 8, lanes)
    lane = lane_of(shape)
    low = low_rows(shape)
    side = jnp.zeros(shape, block.dtype)
    for g in range(rows // 8):
        at = BAND + REACH * (g + 1)
        piece = rolled(block[:, 8 * g : 8 * g + 8], REACH * (g + 1))
        here = ((lane >= at) & (lane < at + REACH)) | (
            (lane >= at + high - BAND - REACH) & (lane < at + high - BAND)
        )
        side = jnp.where(here, piece, side)
    other = rolled(pltpu.roll(side, 4, 1), width + REACH)
    own = ((lane >= BAND) & (lane < BAND + REACH + width)) | ((lane >= high) & (lane < high + width))
    side = jnp.where(own, side, other)
    middle = (lane >= BAND) & (lane < high)
    packed = y_packed(block[:, :count], block[:, rows - count :])
    first = jnp.where(low & middle, side, packed[:, :8])
    last = jnp.where(low | middle, packed[:, count - 8 :], side)
    return jnp.concatenate([first, packed[:, 8 : count - 8], last], axis=1)


def bands_unpacked(packed):
    count, lanes = packed.shape[1:]
    rows = 2 * count - 8
    width, high = REACH * (rows // 8), lanes - BAND
    first, last = packed[:, :8], packed[:, count - 8 :]
    low = low_rows(first.shape)
    lane = lane_of(first.shape)
    middle = (lane >= BAND) & (lane < high)
    side = jnp.where(low, first, last)
    other = rolled(pltpu.roll(side, 4, 1), -width - REACH)
    side = jnp.where(low == middle, side, other)
    beside = ((lane >= BAND) & (lane < BAND + REACH)) | ((lane >= high - REACH) & (lane < high))
    moved = [rolled(packed[:, at : at + 8], lanes // 2) for at in range(0, count, 8)]
    pieces = [packed[:, at : at + 8] for at in range(0, count - 8, 8)]
    pieces += [jnp.where(low, last, moved[0])] + moved[1:]
    result = []
    for g, piece in enumerate(pieces):
        result.append(jnp.where(middle, jnp.where(beside, rolled(side, -REACH * (g + 1)), 0.0), piece))
    return jnp.concatenate(result, axis=1)


def first_kernel(span, skip, decay, coupling, seeds, material, shared, held, labels, table, entries, sems):
    size_x = held.shape[2]
    copies = []

    def fetch(source, target):
        copies.append(pltpu.make_async_copy(source, target, sems.at[len(copies)]))
        copies[-1].start()

    def fetch_rows(lo, hi):
        rows = pl.ds(lo, hi - lo)
        fetch(material.at[0, :, rows], labels.at[:, rows])
        for c in range(0, 6, 2):
            some = pl.ds(c, 2)
            fetch(seeds.at[0, some, :, rows], held.at[some, :, rows])

    fetch_rows(*span)
    early = len(copies)
    fetch(decay, entries.at[0])
    fetch(coupling, entries.at[1])
    fetch_rows(0, span[0])
    fetch_rows(span[1], size_x)
    rows = slice(span[0] + skip, span[1] - skip)
    for copy in copies[:early]:
        copy.wait()
    planes = [held[c, :, rows] for c in range(6)] + [labels[:, rows].astype(jnp.float32)]
    shared[...] = bands_packed(jnp.concatenate(planes, axis=0))
    for copy in copies[early:]:
        copy.wait()
    count = entries.shape[1]
    for k in range(2):
        for m in range(count):
            table[k * count + m : k * count + m + 1] = jnp.full((1, table.shape[1]), entries[k, m], jnp.float32)


def halo_pair_kernel(edges, inner, sub, table, seeds, material, near_edge, far_edge, near, far):
    send_halos(sub, loaded(seeds, material, table, edges), near_edge, far_edge)
    send_halos(sub, loaded(seeds, material, table, inner), near, far)


def shared_fields(table, shared):
    depth = shared.shape[0] // 7
    planes = bands_unpacked(shared[...])
    f = [planes[depth * c : depth * (c + 1)] for c in range(7)]
    return prepared(f[:3], f[3:6], f[6], table_entries(table))


def shared_halo_kernel(sub, table, shared, near, far, done):
    done[...] = jnp.zeros(done.shape, done.dtype)
    send_halos(sub, shared_fields(table, shared), near, far, bands_packed)


def weighted_planes(seeds, material, table, near, far, spans, keeps, sub, sub_size):
    planes = final_fields(loaded(seeds, material, table, spans), near, far, sub, sub_size)
    return weighted(planes, spans, keeps, *seeds.shape[2:])


def weighted(planes, spans, keeps, size_x, size_y):
    at, results = 0, []
    for (lo, hi), (start, stop) in zip(spans, keeps):
        shape = (stop - start, size_y)
        weight = ramp(row_of(shape) + start, size_x) * ramp(lane_of(shape), size_y)
        first = at + start - lo
        results.append(jnp.stack([plane[first : first + stop - start] * weight for part in planes for plane in part]))
        at += hi - lo
    return results


def edge_kernel(spans, sub, sub_size, tile, table, seeds, material, near, far, edge, corner, strip):
    size_x = seeds.shape[2]
    keeps = ((0, BAND), (size_x - BAND, size_x))
    low, high = weighted_planes(seeds, material, table, near, far, spans, keeps, sub, sub_size)
    odd = lax.rem(lax.axis_index(tile), 2) == 1
    edge[:, :BAND] = low
    edge[:, BAND:] = high
    corner[...] = y_packed(low, high)
    strip[...] = strip_packed(jnp.where(odd, high, low))


def middle_kernel(spans, sub, sub_size, tile, table, seeds, material, near, far, edge, _, mid, bands, beside):
    size_x = seeds.shape[2]
    keep = (BAND, size_x - BAND)
    odd = lax.rem(lax.axis_index(tile), 2) == 1
    beside[...] = strip_packed(jnp.where(odd, edge[:, :BAND], edge[:, BAND:]))
    planes, = weighted_planes(seeds, material, table, near, far, spans, (keep,), sub, sub_size)
    half = bands.shape[1]
    mid[...] = planes
    bands[...] = y_packed(planes[:, :half], planes[:, -half:])


def whole_kernel(spans, sub, sub_size, table, seeds, material, near, far, out):
    planes, = weighted_planes(seeds, material, table, near, far, spans, spans, sub, sub_size)
    out[...] = planes


def y_swapped(block):
    below = lane_of(block.shape) < BAND
    return jnp.where(inner_lanes(block.shape), 0.0, jnp.where(below, rolled(block, BAND), rolled(block, -BAND)))


def shared_kernel(span, size_x, sub, sub_size, table, shared, near, far, part):
    planes = final_fields(shared_fields(table, shared), near, far, sub, sub_size, bands_unpacked)
    found, = weighted(planes, (span,), (span,), size_x, part.shape[2])
    part[...] = y_swapped(found)


def corner_kernel(tile, edge, corner, summed, send):
    odd = lax.rem(lax.axis_index(tile), 2) == 1
    half = BAND // 2
    first, second = y_unpacked(corner[...])
    low = edge[:, :BAND] + first
    high = edge[:, BAND:] + second
    summed[:, :BAND] = low
    summed[:, BAND:] = high
    by, away = jnp.where(odd, low, high), jnp.where(odd, high, low)
    send[:, :half] = y_packed(by[:, :half], by[:, half:])
    send[:, half:] = y_packed(away[:, :half], away[:, half:])


def early_kernel(mid, part, out, whole, sem):
    size_x = out.shape[3]
    skip = HALO // 2
    count = part.shape[1] - 2 * skip
    start = (size_x - count) // 2
    found = mid[:, start - BAND : start - BAND + count] + part[:, skip : skip + count]
    whole[...] = found.reshape(whole.shape)
    copy = pltpu.make_async_copy(whole, out.at[0, :, :, pl.ds(start, count)], sem)
    copy.start()
    copy.wait()


def last_kernel(tile, mid, bands, summed, got, strip, beside, _, out, low, high, sems):
    odd = lax.rem(lax.axis_index(tile), 2) == 1
    half, count = bands.shape[1], low.shape[2]
    quarter = BAND // 2
    depth, size_x = out.shape[2:4]
    copies = []
    for c in range(6):
        at = slice(depth * c, depth * (c + 1))
        first, second = y_unpacked(bands[at])
        low[c, :, BAND:] = mid[at, :half] + first
        high[c, :, :half] = mid[at, -half:] + second
        straight = got[at, :quarter]
        by = strip_of((straight, middle_out(straight)), beside[at])
        away = strip_of(y_unpacked(got[at, quarter:]), strip[at])
        low[c, :, :BAND] = summed[at, :BAND] + jnp.where(odd, by, away)
        high[c, :, half:] = summed[at, BAND:] + jnp.where(odd, away, by)
        for k, (rows, start) in enumerate(((low, 0), (high, size_x - count))):
            copies.append(pltpu.make_async_copy(rows.at[c], out.at[0, c, :, pl.ds(start, count)], sems.at[2 * c + k]))
            copies[-1].start()
    for copy in copies:
        copy.wait()


HBM = pl.BlockSpec(memory_space=pltpu.HBM)
VMEM = pl.BlockSpec(memory_space=pltpu.VMEM)
PARAMS = pltpu.CompilerParams(vmem_limit_bytes=32 * 1024 * 1024)


def cost(flops):
    return pl.CostEstimate(flops=flops, bytes_accessed=0, transcendentals=0)


def called(kernel, shapes, *operands, flops=0):
    outs = [jax.ShapeDtypeStruct(shape, jnp.float32) for shape in shapes]
    return pl.pallas_call(
        kernel,
        out_shape=outs,
        in_specs=[VMEM] * len(operands),
        out_specs=[VMEM] * len(outs),
        compiler_params=PARAMS,
        cost_estimate=cost(flops),
    )(*operands)


def after(first, *values):
    return lax.optimization_barrier((first, *values))


def near_exchange(near, sub_size):
    return lax.ppermute(near, "sub", [(i, i ^ 1) for i in range(sub_size)])


def far_exchange(far, sub_size, tile_size):
    pairs = []
    for t in range(tile_size):
        for i in range(sub_size):
            j = ((i + 1) ^ 1) - 1
            other = (t, j) if 0 <= j < sub_size else (t ^ 1, i)
            pairs.append((t * sub_size + i, other[0] * sub_size + other[1]))
    return lax.ppermute(far, ("tile", "sub"), pairs)


def swapped(value, bits, tile_size):
    return lax.ppermute(value, "tile", [(t, t ^ bits) for t in range(tile_size)])


def from_behind(value, steps, count):
    return lax.ppermute(value, "tile", [(t, (t + steps) % count) for t in range(count)])


def table_rows(decay, coupling, size_y):
    entries = jnp.concatenate([decay, coupling])
    return jnp.broadcast_to(entries[:, None], (entries.shape[0], size_y))


def two_by_two(seeds, material, decay, coupling, sub_size, tile_size):
    depth, size_x, size_y = seeds.shape[2:]
    planes = 6 * depth
    edges = ((0, BAND + HALO), (size_x - BAND - HALO, size_x))
    inner = ((BAND - HALO, size_x - BAND + HALO),)
    keep = ((size_x - SHARED) // 2, (size_x + SHARED) // 2)
    span = (keep[0] - HALO // 2, keep[1] + HALO // 2)
    fetched = (keep[0] - HALO, keep[1] + HALO)
    rows = size_x - 2 * BAND
    edge_rows, inner_rows = 2 * (BAND + HALO), rows + 2 * HALO
    packed_rows = (SHARED + HALO) // 2 + 4
    whole = jax.ShapeDtypeStruct(seeds.shape, jnp.float32)

    shared, seeds, material, table = pl.pallas_call(
        functools.partial(first_kernel, fetched, HALO // 2),
        out_shape=[
            jax.ShapeDtypeStruct((7 * depth, packed_rows, size_y), jnp.float32),
            jax.ShapeDtypeStruct(seeds.shape[1:], jnp.float32),
            jax.ShapeDtypeStruct(material.shape[1:], jnp.int32),
            jax.ShapeDtypeStruct((2 * decay.shape[0], size_y), jnp.float32),
        ],
        in_specs=[HBM] * 4,
        out_specs=[VMEM] * 4,
        scratch_shapes=[pltpu.SMEM((2, *decay.shape), jnp.float32), pltpu.SemaphoreType.DMA((14,))],
        compiler_params=PARAMS,
        cost_estimate=cost(0),
    )(*(pltpu.with_memory_space_constraint(x, pltpu.HBM) for x in (decay, coupling, seeds, material)))
    shared = swapped(shared, 2, tile_size)
    edge_near, edge_far, inner_near, inner_far = called(
        functools.partial(halo_pair_kernel, edges, inner, "sub"),
        [(PLANES, edge_rows, size_y)] * 2 + [(PLANES, inner_rows, size_y)] * 2, table, seeds, material,
    )
    edge_near, inner_near = near_exchange(edge_near, sub_size), near_exchange(inner_near, sub_size)
    edge_far = far_exchange(edge_far, sub_size, tile_size)
    inner_far = far_exchange(inner_far, sub_size, tile_size)

    edge, corner, strip = called(
        functools.partial(edge_kernel, edges, "sub", sub_size, "tile"),
        [(planes, 2 * BAND, size_y), (planes, BAND, size_y), (planes, BAND // 2, size_y)],
        table, seeds, material, edge_near, edge_far,
    )
    corner = swapped(corner, 2, tile_size)
    strip = swapped(strip, 3, tile_size)

    shape = (PLANES, packed_rows, size_y)
    shared_near, shared_far, done = called(
        functools.partial(shared_halo_kernel, "sub"), [shape, shape, (8, size_y)], table, shared, flops=LARGE
    )
    shared_near = near_exchange(shared_near, sub_size)
    shared_far = far_exchange(shared_far, sub_size, tile_size)

    mid, bands, beside = called(
        functools.partial(middle_kernel, inner, "sub", sub_size, "tile"),
        [(planes, rows, size_y), (planes, (rows - SHARED) // 2, size_y), (planes, BAND // 2, size_y)],
        table, seeds, material, inner_near, inner_far, edge, done,
    )
    bands = swapped(bands, 2, tile_size)
    beside = swapped(beside, 1, tile_size)

    corner, strip, mid = after(corner, strip, mid)
    summed, send = called(
        functools.partial(corner_kernel, "tile"), [(planes, 2 * BAND, size_y), (planes, BAND, size_y)],
        edge, corner, flops=SMALL,
    )
    got = swapped(send, 1, tile_size)
    beside, shared_near = after(beside, shared_near)
    part, = called(
        functools.partial(shared_kernel, span, size_x, "sub", sub_size),
        [(planes, SHARED + HALO, size_y)], table, shared, shared_near, shared_far, flops=MEDIUM,
    )
    early = pl.pallas_call(
        early_kernel,
        out_shape=whole,
        in_specs=[VMEM] * 2,
        out_specs=HBM,
        scratch_shapes=[pltpu.VMEM((6, depth, SHARED, size_y), jnp.float32), pltpu.SemaphoreType.DMA],
        compiler_params=PARAMS,
        cost_estimate=cost(0),
    )(mid, part)
    return pl.pallas_call(
        functools.partial(last_kernel, "tile"),
        out_shape=whole,
        in_specs=[VMEM] * 6 + [HBM],
        out_specs=HBM,
        scratch_shapes=[pltpu.VMEM((6, depth, (size_x - SHARED) // 2, size_y), jnp.float32)] * 2
        + [pltpu.SemaphoreType.DMA((12,))],
        input_output_aliases={6: 0},
        compiler_params=PARAMS,
        cost_estimate=cost(0),
    )(mid, bands, summed, got, strip, beside, early)


def any_lattice(seeds, material, decay, coupling, sub_size, tile_size):
    depth, size_x, size_y = seeds.shape[2:]
    seeds, material = seeds[0], material[0]
    spans = ((0, size_x),)
    table = table_rows(decay, coupling, size_y)
    shape = (PLANES, size_x, size_y)
    near, far = called(functools.partial(halo_kernel, spans, "sub"), [shape, shape], table, seeds, material)
    near = near_exchange(near, sub_size)
    far = far_exchange(far, sub_size, tile_size)
    weighted, = called(
        functools.partial(whole_kernel, spans, "sub", sub_size), [(6 * depth, size_x, size_y)],
        table, seeds, material, near, far,
    )
    weighted = weighted.reshape(6, depth, size_x, size_y)
    side = math.isqrt(tile_size)
    prev_band = from_behind(weighted[:, :, size_x - BAND :, :], 1, tile_size)
    next_band = from_behind(weighted[:, :, :BAND, :], -1, tile_size)
    combined = weighted.at[:, :, :BAND, :].add(prev_band)
    combined = combined.at[:, :, size_x - BAND :, :].add(next_band)
    flat = (6, depth, size_x * BAND // size_y, size_y)
    thin = (6, depth, size_x, BAND)
    top_slab = combined[..., size_y - BAND :].reshape(flat)
    bottom_slab = combined[..., :BAND].reshape(flat)
    result = combined.at[..., :BAND].add(from_behind(top_slab, side, tile_size).reshape(thin))
    result = result.at[..., size_y - BAND :].add(from_behind(bottom_slab, -side, tile_size).reshape(thin))
    return result[None]


def solution(mesh):
    sub_size, tile_size = mesh.shape["sub"], mesh.shape["tile"]
    body = two_by_two if tile_size == 4 else any_lattice

    def on_device(seeds, material, decay, coupling):
        return body(seeds, material, decay, coupling, sub_size, tile_size)

    placed = (P("tile", None, "sub", None, None), P("tile", "sub", None, None), P(), P())
    return jax.shard_map(
        on_device,
        mesh=mesh,
        in_specs=placed,
        out_specs=P("tile", None, "sub", None, None),
        check_vma=False,
    )
```

```python
import functools
import math

import jax
import jax.numpy as jnp
from jax import lax
from jax.experimental import pallas as pl
from jax.experimental.pallas import tpu as pltpu
from jax.sharding import PartitionSpec as P

BAND = 32
HALO = 8
PLANES = 5
REACH = 2
SHARED = 80
LARGE, MEDIUM, SMALL = 10**10, 25 * 10**8, 0

magnetic_coeff = 0.5


def lane_of(shape):
    return lax.broadcasted_iota(jnp.int32, shape, len(shape) - 1)


def row_of(shape):
    return lax.broadcasted_iota(jnp.int32, shape, len(shape) - 2)


def rolled(v, shift):
    return pltpu.roll(v, shift % v.shape[-1], v.ndim - 1)


def next_x(v):
    rows = v.shape[0]
    return jnp.where(row_of(v.shape) == rows - 1, 0.0, pltpu.roll(v, rows - 1, 0))


def prev_x(v):
    return jnp.where(row_of(v.shape) == 0, 0.0, pltpu.roll(v, 1, 0))


def next_y(v):
    lanes = v.shape[1]
    return jnp.where(lane_of(v.shape) == lanes - 1, 0.0, pltpu.roll(v, lanes - 1, 1))


def prev_y(v):
    return jnp.where(lane_of(v.shape) == 0, 0.0, pltpu.roll(v, 1, 1))


def plus_x(v):
    return next_x(v) - v


def plus_y(v):
    return next_y(v) - v


def minus_x(v):
    return v - prev_x(v)


def minus_y(v):
    return v - prev_y(v)


def looked_up(labels, entries):
    value = jnp.broadcast_to(entries[0], labels.shape)
    for m in range(1, len(entries)):
        value = jnp.where(labels == m, entries[m], value)
    return value


def update_h(h, v, v_after):
    depth = len(v[0])
    new = [[], [], []]
    for p in range(depth):
        vx, vy, vz = v[0][p], v[1][p], v[2][p]
        up_x, up_y = (v[0][p + 1], v[1][p + 1]) if p + 1 < depth else v_after
        dz_x = up_x - vx if up_x is not None else -vx
        dz_y = up_y - vy if up_y is not None else -vy
        new[0].append(h[0][p] + (plus_y(vz) - dz_y))
        new[1].append(h[1][p] + (dz_x - plus_x(vz)))
        new[2].append(h[2][p] + (plus_x(vy) - plus_y(vx)))
    return new


def update_e(e, ca, h, h_before):
    depth = len(h[0])
    new = [[], [], []]
    for p in range(depth):
        hx, hy, hz = h[0][p], h[1][p], h[2][p]
        low_x, low_y = (h[0][p - 1], h[1][p - 1]) if p > 0 else h_before
        dz_x = hx - low_x if low_x is not None else hx
        dz_y = hy - low_y if low_y is not None else hy
        new[0].append(ca[p] * e[0][p] - magnetic_coeff * (minus_y(hz) - dz_y))
        new[1].append(ca[p] * e[1][p] - magnetic_coeff * (dz_x - minus_x(hz)))
        new[2].append(ca[p] * e[2][p] - magnetic_coeff * (minus_x(hy) - minus_y(hx)))
    return new


def scaled(cb, e):
    return [[cb[p] * e[c][p] for p in range(len(cb))] for c in range(3)]


def joined(ref, index, spans):
    return jnp.concatenate([ref[*index, lo:hi] for lo, hi in spans], axis=0)


def prepared(e, h, labels, tables):
    ca = [looked_up(m, tables[0]) for m in labels]
    cb = [looked_up(m, tables[1]) for m in labels]
    return e, h, ca, cb


def raw(seeds, material, spans):
    depth = seeds.shape[1]
    e = [[joined(seeds, (c, p), spans) for p in range(depth)] for c in range(3)]
    h = [[joined(seeds, (3 + c, p), spans) for p in range(depth)] for c in range(3)]
    return e, h, [joined(material, (p,), spans) for p in range(depth)]


def table_entries(table):
    count = table.shape[0] // 2
    rows = [table[m : m + 1] for m in range(2 * count)]
    return rows[:count], rows[count:]


def loaded(seeds, material, table, spans):
    return prepared(*raw(seeds, material, spans), table_entries(table))


NONE = (None, None)


def send_halos(sub, fields, near, far, packed=lambda planes: planes):
    odd = lax.rem(lax.axis_index(sub), 2) == 1
    e, h, ca, cb = fields
    v1 = scaled(cb, e)
    h1 = update_h(h, v1, NONE)
    e1 = update_e(e, ca, h1, NONE)
    v2 = scaled(cb, e1)
    h2 = update_h(h1, v2, NONE)
    up = (h1[0][-1], h1[1][-1], h2[0][-1], h2[1][-1], cb[-1])
    down = (v1[0][0], v1[1][0], v2[0][0], v2[1][0], cb[0])
    up, down = packed(jnp.stack(up)), packed(jnp.stack(down))
    near[...] = jnp.where(odd, down, up)
    far[...] = jnp.where(odd, up, down)


def halo_kernel(spans, sub, table, seeds, material, near, far):
    send_halos(sub, loaded(seeds, material, table, spans), near, far)


def ramp(position, count):
    position = position.astype(jnp.float32) + 0.5
    return jnp.where(
        position < BAND,
        position / BAND,
        jnp.where(position > count - BAND, (count - position) / BAND, 1.0),
    )


def final_fields(fields, near, far, sub, sub_size, unpacked=lambda planes: planes):
    e, h, ca, cb = fields
    index = lax.axis_index(sub)
    odd = lax.rem(index, 2) == 1
    below, above = index > 0, index < sub_size - 1
    a, b = near[...], far[...]
    from_below = unpacked(jnp.where(odd, a, b))
    from_above = unpacked(jnp.where(above, jnp.where(odd, b, a), 0.0))
    part_h1x, part_h1y, part_h2x, part_h2y, cb_low = from_below
    v1x_up, v1y_up, part_v2x, part_v2y, cb_up = from_above

    v1 = scaled(cb, e)
    h1 = update_h(h, v1, (v1x_up, v1y_up))
    dh1x, dh1y = -v1[1][0], v1[0][0]
    h1_low = (jnp.where(below, part_h1x + dh1x, 0.0), jnp.where(below, part_h1y + dh1y, 0.0))
    e1 = update_e(e, ca, h1, h1_low)
    v2 = scaled(cb, e1)
    v2_up = (
        part_v2x - cb_up * (magnetic_coeff * h1[1][-1]),
        part_v2y + cb_up * (magnetic_coeff * h1[0][-1]),
    )
    h2 = update_h(h1, v2, v2_up)
    dv2x = cb_low * (magnetic_coeff * dh1y)
    dv2y = cb_low * (-magnetic_coeff * dh1x)
    dv2z = cb_low * (-magnetic_coeff * (minus_x(dh1y) - minus_y(dh1x)))
    h2x_low = part_h2x + (dh1x + (plus_y(dv2z) - (v2[1][0] - dv2y)))
    h2y_low = part_h2y + (dh1y + ((v2[0][0] - dv2x) - plus_x(dv2z)))
    h2_low = (jnp.where(below, h2x_low, 0.0), jnp.where(below, h2y_low, 0.0))
    e2 = update_e(e1, ca, h2, h2_low)
    return e2 + h2


def middle_out(block):
    return rolled(block, block.shape[-1] // 2)


def y_packed(first, second):
    lane = lane_of(first.shape)
    middle = (lane >= BAND) & (lane < first.shape[-1] - BAND)
    return jnp.where(middle, middle_out(second), first)


def inner_lanes(shape):
    lane = lane_of(shape)
    return (lane >= BAND) & (lane < shape[-1] - BAND)


def y_unpacked(block):
    a, b = rolled(block, BAND), rolled(block, -BAND)
    middle = inner_lanes(block.shape)
    below = lane_of(block.shape) < BAND
    first = jnp.where(middle, 0.0, jnp.where(below, a, b))
    second = jnp.where(middle, 0.0, jnp.where(below, b, a))
    return first, second


def strip_packed(strip):
    half = strip.shape[1] // 2
    first, second = strip[:, :half], strip[:, half:]
    return jnp.where(inner_lanes(first.shape), second, middle_out(first))


def strip_of(corners, block):
    middle = inner_lanes(block.shape)
    first = jnp.where(middle, middle_out(block), corners[0])
    second = jnp.where(middle, block, corners[1])
    return jnp.concatenate([first, second], axis=1)


def low_rows(shape):
    return row_of(shape) < 4


def bands_packed(block):
    rows, lanes = block.shape[1:]
    count, width, high = rows // 2 + 4, REACH * (rows // 8), lanes - BAND
    shape = (block.shape[0], 8, lanes)
    lane = lane_of(shape)
    low = low_rows(shape)
    side = jnp.zeros(shape, block.dtype)
    for g in range(rows // 8):
        at = BAND + REACH * (g + 1)
        piece = rolled(block[:, 8 * g : 8 * g + 8], REACH * (g + 1))
        here = ((lane >= at) & (lane < at + REACH)) | (
            (lane >= at + high - BAND - REACH) & (lane < at + high - BAND)
        )
        side = jnp.where(here, piece, side)
    other = rolled(pltpu.roll(side, 4, 1), width + REACH)
    own = ((lane >= BAND) & (lane < BAND + REACH + width)) | ((lane >= high) & (lane < high + width))
    side = jnp.where(own, side, other)
    middle = (lane >= BAND) & (lane < high)
    packed = y_packed(block[:, :count], block[:, rows - count :])
    first = jnp.where(low & middle, side, packed[:, :8])
    last = jnp.where(low | middle, packed[:, count - 8 :], side)
    return jnp.concatenate([first, packed[:, 8 : count - 8], last], axis=1)


def bands_unpacked(packed):
    count, lanes = packed.shape[1:]
    rows = 2 * count - 8
    width, high = REACH * (rows // 8), lanes - BAND
    first, last = packed[:, :8], packed[:, count - 8 :]
    low = low_rows(first.shape)
    lane = lane_of(first.shape)
    middle = (lane >= BAND) & (lane < high)
    side = jnp.where(low, first, last)
    other = rolled(pltpu.roll(side, 4, 1), -width - REACH)
    side = jnp.where(low == middle, side, other)
    beside = ((lane >= BAND) & (lane < BAND + REACH)) | ((lane >= high - REACH) & (lane < high))
    moved = [rolled(packed[:, at : at + 8], lanes // 2) for at in range(0, count, 8)]
    pieces = [packed[:, at : at + 8] for at in range(0, count - 8, 8)]
    pieces += [jnp.where(low, last, moved[0])] + moved[1:]
    result = []
    for g, piece in enumerate(pieces):
        result.append(jnp.where(middle, jnp.where(beside, rolled(side, -REACH * (g + 1)), 0.0), piece))
    return jnp.concatenate(result, axis=1)


def first_kernel(span, skip, decay, coupling, seeds, material, shared, held, labels, table, entries, sems):
    size_x = held.shape[2]
    copies = []

    def fetch(source, target):
        copies.append(pltpu.make_async_copy(source, target, sems.at[len(copies)]))
        copies[-1].start()

    def fetch_rows(lo, hi):
        rows = pl.ds(lo, hi - lo)
        fetch(material.at[0, :, rows], labels.at[:, rows])
        for c in range(0, 6, 2):
            some = pl.ds(c, 2)
            fetch(seeds.at[0, some, :, rows], held.at[some, :, rows])

    fetch_rows(*span)
    early = len(copies)
    fetch(decay, entries.at[0])
    fetch(coupling, entries.at[1])
    fetch_rows(0, span[0])
    fetch_rows(span[1], size_x)
    rows = slice(span[0] + skip, span[1] - skip)
    for copy in copies[:early]:
        copy.wait()
    planes = [held[c, :, rows] for c in range(6)] + [labels[:, rows].astype(jnp.float32)]
    shared[...] = bands_packed(jnp.concatenate(planes, axis=0))
    for copy in copies[early:]:
        copy.wait()
    count = entries.shape[1]
    for k in range(2):
        for m in range(count):
            table[k * count + m : k * count + m + 1] = jnp.full((1, table.shape[1]), entries[k, m], jnp.float32)


def halo_pair_kernel(edges, inner, sub, table, seeds, material, near_edge, far_edge, near, far):
    send_halos(sub, loaded(seeds, material, table, edges), near_edge, far_edge)
    send_halos(sub, loaded(seeds, material, table, inner), near, far)


def shared_fields(table, shared):
    depth = shared.shape[0] // 7
    planes = bands_unpacked(shared[...])
    f = [planes[depth * c : depth * (c + 1)] for c in range(7)]
    return prepared(f[:3], f[3:6], f[6], table_entries(table))


def shared_halo_kernel(sub, table, shared, near, far, done):
    done[...] = jnp.zeros(done.shape, done.dtype)
    send_halos(sub, shared_fields(table, shared), near, far, bands_packed)


def weighted_planes(seeds, material, table, near, far, spans, keeps, sub, sub_size):
    planes = final_fields(loaded(seeds, material, table, spans), near, far, sub, sub_size)
    return weighted(planes, spans, keeps, *seeds.shape[2:])


def weighted(planes, spans, keeps, size_x, size_y):
    at, results = 0, []
    for (lo, hi), (start, stop) in zip(spans, keeps):
        shape = (stop - start, size_y)
        weight = ramp(row_of(shape) + start, size_x) * ramp(lane_of(shape), size_y)
        first = at + start - lo
        results.append(jnp.stack([plane[first : first + stop - start] * weight for part in planes for plane in part]))
        at += hi - lo
    return results


def edge_kernel(spans, sub, sub_size, tile, table, seeds, material, near, far, edge, corner, strip):
    size_x = seeds.shape[2]
    keeps = ((0, BAND), (size_x - BAND, size_x))
    low, high = weighted_planes(seeds, material, table, near, far, spans, keeps, sub, sub_size)
    odd = lax.rem(lax.axis_index(tile), 2) == 1
    edge[:, :BAND] = low
    edge[:, BAND:] = high
    corner[...] = y_packed(low, high)
    strip[...] = strip_packed(jnp.where(odd, high, low))


def middle_kernel(spans, sub, sub_size, tile, table, seeds, material, near, far, edge, _, mid, bands, beside):
    size_x = seeds.shape[2]
    keep = (BAND, size_x - BAND)
    odd = lax.rem(lax.axis_index(tile), 2) == 1
    beside[...] = strip_packed(jnp.where(odd, edge[:, :BAND], edge[:, BAND:]))
    planes, = weighted_planes(seeds, material, table, near, far, spans, (keep,), sub, sub_size)
    half = bands.shape[1]
    mid[...] = planes
    bands[...] = y_packed(planes[:, :half], planes[:, -half:])


def whole_kernel(spans, sub, sub_size, table, seeds, material, near, far, out):
    planes, = weighted_planes(seeds, material, table, near, far, spans, spans, sub, sub_size)
    out[...] = planes


def y_swapped(block):
    below = lane_of(block.shape) < BAND
    return jnp.where(inner_lanes(block.shape), 0.0, jnp.where(below, rolled(block, BAND), rolled(block, -BAND)))


def shared_kernel(span, size_x, sub, sub_size, table, shared, near, far, part):
    planes = final_fields(shared_fields(table, shared), near, far, sub, sub_size, bands_unpacked)
    found, = weighted(planes, (span,), (span,), size_x, part.shape[2])
    part[...] = y_swapped(found)


def corner_kernel(tile, edge, corner, summed, send):
    odd = lax.rem(lax.axis_index(tile), 2) == 1
    half = BAND // 2
    first, second = y_unpacked(corner[...])
    low = edge[:, :BAND] + first
    high = edge[:, BAND:] + second
    summed[:, :BAND] = low
    summed[:, BAND:] = high
    by, away = jnp.where(odd, low, high), jnp.where(odd, high, low)
    send[:, :half] = y_packed(by[:, :half], by[:, half:])
    send[:, half:] = y_packed(away[:, :half], away[:, half:])


def early_kernel(mid, part, out, whole, sem):
    size_x = out.shape[3]
    skip = HALO // 2
    count = part.shape[1] - 2 * skip
    start = (size_x - count) // 2
    found = mid[:, start - BAND : start - BAND + count] + part[:, skip : skip + count]
    whole[...] = found.reshape(whole.shape)
    copy = pltpu.make_async_copy(whole, out.at[0, :, :, pl.ds(start, count)], sem)
    copy.start()
    copy.wait()


def last_kernel(tile, mid, bands, summed, got, strip, beside, _, out, low, high, sems):
    odd = lax.rem(lax.axis_index(tile), 2) == 1
    half, count = bands.shape[1], low.shape[2]
    quarter = BAND // 2
    depth, size_x = out.shape[2:4]
    copies = []
    for c in range(6):
        at = slice(depth * c, depth * (c + 1))
        first, second = y_unpacked(bands[at])
        low[c, :, BAND:] = mid[at, :half] + first
        high[c, :, :half] = mid[at, -half:] + second
        straight = got[at, :quarter]
        by = strip_of((straight, middle_out(straight)), beside[at])
        away = strip_of(y_unpacked(got[at, quarter:]), strip[at])
        low[c, :, :BAND] = summed[at, :BAND] + jnp.where(odd, by, away)
        high[c, :, half:] = summed[at, BAND:] + jnp.where(odd, away, by)
        for k, (rows, start) in enumerate(((low, 0), (high, size_x - count))):
            copies.append(pltpu.make_async_copy(rows.at[c], out.at[0, c, :, pl.ds(start, count)], sems.at[2 * c + k]))
            copies[-1].start()
    for copy in copies:
        copy.wait()


HBM = pl.BlockSpec(memory_space=pltpu.HBM)
VMEM = pl.BlockSpec(memory_space=pltpu.VMEM)
PARAMS = pltpu.CompilerParams(vmem_limit_bytes=32 * 1024 * 1024)


def cost(flops):
    return pl.CostEstimate(flops=flops, bytes_accessed=0, transcendentals=0)


def called(kernel, shapes, *operands, flops=0):
    outs = [jax.ShapeDtypeStruct(shape, jnp.float32) for shape in shapes]
    return pl.pallas_call(
        kernel,
        out_shape=outs,
        in_specs=[VMEM] * len(operands),
        out_specs=[VMEM] * len(outs),
        compiler_params=PARAMS,
        cost_estimate=cost(flops),
    )(*operands)


def after(first, *values):
    return lax.optimization_barrier((first, *values))


def near_exchange(near, sub_size):
    return lax.ppermute(near, "sub", [(i, i ^ 1) for i in range(sub_size)])


def far_exchange(far, sub_size, tile_size):
    pairs = []
    for t in range(tile_size):
        for i in range(sub_size):
            j = ((i + 1) ^ 1) - 1
            other = (t, j) if 0 <= j < sub_size else (t ^ 1, i)
            pairs.append((t * sub_size + i, other[0] * sub_size + other[1]))
    return lax.ppermute(far, ("tile", "sub"), pairs)


def swapped(value, bits, tile_size):
    return lax.ppermute(value, "tile", [(t, t ^ bits) for t in range(tile_size)])


def from_behind(value, steps, count):
    return lax.ppermute(value, "tile", [(t, (t + steps) % count) for t in range(count)])


def table_rows(decay, coupling, size_y):
    entries = jnp.concatenate([decay, coupling])
    return jnp.broadcast_to(entries[:, None], (entries.shape[0], size_y))


def two_by_two(seeds, material, decay, coupling, sub_size, tile_size):
    depth, size_x, size_y = seeds.shape[2:]
    planes = 6 * depth
    edges = ((0, BAND + HALO), (size_x - BAND - HALO, size_x))
    inner = ((BAND - HALO, size_x - BAND + HALO),)
    keep = ((size_x - SHARED) // 2, (size_x + SHARED) // 2)
    span = (keep[0] - HALO // 2, keep[1] + HALO // 2)
    fetched = (keep[0] - HALO, keep[1] + HALO)
    rows = size_x - 2 * BAND
    edge_rows, inner_rows = 2 * (BAND + HALO), rows + 2 * HALO
    packed_rows = (SHARED + HALO) // 2 + 4
    whole = jax.ShapeDtypeStruct(seeds.shape, jnp.float32)

    shared, seeds, material, table = pl.pallas_call(
        functools.partial(first_kernel, fetched, HALO // 2),
        out_shape=[
            jax.ShapeDtypeStruct((7 * depth, packed_rows, size_y), jnp.float32),
            jax.ShapeDtypeStruct(seeds.shape[1:], jnp.float32),
            jax.ShapeDtypeStruct(material.shape[1:], jnp.int32),
            jax.ShapeDtypeStruct((2 * decay.shape[0], size_y), jnp.float32),
        ],
        in_specs=[HBM] * 4,
        out_specs=[VMEM] * 4,
        scratch_shapes=[pltpu.SMEM((2, *decay.shape), jnp.float32), pltpu.SemaphoreType.DMA((14,))],
        compiler_params=PARAMS,
        cost_estimate=cost(0),
    )(*(pltpu.with_memory_space_constraint(x, pltpu.HBM) for x in (decay, coupling, seeds, material)))
    shared = swapped(shared, 2, tile_size)
    edge_near, edge_far, inner_near, inner_far = called(
        functools.partial(halo_pair_kernel, edges, inner, "sub"),
        [(PLANES, edge_rows, size_y)] * 2 + [(PLANES, inner_rows, size_y)] * 2, table, seeds, material,
    )
    edge_near, inner_near = near_exchange(edge_near, sub_size), near_exchange(inner_near, sub_size)
    edge_far = far_exchange(edge_far, sub_size, tile_size)
    inner_far = far_exchange(inner_far, sub_size, tile_size)

    edge, corner, strip = called(
        functools.partial(edge_kernel, edges, "sub", sub_size, "tile"),
        [(planes, 2 * BAND, size_y), (planes, BAND, size_y), (planes, BAND // 2, size_y)],
        table, seeds, material, edge_near, edge_far,
    )
    corner = swapped(corner, 2, tile_size)
    strip = swapped(strip, 3, tile_size)

    shape = (PLANES, packed_rows, size_y)
    shared_near, shared_far, done = called(
        functools.partial(shared_halo_kernel, "sub"), [shape, shape, (8, size_y)], table, shared, flops=LARGE
    )
    shared_near = near_exchange(shared_near, sub_size)
    shared_far = far_exchange(shared_far, sub_size, tile_size)

    mid, bands, beside = called(
        functools.partial(middle_kernel, inner, "sub", sub_size, "tile"),
        [(planes, rows, size_y), (planes, (rows - SHARED) // 2, size_y), (planes, BAND // 2, size_y)],
        table, seeds, material, inner_near, inner_far, edge, done,
    )
    bands = swapped(bands, 2, tile_size)
    beside = swapped(beside, 1, tile_size)

    corner, strip, mid = after(corner, strip, mid)
    summed, send = called(
        functools.partial(corner_kernel, "tile"), [(planes, 2 * BAND, size_y), (planes, BAND, size_y)],
        edge, corner, flops=SMALL,
    )
    got = swapped(send, 1, tile_size)
    beside, shared_near = after(beside, shared_near)
    part, = called(
        functools.partial(shared_kernel, span, size_x, "sub", sub_size),
        [(planes, SHARED + HALO, size_y)], table, shared, shared_near, shared_far, flops=MEDIUM,
    )
    early = pl.pallas_call(
        early_kernel,
        out_shape=whole,
        in_specs=[VMEM] * 2,
        out_specs=HBM,
        scratch_shapes=[pltpu.VMEM((6, depth, SHARED, size_y), jnp.float32), pltpu.SemaphoreType.DMA],
        compiler_params=PARAMS,
        cost_estimate=cost(0),
    )(mid, part)
    return pl.pallas_call(
        functools.partial(last_kernel, "tile"),
        out_shape=whole,
        in_specs=[VMEM] * 6 + [HBM],
        out_specs=HBM,
        scratch_shapes=[pltpu.VMEM((6, depth, (size_x - SHARED) // 2, size_y), jnp.float32)] * 2
        + [pltpu.SemaphoreType.DMA((12,))],
        input_output_aliases={6: 0},
        compiler_params=PARAMS,
        cost_estimate=cost(0),
    )(mid, bands, summed, got, strip, beside, early)


def any_lattice(seeds, material, decay, coupling, sub_size, tile_size):
    depth, size_x, size_y = seeds.shape[2:]
    seeds, material = seeds[0], material[0]
    spans = ((0, size_x),)
    table = table_rows(decay, coupling, size_y)
    shape = (PLANES, size_x, size_y)
    near, far = called(functools.partial(halo_kernel, spans, "sub"), [shape, shape], table, seeds, material)
    near = near_exchange(near, sub_size)
    far = far_exchange(far, sub_size, tile_size)
    weighted, = called(
        functools.partial(whole_kernel, spans, "sub", sub_size), [(6 * depth, size_x, size_y)],
        table, seeds, material, near, far,
    )
    weighted = weighted.reshape(6, depth, size_x, size_y)
    side = math.isqrt(tile_size)
    prev_band = from_behind(weighted[:, :, size_x - BAND :, :], 1, tile_size)
    next_band = from_behind(weighted[:, :, :BAND, :], -1, tile_size)
    combined = weighted.at[:, :, :BAND, :].add(prev_band)
    combined = combined.at[:, :, size_x - BAND :, :].add(next_band)
    flat = (6, depth, size_x * BAND // size_y, size_y)
    thin = (6, depth, size_x, BAND)
    top_slab = combined[..., size_y - BAND :].reshape(flat)
    bottom_slab = combined[..., :BAND].reshape(flat)
    result = combined.at[..., :BAND].add(from_behind(top_slab, side, tile_size).reshape(thin))
    result = result.at[..., size_y - BAND :].add(from_behind(bottom_slab, -side, tile_size).reshape(thin))
    return result[None]


def solution(mesh):
    sub_size, tile_size = mesh.shape["sub"], mesh.shape["tile"]
    body = two_by_two if tile_size == 4 else any_lattice

    def on_device(seeds, material, decay, coupling):
        return body(seeds, material, decay, coupling, sub_size, tile_size)

    placed = (P("tile", None, "sub", None, None), P("tile", "sub", None, None), P(), P())
    return jax.shard_map(
        on_device,
        mesh=mesh,
        in_specs=placed,
        out_specs=P("tile", None, "sub", None, None),
        check_vma=False,
    )
```

```python
import functools
import math

import jax
import jax.numpy as jnp
from jax import lax
from jax.experimental import pallas as pl
from jax.experimental.pallas import tpu as pltpu
from jax.sharding import PartitionSpec as P

BAND = 32
HALO = 8
PLANES = 5
REACH = 2
SHARED = 96
LARGE, MEDIUM, SMALL = 10**10, 2 * 10**9, 0

magnetic_coeff = 0.5


def lane_of(shape):
    return lax.broadcasted_iota(jnp.int32, shape, len(shape) - 1)


def row_of(shape):
    return lax.broadcasted_iota(jnp.int32, shape, len(shape) - 2)


def rolled(v, shift):
    return pltpu.roll(v, shift % v.shape[-1], v.ndim - 1)


def next_x(v):
    rows = v.shape[0]
    return jnp.where(row_of(v.shape) == rows - 1, 0.0, pltpu.roll(v, rows - 1, 0))


def prev_x(v):
    return jnp.where(row_of(v.shape) == 0, 0.0, pltpu.roll(v, 1, 0))


def next_y(v):
    lanes = v.shape[1]
    return jnp.where(lane_of(v.shape) == lanes - 1, 0.0, pltpu.roll(v, lanes - 1, 1))


def prev_y(v):
    return jnp.where(lane_of(v.shape) == 0, 0.0, pltpu.roll(v, 1, 1))


def plus_x(v):
    return next_x(v) - v


def plus_y(v):
    return next_y(v) - v


def minus_x(v):
    return v - prev_x(v)


def minus_y(v):
    return v - prev_y(v)


def looked_up(labels, entries):
    value = jnp.broadcast_to(entries[0], labels.shape)
    for m in range(1, len(entries)):
        value = jnp.where(labels == m, entries[m], value)
    return value


def update_h(h, v, v_after):
    depth = len(v[0])
    new = [[], [], []]
    for p in range(depth):
        vx, vy, vz = v[0][p], v[1][p], v[2][p]
        up_x, up_y = (v[0][p + 1], v[1][p + 1]) if p + 1 < depth else v_after
        dz_x = up_x - vx if up_x is not None else -vx
        dz_y = up_y - vy if up_y is not None else -vy
        new[0].append(h[0][p] + (plus_y(vz) - dz_y))
        new[1].append(h[1][p] + (dz_x - plus_x(vz)))
        new[2].append(h[2][p] + (plus_x(vy) - plus_y(vx)))
    return new


def update_e(e, ca, h, h_before):
    depth = len(h[0])
    new = [[], [], []]
    for p in range(depth):
        hx, hy, hz = h[0][p], h[1][p], h[2][p]
        low_x, low_y = (h[0][p - 1], h[1][p - 1]) if p > 0 else h_before
        dz_x = hx - low_x if low_x is not None else hx
        dz_y = hy - low_y if low_y is not None else hy
        new[0].append(ca[p] * e[0][p] - magnetic_coeff * (minus_y(hz) - dz_y))
        new[1].append(ca[p] * e[1][p] - magnetic_coeff * (dz_x - minus_x(hz)))
        new[2].append(ca[p] * e[2][p] - magnetic_coeff * (minus_x(hy) - minus_y(hx)))
    return new


def scaled(cb, e):
    return [[cb[p] * e[c][p] for p in range(len(cb))] for c in range(3)]


def joined(ref, index, spans):
    return jnp.concatenate([ref[*index, lo:hi] for lo, hi in spans], axis=0)


def prepared(e, h, labels, tables):
    ca = [looked_up(m, tables[0]) for m in labels]
    cb = [looked_up(m, tables[1]) for m in labels]
    return e, h, ca, cb


def raw(seeds, material, spans):
    depth = seeds.shape[1]
    e = [[joined(seeds, (c, p), spans) for p in range(depth)] for c in range(3)]
    h = [[joined(seeds, (3 + c, p), spans) for p in range(depth)] for c in range(3)]
    return e, h, [joined(material, (p,), spans) for p in range(depth)]


def table_entries(table):
    count = table.shape[0] // 2
    rows = [table[m : m + 1] for m in range(2 * count)]
    return rows[:count], rows[count:]


def loaded(seeds, material, table, spans):
    return prepared(*raw(seeds, material, spans), table_entries(table))


NONE = (None, None)


def send_halos(sub, fields, near, far, packed=lambda planes: planes):
    odd = lax.rem(lax.axis_index(sub), 2) == 1
    e, h, ca, cb = fields
    v1 = scaled(cb, e)
    h1 = update_h(h, v1, NONE)
    e1 = update_e(e, ca, h1, NONE)
    v2 = scaled(cb, e1)
    h2 = update_h(h1, v2, NONE)
    up = (h1[0][-1], h1[1][-1], h2[0][-1], h2[1][-1], cb[-1])
    down = (v1[0][0], v1[1][0], v2[0][0], v2[1][0], cb[0])
    up, down = packed(jnp.stack(up)), packed(jnp.stack(down))
    near[...] = jnp.where(odd, down, up)
    far[...] = jnp.where(odd, up, down)


def halo_kernel(spans, sub, table, seeds, material, near, far):
    send_halos(sub, loaded(seeds, material, table, spans), near, far)


def ramp(position, count):
    position = position.astype(jnp.float32) + 0.5
    return jnp.where(
        position < BAND,
        position / BAND,
        jnp.where(position > count - BAND, (count - position) / BAND, 1.0),
    )


def final_fields(fields, near, far, sub, sub_size, unpacked=lambda planes: planes):
    e, h, ca, cb = fields
    index = lax.axis_index(sub)
    odd = lax.rem(index, 2) == 1
    below, above = index > 0, index < sub_size - 1
    a, b = near[...], far[...]
    from_below = unpacked(jnp.where(odd, a, b))
    from_above = unpacked(jnp.where(above, jnp.where(odd, b, a), 0.0))
    part_h1x, part_h1y, part_h2x, part_h2y, cb_low = from_below
    v1x_up, v1y_up, part_v2x, part_v2y, cb_up = from_above

    v1 = scaled(cb, e)
    h1 = update_h(h, v1, (v1x_up, v1y_up))
    dh1x, dh1y = -v1[1][0], v1[0][0]
    h1_low = (jnp.where(below, part_h1x + dh1x, 0.0), jnp.where(below, part_h1y + dh1y, 0.0))
    e1 = update_e(e, ca, h1, h1_low)
    v2 = scaled(cb, e1)
    v2_up = (
        part_v2x - cb_up * (magnetic_coeff * h1[1][-1]),
        part_v2y + cb_up * (magnetic_coeff * h1[0][-1]),
    )
    h2 = update_h(h1, v2, v2_up)
    dv2x = cb_low * (magnetic_coeff * dh1y)
    dv2y = cb_low * (-magnetic_coeff * dh1x)
    dv2z = cb_low * (-magnetic_coeff * (minus_x(dh1y) - minus_y(dh1x)))
    h2x_low = part_h2x + (dh1x + (plus_y(dv2z) - (v2[1][0] - dv2y)))
    h2y_low = part_h2y + (dh1y + ((v2[0][0] - dv2x) - plus_x(dv2z)))
    h2_low = (jnp.where(below, h2x_low, 0.0), jnp.where(below, h2y_low, 0.0))
    e2 = update_e(e1, ca, h2, h2_low)
    return e2 + h2


def middle_out(block):
    return rolled(block, block.shape[-1] // 2)


def y_packed(first, second):
    lane = lane_of(first.shape)
    middle = (lane >= BAND) & (lane < first.shape[-1] - BAND)
    return jnp.where(middle, middle_out(second), first)


def inner_lanes(shape):
    lane = lane_of(shape)
    return (lane >= BAND) & (lane < shape[-1] - BAND)


def y_unpacked(block):
    a, b = rolled(block, BAND), rolled(block, -BAND)
    middle = inner_lanes(block.shape)
    below = lane_of(block.shape) < BAND
    first = jnp.where(middle, 0.0, jnp.where(below, a, b))
    second = jnp.where(middle, 0.0, jnp.where(below, b, a))
    return first, second


def strip_packed(strip):
    half = strip.shape[1] // 2
    first, second = strip[:, :half], strip[:, half:]
    return jnp.where(inner_lanes(first.shape), second, middle_out(first))


def strip_of(corners, block):
    middle = inner_lanes(block.shape)
    first = jnp.where(middle, middle_out(block), corners[0])
    second = jnp.where(middle, block, corners[1])
    return jnp.concatenate([first, second], axis=1)


def low_rows(shape):
    return row_of(shape) < 4


def bands_packed(block):
    rows, lanes = block.shape[1:]
    count, width, high = rows // 2 + 4, REACH * (rows // 8), lanes - BAND
    shape = (block.shape[0], 8, lanes)
    lane = lane_of(shape)
    low = low_rows(shape)
    side = jnp.zeros(shape, block.dtype)
    for g in range(rows // 8):
        at = BAND + REACH * (g + 1)
        piece = rolled(block[:, 8 * g : 8 * g + 8], REACH * (g + 1))
        here = ((lane >= at) & (lane < at + REACH)) | (
            (lane >= at + high - BAND - REACH) & (lane < at + high - BAND)
        )
        side = jnp.where(here, piece, side)
    other = rolled(pltpu.roll(side, 4, 1), width + REACH)
    own = ((lane >= BAND) & (lane < BAND + REACH + width)) | ((lane >= high) & (lane < high + width))
    side = jnp.where(own, side, other)
    middle = (lane >= BAND) & (lane < high)
    packed = y_packed(block[:, :count], block[:, rows - count :])
    first = jnp.where(low & middle, side, packed[:, :8])
    last = jnp.where(low | middle, packed[:, count - 8 :], side)
    return jnp.concatenate([first, packed[:, 8 : count - 8], last], axis=1)


def bands_unpacked(packed):
    count, lanes = packed.shape[1:]
    rows = 2 * count - 8
    width, high = REACH * (rows // 8), lanes - BAND
    first, last = packed[:, :8], packed[:, count - 8 :]
    low = low_rows(first.shape)
    lane = lane_of(first.shape)
    middle = (lane >= BAND) & (lane < high)
    side = jnp.where(low, first, last)
    other = rolled(pltpu.roll(side, 4, 1), -width - REACH)
    side = jnp.where(low == middle, side, other)
    beside = ((lane >= BAND) & (lane < BAND + REACH)) | ((lane >= high - REACH) & (lane < high))
    moved = [rolled(packed[:, at : at + 8], lanes // 2) for at in range(0, count, 8)]
    pieces = [packed[:, at : at + 8] for at in range(0, count - 8, 8)]
    pieces += [jnp.where(low, last, moved[0])] + moved[1:]
    result = []
    for g, piece in enumerate(pieces):
        result.append(jnp.where(middle, jnp.where(beside, rolled(side, -REACH * (g + 1)), 0.0), piece))
    return jnp.concatenate(result, axis=1)


def first_kernel(span, skip, decay, coupling, seeds, material, shared, held, labels, table, entries, sems):
    size_x = held.shape[2]
    copies = []

    def fetch(source, target):
        copies.append(pltpu.make_async_copy(source, target, sems.at[len(copies)]))
        copies[-1].start()

    def fetch_rows(lo, hi):
        rows = pl.ds(lo, hi - lo)
        fetch(material.at[0, :, rows], labels.at[:, rows])
        for c in range(0, 6, 2):
            some = pl.ds(c, 2)
            fetch(seeds.at[0, some, :, rows], held.at[some, :, rows])

    fetch_rows(*span)
    early = len(copies)
    fetch(decay, entries.at[0])
    fetch(coupling, entries.at[1])
    fetch_rows(0, span[0])
    fetch_rows(span[1], size_x)
    rows = slice(span[0] + skip, span[1] - skip)
    for copy in copies[:early]:
        copy.wait()
    planes = [held[c, :, rows] for c in range(6)] + [labels[:, rows].astype(jnp.float32)]
    shared[...] = bands_packed(jnp.concatenate(planes, axis=0))
    for copy in copies[early:]:
        copy.wait()
    count = entries.shape[1]
    for k in range(2):
        for m in range(count):
            table[k * count + m : k * count + m + 1] = jnp.full((1, table.shape[1]), entries[k, m], jnp.float32)


def halo_pair_kernel(edges, inner, sub, table, seeds, material, near_edge, far_edge, near, far):
    send_halos(sub, loaded(seeds, material, table, edges), near_edge, far_edge)
    send_halos(sub, loaded(seeds, material, table, inner), near, far)


def shared_fields(table, shared):
    depth = shared.shape[0] // 7
    planes = bands_unpacked(shared[...])
    f = [planes[depth * c : depth * (c + 1)] for c in range(7)]
    return prepared(f[:3], f[3:6], f[6], table_entries(table))


def shared_halo_kernel(sub, table, shared, near, far, done):
    done[...] = jnp.zeros(done.shape, done.dtype)
    send_halos(sub, shared_fields(table, shared), near, far, bands_packed)


def weighted_planes(seeds, material, table, near, far, spans, keeps, sub, sub_size):
    planes = final_fields(loaded(seeds, material, table, spans), near, far, sub, sub_size)
    return weighted(planes, spans, keeps, *seeds.shape[2:])


def weighted(planes, spans, keeps, size_x, size_y):
    at, results = 0, []
    for (lo, hi), (start, stop) in zip(spans, keeps):
        shape = (stop - start, size_y)
        weight = ramp(row_of(shape) + start, size_x) * ramp(lane_of(shape), size_y)
        first = at + start - lo
        results.append(jnp.stack([plane[first : first + stop - start] * weight for part in planes for plane in part]))
        at += hi - lo
    return results


def edge_kernel(spans, sub, sub_size, tile, table, seeds, material, near, far, edge, corner, strip):
    size_x = seeds.shape[2]
    keeps = ((0, BAND), (size_x - BAND, size_x))
    low, high = weighted_planes(seeds, material, table, near, far, spans, keeps, sub, sub_size)
    odd = lax.rem(lax.axis_index(tile), 2) == 1
    edge[:, :BAND] = low
    edge[:, BAND:] = high
    corner[...] = y_packed(low, high)
    strip[...] = strip_packed(jnp.where(odd, high, low))


def middle_kernel(spans, sub, sub_size, tile, table, seeds, material, near, far, edge, _, mid, bands, beside):
    size_x = seeds.shape[2]
    keep = (BAND, size_x - BAND)
    odd = lax.rem(lax.axis_index(tile), 2) == 1
    beside[...] = strip_packed(jnp.where(odd, edge[:, :BAND], edge[:, BAND:]))
    planes, = weighted_planes(seeds, material, table, near, far, spans, (keep,), sub, sub_size)
    half = bands.shape[1]
    mid[...] = planes
    bands[...] = y_packed(planes[:, :half], planes[:, -half:])


def whole_kernel(spans, sub, sub_size, table, seeds, material, near, far, out):
    planes, = weighted_planes(seeds, material, table, near, far, spans, spans, sub, sub_size)
    out[...] = planes


def y_swapped(block):
    below = lane_of(block.shape) < BAND
    return jnp.where(inner_lanes(block.shape), 0.0, jnp.where(below, rolled(block, BAND), rolled(block, -BAND)))


def shared_kernel(span, size_x, sub, sub_size, table, shared, near, far, part):
    planes = final_fields(shared_fields(table, shared), near, far, sub, sub_size, bands_unpacked)
    found, = weighted(planes, (span,), (span,), size_x, part.shape[2])
    part[...] = y_swapped(found)


def corner_kernel(tile, edge, corner, summed, send):
    odd = lax.rem(lax.axis_index(tile), 2) == 1
    half = BAND // 2
    first, second = y_unpacked(corner[...])
    low = edge[:, :BAND] + first
    high = edge[:, BAND:] + second
    summed[:, :BAND] = low
    summed[:, BAND:] = high
    by, away = jnp.where(odd, low, high), jnp.where(odd, high, low)
    send[:, :half] = y_packed(by[:, :half], by[:, half:])
    send[:, half:] = y_packed(away[:, :half], away[:, half:])


def early_kernel(mid, part, out, whole, sem):
    size_x = out.shape[3]
    skip = HALO // 2
    count = part.shape[1] - 2 * skip
    start = (size_x - count) // 2
    found = mid[:, start - BAND : start - BAND + count] + part[:, skip : skip + count]
    whole[...] = found.reshape(whole.shape)
    copy = pltpu.make_async_copy(whole, out.at[0, :, :, pl.ds(start, count)], sem)
    copy.start()
    copy.wait()


def late_kernel(tile, mid, bands, summed, strip, beside, low, high):
    odd = lax.rem(lax.axis_index(tile), 2) == 1
    half = bands.shape[1]
    first, second = y_unpacked(bands[...])
    low[:, BAND:] = mid[:, :half] + first
    high[:, :half] = mid[:, -half:] + second
    nothing = (jnp.zeros(strip.shape, jnp.float32),) * 2
    by, away = strip_of(nothing, beside[...]), strip_of(nothing, strip[...])
    low[:, :BAND] = summed[:, :BAND] + jnp.where(odd, by, away)
    high[:, half:] = summed[:, BAND:] + jnp.where(odd, away, by)


def last_kernel(tile, low, high, got, _, out, edges, sems):
    odd = lax.rem(lax.axis_index(tile), 2) == 1
    depth, size_x = out.shape[2:4]
    count = low.shape[1]
    half, quarter = count - BAND, BAND // 2
    copies = []

    def write(source, target):
        copies.append(pltpu.make_async_copy(source, target, sems.at[len(copies)]))
        copies[-1].start()

    for c in range(6):
        at = pl.ds(depth * c, depth)
        write(low.at[at, pl.ds(BAND, half)], out.at[0, c, :, pl.ds(BAND, half)])
        write(high.at[at, pl.ds(0, half)], out.at[0, c, :, pl.ds(size_x - count, half)])
    straight = got[:, :quarter]
    middle = inner_lanes(straight.shape)
    by = jnp.where(middle, 0.0, straight), jnp.where(middle, 0.0, middle_out(straight))
    by = jnp.concatenate(by, axis=1)
    away = jnp.concatenate(y_unpacked(got[:, quarter:]), axis=1)
    edges[0] = low[:, :BAND] + jnp.where(odd, by, away)
    edges[1] = high[:, half:] + jnp.where(odd, away, by)
    for c in range(6):
        at = pl.ds(depth * c, depth)
        write(edges.at[0, at], out.at[0, c, :, pl.ds(0, BAND)])
        write(edges.at[1, at], out.at[0, c, :, pl.ds(size_x - BAND, BAND)])
    for copy in copies:
        copy.wait()


HBM = pl.BlockSpec(memory_space=pltpu.HBM)
VMEM = pl.BlockSpec(memory_space=pltpu.VMEM)
PARAMS = pltpu.CompilerParams(vmem_limit_bytes=32 * 1024 * 1024)


def cost(flops):
    return pl.CostEstimate(flops=flops, bytes_accessed=0, transcendentals=0)


def called(kernel, shapes, *operands, flops=0):
    outs = [jax.ShapeDtypeStruct(shape, jnp.float32) for shape in shapes]
    return pl.pallas_call(
        kernel,
        out_shape=outs,
        in_specs=[VMEM] * len(operands),
        out_specs=[VMEM] * len(outs),
        compiler_params=PARAMS,
        cost_estimate=cost(flops),
    )(*operands)


def after(first, *values):
    return lax.optimization_barrier((first, *values))


def near_exchange(near, sub_size):
    return lax.ppermute(near, "sub", [(i, i ^ 1) for i in range(sub_size)])


def far_exchange(far, sub_size, tile_size):
    pairs = []
    for t in range(tile_size):
        for i in range(sub_size):
            j = ((i + 1) ^ 1) - 1
            other = (t, j) if 0 <= j < sub_size else (t ^ 1, i)
            pairs.append((t * sub_size + i, other[0] * sub_size + other[1]))
    return lax.ppermute(far, ("tile", "sub"), pairs)


def swapped(value, bits, tile_size):
    return lax.ppermute(value, "tile", [(t, t ^ bits) for t in range(tile_size)])


def from_behind(value, steps, count):
    return lax.ppermute(value, "tile", [(t, (t + steps) % count) for t in range(count)])


def table_rows(decay, coupling, size_y):
    entries = jnp.concatenate([decay, coupling])
    return jnp.broadcast_to(entries[:, None], (entries.shape[0], size_y))


def two_by_two(seeds, material, decay, coupling, sub_size, tile_size):
    depth, size_x, size_y = seeds.shape[2:]
    planes = 6 * depth
    edges = ((0, BAND + HALO), (size_x - BAND - HALO, size_x))
    inner = ((BAND - HALO, size_x - BAND + HALO),)
    keep = ((size_x - SHARED) // 2, (size_x + SHARED) // 2)
    span = (keep[0] - HALO // 2, keep[1] + HALO // 2)
    fetched = (keep[0] - HALO, keep[1] + HALO)
    rows = size_x - 2 * BAND
    edge_rows, inner_rows = 2 * (BAND + HALO), rows + 2 * HALO
    packed_rows = (SHARED + HALO) // 2 + 4
    whole = jax.ShapeDtypeStruct(seeds.shape, jnp.float32)

    shared, seeds, material, table = pl.pallas_call(
        functools.partial(first_kernel, fetched, HALO // 2),
        out_shape=[
            jax.ShapeDtypeStruct((7 * depth, packed_rows, size_y), jnp.float32),
            jax.ShapeDtypeStruct(seeds.shape[1:], jnp.float32),
            jax.ShapeDtypeStruct(material.shape[1:], jnp.int32),
            jax.ShapeDtypeStruct((2 * decay.shape[0], size_y), jnp.float32),
        ],
        in_specs=[HBM] * 4,
        out_specs=[VMEM] * 4,
        scratch_shapes=[pltpu.SMEM((2, *decay.shape), jnp.float32), pltpu.SemaphoreType.DMA((14,))],
        compiler_params=PARAMS,
        cost_estimate=cost(0),
    )(*(pltpu.with_memory_space_constraint(x, pltpu.HBM) for x in (decay, coupling, seeds, material)))
    shared = swapped(shared, 2, tile_size)
    edge_near, edge_far, inner_near, inner_far = called(
        functools.partial(halo_pair_kernel, edges, inner, "sub"),
        [(PLANES, edge_rows, size_y)] * 2 + [(PLANES, inner_rows, size_y)] * 2, table, seeds, material,
    )
    edge_near, inner_near = near_exchange(edge_near, sub_size), near_exchange(inner_near, sub_size)
    edge_far = far_exchange(edge_far, sub_size, tile_size)
    inner_far = far_exchange(inner_far, sub_size, tile_size)

    edge, corner, strip = called(
        functools.partial(edge_kernel, edges, "sub", sub_size, "tile"),
        [(planes, 2 * BAND, size_y), (planes, BAND, size_y), (planes, BAND // 2, size_y)],
        table, seeds, material, edge_near, edge_far,
    )
    corner = swapped(corner, 2, tile_size)
    strip = swapped(strip, 3, tile_size)

    shape = (PLANES, packed_rows, size_y)
    shared_near, shared_far, done = called(
        functools.partial(shared_halo_kernel, "sub"), [shape, shape, (8, size_y)], table, shared, flops=LARGE
    )
    shared_near = near_exchange(shared_near, sub_size)
    shared_far = far_exchange(shared_far, sub_size, tile_size)

    mid, bands, beside = called(
        functools.partial(middle_kernel, inner, "sub", sub_size, "tile"),
        [(planes, rows, size_y), (planes, (rows - SHARED) // 2, size_y), (planes, BAND // 2, size_y)],
        table, seeds, material, inner_near, inner_far, edge, done,
    )
    bands = swapped(bands, 2, tile_size)
    beside = swapped(beside, 1, tile_size)

    corner, strip, mid = after(corner, strip, mid)
    summed, send = called(
        functools.partial(corner_kernel, "tile"), [(planes, 2 * BAND, size_y), (planes, BAND, size_y)],
        edge, corner, flops=SMALL,
    )
    got = swapped(send, 1, tile_size)
    beside, shared_near = after(beside, shared_near)
    part, = called(
        functools.partial(shared_kernel, span, size_x, "sub", sub_size),
        [(planes, SHARED + HALO, size_y)], table, shared, shared_near, shared_far, flops=MEDIUM,
    )
    early = pl.pallas_call(
        early_kernel,
        out_shape=whole,
        in_specs=[VMEM] * 2,
        out_specs=HBM,
        scratch_shapes=[pltpu.VMEM((6, depth, SHARED, size_y), jnp.float32), pltpu.SemaphoreType.DMA],
        compiler_params=PARAMS,
        cost_estimate=cost(0),
    )(mid, part)
    low, high = called(
        functools.partial(late_kernel, "tile"), [(planes, (size_x - SHARED) // 2, size_y)] * 2,
        mid, bands, summed, strip, beside,
    )
    return pl.pallas_call(
        functools.partial(last_kernel, "tile"),
        out_shape=whole,
        in_specs=[VMEM] * 3 + [HBM],
        out_specs=HBM,
        scratch_shapes=[pltpu.VMEM((2, planes, BAND, size_y), jnp.float32), pltpu.SemaphoreType.DMA((24,))],
        input_output_aliases={3: 0},
        compiler_params=PARAMS,
        cost_estimate=cost(0),
    )(low, high, got, early)


def any_lattice(seeds, material, decay, coupling, sub_size, tile_size):
    depth, size_x, size_y = seeds.shape[2:]
    seeds, material = seeds[0], material[0]
    spans = ((0, size_x),)
    table = table_rows(decay, coupling, size_y)
    shape = (PLANES, size_x, size_y)
    near, far = called(functools.partial(halo_kernel, spans, "sub"), [shape, shape], table, seeds, material)
    near = near_exchange(near, sub_size)
    far = far_exchange(far, sub_size, tile_size)
    weighted, = called(
        functools.partial(whole_kernel, spans, "sub", sub_size), [(6 * depth, size_x, size_y)],
        table, seeds, material, near, far,
    )
    weighted = weighted.reshape(6, depth, size_x, size_y)
    side = math.isqrt(tile_size)
    prev_band = from_behind(weighted[:, :, size_x - BAND :, :], 1, tile_size)
    next_band = from_behind(weighted[:, :, :BAND, :], -1, tile_size)
    combined = weighted.at[:, :, :BAND, :].add(prev_band)
    combined = combined.at[:, :, size_x - BAND :, :].add(next_band)
    flat = (6, depth, size_x * BAND // size_y, size_y)
    thin = (6, depth, size_x, BAND)
    top_slab = combined[..., size_y - BAND :].reshape(flat)
    bottom_slab = combined[..., :BAND].reshape(flat)
    result = combined.at[..., :BAND].add(from_behind(top_slab, side, tile_size).reshape(thin))
    result = result.at[..., size_y - BAND :].add(from_behind(bottom_slab, -side, tile_size).reshape(thin))
    return result[None]


def solution(mesh):
    sub_size, tile_size = mesh.shape["sub"], mesh.shape["tile"]
    body = two_by_two if tile_size == 4 else any_lattice

    def on_device(seeds, material, decay, coupling):
        return body(seeds, material, decay, coupling, sub_size, tile_size)

    placed = (P("tile", None, "sub", None, None), P("tile", "sub", None, None), P(), P())
    return jax.shard_map(
        on_device,
        mesh=mesh,
        in_specs=placed,
        out_specs=P("tile", None, "sub", None, None),
        check_vma=False,
    )
```

```python
import functools
import math

import jax
import jax.numpy as jnp
from jax import lax
from jax.experimental import pallas as pl
from jax.experimental.pallas import tpu as pltpu
from jax.sharding import PartitionSpec as P

BAND = 32
HALO = 8
PLANES = 5
REACH = 2
SHARED = 96
LARGE, MEDIUM, SMALL = 10**10, 2 * 10**9, 0

magnetic_coeff = 0.5


def lane_of(shape):
    return lax.broadcasted_iota(jnp.int32, shape, len(shape) - 1)


def row_of(shape):
    return lax.broadcasted_iota(jnp.int32, shape, len(shape) - 2)


def rolled(v, shift):
    return pltpu.roll(v, shift % v.shape[-1], v.ndim - 1)


def next_x(v):
    rows = v.shape[0]
    return jnp.where(row_of(v.shape) == rows - 1, 0.0, pltpu.roll(v, rows - 1, 0))


def prev_x(v):
    return jnp.where(row_of(v.shape) == 0, 0.0, pltpu.roll(v, 1, 0))


def next_y(v):
    lanes = v.shape[1]
    return jnp.where(lane_of(v.shape) == lanes - 1, 0.0, pltpu.roll(v, lanes - 1, 1))


def prev_y(v):
    return jnp.where(lane_of(v.shape) == 0, 0.0, pltpu.roll(v, 1, 1))


def plus_x(v):
    return next_x(v) - v


def plus_y(v):
    return next_y(v) - v


def minus_x(v):
    return v - prev_x(v)


def minus_y(v):
    return v - prev_y(v)


def looked_up(labels, entries):
    value = jnp.broadcast_to(entries[0], labels.shape)
    for m in range(1, len(entries)):
        value = jnp.where(labels == m, entries[m], value)
    return value


def update_h(h, v, v_after):
    depth = len(v[0])
    new = [[], [], []]
    for p in range(depth):
        vx, vy, vz = v[0][p], v[1][p], v[2][p]
        up_x, up_y = (v[0][p + 1], v[1][p + 1]) if p + 1 < depth else v_after
        dz_x = up_x - vx if up_x is not None else -vx
        dz_y = up_y - vy if up_y is not None else -vy
        new[0].append(h[0][p] + (plus_y(vz) - dz_y))
        new[1].append(h[1][p] + (dz_x - plus_x(vz)))
        new[2].append(h[2][p] + (plus_x(vy) - plus_y(vx)))
    return new


def update_e(e, ca, h, h_before):
    depth = len(h[0])
    new = [[], [], []]
    for p in range(depth):
        hx, hy, hz = h[0][p], h[1][p], h[2][p]
        low_x, low_y = (h[0][p - 1], h[1][p - 1]) if p > 0 else h_before
        dz_x = hx - low_x if low_x is not None else hx
        dz_y = hy - low_y if low_y is not None else hy
        new[0].append(ca[p] * e[0][p] - magnetic_coeff * (minus_y(hz) - dz_y))
        new[1].append(ca[p] * e[1][p] - magnetic_coeff * (dz_x - minus_x(hz)))
        new[2].append(ca[p] * e[2][p] - magnetic_coeff * (minus_x(hy) - minus_y(hx)))
    return new


def scaled(cb, e):
    return [[cb[p] * e[c][p] for p in range(len(cb))] for c in range(3)]


def joined(ref, index, spans):
    return jnp.concatenate([ref[*index, lo:hi] for lo, hi in spans], axis=0)


def prepared(e, h, labels, tables):
    ca = [looked_up(m, tables[0]) for m in labels]
    cb = [looked_up(m, tables[1]) for m in labels]
    return e, h, ca, cb


def raw(seeds, material, spans):
    depth = seeds.shape[1]
    e = [[joined(seeds, (c, p), spans) for p in range(depth)] for c in range(3)]
    h = [[joined(seeds, (3 + c, p), spans) for p in range(depth)] for c in range(3)]
    return e, h, [joined(material, (p,), spans) for p in range(depth)]


def table_entries(table):
    count = table.shape[0] // 2
    rows = [table[m : m + 1] for m in range(2 * count)]
    return rows[:count], rows[count:]


def loaded(seeds, material, table, spans):
    return prepared(*raw(seeds, material, spans), table_entries(table))


NONE = (None, None)


def send_halos(sub, fields, near, far, packed=lambda planes: planes):
    odd = lax.rem(lax.axis_index(sub), 2) == 1
    e, h, ca, cb = fields
    v1 = scaled(cb, e)
    h1 = update_h(h, v1, NONE)
    e1 = update_e(e, ca, h1, NONE)
    v2 = scaled(cb, e1)
    h2 = update_h(h1, v2, NONE)
    up = (h1[0][-1], h1[1][-1], h2[0][-1], h2[1][-1], cb[-1])
    down = (v1[0][0], v1[1][0], v2[0][0], v2[1][0], cb[0])
    up, down = packed(jnp.stack(up)), packed(jnp.stack(down))
    near[...] = jnp.where(odd, down, up)
    far[...] = jnp.where(odd, up, down)


def halo_kernel(spans, sub, table, seeds, material, near, far):
    send_halos(sub, loaded(seeds, material, table, spans), near, far)


def ramp(position, count):
    position = position.astype(jnp.float32) + 0.5
    return jnp.where(
        position < BAND,
        position / BAND,
        jnp.where(position > count - BAND, (count - position) / BAND, 1.0),
    )


def final_fields(fields, near, far, sub, sub_size, unpacked=lambda planes: planes):
    e, h, ca, cb = fields
    index = lax.axis_index(sub)
    odd = lax.rem(index, 2) == 1
    below, above = index > 0, index < sub_size - 1
    a, b = near[...], far[...]
    from_below = unpacked(jnp.where(odd, a, b))
    from_above = unpacked(jnp.where(above, jnp.where(odd, b, a), 0.0))
    part_h1x, part_h1y, part_h2x, part_h2y, cb_low = from_below
    v1x_up, v1y_up, part_v2x, part_v2y, cb_up = from_above

    v1 = scaled(cb, e)
    h1 = update_h(h, v1, (v1x_up, v1y_up))
    dh1x, dh1y = -v1[1][0], v1[0][0]
    h1_low = (jnp.where(below, part_h1x + dh1x, 0.0), jnp.where(below, part_h1y + dh1y, 0.0))
    e1 = update_e(e, ca, h1, h1_low)
    v2 = scaled(cb, e1)
    v2_up = (
        part_v2x - cb_up * (magnetic_coeff * h1[1][-1]),
        part_v2y + cb_up * (magnetic_coeff * h1[0][-1]),
    )
    h2 = update_h(h1, v2, v2_up)
    dv2x = cb_low * (magnetic_coeff * dh1y)
    dv2y = cb_low * (-magnetic_coeff * dh1x)
    dv2z = cb_low * (-magnetic_coeff * (minus_x(dh1y) - minus_y(dh1x)))
    h2x_low = part_h2x + (dh1x + (plus_y(dv2z) - (v2[1][0] - dv2y)))
    h2y_low = part_h2y + (dh1y + ((v2[0][0] - dv2x) - plus_x(dv2z)))
    h2_low = (jnp.where(below, h2x_low, 0.0), jnp.where(below, h2y_low, 0.0))
    e2 = update_e(e1, ca, h2, h2_low)
    return e2 + h2


def middle_out(block):
    return rolled(block, block.shape[-1] // 2)


def y_packed(first, second):
    lane = lane_of(first.shape)
    middle = (lane >= BAND) & (lane < first.shape[-1] - BAND)
    return jnp.where(middle, middle_out(second), first)


def inner_lanes(shape):
    lane = lane_of(shape)
    return (lane >= BAND) & (lane < shape[-1] - BAND)


def y_unpacked(block):
    a, b = rolled(block, BAND), rolled(block, -BAND)
    middle = inner_lanes(block.shape)
    below = lane_of(block.shape) < BAND
    first = jnp.where(middle, 0.0, jnp.where(below, a, b))
    second = jnp.where(middle, 0.0, jnp.where(below, b, a))
    return first, second


def strip_packed(strip):
    half = strip.shape[1] // 2
    first, second = strip[:, :half], strip[:, half:]
    return jnp.where(inner_lanes(first.shape), second, middle_out(first))


def strip_of(corners, block):
    middle = inner_lanes(block.shape)
    first = jnp.where(middle, middle_out(block), corners[0])
    second = jnp.where(middle, block, corners[1])
    return jnp.concatenate([first, second], axis=1)


def low_rows(shape):
    return row_of(shape) < 4


def bands_packed(block):
    rows, lanes = block.shape[1:]
    count, width, high = rows // 2 + 4, REACH * (rows // 8), lanes - BAND
    shape = (block.shape[0], 8, lanes)
    lane = lane_of(shape)
    low = low_rows(shape)
    side = jnp.zeros(shape, block.dtype)
    for g in range(rows // 8):
        at = BAND + REACH * (g + 1)
        piece = rolled(block[:, 8 * g : 8 * g + 8], REACH * (g + 1))
        here = ((lane >= at) & (lane < at + REACH)) | (
            (lane >= at + high - BAND - REACH) & (lane < at + high - BAND)
        )
        side = jnp.where(here, piece, side)
    other = rolled(pltpu.roll(side, 4, 1), width + REACH)
    own = ((lane >= BAND) & (lane < BAND + REACH + width)) | ((lane >= high) & (lane < high + width))
    side = jnp.where(own, side, other)
    middle = (lane >= BAND) & (lane < high)
    packed = y_packed(block[:, :count], block[:, rows - count :])
    first = jnp.where(low & middle, side, packed[:, :8])
    last = jnp.where(low | middle, packed[:, count - 8 :], side)
    return jnp.concatenate([first, packed[:, 8 : count - 8], last], axis=1)


def bands_unpacked(packed):
    count, lanes = packed.shape[1:]
    rows = 2 * count - 8
    width, high = REACH * (rows // 8), lanes - BAND
    first, last = packed[:, :8], packed[:, count - 8 :]
    low = low_rows(first.shape)
    lane = lane_of(first.shape)
    middle = (lane >= BAND) & (lane < high)
    side = jnp.where(low, first, last)
    other = rolled(pltpu.roll(side, 4, 1), -width - REACH)
    side = jnp.where(low == middle, side, other)
    beside = ((lane >= BAND) & (lane < BAND + REACH)) | ((lane >= high - REACH) & (lane < high))
    moved = [rolled(packed[:, at : at + 8], lanes // 2) for at in range(0, count, 8)]
    pieces = [packed[:, at : at + 8] for at in range(0, count - 8, 8)]
    pieces += [jnp.where(low, last, moved[0])] + moved[1:]
    result = []
    for g, piece in enumerate(pieces):
        result.append(jnp.where(middle, jnp.where(beside, rolled(side, -REACH * (g + 1)), 0.0), piece))
    return jnp.concatenate(result, axis=1)


def first_kernel(span, skip, decay, coupling, seeds, material, shared, held, labels, table, entries, sems):
    size_x = held.shape[2]
    copies = []

    def fetch(source, target):
        copies.append(pltpu.make_async_copy(source, target, sems.at[len(copies)]))
        copies[-1].start()

    def fetch_rows(lo, hi):
        rows = pl.ds(lo, hi - lo)
        fetch(material.at[0, :, rows], labels.at[:, rows])
        for c in range(0, 6, 2):
            some = pl.ds(c, 2)
            fetch(seeds.at[0, some, :, rows], held.at[some, :, rows])

    fetch_rows(*span)
    early = len(copies)
    fetch(decay, entries.at[0])
    fetch(coupling, entries.at[1])
    fetch_rows(0, span[0])
    fetch_rows(span[1], size_x)
    rows = slice(span[0] + skip, span[1] - skip)
    for copy in copies[:early]:
        copy.wait()
    planes = [held[c, :, rows] for c in range(6)] + [labels[:, rows].astype(jnp.float32)]
    shared[...] = bands_packed(jnp.concatenate(planes, axis=0))
    for copy in copies[early:]:
        copy.wait()
    count = entries.shape[1]
    for k in range(2):
        for m in range(count):
            table[k * count + m : k * count + m + 1] = jnp.full((1, table.shape[1]), entries[k, m], jnp.float32)


def halo_pair_kernel(edges, inner, sub, table, seeds, material, near_edge, far_edge, near, far):
    send_halos(sub, loaded(seeds, material, table, edges), near_edge, far_edge)
    send_halos(sub, loaded(seeds, material, table, inner), near, far)


def shared_fields(table, shared):
    depth = shared.shape[0] // 7
    planes = bands_unpacked(shared[...])
    f = [planes[depth * c : depth * (c + 1)] for c in range(7)]
    return prepared(f[:3], f[3:6], f[6], table_entries(table))


def shared_halo_kernel(sub, table, shared, near, far, done):
    done[...] = jnp.zeros(done.shape, done.dtype)
    send_halos(sub, shared_fields(table, shared), near, far, bands_packed)


def weighted_planes(seeds, material, table, near, far, spans, keeps, sub, sub_size):
    planes = final_fields(loaded(seeds, material, table, spans), near, far, sub, sub_size)
    return weighted(planes, spans, keeps, *seeds.shape[2:])


def weighted(planes, spans, keeps, size_x, size_y):
    at, results = 0, []
    for (lo, hi), (start, stop) in zip(spans, keeps):
        shape = (stop - start, size_y)
        weight = ramp(row_of(shape) + start, size_x) * ramp(lane_of(shape), size_y)
        first = at + start - lo
        results.append(jnp.stack([plane[first : first + stop - start] * weight for part in planes for plane in part]))
        at += hi - lo
    return results


def edge_kernel(spans, sub, sub_size, tile, table, seeds, material, near, far, edge, corner, strip):
    size_x = seeds.shape[2]
    keeps = ((0, BAND), (size_x - BAND, size_x))
    low, high = weighted_planes(seeds, material, table, near, far, spans, keeps, sub, sub_size)
    odd = lax.rem(lax.axis_index(tile), 2) == 1
    edge[:, :BAND] = low
    edge[:, BAND:] = high
    corner[...] = y_packed(low, high)
    strip[...] = strip_packed(jnp.where(odd, high, low))


def middle_kernel(spans, sub, sub_size, tile, table, seeds, material, near, far, edge, _, mid, bands, beside):
    size_x = seeds.shape[2]
    keep = (BAND, size_x - BAND)
    odd = lax.rem(lax.axis_index(tile), 2) == 1
    beside[...] = strip_packed(jnp.where(odd, edge[:, :BAND], edge[:, BAND:]))
    planes, = weighted_planes(seeds, material, table, near, far, spans, (keep,), sub, sub_size)
    half = bands.shape[1]
    mid[...] = planes
    bands[...] = y_packed(planes[:, :half], planes[:, -half:])


def whole_kernel(spans, sub, sub_size, table, seeds, material, near, far, out):
    planes, = weighted_planes(seeds, material, table, near, far, spans, spans, sub, sub_size)
    out[...] = planes


def y_swapped(block):
    below = lane_of(block.shape) < BAND
    return jnp.where(inner_lanes(block.shape), 0.0, jnp.where(below, rolled(block, BAND), rolled(block, -BAND)))


def shared_kernel(span, size_x, sub, sub_size, table, shared, near, far, part):
    planes = final_fields(shared_fields(table, shared), near, far, sub, sub_size, bands_unpacked)
    found, = weighted(planes, (span,), (span,), size_x, part.shape[2])
    part[...] = y_swapped(found)


def corner_kernel(tile, edge, corner, summed, send):
    odd = lax.rem(lax.axis_index(tile), 2) == 1
    half = BAND // 2
    first, second = y_unpacked(corner[...])
    low = edge[:, :BAND] + first
    high = edge[:, BAND:] + second
    summed[:, :BAND] = low
    summed[:, BAND:] = high
    by, away = jnp.where(odd, low, high), jnp.where(odd, high, low)
    send[:, :half] = y_packed(by[:, :half], by[:, half:])
    send[:, half:] = y_packed(away[:, :half], away[:, half:])


def early_kernel(mid, part, out, whole, sem):
    size_x = out.shape[3]
    skip = HALO // 2
    count = part.shape[1] - 2 * skip
    start = (size_x - count) // 2
    found = mid[:, start - BAND : start - BAND + count] + part[:, skip : skip + count]
    whole[...] = found.reshape(whole.shape)
    copy = pltpu.make_async_copy(whole, out.at[0, :, :, pl.ds(start, count)], sem)
    copy.start()
    copy.wait()


def late_kernel(tile, mid, bands, summed, strip, beside, low, high):
    odd = lax.rem(lax.axis_index(tile), 2) == 1
    half = bands.shape[1]
    first, second = y_unpacked(bands[...])
    nothing = (jnp.zeros(strip.shape, jnp.float32),) * 2
    by, away = strip_of(nothing, beside[...]), strip_of(nothing, strip[...])

    def by_component(rows):
        return rows.reshape(*low.shape[:2], *rows.shape[1:])

    low[:, :, BAND:] = by_component(mid[:, :half] + first)
    high[:, :, :half] = by_component(mid[:, -half:] + second)
    low[:, :, :BAND] = by_component(summed[:, :BAND] + jnp.where(odd, by, away))
    high[:, :, half:] = by_component(summed[:, BAND:] + jnp.where(odd, away, by))


def last_kernel(tile, low, high, got, _, out, edges, sems):
    odd = lax.rem(lax.axis_index(tile), 2) == 1
    size_x, count = out.shape[3], low.shape[2]
    half, quarter = count - BAND, BAND // 2
    copies = []

    def write(source, start, rows):
        target = out.at[0, :, :, pl.ds(start, rows)]
        copies.append(pltpu.make_async_copy(source, target, sems.at[len(copies)]))
        copies[-1].start()

    write(low.at[:, :, pl.ds(BAND, half)], BAND, half)
    write(high.at[:, :, pl.ds(0, half)], size_x - count, half)
    straight = got[:, :quarter]
    middle = inner_lanes(straight.shape)
    by = jnp.where(middle, 0.0, straight), jnp.where(middle, 0.0, middle_out(straight))
    by = jnp.concatenate(by, axis=1)
    away = jnp.concatenate(y_unpacked(got[:, quarter:]), axis=1)
    shape = edges.shape[1:]
    edges[0] = low[:, :, :BAND] + jnp.where(odd, by, away).reshape(shape)
    write(edges.at[0], 0, BAND)
    edges[1] = high[:, :, half:] + jnp.where(odd, away, by).reshape(shape)
    write(edges.at[1], size_x - BAND, BAND)
    for copy in copies:
        copy.wait()


HBM = pl.BlockSpec(memory_space=pltpu.HBM)
VMEM = pl.BlockSpec(memory_space=pltpu.VMEM)
PARAMS = pltpu.CompilerParams(vmem_limit_bytes=32 * 1024 * 1024)


def cost(flops):
    return pl.CostEstimate(flops=flops, bytes_accessed=0, transcendentals=0)


def called(kernel, shapes, *operands, flops=0):
    outs = [jax.ShapeDtypeStruct(shape, jnp.float32) for shape in shapes]
    return pl.pallas_call(
        kernel,
        out_shape=outs,
        in_specs=[VMEM] * len(operands),
        out_specs=[VMEM] * len(outs),
        compiler_params=PARAMS,
        cost_estimate=cost(flops),
    )(*operands)


def after(first, *values):
    return lax.optimization_barrier((first, *values))


def near_exchange(near, sub_size):
    return lax.ppermute(near, "sub", [(i, i ^ 1) for i in range(sub_size)])


def far_exchange(far, sub_size, tile_size):
    pairs = []
    for t in range(tile_size):
        for i in range(sub_size):
            j = ((i + 1) ^ 1) - 1
            other = (t, j) if 0 <= j < sub_size else (t ^ 1, i)
            pairs.append((t * sub_size + i, other[0] * sub_size + other[1]))
    return lax.ppermute(far, ("tile", "sub"), pairs)


def swapped(value, bits, tile_size):
    return lax.ppermute(value, "tile", [(t, t ^ bits) for t in range(tile_size)])


def from_behind(value, steps, count):
    return lax.ppermute(value, "tile", [(t, (t + steps) % count) for t in range(count)])


def table_rows(decay, coupling, size_y):
    entries = jnp.concatenate([decay, coupling])
    return jnp.broadcast_to(entries[:, None], (entries.shape[0], size_y))


def two_by_two(seeds, material, decay, coupling, sub_size, tile_size):
    depth, size_x, size_y = seeds.shape[2:]
    planes = 6 * depth
    edges = ((0, BAND + HALO), (size_x - BAND - HALO, size_x))
    inner = ((BAND - HALO, size_x - BAND + HALO),)
    keep = ((size_x - SHARED) // 2, (size_x + SHARED) // 2)
    span = (keep[0] - HALO // 2, keep[1] + HALO // 2)
    fetched = (keep[0] - HALO, keep[1] + HALO)
    rows = size_x - 2 * BAND
    edge_rows, inner_rows = 2 * (BAND + HALO), rows + 2 * HALO
    packed_rows = (SHARED + HALO) // 2 + 4
    whole = jax.ShapeDtypeStruct(seeds.shape, jnp.float32)

    shared, seeds, material, table = pl.pallas_call(
        functools.partial(first_kernel, fetched, HALO // 2),
        out_shape=[
            jax.ShapeDtypeStruct((7 * depth, packed_rows, size_y), jnp.float32),
            jax.ShapeDtypeStruct(seeds.shape[1:], jnp.float32),
            jax.ShapeDtypeStruct(material.shape[1:], jnp.int32),
            jax.ShapeDtypeStruct((2 * decay.shape[0], size_y), jnp.float32),
        ],
        in_specs=[HBM] * 4,
        out_specs=[VMEM] * 4,
        scratch_shapes=[pltpu.SMEM((2, *decay.shape), jnp.float32), pltpu.SemaphoreType.DMA((14,))],
        compiler_params=PARAMS,
        cost_estimate=cost(0),
    )(*(pltpu.with_memory_space_constraint(x, pltpu.HBM) for x in (decay, coupling, seeds, material)))
    shared = swapped(shared, 2, tile_size)
    edge_near, edge_far, inner_near, inner_far = called(
        functools.partial(halo_pair_kernel, edges, inner, "sub"),
        [(PLANES, edge_rows, size_y)] * 2 + [(PLANES, inner_rows, size_y)] * 2, table, seeds, material,
    )
    edge_near, inner_near = near_exchange(edge_near, sub_size), near_exchange(inner_near, sub_size)
    edge_far = far_exchange(edge_far, sub_size, tile_size)
    inner_far = far_exchange(inner_far, sub_size, tile_size)

    edge, corner, strip = called(
        functools.partial(edge_kernel, edges, "sub", sub_size, "tile"),
        [(planes, 2 * BAND, size_y), (planes, BAND, size_y), (planes, BAND // 2, size_y)],
        table, seeds, material, edge_near, edge_far,
    )
    corner = swapped(corner, 2, tile_size)
    strip = swapped(strip, 3, tile_size)

    shape = (PLANES, packed_rows, size_y)
    shared_near, shared_far, done = called(
        functools.partial(shared_halo_kernel, "sub"), [shape, shape, (8, size_y)], table, shared, flops=LARGE
    )
    shared_near = near_exchange(shared_near, sub_size)
    shared_far = far_exchange(shared_far, sub_size, tile_size)

    mid, bands, beside = called(
        functools.partial(middle_kernel, inner, "sub", sub_size, "tile"),
        [(planes, rows, size_y), (planes, (rows - SHARED) // 2, size_y), (planes, BAND // 2, size_y)],
        table, seeds, material, inner_near, inner_far, edge, done,
    )
    bands = swapped(bands, 2, tile_size)
    beside = swapped(beside, 1, tile_size)

    corner, strip, mid = after(corner, strip, mid)
    summed, send = called(
        functools.partial(corner_kernel, "tile"), [(planes, 2 * BAND, size_y), (planes, BAND, size_y)],
        edge, corner, flops=SMALL,
    )
    got = swapped(send, 1, tile_size)
    beside, shared_near = after(beside, shared_near)
    part, = called(
        functools.partial(shared_kernel, span, size_x, "sub", sub_size),
        [(planes, SHARED + HALO, size_y)], table, shared, shared_near, shared_far, flops=MEDIUM,
    )
    early = pl.pallas_call(
        early_kernel,
        out_shape=whole,
        in_specs=[VMEM] * 2,
        out_specs=HBM,
        scratch_shapes=[pltpu.VMEM((6, depth, SHARED, size_y), jnp.float32), pltpu.SemaphoreType.DMA],
        compiler_params=PARAMS,
        cost_estimate=cost(0),
    )(mid, part)
    low, high = called(
        functools.partial(late_kernel, "tile"), [(6, depth, (size_x - SHARED) // 2, size_y)] * 2,
        mid, bands, summed, strip, beside,
    )
    return pl.pallas_call(
        functools.partial(last_kernel, "tile"),
        out_shape=whole,
        in_specs=[VMEM] * 3 + [HBM],
        out_specs=HBM,
        scratch_shapes=[pltpu.VMEM((2, 6, depth, BAND, size_y), jnp.float32), pltpu.SemaphoreType.DMA((4,))],
        input_output_aliases={3: 0},
        compiler_params=PARAMS,
        cost_estimate=cost(0),
    )(low, high, got, early)


def any_lattice(seeds, material, decay, coupling, sub_size, tile_size):
    depth, size_x, size_y = seeds.shape[2:]
    seeds, material = seeds[0], material[0]
    spans = ((0, size_x),)
    table = table_rows(decay, coupling, size_y)
    shape = (PLANES, size_x, size_y)
    near, far = called(functools.partial(halo_kernel, spans, "sub"), [shape, shape], table, seeds, material)
    near = near_exchange(near, sub_size)
    far = far_exchange(far, sub_size, tile_size)
    weighted, = called(
        functools.partial(whole_kernel, spans, "sub", sub_size), [(6 * depth, size_x, size_y)],
        table, seeds, material, near, far,
    )
    weighted = weighted.reshape(6, depth, size_x, size_y)
    side = math.isqrt(tile_size)
    prev_band = from_behind(weighted[:, :, size_x - BAND :, :], 1, tile_size)
    next_band = from_behind(weighted[:, :, :BAND, :], -1, tile_size)
    combined = weighted.at[:, :, :BAND, :].add(prev_band)
    combined = combined.at[:, :, size_x - BAND :, :].add(next_band)
    flat = (6, depth, size_x * BAND // size_y, size_y)
    thin = (6, depth, size_x, BAND)
    top_slab = combined[..., size_y - BAND :].reshape(flat)
    bottom_slab = combined[..., :BAND].reshape(flat)
    result = combined.at[..., :BAND].add(from_behind(top_slab, side, tile_size).reshape(thin))
    result = result.at[..., size_y - BAND :].add(from_behind(bottom_slab, -side, tile_size).reshape(thin))
    return result[None]


def solution(mesh):
    sub_size, tile_size = mesh.shape["sub"], mesh.shape["tile"]
    body = two_by_two if tile_size == 4 else any_lattice

    def on_device(seeds, material, decay, coupling):
        return body(seeds, material, decay, coupling, sub_size, tile_size)

    placed = (P("tile", None, "sub", None, None), P("tile", "sub", None, None), P(), P())
    return jax.shard_map(
        on_device,
        mesh=mesh,
        in_specs=placed,
        out_specs=P("tile", None, "sub", None, None),
        check_vma=False,
    )
```

```python
import functools
import math

import jax
import jax.numpy as jnp
from jax import lax
from jax.experimental import pallas as pl
from jax.experimental.pallas import tpu as pltpu
from jax.sharding import PartitionSpec as P

BAND = 32
HALO = 8
PLANES = 5
REACH = 2
SHARED = 112
LARGE, MEDIUM, SMALL = 10**10, 15 * 10**8, 0

magnetic_coeff = 0.5


def lane_of(shape):
    return lax.broadcasted_iota(jnp.int32, shape, len(shape) - 1)


def row_of(shape):
    return lax.broadcasted_iota(jnp.int32, shape, len(shape) - 2)


def rolled(v, shift):
    return pltpu.roll(v, shift % v.shape[-1], v.ndim - 1)


def next_x(v):
    rows = v.shape[0]
    return jnp.where(row_of(v.shape) == rows - 1, 0.0, pltpu.roll(v, rows - 1, 0))


def prev_x(v):
    return jnp.where(row_of(v.shape) == 0, 0.0, pltpu.roll(v, 1, 0))


def next_y(v):
    lanes = v.shape[1]
    return jnp.where(lane_of(v.shape) == lanes - 1, 0.0, pltpu.roll(v, lanes - 1, 1))


def prev_y(v):
    return jnp.where(lane_of(v.shape) == 0, 0.0, pltpu.roll(v, 1, 1))


def plus_x(v):
    return next_x(v) - v


def plus_y(v):
    return next_y(v) - v


def minus_x(v):
    return v - prev_x(v)


def minus_y(v):
    return v - prev_y(v)


def looked_up(labels, entries):
    value = jnp.broadcast_to(entries[0], labels.shape)
    for m in range(1, len(entries)):
        value = jnp.where(labels == m, entries[m], value)
    return value


def update_h(h, v, v_after):
    depth = len(v[0])
    new = [[], [], []]
    for p in range(depth):
        vx, vy, vz = v[0][p], v[1][p], v[2][p]
        up_x, up_y = (v[0][p + 1], v[1][p + 1]) if p + 1 < depth else v_after
        dz_x = up_x - vx if up_x is not None else -vx
        dz_y = up_y - vy if up_y is not None else -vy
        new[0].append(h[0][p] + (plus_y(vz) - dz_y))
        new[1].append(h[1][p] + (dz_x - plus_x(vz)))
        new[2].append(h[2][p] + (plus_x(vy) - plus_y(vx)))
    return new


def update_e(e, ca, h, h_before):
    depth = len(h[0])
    new = [[], [], []]
    for p in range(depth):
        hx, hy, hz = h[0][p], h[1][p], h[2][p]
        low_x, low_y = (h[0][p - 1], h[1][p - 1]) if p > 0 else h_before
        dz_x = hx - low_x if low_x is not None else hx
        dz_y = hy - low_y if low_y is not None else hy
        new[0].append(ca[p] * e[0][p] - magnetic_coeff * (minus_y(hz) - dz_y))
        new[1].append(ca[p] * e[1][p] - magnetic_coeff * (dz_x - minus_x(hz)))
        new[2].append(ca[p] * e[2][p] - magnetic_coeff * (minus_x(hy) - minus_y(hx)))
    return new


def scaled(cb, e):
    return [[cb[p] * e[c][p] for p in range(len(cb))] for c in range(3)]


def joined(ref, index, spans):
    return jnp.concatenate([ref[*index, lo:hi] for lo, hi in spans], axis=0)


def prepared(e, h, labels, tables):
    ca = [looked_up(m, tables[0]) for m in labels]
    cb = [looked_up(m, tables[1]) for m in labels]
    return e, h, ca, cb


def raw(seeds, material, spans):
    depth = seeds.shape[1]
    e = [[joined(seeds, (c, p), spans) for p in range(depth)] for c in range(3)]
    h = [[joined(seeds, (3 + c, p), spans) for p in range(depth)] for c in range(3)]
    return e, h, [joined(material, (p,), spans) for p in range(depth)]


def table_entries(table):
    count = table.shape[0] // 2
    rows = [table[m : m + 1] for m in range(2 * count)]
    return rows[:count], rows[count:]


def loaded(seeds, material, table, spans):
    return prepared(*raw(seeds, material, spans), table_entries(table))


NONE = (None, None)


def send_halos(sub, fields, near, far, packed=lambda planes: planes):
    odd = lax.rem(lax.axis_index(sub), 2) == 1
    e, h, ca, cb = fields
    v1 = scaled(cb, e)
    h1 = update_h(h, v1, NONE)
    e1 = update_e(e, ca, h1, NONE)
    v2 = scaled(cb, e1)
    h2 = update_h(h1, v2, NONE)
    up = (h1[0][-1], h1[1][-1], h2[0][-1], h2[1][-1], cb[-1])
    down = (v1[0][0], v1[1][0], v2[0][0], v2[1][0], cb[0])
    up, down = packed(jnp.stack(up)), packed(jnp.stack(down))
    near[...] = jnp.where(odd, down, up)
    far[...] = jnp.where(odd, up, down)


def halo_kernel(spans, sub, table, seeds, material, near, far):
    send_halos(sub, loaded(seeds, material, table, spans), near, far)


def ramp(position, count):
    position = position.astype(jnp.float32) + 0.5
    return jnp.where(
        position < BAND,
        position / BAND,
        jnp.where(position > count - BAND, (count - position) / BAND, 1.0),
    )


def final_fields(fields, near, far, sub, sub_size, unpacked=lambda planes: planes):
    e, h, ca, cb = fields
    index = lax.axis_index(sub)
    odd = lax.rem(index, 2) == 1
    below, above = index > 0, index < sub_size - 1
    a, b = near[...], far[...]
    from_below = unpacked(jnp.where(odd, a, b))
    from_above = unpacked(jnp.where(above, jnp.where(odd, b, a), 0.0))
    part_h1x, part_h1y, part_h2x, part_h2y, cb_low = from_below
    v1x_up, v1y_up, part_v2x, part_v2y, cb_up = from_above

    v1 = scaled(cb, e)
    h1 = update_h(h, v1, (v1x_up, v1y_up))
    dh1x, dh1y = -v1[1][0], v1[0][0]
    h1_low = (jnp.where(below, part_h1x + dh1x, 0.0), jnp.where(below, part_h1y + dh1y, 0.0))
    e1 = update_e(e, ca, h1, h1_low)
    v2 = scaled(cb, e1)
    v2_up = (
        part_v2x - cb_up * (magnetic_coeff * h1[1][-1]),
        part_v2y + cb_up * (magnetic_coeff * h1[0][-1]),
    )
    h2 = update_h(h1, v2, v2_up)
    dv2x = cb_low * (magnetic_coeff * dh1y)
    dv2y = cb_low * (-magnetic_coeff * dh1x)
    dv2z = cb_low * (-magnetic_coeff * (minus_x(dh1y) - minus_y(dh1x)))
    h2x_low = part_h2x + (dh1x + (plus_y(dv2z) - (v2[1][0] - dv2y)))
    h2y_low = part_h2y + (dh1y + ((v2[0][0] - dv2x) - plus_x(dv2z)))
    h2_low = (jnp.where(below, h2x_low, 0.0), jnp.where(below, h2y_low, 0.0))
    e2 = update_e(e1, ca, h2, h2_low)
    return e2 + h2


def middle_out(block):
    return rolled(block, block.shape[-1] // 2)


def y_packed(first, second):
    lane = lane_of(first.shape)
    middle = (lane >= BAND) & (lane < first.shape[-1] - BAND)
    return jnp.where(middle, middle_out(second), first)


def inner_lanes(shape):
    lane = lane_of(shape)
    return (lane >= BAND) & (lane < shape[-1] - BAND)


def y_unpacked(block):
    a, b = rolled(block, BAND), rolled(block, -BAND)
    middle = inner_lanes(block.shape)
    below = lane_of(block.shape) < BAND
    first = jnp.where(middle, 0.0, jnp.where(below, a, b))
    second = jnp.where(middle, 0.0, jnp.where(below, b, a))
    return first, second


def strip_packed(strip):
    half = strip.shape[1] // 2
    first, second = strip[:, :half], strip[:, half:]
    return jnp.where(inner_lanes(first.shape), second, middle_out(first))


def strip_of(corners, block):
    middle = inner_lanes(block.shape)
    first = jnp.where(middle, middle_out(block), corners[0])
    second = jnp.where(middle, block, corners[1])
    return jnp.concatenate([first, second], axis=1)


def low_rows(shape):
    return row_of(shape) < 4


def bands_packed(block):
    rows, lanes = block.shape[1:]
    count, width, high = rows // 2 + 4, REACH * (rows // 8), lanes - BAND
    shape = (block.shape[0], 8, lanes)
    lane = lane_of(shape)
    low = low_rows(shape)
    side = jnp.zeros(shape, block.dtype)
    for g in range(rows // 8):
        at = BAND + REACH * (g + 1)
        piece = rolled(block[:, 8 * g : 8 * g + 8], REACH * (g + 1))
        here = ((lane >= at) & (lane < at + REACH)) | (
            (lane >= at + high - BAND - REACH) & (lane < at + high - BAND)
        )
        side = jnp.where(here, piece, side)
    other = rolled(pltpu.roll(side, 4, 1), width + REACH)
    own = ((lane >= BAND) & (lane < BAND + REACH + width)) | ((lane >= high) & (lane < high + width))
    side = jnp.where(own, side, other)
    middle = (lane >= BAND) & (lane < high)
    packed = y_packed(block[:, :count], block[:, rows - count :])
    first = jnp.where(low & middle, side, packed[:, :8])
    last = jnp.where(low | middle, packed[:, count - 8 :], side)
    return jnp.concatenate([first, packed[:, 8 : count - 8], last], axis=1)


def bands_unpacked(packed):
    count, lanes = packed.shape[1:]
    rows = 2 * count - 8
    width, high = REACH * (rows // 8), lanes - BAND
    first, last = packed[:, :8], packed[:, count - 8 :]
    low = low_rows(first.shape)
    lane = lane_of(first.shape)
    middle = (lane >= BAND) & (lane < high)
    side = jnp.where(low, first, last)
    other = rolled(pltpu.roll(side, 4, 1), -width - REACH)
    side = jnp.where(low == middle, side, other)
    beside = ((lane >= BAND) & (lane < BAND + REACH)) | ((lane >= high - REACH) & (lane < high))
    moved = [rolled(packed[:, at : at + 8], lanes // 2) for at in range(0, count, 8)]
    pieces = [packed[:, at : at + 8] for at in range(0, count - 8, 8)]
    pieces += [jnp.where(low, last, moved[0])] + moved[1:]
    result = []
    for g, piece in enumerate(pieces):
        result.append(jnp.where(middle, jnp.where(beside, rolled(side, -REACH * (g + 1)), 0.0), piece))
    return jnp.concatenate(result, axis=1)


def first_kernel(span, skip, decay, coupling, seeds, material, shared, held, labels, table, entries, sems):
    size_x = held.shape[2]
    copies = []

    def fetch(source, target):
        copies.append(pltpu.make_async_copy(source, target, sems.at[len(copies)]))
        copies[-1].start()

    def fetch_rows(lo, hi):
        rows = pl.ds(lo, hi - lo)
        fetch(material.at[0, :, rows], labels.at[:, rows])
        for c in range(0, 6, 2):
            some = pl.ds(c, 2)
            fetch(seeds.at[0, some, :, rows], held.at[some, :, rows])

    fetch_rows(*span)
    early = len(copies)
    fetch(decay, entries.at[0])
    fetch(coupling, entries.at[1])
    fetch_rows(0, span[0])
    fetch_rows(span[1], size_x)
    rows = slice(span[0] + skip, span[1] - skip)
    for copy in copies[:early]:
        copy.wait()
    planes = [held[c, :, rows] for c in range(6)] + [labels[:, rows].astype(jnp.float32)]
    shared[...] = bands_packed(jnp.concatenate(planes, axis=0))
    for copy in copies[early:]:
        copy.wait()
    count = entries.shape[1]
    for k in range(2):
        for m in range(count):
            table[k * count + m : k * count + m + 1] = jnp.full((1, table.shape[1]), entries[k, m], jnp.float32)


def halo_pair_kernel(edges, inner, sub, table, seeds, material, near_edge, far_edge, near, far):
    send_halos(sub, loaded(seeds, material, table, edges), near_edge, far_edge)
    send_halos(sub, loaded(seeds, material, table, inner), near, far)


def shared_fields(table, shared):
    depth = shared.shape[0] // 7
    planes = bands_unpacked(shared[...])
    f = [planes[depth * c : depth * (c + 1)] for c in range(7)]
    return prepared(f[:3], f[3:6], f[6], table_entries(table))


def shared_halo_kernel(sub, table, shared, near, far, done):
    done[...] = jnp.zeros(done.shape, done.dtype)
    send_halos(sub, shared_fields(table, shared), near, far, bands_packed)


def weighted_planes(seeds, material, table, near, far, spans, keeps, sub, sub_size):
    planes = final_fields(loaded(seeds, material, table, spans), near, far, sub, sub_size)
    return weighted(planes, spans, keeps, *seeds.shape[2:])


def weighted(planes, spans, keeps, size_x, size_y):
    at, results = 0, []
    for (lo, hi), (start, stop) in zip(spans, keeps):
        shape = (stop - start, size_y)
        weight = ramp(row_of(shape) + start, size_x) * ramp(lane_of(shape), size_y)
        first = at + start - lo
        results.append(jnp.stack([plane[first : first + stop - start] * weight for part in planes for plane in part]))
        at += hi - lo
    return results


def edge_kernel(spans, sub, sub_size, tile, table, seeds, material, near, far, edge, corner, strip):
    size_x = seeds.shape[2]
    keeps = ((0, BAND), (size_x - BAND, size_x))
    low, high = weighted_planes(seeds, material, table, near, far, spans, keeps, sub, sub_size)
    odd = lax.rem(lax.axis_index(tile), 2) == 1
    edge[:, :BAND] = low
    edge[:, BAND:] = high
    corner[...] = y_packed(low, high)
    strip[...] = strip_packed(jnp.where(odd, high, low))


def middle_kernel(spans, sub, sub_size, tile, table, seeds, material, near, far, edge, _, mid, bands, beside):
    size_x = seeds.shape[2]
    keep = (BAND, size_x - BAND)
    odd = lax.rem(lax.axis_index(tile), 2) == 1
    beside[...] = strip_packed(jnp.where(odd, edge[:, :BAND], edge[:, BAND:]))
    planes, = weighted_planes(seeds, material, table, near, far, spans, (keep,), sub, sub_size)
    half = bands.shape[1]
    mid[...] = planes
    bands[...] = y_packed(planes[:, :half], planes[:, -half:])


def whole_kernel(spans, sub, sub_size, table, seeds, material, near, far, out):
    planes, = weighted_planes(seeds, material, table, near, far, spans, spans, sub, sub_size)
    out[...] = planes


def y_swapped(block):
    below = lane_of(block.shape) < BAND
    return jnp.where(inner_lanes(block.shape), 0.0, jnp.where(below, rolled(block, BAND), rolled(block, -BAND)))


def shared_kernel(span, size_x, sub, sub_size, table, shared, near, far, part):
    planes = final_fields(shared_fields(table, shared), near, far, sub, sub_size, bands_unpacked)
    found, = weighted(planes, (span,), (span,), size_x, part.shape[2])
    part[...] = y_swapped(found)


def corner_kernel(tile, edge, corner, summed, send):
    odd = lax.rem(lax.axis_index(tile), 2) == 1
    half = BAND // 2
    first, second = y_unpacked(corner[...])
    low = edge[:, :BAND] + first
    high = edge[:, BAND:] + second
    summed[:, :BAND] = low
    summed[:, BAND:] = high
    by, away = jnp.where(odd, low, high), jnp.where(odd, high, low)
    send[:, :half] = y_packed(by[:, :half], by[:, half:])
    send[:, half:] = y_packed(away[:, :half], away[:, half:])


def early_kernel(mid, part, out, whole, sem):
    size_x = out.shape[3]
    skip = HALO // 2
    count = part.shape[1] - 2 * skip
    start = (size_x - count) // 2
    found = mid[:, start - BAND : start - BAND + count] + part[:, skip : skip + count]
    whole[...] = found.reshape(whole.shape)
    copy = pltpu.make_async_copy(whole, out.at[0, :, :, pl.ds(start, count)], sem)
    copy.start()
    copy.wait()


def late_kernel(tile, mid, bands, summed, strip, beside, low, high):
    odd = lax.rem(lax.axis_index(tile), 2) == 1
    half = bands.shape[1]
    first, second = y_unpacked(bands[...])
    nothing = (jnp.zeros(strip.shape, jnp.float32),) * 2
    by, away = strip_of(nothing, beside[...]), strip_of(nothing, strip[...])

    def by_component(rows):
        return rows.reshape(*low.shape[:2], *rows.shape[1:])

    low[:, :, BAND:] = by_component(mid[:, :half] + first)
    high[:, :, :half] = by_component(mid[:, -half:] + second)
    low[:, :, :BAND] = by_component(summed[:, :BAND] + jnp.where(odd, by, away))
    high[:, :, half:] = by_component(summed[:, BAND:] + jnp.where(odd, away, by))


def last_kernel(tile, low, high, got, _, out, edges, sems):
    odd = lax.rem(lax.axis_index(tile), 2) == 1
    size_x, count = out.shape[3], low.shape[2]
    half, quarter = count - BAND, BAND // 2
    copies = []

    def write(source, start, rows):
        target = out.at[0, :, :, pl.ds(start, rows)]
        copies.append(pltpu.make_async_copy(source, target, sems.at[len(copies)]))
        copies[-1].start()

    write(low.at[:, :, pl.ds(BAND, half)], BAND, half)
    write(high.at[:, :, pl.ds(0, half)], size_x - count, half)
    straight = got[:, :quarter]
    middle = inner_lanes(straight.shape)
    by = jnp.where(middle, 0.0, straight), jnp.where(middle, 0.0, middle_out(straight))
    by = jnp.concatenate(by, axis=1)
    away = jnp.concatenate(y_unpacked(got[:, quarter:]), axis=1)
    shape = edges.shape[1:]
    edges[0] = low[:, :, :BAND] + jnp.where(odd, by, away).reshape(shape)
    write(edges.at[0], 0, BAND)
    edges[1] = high[:, :, half:] + jnp.where(odd, away, by).reshape(shape)
    write(edges.at[1], size_x - BAND, BAND)
    for copy in copies:
        copy.wait()


HBM = pl.BlockSpec(memory_space=pltpu.HBM)
VMEM = pl.BlockSpec(memory_space=pltpu.VMEM)
PARAMS = pltpu.CompilerParams(vmem_limit_bytes=32 * 1024 * 1024)


def cost(flops):
    return pl.CostEstimate(flops=flops, bytes_accessed=0, transcendentals=0)


def called(kernel, shapes, *operands, flops=0):
    outs = [jax.ShapeDtypeStruct(shape, jnp.float32) for shape in shapes]
    return pl.pallas_call(
        kernel,
        out_shape=outs,
        in_specs=[VMEM] * len(operands),
        out_specs=[VMEM] * len(outs),
        compiler_params=PARAMS,
        cost_estimate=cost(flops),
    )(*operands)


def after(first, *values):
    return lax.optimization_barrier((first, *values))


def near_exchange(near, sub_size):
    return lax.ppermute(near, "sub", [(i, i ^ 1) for i in range(sub_size)])


def far_exchange(far, sub_size, tile_size):
    pairs = []
    for t in range(tile_size):
        for i in range(sub_size):
            j = ((i + 1) ^ 1) - 1
            other = (t, j) if 0 <= j < sub_size else (t ^ 1, i)
            pairs.append((t * sub_size + i, other[0] * sub_size + other[1]))
    return lax.ppermute(far, ("tile", "sub"), pairs)


def swapped(value, bits, tile_size):
    return lax.ppermute(value, "tile", [(t, t ^ bits) for t in range(tile_size)])


def from_behind(value, steps, count):
    return lax.ppermute(value, "tile", [(t, (t + steps) % count) for t in range(count)])


def table_rows(decay, coupling, size_y):
    entries = jnp.concatenate([decay, coupling])
    return jnp.broadcast_to(entries[:, None], (entries.shape[0], size_y))


def two_by_two(seeds, material, decay, coupling, sub_size, tile_size):
    depth, size_x, size_y = seeds.shape[2:]
    planes = 6 * depth
    edges = ((0, BAND + HALO), (size_x - BAND - HALO, size_x))
    inner = ((BAND - HALO, size_x - BAND + HALO),)
    keep = ((size_x - SHARED) // 2, (size_x + SHARED) // 2)
    span = (keep[0] - HALO // 2, keep[1] + HALO // 2)
    fetched = (keep[0] - HALO, keep[1] + HALO)
    rows = size_x - 2 * BAND
    edge_rows, inner_rows = 2 * (BAND + HALO), rows + 2 * HALO
    packed_rows = (SHARED + HALO) // 2 + 4
    whole = jax.ShapeDtypeStruct(seeds.shape, jnp.float32)

    shared, seeds, material, table = pl.pallas_call(
        functools.partial(first_kernel, fetched, HALO // 2),
        out_shape=[
            jax.ShapeDtypeStruct((7 * depth, packed_rows, size_y), jnp.float32),
            jax.ShapeDtypeStruct(seeds.shape[1:], jnp.float32),
            jax.ShapeDtypeStruct(material.shape[1:], jnp.int32),
            jax.ShapeDtypeStruct((2 * decay.shape[0], size_y), jnp.float32),
        ],
        in_specs=[HBM] * 4,
        out_specs=[VMEM] * 4,
        scratch_shapes=[pltpu.SMEM((2, *decay.shape), jnp.float32), pltpu.SemaphoreType.DMA((14,))],
        compiler_params=PARAMS,
        cost_estimate=cost(0),
    )(*(pltpu.with_memory_space_constraint(x, pltpu.HBM) for x in (decay, coupling, seeds, material)))
    shared = swapped(shared, 2, tile_size)
    edge_near, edge_far, inner_near, inner_far = called(
        functools.partial(halo_pair_kernel, edges, inner, "sub"),
        [(PLANES, edge_rows, size_y)] * 2 + [(PLANES, inner_rows, size_y)] * 2, table, seeds, material,
    )
    edge_near, inner_near = near_exchange(edge_near, sub_size), near_exchange(inner_near, sub_size)
    edge_far = far_exchange(edge_far, sub_size, tile_size)
    inner_far = far_exchange(inner_far, sub_size, tile_size)

    edge, corner, strip = called(
        functools.partial(edge_kernel, edges, "sub", sub_size, "tile"),
        [(planes, 2 * BAND, size_y), (planes, BAND, size_y), (planes, BAND // 2, size_y)],
        table, seeds, material, edge_near, edge_far,
    )
    corner = swapped(corner, 2, tile_size)
    strip = swapped(strip, 3, tile_size)

    shape = (PLANES, packed_rows, size_y)
    shared_near, shared_far, done = called(
        functools.partial(shared_halo_kernel, "sub"), [shape, shape, (8, size_y)], table, shared, flops=LARGE
    )
    shared_near = near_exchange(shared_near, sub_size)
    shared_far = far_exchange(shared_far, sub_size, tile_size)

    mid, bands, beside = called(
        functools.partial(middle_kernel, inner, "sub", sub_size, "tile"),
        [(planes, rows, size_y), (planes, (rows - SHARED) // 2, size_y), (planes, BAND // 2, size_y)],
        table, seeds, material, inner_near, inner_far, edge, done,
    )
    bands = swapped(bands, 2, tile_size)
    beside = swapped(beside, 1, tile_size)

    corner, strip, mid = after(corner, strip, mid)
    summed, send = called(
        functools.partial(corner_kernel, "tile"), [(planes, 2 * BAND, size_y), (planes, BAND, size_y)],
        edge, corner, flops=SMALL,
    )
    got = swapped(send, 1, tile_size)
    beside, shared_near = after(beside, shared_near)
    part, = called(
        functools.partial(shared_kernel, span, size_x, "sub", sub_size),
        [(planes, SHARED + HALO, size_y)], table, shared, shared_near, shared_far, flops=MEDIUM,
    )
    early = pl.pallas_call(
        early_kernel,
        out_shape=whole,
        in_specs=[VMEM] * 2,
        out_specs=HBM,
        scratch_shapes=[pltpu.VMEM((6, depth, SHARED, size_y), jnp.float32), pltpu.SemaphoreType.DMA],
        compiler_params=PARAMS,
        cost_estimate=cost(0),
    )(mid, part)
    low, high = called(
        functools.partial(late_kernel, "tile"), [(6, depth, (size_x - SHARED) // 2, size_y)] * 2,
        mid, bands, summed, strip, beside,
    )
    return pl.pallas_call(
        functools.partial(last_kernel, "tile"),
        out_shape=whole,
        in_specs=[VMEM] * 3 + [HBM],
        out_specs=HBM,
        scratch_shapes=[pltpu.VMEM((2, 6, depth, BAND, size_y), jnp.float32), pltpu.SemaphoreType.DMA((4,))],
        input_output_aliases={3: 0},
        compiler_params=PARAMS,
        cost_estimate=cost(0),
    )(low, high, got, early)


def any_lattice(seeds, material, decay, coupling, sub_size, tile_size):
    depth, size_x, size_y = seeds.shape[2:]
    seeds, material = seeds[0], material[0]
    spans = ((0, size_x),)
    table = table_rows(decay, coupling, size_y)
    shape = (PLANES, size_x, size_y)
    near, far = called(functools.partial(halo_kernel, spans, "sub"), [shape, shape], table, seeds, material)
    near = near_exchange(near, sub_size)
    far = far_exchange(far, sub_size, tile_size)
    weighted, = called(
        functools.partial(whole_kernel, spans, "sub", sub_size), [(6 * depth, size_x, size_y)],
        table, seeds, material, near, far,
    )
    weighted = weighted.reshape(6, depth, size_x, size_y)
    side = math.isqrt(tile_size)
    prev_band = from_behind(weighted[:, :, size_x - BAND :, :], 1, tile_size)
    next_band = from_behind(weighted[:, :, :BAND, :], -1, tile_size)
    combined = weighted.at[:, :, :BAND, :].add(prev_band)
    combined = combined.at[:, :, size_x - BAND :, :].add(next_band)
    flat = (6, depth, size_x * BAND // size_y, size_y)
    thin = (6, depth, size_x, BAND)
    top_slab = combined[..., size_y - BAND :].reshape(flat)
    bottom_slab = combined[..., :BAND].reshape(flat)
    result = combined.at[..., :BAND].add(from_behind(top_slab, side, tile_size).reshape(thin))
    result = result.at[..., size_y - BAND :].add(from_behind(bottom_slab, -side, tile_size).reshape(thin))
    return result[None]


def solution(mesh):
    sub_size, tile_size = mesh.shape["sub"], mesh.shape["tile"]
    body = two_by_two if tile_size == 4 else any_lattice

    def on_device(seeds, material, decay, coupling):
        return body(seeds, material, decay, coupling, sub_size, tile_size)

    placed = (P("tile", None, "sub", None, None), P("tile", "sub", None, None), P(), P())
    return jax.shard_map(
        on_device,
        mesh=mesh,
        in_specs=placed,
        out_specs=P("tile", None, "sub", None, None),
        check_vma=False,
    )
```

```python
import functools
import math

import jax
import jax.numpy as jnp
from jax import lax
from jax.experimental import pallas as pl
from jax.experimental.pallas import tpu as pltpu
from jax.sharding import PartitionSpec as P

BAND = 32
HALO = 8
PLANES = 5
REACH = 2
SHARED = 96
LARGE, MEDIUM, SMALL = 10**10, 25 * 10**8, 0

magnetic_coeff = 0.5


def lane_of(shape):
    return lax.broadcasted_iota(jnp.int32, shape, len(shape) - 1)


def row_of(shape):
    return lax.broadcasted_iota(jnp.int32, shape, len(shape) - 2)


def rolled(v, shift):
    return pltpu.roll(v, shift % v.shape[-1], v.ndim - 1)


def next_x(v):
    rows = v.shape[0]
    return jnp.where(row_of(v.shape) == rows - 1, 0.0, pltpu.roll(v, rows - 1, 0))


def prev_x(v):
    return jnp.where(row_of(v.shape) == 0, 0.0, pltpu.roll(v, 1, 0))


def next_y(v):
    lanes = v.shape[1]
    return jnp.where(lane_of(v.shape) == lanes - 1, 0.0, pltpu.roll(v, lanes - 1, 1))


def prev_y(v):
    return jnp.where(lane_of(v.shape) == 0, 0.0, pltpu.roll(v, 1, 1))


def plus_x(v):
    return next_x(v) - v


def plus_y(v):
    return next_y(v) - v


def minus_x(v):
    return v - prev_x(v)


def minus_y(v):
    return v - prev_y(v)


def looked_up(labels, entries):
    value = jnp.broadcast_to(entries[0], labels.shape)
    for m in range(1, len(entries)):
        value = jnp.where(labels == m, entries[m], value)
    return value


def update_h(h, v, v_after):
    depth = len(v[0])
    new = [[], [], []]
    for p in range(depth):
        vx, vy, vz = v[0][p], v[1][p], v[2][p]
        up_x, up_y = (v[0][p + 1], v[1][p + 1]) if p + 1 < depth else v_after
        dz_x = up_x - vx if up_x is not None else -vx
        dz_y = up_y - vy if up_y is not None else -vy
        new[0].append(h[0][p] + (plus_y(vz) - dz_y))
        new[1].append(h[1][p] + (dz_x - plus_x(vz)))
        new[2].append(h[2][p] + (plus_x(vy) - plus_y(vx)))
    return new


def update_e(e, ca, h, h_before):
    depth = len(h[0])
    new = [[], [], []]
    for p in range(depth):
        hx, hy, hz = h[0][p], h[1][p], h[2][p]
        low_x, low_y = (h[0][p - 1], h[1][p - 1]) if p > 0 else h_before
        dz_x = hx - low_x if low_x is not None else hx
        dz_y = hy - low_y if low_y is not None else hy
        new[0].append(ca[p] * e[0][p] - magnetic_coeff * (minus_y(hz) - dz_y))
        new[1].append(ca[p] * e[1][p] - magnetic_coeff * (dz_x - minus_x(hz)))
        new[2].append(ca[p] * e[2][p] - magnetic_coeff * (minus_x(hy) - minus_y(hx)))
    return new


def scaled(cb, e):
    return [[cb[p] * e[c][p] for p in range(len(cb))] for c in range(3)]


def joined(ref, index, spans):
    return jnp.concatenate([ref[*index, lo:hi] for lo, hi in spans], axis=0)


def prepared(e, h, labels, tables):
    ca = [looked_up(m, tables[0]) for m in labels]
    cb = [looked_up(m, tables[1]) for m in labels]
    return e, h, ca, cb


def raw(seeds, material, spans):
    depth = seeds.shape[1]
    e = [[joined(seeds, (c, p), spans) for p in range(depth)] for c in range(3)]
    h = [[joined(seeds, (3 + c, p), spans) for p in range(depth)] for c in range(3)]
    return e, h, [joined(material, (p,), spans) for p in range(depth)]


def table_entries(table):
    count = table.shape[0] // 2
    rows = [table[m : m + 1] for m in range(2 * count)]
    return rows[:count], rows[count:]


def loaded(seeds, material, table, spans):
    return prepared(*raw(seeds, material, spans), table_entries(table))


NONE = (None, None)


def send_halos(sub, fields, near, far, packed=lambda planes: planes):
    odd = lax.rem(lax.axis_index(sub), 2) == 1
    e, h, ca, cb = fields
    v1 = scaled(cb, e)
    h1 = update_h(h, v1, NONE)
    e1 = update_e(e, ca, h1, NONE)
    v2 = scaled(cb, e1)
    h2 = update_h(h1, v2, NONE)
    up = (h1[0][-1], h1[1][-1], h2[0][-1], h2[1][-1], cb[-1])
    down = (v1[0][0], v1[1][0], v2[0][0], v2[1][0], cb[0])
    up, down = packed(jnp.stack(up)), packed(jnp.stack(down))
    near[...] = jnp.where(odd, down, up)
    far[...] = jnp.where(odd, up, down)


def halo_kernel(spans, sub, table, seeds, material, near, far):
    send_halos(sub, loaded(seeds, material, table, spans), near, far)


def ramp(position, count):
    position = position.astype(jnp.float32) + 0.5
    return jnp.where(
        position < BAND,
        position / BAND,
        jnp.where(position > count - BAND, (count - position) / BAND, 1.0),
    )


def final_fields(fields, near, far, sub, sub_size, unpacked=lambda planes: planes):
    e, h, ca, cb = fields
    index = lax.axis_index(sub)
    odd = lax.rem(index, 2) == 1
    below, above = index > 0, index < sub_size - 1
    a, b = near[...], far[...]
    from_below = unpacked(jnp.where(odd, a, b))
    from_above = unpacked(jnp.where(above, jnp.where(odd, b, a), 0.0))
    part_h1x, part_h1y, part_h2x, part_h2y, cb_low = from_below
    v1x_up, v1y_up, part_v2x, part_v2y, cb_up = from_above

    v1 = scaled(cb, e)
    h1 = update_h(h, v1, (v1x_up, v1y_up))
    dh1x, dh1y = -v1[1][0], v1[0][0]
    h1_low = (jnp.where(below, part_h1x + dh1x, 0.0), jnp.where(below, part_h1y + dh1y, 0.0))
    e1 = update_e(e, ca, h1, h1_low)
    v2 = scaled(cb, e1)
    v2_up = (
        part_v2x - cb_up * (magnetic_coeff * h1[1][-1]),
        part_v2y + cb_up * (magnetic_coeff * h1[0][-1]),
    )
    h2 = update_h(h1, v2, v2_up)
    dv2x = cb_low * (magnetic_coeff * dh1y)
    dv2y = cb_low * (-magnetic_coeff * dh1x)
    dv2z = cb_low * (-magnetic_coeff * (minus_x(dh1y) - minus_y(dh1x)))
    h2x_low = part_h2x + (dh1x + (plus_y(dv2z) - (v2[1][0] - dv2y)))
    h2y_low = part_h2y + (dh1y + ((v2[0][0] - dv2x) - plus_x(dv2z)))
    h2_low = (jnp.where(below, h2x_low, 0.0), jnp.where(below, h2y_low, 0.0))
    e2 = update_e(e1, ca, h2, h2_low)
    return e2 + h2


def middle_out(block):
    return rolled(block, block.shape[-1] // 2)


def y_packed(first, second):
    lane = lane_of(first.shape)
    middle = (lane >= BAND) & (lane < first.shape[-1] - BAND)
    return jnp.where(middle, middle_out(second), first)


def inner_lanes(shape):
    lane = lane_of(shape)
    return (lane >= BAND) & (lane < shape[-1] - BAND)


def y_unpacked(block):
    a, b = rolled(block, BAND), rolled(block, -BAND)
    middle = inner_lanes(block.shape)
    below = lane_of(block.shape) < BAND
    first = jnp.where(middle, 0.0, jnp.where(below, a, b))
    second = jnp.where(middle, 0.0, jnp.where(below, b, a))
    return first, second


def strip_packed(strip):
    half = strip.shape[1] // 2
    first, second = strip[:, :half], strip[:, half:]
    return jnp.where(inner_lanes(first.shape), second, middle_out(first))


def strip_of(corners, block):
    middle = inner_lanes(block.shape)
    first = jnp.where(middle, middle_out(block), corners[0])
    second = jnp.where(middle, block, corners[1])
    return jnp.concatenate([first, second], axis=1)


def low_rows(shape):
    return row_of(shape) < 4


def bands_packed(block):
    rows, lanes = block.shape[1:]
    count, width, high = rows // 2 + 4, REACH * (rows // 8), lanes - BAND
    shape = (block.shape[0], 8, lanes)
    lane = lane_of(shape)
    low = low_rows(shape)
    side = jnp.zeros(shape, block.dtype)
    for g in range(rows // 8):
        at = BAND + REACH * (g + 1)
        piece = rolled(block[:, 8 * g : 8 * g + 8], REACH * (g + 1))
        here = ((lane >= at) & (lane < at + REACH)) | (
            (lane >= at + high - BAND - REACH) & (lane < at + high - BAND)
        )
        side = jnp.where(here, piece, side)
    other = rolled(pltpu.roll(side, 4, 1), width + REACH)
    own = ((lane >= BAND) & (lane < BAND + REACH + width)) | ((lane >= high) & (lane < high + width))
    side = jnp.where(own, side, other)
    middle = (lane >= BAND) & (lane < high)
    packed = y_packed(block[:, :count], block[:, rows - count :])
    first = jnp.where(low & middle, side, packed[:, :8])
    last = jnp.where(low | middle, packed[:, count - 8 :], side)
    return jnp.concatenate([first, packed[:, 8 : count - 8], last], axis=1)


def bands_unpacked(packed):
    count, lanes = packed.shape[1:]
    rows = 2 * count - 8
    width, high = REACH * (rows // 8), lanes - BAND
    first, last = packed[:, :8], packed[:, count - 8 :]
    low = low_rows(first.shape)
    lane = lane_of(first.shape)
    middle = (lane >= BAND) & (lane < high)
    side = jnp.where(low, first, last)
    other = rolled(pltpu.roll(side, 4, 1), -width - REACH)
    side = jnp.where(low == middle, side, other)
    beside = ((lane >= BAND) & (lane < BAND + REACH)) | ((lane >= high - REACH) & (lane < high))
    moved = [rolled(packed[:, at : at + 8], lanes // 2) for at in range(0, count, 8)]
    pieces = [packed[:, at : at + 8] for at in range(0, count - 8, 8)]
    pieces += [jnp.where(low, last, moved[0])] + moved[1:]
    result = []
    for g, piece in enumerate(pieces):
        result.append(jnp.where(middle, jnp.where(beside, rolled(side, -REACH * (g + 1)), 0.0), piece))
    return jnp.concatenate(result, axis=1)


def first_kernel(span, skip, decay, coupling, seeds, material, shared, held, labels, table, entries, sems):
    size_x = held.shape[2]
    copies = []

    def fetch(source, target):
        copies.append(pltpu.make_async_copy(source, target, sems.at[len(copies)]))
        copies[-1].start()

    def fetch_rows(lo, hi):
        rows = pl.ds(lo, hi - lo)
        fetch(material.at[0, :, rows], labels.at[:, rows])
        for c in range(0, 6, 2):
            some = pl.ds(c, 2)
            fetch(seeds.at[0, some, :, rows], held.at[some, :, rows])

    fetch_rows(*span)
    early = len(copies)
    fetch(decay, entries.at[0])
    fetch(coupling, entries.at[1])
    fetch_rows(0, span[0])
    fetch_rows(span[1], size_x)
    rows = slice(span[0] + skip, span[1] - skip)
    for copy in copies[:early]:
        copy.wait()
    planes = [held[c, :, rows] for c in range(6)] + [labels[:, rows].astype(jnp.float32)]
    shared[...] = bands_packed(jnp.concatenate(planes, axis=0))
    for copy in copies[early:]:
        copy.wait()
    count = entries.shape[1]
    for k in range(2):
        for m in range(count):
            table[k * count + m : k * count + m + 1] = jnp.full((1, table.shape[1]), entries[k, m], jnp.float32)


def halo_pair_kernel(edges, inner, sub, table, seeds, material, near_edge, far_edge, near, far):
    send_halos(sub, loaded(seeds, material, table, edges), near_edge, far_edge)
    send_halos(sub, loaded(seeds, material, table, inner), near, far)


def shared_fields(table, shared):
    depth = shared.shape[0] // 7
    planes = bands_unpacked(shared[...])
    f = [planes[depth * c : depth * (c + 1)] for c in range(7)]
    return prepared(f[:3], f[3:6], f[6], table_entries(table))


def shared_halo_kernel(sub, table, shared, near, far, done):
    done[...] = jnp.zeros(done.shape, done.dtype)
    send_halos(sub, shared_fields(table, shared), near, far, bands_packed)


def weighted_planes(seeds, material, table, near, far, spans, keeps, sub, sub_size):
    planes = final_fields(loaded(seeds, material, table, spans), near, far, sub, sub_size)
    return weighted(planes, spans, keeps, *seeds.shape[2:])


def weighted(planes, spans, keeps, size_x, size_y):
    at, results = 0, []
    for (lo, hi), (start, stop) in zip(spans, keeps):
        shape = (stop - start, size_y)
        weight = ramp(row_of(shape) + start, size_x) * ramp(lane_of(shape), size_y)
        first = at + start - lo
        results.append(jnp.stack([plane[first : first + stop - start] * weight for part in planes for plane in part]))
        at += hi - lo
    return results


def edge_kernel(spans, sub, sub_size, tile, table, seeds, material, near, far, edge, corner, strip):
    size_x = seeds.shape[2]
    keeps = ((0, BAND), (size_x - BAND, size_x))
    low, high = weighted_planes(seeds, material, table, near, far, spans, keeps, sub, sub_size)
    odd = lax.rem(lax.axis_index(tile), 2) == 1
    edge[:, :BAND] = low
    edge[:, BAND:] = high
    corner[...] = y_packed(low, high)
    strip[...] = strip_packed(jnp.where(odd, high, low))


def middle_kernel(spans, sub, sub_size, tile, table, seeds, material, near, far, edge, _, mid, bands, beside):
    size_x = seeds.shape[2]
    keep = (BAND, size_x - BAND)
    odd = lax.rem(lax.axis_index(tile), 2) == 1
    beside[...] = strip_packed(jnp.where(odd, edge[:, :BAND], edge[:, BAND:]))
    planes, = weighted_planes(seeds, material, table, near, far, spans, (keep,), sub, sub_size)
    half = bands.shape[1]
    mid[...] = planes
    bands[...] = y_packed(planes[:, :half], planes[:, -half:])


def whole_kernel(spans, sub, sub_size, table, seeds, material, near, far, out):
    planes, = weighted_planes(seeds, material, table, near, far, spans, spans, sub, sub_size)
    out[...] = planes


def y_swapped(block):
    below = lane_of(block.shape) < BAND
    return jnp.where(inner_lanes(block.shape), 0.0, jnp.where(below, rolled(block, BAND), rolled(block, -BAND)))


def shared_kernel(span, size_x, sub, sub_size, table, shared, near, far, part):
    planes = final_fields(shared_fields(table, shared), near, far, sub, sub_size, bands_unpacked)
    found, = weighted(planes, (span,), (span,), size_x, part.shape[2])
    part[...] = y_swapped(found)


def corner_kernel(tile, edge, corner, summed, send):
    odd = lax.rem(lax.axis_index(tile), 2) == 1
    half = BAND // 2
    first, second = y_unpacked(corner[...])
    low = edge[:, :BAND] + first
    high = edge[:, BAND:] + second
    summed[:, :BAND] = low
    summed[:, BAND:] = high
    by, away = jnp.where(odd, low, high), jnp.where(odd, high, low)
    send[:, :half] = y_packed(by[:, :half], by[:, half:])
    send[:, half:] = y_packed(away[:, :half], away[:, half:])


def early_kernel(mid, part, out, whole, sem):
    size_x = out.shape[3]
    skip = HALO // 2
    count = part.shape[1] - 2 * skip
    start = (size_x - count) // 2
    found = mid[:, start - BAND : start - BAND + count] + part[:, skip : skip + count]
    whole[...] = found.reshape(whole.shape)
    copy = pltpu.make_async_copy(whole, out.at[0, :, :, pl.ds(start, count)], sem)
    copy.start()
    copy.wait()


def late_kernel(tile, mid, bands, summed, strip, beside, low, high):
    odd = lax.rem(lax.axis_index(tile), 2) == 1
    half = bands.shape[1]
    first, second = y_unpacked(bands[...])
    nothing = (jnp.zeros(strip.shape, jnp.float32),) * 2
    by, away = strip_of(nothing, beside[...]), strip_of(nothing, strip[...])

    def by_component(rows):
        return rows.reshape(*low.shape[:2], *rows.shape[1:])

    low[:, :, BAND:] = by_component(mid[:, :half] + first)
    high[:, :, :half] = by_component(mid[:, -half:] + second)
    low[:, :, :BAND] = by_component(summed[:, :BAND] + jnp.where(odd, by, away))
    high[:, :, half:] = by_component(summed[:, BAND:] + jnp.where(odd, away, by))


def last_kernel(tile, low, high, got, _, out, edges, sems):
    odd = lax.rem(lax.axis_index(tile), 2) == 1
    size_x, count = out.shape[3], low.shape[2]
    half, quarter = count - BAND, BAND // 2
    copies = []

    def write(source, start, rows):
        target = out.at[0, :, :, pl.ds(start, rows)]
        copies.append(pltpu.make_async_copy(source, target, sems.at[len(copies)]))
        copies[-1].start()

    write(low.at[:, :, pl.ds(BAND, half)], BAND, half)
    write(high.at[:, :, pl.ds(0, half)], size_x - count, half)
    straight = got[:, :quarter]
    middle = inner_lanes(straight.shape)
    by = jnp.where(middle, 0.0, straight), jnp.where(middle, 0.0, middle_out(straight))
    by = jnp.concatenate(by, axis=1)
    away = jnp.concatenate(y_unpacked(got[:, quarter:]), axis=1)
    shape = edges.shape[1:]
    edges[0] = low[:, :, :BAND] + jnp.where(odd, by, away).reshape(shape)
    write(edges.at[0], 0, BAND)
    edges[1] = high[:, :, half:] + jnp.where(odd, away, by).reshape(shape)
    write(edges.at[1], size_x - BAND, BAND)
    for copy in copies:
        copy.wait()


HBM = pl.BlockSpec(memory_space=pltpu.HBM)
VMEM = pl.BlockSpec(memory_space=pltpu.VMEM)
PARAMS = pltpu.CompilerParams(vmem_limit_bytes=32 * 1024 * 1024)


def cost(flops):
    return pl.CostEstimate(flops=flops, bytes_accessed=0, transcendentals=0)


def called(kernel, shapes, *operands, flops=0):
    outs = [jax.ShapeDtypeStruct(shape, jnp.float32) for shape in shapes]
    return pl.pallas_call(
        kernel,
        out_shape=outs,
        in_specs=[VMEM] * len(operands),
        out_specs=[VMEM] * len(outs),
        compiler_params=PARAMS,
        cost_estimate=cost(flops),
    )(*operands)


def after(first, *values):
    return lax.optimization_barrier((first, *values))


def near_exchange(near, sub_size):
    return lax.ppermute(near, "sub", [(i, i ^ 1) for i in range(sub_size)])


def far_exchange(far, sub_size, tile_size):
    pairs = []
    for t in range(tile_size):
        for i in range(sub_size):
            j = ((i + 1) ^ 1) - 1
            other = (t, j) if 0 <= j < sub_size else (t ^ 1, i)
            pairs.append((t * sub_size + i, other[0] * sub_size + other[1]))
    return lax.ppermute(far, ("tile", "sub"), pairs)


def swapped(value, bits, tile_size):
    return lax.ppermute(value, "tile", [(t, t ^ bits) for t in range(tile_size)])


def from_behind(value, steps, count):
    return lax.ppermute(value, "tile", [(t, (t + steps) % count) for t in range(count)])


def table_rows(decay, coupling, size_y):
    entries = jnp.concatenate([decay, coupling])
    return jnp.broadcast_to(entries[:, None], (entries.shape[0], size_y))


def two_by_two(seeds, material, decay, coupling, sub_size, tile_size):
    depth, size_x, size_y = seeds.shape[2:]
    planes = 6 * depth
    edges = ((0, BAND + HALO), (size_x - BAND - HALO, size_x))
    inner = ((BAND - HALO, size_x - BAND + HALO),)
    keep = ((size_x - SHARED) // 2, (size_x + SHARED) // 2)
    span = (keep[0] - HALO // 2, keep[1] + HALO // 2)
    fetched = (keep[0] - HALO, keep[1] + HALO)
    rows = size_x - 2 * BAND
    edge_rows, inner_rows = 2 * (BAND + HALO), rows + 2 * HALO
    packed_rows = (SHARED + HALO) // 2 + 4
    whole = jax.ShapeDtypeStruct(seeds.shape, jnp.float32)

    shared, seeds, material, table = pl.pallas_call(
        functools.partial(first_kernel, fetched, HALO // 2),
        out_shape=[
            jax.ShapeDtypeStruct((7 * depth, packed_rows, size_y), jnp.float32),
            jax.ShapeDtypeStruct(seeds.shape[1:], jnp.float32),
            jax.ShapeDtypeStruct(material.shape[1:], jnp.int32),
            jax.ShapeDtypeStruct((2 * decay.shape[0], size_y), jnp.float32),
        ],
        in_specs=[HBM] * 4,
        out_specs=[VMEM] * 4,
        scratch_shapes=[pltpu.SMEM((2, *decay.shape), jnp.float32), pltpu.SemaphoreType.DMA((14,))],
        compiler_params=PARAMS,
        cost_estimate=cost(0),
    )(*(pltpu.with_memory_space_constraint(x, pltpu.HBM) for x in (decay, coupling, seeds, material)))
    shared = swapped(shared, 2, tile_size)
    edge_near, edge_far, inner_near, inner_far = called(
        functools.partial(halo_pair_kernel, edges, inner, "sub"),
        [(PLANES, edge_rows, size_y)] * 2 + [(PLANES, inner_rows, size_y)] * 2, table, seeds, material,
    )
    edge_near, inner_near = near_exchange(edge_near, sub_size), near_exchange(inner_near, sub_size)
    edge_far = far_exchange(edge_far, sub_size, tile_size)
    inner_far = far_exchange(inner_far, sub_size, tile_size)

    edge, corner, strip = called(
        functools.partial(edge_kernel, edges, "sub", sub_size, "tile"),
        [(planes, 2 * BAND, size_y), (planes, BAND, size_y), (planes, BAND // 2, size_y)],
        table, seeds, material, edge_near, edge_far,
    )
    corner = swapped(corner, 2, tile_size)
    strip = swapped(strip, 3, tile_size)

    shape = (PLANES, packed_rows, size_y)
    shared_near, shared_far, done = called(
        functools.partial(shared_halo_kernel, "sub"), [shape, shape, (8, size_y)], table, shared, flops=LARGE
    )
    shared_near = near_exchange(shared_near, sub_size)
    shared_far = far_exchange(shared_far, sub_size, tile_size)

    mid, bands, beside = called(
        functools.partial(middle_kernel, inner, "sub", sub_size, "tile"),
        [(planes, rows, size_y), (planes, (rows - SHARED) // 2, size_y), (planes, BAND // 2, size_y)],
        table, seeds, material, inner_near, inner_far, edge, done,
    )
    bands = swapped(bands, 2, tile_size)
    beside = swapped(beside, 1, tile_size)

    corner, strip, mid = after(corner, strip, mid)
    summed, send = called(
        functools.partial(corner_kernel, "tile"), [(planes, 2 * BAND, size_y), (planes, BAND, size_y)],
        edge, corner, flops=SMALL,
    )
    got = swapped(send, 1, tile_size)
    beside, shared_near = after(beside, shared_near)
    part, = called(
        functools.partial(shared_kernel, span, size_x, "sub", sub_size),
        [(planes, SHARED + HALO, size_y)], table, shared, shared_near, shared_far, flops=MEDIUM,
    )
    early = pl.pallas_call(
        early_kernel,
        out_shape=whole,
        in_specs=[VMEM] * 2,
        out_specs=HBM,
        scratch_shapes=[pltpu.VMEM((6, depth, SHARED, size_y), jnp.float32), pltpu.SemaphoreType.DMA],
        compiler_params=PARAMS,
        cost_estimate=cost(0),
    )(mid, part)
    low, high = called(
        functools.partial(late_kernel, "tile"), [(6, depth, (size_x - SHARED) // 2, size_y)] * 2,
        mid, bands, summed, strip, beside,
    )
    return pl.pallas_call(
        functools.partial(last_kernel, "tile"),
        out_shape=whole,
        in_specs=[VMEM] * 3 + [HBM],
        out_specs=HBM,
        scratch_shapes=[pltpu.VMEM((2, 6, depth, BAND, size_y), jnp.float32), pltpu.SemaphoreType.DMA((4,))],
        input_output_aliases={3: 0},
        compiler_params=PARAMS,
        cost_estimate=cost(0),
    )(low, high, got, early)


def any_lattice(seeds, material, decay, coupling, sub_size, tile_size):
    depth, size_x, size_y = seeds.shape[2:]
    seeds, material = seeds[0], material[0]
    spans = ((0, size_x),)
    table = table_rows(decay, coupling, size_y)
    shape = (PLANES, size_x, size_y)
    near, far = called(functools.partial(halo_kernel, spans, "sub"), [shape, shape], table, seeds, material)
    near = near_exchange(near, sub_size)
    far = far_exchange(far, sub_size, tile_size)
    weighted, = called(
        functools.partial(whole_kernel, spans, "sub", sub_size), [(6 * depth, size_x, size_y)],
        table, seeds, material, near, far,
    )
    weighted = weighted.reshape(6, depth, size_x, size_y)
    side = math.isqrt(tile_size)
    prev_band = from_behind(weighted[:, :, size_x - BAND :, :], 1, tile_size)
    next_band = from_behind(weighted[:, :, :BAND, :], -1, tile_size)
    combined = weighted.at[:, :, :BAND, :].add(prev_band)
    combined = combined.at[:, :, size_x - BAND :, :].add(next_band)
    flat = (6, depth, size_x * BAND // size_y, size_y)
    thin = (6, depth, size_x, BAND)
    top_slab = combined[..., size_y - BAND :].reshape(flat)
    bottom_slab = combined[..., :BAND].reshape(flat)
    result = combined.at[..., :BAND].add(from_behind(top_slab, side, tile_size).reshape(thin))
    result = result.at[..., size_y - BAND :].add(from_behind(bottom_slab, -side, tile_size).reshape(thin))
    return result[None]


def solution(mesh):
    sub_size, tile_size = mesh.shape["sub"], mesh.shape["tile"]
    body = two_by_two if tile_size == 4 else any_lattice

    def on_device(seeds, material, decay, coupling):
        return body(seeds, material, decay, coupling, sub_size, tile_size)

    placed = (P("tile", None, "sub", None, None), P("tile", "sub", None, None), P(), P())
    return jax.shard_map(
        on_device,
        mesh=mesh,
        in_specs=placed,
        out_specs=P("tile", None, "sub", None, None),
        check_vma=False,
    )
```

```python
import functools
import math

import jax
import jax.numpy as jnp
from jax import lax
from jax.experimental import pallas as pl
from jax.experimental.pallas import tpu as pltpu
from jax.sharding import PartitionSpec as P

BAND = 32
HALO = 8
PLANES = 5
REACH = 2
SHARED = 96
LARGE, MEDIUM, SMALL = 10**10, 2 * 10**9, 0

magnetic_coeff = 0.5


def lane_of(shape):
    return lax.broadcasted_iota(jnp.int32, shape, len(shape) - 1)


def row_of(shape):
    return lax.broadcasted_iota(jnp.int32, shape, len(shape) - 2)


def rolled(v, shift):
    return pltpu.roll(v, shift % v.shape[-1], v.ndim - 1)


def next_x(v):
    rows = v.shape[0]
    return jnp.where(row_of(v.shape) == rows - 1, 0.0, pltpu.roll(v, rows - 1, 0))


def prev_x(v):
    return jnp.where(row_of(v.shape) == 0, 0.0, pltpu.roll(v, 1, 0))


def next_y(v):
    lanes = v.shape[1]
    return jnp.where(lane_of(v.shape) == lanes - 1, 0.0, pltpu.roll(v, lanes - 1, 1))


def prev_y(v):
    return jnp.where(lane_of(v.shape) == 0, 0.0, pltpu.roll(v, 1, 1))


def plus_x(v):
    return next_x(v) - v


def plus_y(v):
    return next_y(v) - v


def minus_x(v):
    return v - prev_x(v)


def minus_y(v):
    return v - prev_y(v)


def looked_up(labels, entries):
    value = jnp.broadcast_to(entries[0], labels.shape)
    for m in range(1, len(entries)):
        value = jnp.where(labels == m, entries[m], value)
    return value


def update_h(h, v, v_after):
    depth = len(v[0])
    new = [[], [], []]
    for p in range(depth):
        vx, vy, vz = v[0][p], v[1][p], v[2][p]
        up_x, up_y = (v[0][p + 1], v[1][p + 1]) if p + 1 < depth else v_after
        dz_x = up_x - vx if up_x is not None else -vx
        dz_y = up_y - vy if up_y is not None else -vy
        new[0].append(h[0][p] + (plus_y(vz) - dz_y))
        new[1].append(h[1][p] + (dz_x - plus_x(vz)))
        new[2].append(h[2][p] + (plus_x(vy) - plus_y(vx)))
    return new


def update_e(e, ca, h, h_before):
    depth = len(h[0])
    new = [[], [], []]
    for p in range(depth):
        hx, hy, hz = h[0][p], h[1][p], h[2][p]
        low_x, low_y = (h[0][p - 1], h[1][p - 1]) if p > 0 else h_before
        dz_x = hx - low_x if low_x is not None else hx
        dz_y = hy - low_y if low_y is not None else hy
        new[0].append(ca[p] * e[0][p] - magnetic_coeff * (minus_y(hz) - dz_y))
        new[1].append(ca[p] * e[1][p] - magnetic_coeff * (dz_x - minus_x(hz)))
        new[2].append(ca[p] * e[2][p] - magnetic_coeff * (minus_x(hy) - minus_y(hx)))
    return new


def scaled(cb, e):
    return [[cb[p] * e[c][p] for p in range(len(cb))] for c in range(3)]


def joined(ref, index, spans):
    return jnp.concatenate([ref[*index, lo:hi] for lo, hi in spans], axis=0)


def prepared(e, h, labels, tables):
    ca = [looked_up(m, tables[0]) for m in labels]
    cb = [looked_up(m, tables[1]) for m in labels]
    return e, h, ca, cb


def raw(seeds, material, spans):
    depth = seeds.shape[1]
    e = [[joined(seeds, (c, p), spans) for p in range(depth)] for c in range(3)]
    h = [[joined(seeds, (3 + c, p), spans) for p in range(depth)] for c in range(3)]
    return e, h, [joined(material, (p,), spans) for p in range(depth)]


def table_entries(table):
    count = table.shape[0] // 2
    rows = [table[m : m + 1] for m in range(2 * count)]
    return rows[:count], rows[count:]


def loaded(seeds, material, table, spans):
    return prepared(*raw(seeds, material, spans), table_entries(table))


NONE = (None, None)


def send_halos(sub, fields, near, far, packed=lambda planes: planes):
    odd = lax.rem(lax.axis_index(sub), 2) == 1
    e, h, ca, cb = fields
    v1 = scaled(cb, e)
    h1 = update_h(h, v1, NONE)
    e1 = update_e(e, ca, h1, NONE)
    v2 = scaled(cb, e1)
    h2 = update_h(h1, v2, NONE)
    up = (h1[0][-1], h1[1][-1], h2[0][-1], h2[1][-1], cb[-1])
    down = (v1[0][0], v1[1][0], v2[0][0], v2[1][0], cb[0])
    up, down = packed(jnp.stack(up)), packed(jnp.stack(down))
    near[...] = jnp.where(odd, down, up)
    far[...] = jnp.where(odd, up, down)


def halo_kernel(spans, sub, table, seeds, material, *rest):
    near, far = rest[-2:]
    send_halos(sub, loaded(seeds, material, table, spans), near, far)


def ramp(position, count):
    position = position.astype(jnp.float32) + 0.5
    return jnp.where(
        position < BAND,
        position / BAND,
        jnp.where(position > count - BAND, (count - position) / BAND, 1.0),
    )


def final_fields(fields, near, far, sub, sub_size, unpacked=lambda planes: planes):
    e, h, ca, cb = fields
    index = lax.axis_index(sub)
    odd = lax.rem(index, 2) == 1
    below, above = index > 0, index < sub_size - 1
    a, b = near[...], far[...]
    from_below = unpacked(jnp.where(odd, a, b))
    from_above = unpacked(jnp.where(above, jnp.where(odd, b, a), 0.0))
    part_h1x, part_h1y, part_h2x, part_h2y, cb_low = from_below
    v1x_up, v1y_up, part_v2x, part_v2y, cb_up = from_above

    v1 = scaled(cb, e)
    h1 = update_h(h, v1, (v1x_up, v1y_up))
    dh1x, dh1y = -v1[1][0], v1[0][0]
    h1_low = (jnp.where(below, part_h1x + dh1x, 0.0), jnp.where(below, part_h1y + dh1y, 0.0))
    e1 = update_e(e, ca, h1, h1_low)
    v2 = scaled(cb, e1)
    v2_up = (
        part_v2x - cb_up * (magnetic_coeff * h1[1][-1]),
        part_v2y + cb_up * (magnetic_coeff * h1[0][-1]),
    )
    h2 = update_h(h1, v2, v2_up)
    dv2x = cb_low * (magnetic_coeff * dh1y)
    dv2y = cb_low * (-magnetic_coeff * dh1x)
    dv2z = cb_low * (-magnetic_coeff * (minus_x(dh1y) - minus_y(dh1x)))
    h2x_low = part_h2x + (dh1x + (plus_y(dv2z) - (v2[1][0] - dv2y)))
    h2y_low = part_h2y + (dh1y + ((v2[0][0] - dv2x) - plus_x(dv2z)))
    h2_low = (jnp.where(below, h2x_low, 0.0), jnp.where(below, h2y_low, 0.0))
    e2 = update_e(e1, ca, h2, h2_low)
    return e2 + h2


def middle_out(block):
    return rolled(block, block.shape[-1] // 2)


def y_packed(first, second):
    lane = lane_of(first.shape)
    middle = (lane >= BAND) & (lane < first.shape[-1] - BAND)
    return jnp.where(middle, middle_out(second), first)


def inner_lanes(shape):
    lane = lane_of(shape)
    return (lane >= BAND) & (lane < shape[-1] - BAND)


def y_unpacked(block):
    a, b = rolled(block, BAND), rolled(block, -BAND)
    middle = inner_lanes(block.shape)
    below = lane_of(block.shape) < BAND
    first = jnp.where(middle, 0.0, jnp.where(below, a, b))
    second = jnp.where(middle, 0.0, jnp.where(below, b, a))
    return first, second


def strip_packed(strip):
    half = strip.shape[1] // 2
    first, second = strip[:, :half], strip[:, half:]
    return jnp.where(inner_lanes(first.shape), second, middle_out(first))


def strip_of(corners, block):
    middle = inner_lanes(block.shape)
    first = jnp.where(middle, middle_out(block), corners[0])
    second = jnp.where(middle, block, corners[1])
    return jnp.concatenate([first, second], axis=1)


def low_rows(shape):
    return row_of(shape) < 4


def bands_packed(block):
    rows, lanes = block.shape[1:]
    count, width, high = rows // 2 + 4, REACH * (rows // 8), lanes - BAND
    shape = (block.shape[0], 8, lanes)
    lane = lane_of(shape)
    low = low_rows(shape)
    side = jnp.zeros(shape, block.dtype)
    for g in range(rows // 8):
        at = BAND + REACH * (g + 1)
        piece = rolled(block[:, 8 * g : 8 * g + 8], REACH * (g + 1))
        here = ((lane >= at) & (lane < at + REACH)) | (
            (lane >= at + high - BAND - REACH) & (lane < at + high - BAND)
        )
        side = jnp.where(here, piece, side)
    other = rolled(pltpu.roll(side, 4, 1), width + REACH)
    own = ((lane >= BAND) & (lane < BAND + REACH + width)) | ((lane >= high) & (lane < high + width))
    side = jnp.where(own, side, other)
    middle = (lane >= BAND) & (lane < high)
    packed = y_packed(block[:, :count], block[:, rows - count :])
    first = jnp.where(low & middle, side, packed[:, :8])
    last = jnp.where(low | middle, packed[:, count - 8 :], side)
    return jnp.concatenate([first, packed[:, 8 : count - 8], last], axis=1)


def bands_unpacked(packed):
    count, lanes = packed.shape[1:]
    rows = 2 * count - 8
    width, high = REACH * (rows // 8), lanes - BAND
    first, last = packed[:, :8], packed[:, count - 8 :]
    low = low_rows(first.shape)
    lane = lane_of(first.shape)
    middle = (lane >= BAND) & (lane < high)
    side = jnp.where(low, first, last)
    other = rolled(pltpu.roll(side, 4, 1), -width - REACH)
    side = jnp.where(low == middle, side, other)
    beside = ((lane >= BAND) & (lane < BAND + REACH)) | ((lane >= high - REACH) & (lane < high))
    moved = [rolled(packed[:, at : at + 8], lanes // 2) for at in range(0, count, 8)]
    pieces = [packed[:, at : at + 8] for at in range(0, count - 8, 8)]
    pieces += [jnp.where(low, last, moved[0])] + moved[1:]
    result = []
    for g, piece in enumerate(pieces):
        result.append(jnp.where(middle, jnp.where(beside, rolled(side, -REACH * (g + 1)), 0.0), piece))
    return jnp.concatenate(result, axis=1)


def first_kernel(span, skip, decay, coupling, seeds, material, shared, held, labels, table, entries, sems):
    size_x = held.shape[2]
    copies = []

    def fetch(source, target):
        copies.append(pltpu.make_async_copy(source, target, sems.at[len(copies)]))
        copies[-1].start()

    def fetch_rows(lo, hi):
        rows = pl.ds(lo, hi - lo)
        fetch(material.at[0, :, rows], labels.at[:, rows])
        for c in range(0, 6, 2):
            some = pl.ds(c, 2)
            fetch(seeds.at[0, some, :, rows], held.at[some, :, rows])

    fetch_rows(*span)
    early = len(copies)
    fetch(decay, entries.at[0])
    fetch(coupling, entries.at[1])
    fetch_rows(0, span[0])
    fetch_rows(span[1], size_x)
    rows = slice(span[0] + skip, span[1] - skip)
    for copy in copies[:early]:
        copy.wait()
    planes = [held[c, :, rows] for c in range(6)] + [labels[:, rows].astype(jnp.float32)]
    shared[...] = bands_packed(jnp.concatenate(planes, axis=0))
    for copy in copies[early:]:
        copy.wait()
    count = entries.shape[1]
    for k in range(2):
        for m in range(count):
            table[k * count + m : k * count + m + 1] = jnp.full((1, table.shape[1]), entries[k, m], jnp.float32)


def shared_fields(table, shared):
    depth = shared.shape[0] // 7
    planes = bands_unpacked(shared[...])
    f = [planes[depth * c : depth * (c + 1)] for c in range(7)]
    return prepared(f[:3], f[3:6], f[6], table_entries(table))


def shared_halo_kernel(sub, table, shared, near, far, done):
    done[...] = jnp.zeros(done.shape, done.dtype)
    send_halos(sub, shared_fields(table, shared), near, far, bands_packed)


def weighted_planes(seeds, material, table, near, far, spans, keeps, sub, sub_size):
    planes = final_fields(loaded(seeds, material, table, spans), near, far, sub, sub_size)
    return weighted(planes, spans, keeps, *seeds.shape[2:])


def weighted(planes, spans, keeps, size_x, size_y):
    at, results = 0, []
    for (lo, hi), (start, stop) in zip(spans, keeps):
        shape = (stop - start, size_y)
        weight = ramp(row_of(shape) + start, size_x) * ramp(lane_of(shape), size_y)
        first = at + start - lo
        results.append(jnp.stack([plane[first : first + stop - start] * weight for part in planes for plane in part]))
        at += hi - lo
    return results


def edge_kernel(spans, sub, sub_size, tile, table, seeds, material, near, far, edge, corner, strip):
    size_x = seeds.shape[2]
    keeps = ((0, BAND), (size_x - BAND, size_x))
    low, high = weighted_planes(seeds, material, table, near, far, spans, keeps, sub, sub_size)
    odd = lax.rem(lax.axis_index(tile), 2) == 1
    edge[:, :BAND] = low
    edge[:, BAND:] = high
    corner[...] = y_packed(low, high)
    strip[...] = strip_packed(jnp.where(odd, high, low))


def middle_kernel(spans, sub, sub_size, tile, table, seeds, material, near, far, edge, _, mid, bands, beside):
    size_x = seeds.shape[2]
    keep = (BAND, size_x - BAND)
    odd = lax.rem(lax.axis_index(tile), 2) == 1
    beside[...] = strip_packed(jnp.where(odd, edge[:, :BAND], edge[:, BAND:]))
    planes, = weighted_planes(seeds, material, table, near, far, spans, (keep,), sub, sub_size)
    half = bands.shape[1]
    mid[...] = planes
    bands[...] = y_packed(planes[:, :half], planes[:, -half:])


def whole_kernel(spans, sub, sub_size, table, seeds, material, near, far, out):
    planes, = weighted_planes(seeds, material, table, near, far, spans, spans, sub, sub_size)
    out[...] = planes


def y_swapped(block):
    below = lane_of(block.shape) < BAND
    return jnp.where(inner_lanes(block.shape), 0.0, jnp.where(below, rolled(block, BAND), rolled(block, -BAND)))


def shared_kernel(span, size_x, sub, sub_size, table, shared, near, far, part):
    planes = final_fields(shared_fields(table, shared), near, far, sub, sub_size, bands_unpacked)
    found, = weighted(planes, (span,), (span,), size_x, part.shape[2])
    part[...] = y_swapped(found)


def corner_kernel(tile, edge, corner, summed, send):
    odd = lax.rem(lax.axis_index(tile), 2) == 1
    half = BAND // 2
    first, second = y_unpacked(corner[...])
    low = edge[:, :BAND] + first
    high = edge[:, BAND:] + second
    summed[:, :BAND] = low
    summed[:, BAND:] = high
    by, away = jnp.where(odd, low, high), jnp.where(odd, high, low)
    send[:, :half] = y_packed(by[:, :half], by[:, half:])
    send[:, half:] = y_packed(away[:, :half], away[:, half:])


def early_kernel(mid, part, out, whole, sem):
    size_x = out.shape[3]
    skip = HALO // 2
    count = part.shape[1] - 2 * skip
    start = (size_x - count) // 2
    found = mid[:, start - BAND : start - BAND + count] + part[:, skip : skip + count]
    whole[...] = found.reshape(whole.shape)
    copy = pltpu.make_async_copy(whole, out.at[0, :, :, pl.ds(start, count)], sem)
    copy.start()
    copy.wait()


def late_kernel(tile, mid, bands, summed, strip, beside, low, high):
    odd = lax.rem(lax.axis_index(tile), 2) == 1
    half = bands.shape[1]
    first, second = y_unpacked(bands[...])
    nothing = (jnp.zeros(strip.shape, jnp.float32),) * 2
    by, away = strip_of(nothing, beside[...]), strip_of(nothing, strip[...])

    def by_component(rows):
        return rows.reshape(*low.shape[:2], *rows.shape[1:])

    low[:, :, BAND:] = by_component(mid[:, :half] + first)
    high[:, :, :half] = by_component(mid[:, -half:] + second)
    low[:, :, :BAND] = by_component(summed[:, :BAND] + jnp.where(odd, by, away))
    high[:, :, half:] = by_component(summed[:, BAND:] + jnp.where(odd, away, by))


def last_kernel(tile, low, high, got, _, out, edges, sems):
    odd = lax.rem(lax.axis_index(tile), 2) == 1
    size_x, count = out.shape[3], low.shape[2]
    half, quarter = count - BAND, BAND // 2
    copies = []

    def write(source, start, rows):
        target = out.at[0, :, :, pl.ds(start, rows)]
        copies.append(pltpu.make_async_copy(source, target, sems.at[len(copies)]))
        copies[-1].start()

    write(low.at[:, :, pl.ds(BAND, half)], BAND, half)
    write(high.at[:, :, pl.ds(0, half)], size_x - count, half)
    straight = got[:, :quarter]
    middle = inner_lanes(straight.shape)
    by = jnp.where(middle, 0.0, straight), jnp.where(middle, 0.0, middle_out(straight))
    by = jnp.concatenate(by, axis=1)
    away = jnp.concatenate(y_unpacked(got[:, quarter:]), axis=1)
    shape = edges.shape[1:]
    edges[0] = low[:, :, :BAND] + jnp.where(odd, by, away).reshape(shape)
    write(edges.at[0], 0, BAND)
    edges[1] = high[:, :, half:] + jnp.where(odd, away, by).reshape(shape)
    write(edges.at[1], size_x - BAND, BAND)
    for copy in copies:
        copy.wait()


HBM = pl.BlockSpec(memory_space=pltpu.HBM)
VMEM = pl.BlockSpec(memory_space=pltpu.VMEM)
PARAMS = pltpu.CompilerParams(vmem_limit_bytes=32 * 1024 * 1024)


def cost(flops):
    return pl.CostEstimate(flops=flops, bytes_accessed=0, transcendentals=0)


def called(kernel, shapes, *operands, flops=0):
    outs = [jax.ShapeDtypeStruct(shape, jnp.float32) for shape in shapes]
    return pl.pallas_call(
        kernel,
        out_shape=outs,
        in_specs=[VMEM] * len(operands),
        out_specs=[VMEM] * len(outs),
        compiler_params=PARAMS,
        cost_estimate=cost(flops),
    )(*operands)


def after(first, *values):
    return lax.optimization_barrier((first, *values))


def near_exchange(near, sub_size):
    return lax.ppermute(near, "sub", [(i, i ^ 1) for i in range(sub_size)])


def far_exchange(far, sub_size, tile_size):
    pairs = []
    for t in range(tile_size):
        for i in range(sub_size):
            j = ((i + 1) ^ 1) - 1
            other = (t, j) if 0 <= j < sub_size else (t ^ 1, i)
            pairs.append((t * sub_size + i, other[0] * sub_size + other[1]))
    return lax.ppermute(far, ("tile", "sub"), pairs)


def swapped(value, bits, tile_size):
    return lax.ppermute(value, "tile", [(t, t ^ bits) for t in range(tile_size)])


def from_behind(value, steps, count):
    return lax.ppermute(value, "tile", [(t, (t + steps) % count) for t in range(count)])


def table_rows(decay, coupling, size_y):
    entries = jnp.concatenate([decay, coupling])
    return jnp.broadcast_to(entries[:, None], (entries.shape[0], size_y))


def two_by_two(seeds, material, decay, coupling, sub_size, tile_size):
    depth, size_x, size_y = seeds.shape[2:]
    planes = 6 * depth
    edges = ((0, BAND + HALO), (size_x - BAND - HALO, size_x))
    inner = ((BAND - HALO, size_x - BAND + HALO),)
    keep = ((size_x - SHARED) // 2, (size_x + SHARED) // 2)
    span = (keep[0] - HALO // 2, keep[1] + HALO // 2)
    fetched = (keep[0] - HALO, keep[1] + HALO)
    rows = size_x - 2 * BAND
    edge_rows, inner_rows = 2 * (BAND + HALO), rows + 2 * HALO
    packed_rows = (SHARED + HALO) // 2 + 4
    whole = jax.ShapeDtypeStruct(seeds.shape, jnp.float32)

    shared, seeds, material, table = pl.pallas_call(
        functools.partial(first_kernel, fetched, HALO // 2),
        out_shape=[
            jax.ShapeDtypeStruct((7 * depth, packed_rows, size_y), jnp.float32),
            jax.ShapeDtypeStruct(seeds.shape[1:], jnp.float32),
            jax.ShapeDtypeStruct(material.shape[1:], jnp.int32),
            jax.ShapeDtypeStruct((2 * decay.shape[0], size_y), jnp.float32),
        ],
        in_specs=[HBM] * 4,
        out_specs=[VMEM] * 4,
        scratch_shapes=[pltpu.SMEM((2, *decay.shape), jnp.float32), pltpu.SemaphoreType.DMA((14,))],
        compiler_params=PARAMS,
        cost_estimate=cost(0),
    )(*(pltpu.with_memory_space_constraint(x, pltpu.HBM) for x in (decay, coupling, seeds, material)))
    shared = swapped(shared, 2, tile_size)
    edge_near, edge_far = called(
        functools.partial(halo_kernel, edges, "sub"), [(PLANES, edge_rows, size_y)] * 2, table, seeds, material
    )
    inner_near, inner_far = called(
        functools.partial(halo_kernel, inner, "sub"), [(PLANES, inner_rows, size_y)] * 2,
        table, seeds, material, edge_near,
    )
    edge_near, inner_near = near_exchange(edge_near, sub_size), near_exchange(inner_near, sub_size)
    edge_far = far_exchange(edge_far, sub_size, tile_size)
    inner_far = far_exchange(inner_far, sub_size, tile_size)

    edge, corner, strip = called(
        functools.partial(edge_kernel, edges, "sub", sub_size, "tile"),
        [(planes, 2 * BAND, size_y), (planes, BAND, size_y), (planes, BAND // 2, size_y)],
        table, seeds, material, edge_near, edge_far,
    )
    corner = swapped(corner, 2, tile_size)
    strip = swapped(strip, 3, tile_size)

    shape = (PLANES, packed_rows, size_y)
    shared_near, shared_far, done = called(
        functools.partial(shared_halo_kernel, "sub"), [shape, shape, (8, size_y)], table, shared, flops=LARGE
    )
    shared_near = near_exchange(shared_near, sub_size)
    shared_far = far_exchange(shared_far, sub_size, tile_size)

    mid, bands, beside = called(
        functools.partial(middle_kernel, inner, "sub", sub_size, "tile"),
        [(planes, rows, size_y), (planes, (rows - SHARED) // 2, size_y), (planes, BAND // 2, size_y)],
        table, seeds, material, inner_near, inner_far, edge, done,
    )
    bands = swapped(bands, 2, tile_size)
    beside = swapped(beside, 1, tile_size)

    corner, strip, mid = after(corner, strip, mid)
    summed, send = called(
        functools.partial(corner_kernel, "tile"), [(planes, 2 * BAND, size_y), (planes, BAND, size_y)],
        edge, corner, flops=SMALL,
    )
    got = swapped(send, 1, tile_size)
    beside, shared_near = after(beside, shared_near)
    part, = called(
        functools.partial(shared_kernel, span, size_x, "sub", sub_size),
        [(planes, SHARED + HALO, size_y)], table, shared, shared_near, shared_far, flops=MEDIUM,
    )
    early = pl.pallas_call(
        early_kernel,
        out_shape=whole,
        in_specs=[VMEM] * 2,
        out_specs=HBM,
        scratch_shapes=[pltpu.VMEM((6, depth, SHARED, size_y), jnp.float32), pltpu.SemaphoreType.DMA],
        compiler_params=PARAMS,
        cost_estimate=cost(0),
    )(mid, part)
    low, high = called(
        functools.partial(late_kernel, "tile"), [(6, depth, (size_x - SHARED) // 2, size_y)] * 2,
        mid, bands, summed, strip, beside,
    )
    return pl.pallas_call(
        functools.partial(last_kernel, "tile"),
        out_shape=whole,
        in_specs=[VMEM] * 3 + [HBM],
        out_specs=HBM,
        scratch_shapes=[pltpu.VMEM((2, 6, depth, BAND, size_y), jnp.float32), pltpu.SemaphoreType.DMA((4,))],
        input_output_aliases={3: 0},
        compiler_params=PARAMS,
        cost_estimate=cost(0),
    )(low, high, got, early)


def any_lattice(seeds, material, decay, coupling, sub_size, tile_size):
    depth, size_x, size_y = seeds.shape[2:]
    seeds, material = seeds[0], material[0]
    spans = ((0, size_x),)
    table = table_rows(decay, coupling, size_y)
    shape = (PLANES, size_x, size_y)
    near, far = called(functools.partial(halo_kernel, spans, "sub"), [shape, shape], table, seeds, material)
    near = near_exchange(near, sub_size)
    far = far_exchange(far, sub_size, tile_size)
    weighted, = called(
        functools.partial(whole_kernel, spans, "sub", sub_size), [(6 * depth, size_x, size_y)],
        table, seeds, material, near, far,
    )
    weighted = weighted.reshape(6, depth, size_x, size_y)
    side = math.isqrt(tile_size)
    prev_band = from_behind(weighted[:, :, size_x - BAND :, :], 1, tile_size)
    next_band = from_behind(weighted[:, :, :BAND, :], -1, tile_size)
    combined = weighted.at[:, :, :BAND, :].add(prev_band)
    combined = combined.at[:, :, size_x - BAND :, :].add(next_band)
    flat = (6, depth, size_x * BAND // size_y, size_y)
    thin = (6, depth, size_x, BAND)
    top_slab = combined[..., size_y - BAND :].reshape(flat)
    bottom_slab = combined[..., :BAND].reshape(flat)
    result = combined.at[..., :BAND].add(from_behind(top_slab, side, tile_size).reshape(thin))
    result = result.at[..., size_y - BAND :].add(from_behind(bottom_slab, -side, tile_size).reshape(thin))
    return result[None]


def solution(mesh):
    sub_size, tile_size = mesh.shape["sub"], mesh.shape["tile"]
    body = two_by_two if tile_size == 4 else any_lattice

    def on_device(seeds, material, decay, coupling):
        return body(seeds, material, decay, coupling, sub_size, tile_size)

    placed = (P("tile", None, "sub", None, None), P("tile", "sub", None, None), P(), P())
    return jax.shard_map(
        on_device,
        mesh=mesh,
        in_specs=placed,
        out_specs=P("tile", None, "sub", None, None),
        check_vma=False,
    )
```

```python
import functools
import math

import jax
import jax.numpy as jnp
from jax import lax
from jax.experimental import pallas as pl
from jax.experimental.pallas import tpu as pltpu
from jax.sharding import PartitionSpec as P

BAND = 32
HALO = 8
PLANES = 5
REACH = 2
SHARED = 96
LARGE, MEDIUM, SMALL = 10**10, 2 * 10**9, 0

magnetic_coeff = 0.5


def lane_of(shape):
    return lax.broadcasted_iota(jnp.int32, shape, len(shape) - 1)


def row_of(shape):
    return lax.broadcasted_iota(jnp.int32, shape, len(shape) - 2)


def rolled(v, shift):
    return pltpu.roll(v, shift % v.shape[-1], v.ndim - 1)


def next_x(v):
    rows = v.shape[0]
    return jnp.where(row_of(v.shape) == rows - 1, 0.0, pltpu.roll(v, rows - 1, 0))


def prev_x(v):
    return jnp.where(row_of(v.shape) == 0, 0.0, pltpu.roll(v, 1, 0))


def next_y(v):
    lanes = v.shape[1]
    return jnp.where(lane_of(v.shape) == lanes - 1, 0.0, pltpu.roll(v, lanes - 1, 1))


def prev_y(v):
    return jnp.where(lane_of(v.shape) == 0, 0.0, pltpu.roll(v, 1, 1))


def plus_x(v):
    return next_x(v) - v


def plus_y(v):
    return next_y(v) - v


def minus_x(v):
    return v - prev_x(v)


def minus_y(v):
    return v - prev_y(v)


def looked_up(labels, entries):
    value = jnp.broadcast_to(entries[0], labels.shape)
    for m in range(1, len(entries)):
        value = jnp.where(labels == m, entries[m], value)
    return value


def update_h(h, v, v_after):
    depth = len(v[0])
    new = [[], [], []]
    for p in range(depth):
        vx, vy, vz = v[0][p], v[1][p], v[2][p]
        up_x, up_y = (v[0][p + 1], v[1][p + 1]) if p + 1 < depth else v_after
        dz_x = up_x - vx if up_x is not None else -vx
        dz_y = up_y - vy if up_y is not None else -vy
        new[0].append(h[0][p] + (plus_y(vz) - dz_y))
        new[1].append(h[1][p] + (dz_x - plus_x(vz)))
        new[2].append(h[2][p] + (plus_x(vy) - plus_y(vx)))
    return new


def update_e(e, ca, h, h_before):
    depth = len(h[0])
    new = [[], [], []]
    for p in range(depth):
        hx, hy, hz = h[0][p], h[1][p], h[2][p]
        low_x, low_y = (h[0][p - 1], h[1][p - 1]) if p > 0 else h_before
        dz_x = hx - low_x if low_x is not None else hx
        dz_y = hy - low_y if low_y is not None else hy
        new[0].append(ca[p] * e[0][p] - magnetic_coeff * (minus_y(hz) - dz_y))
        new[1].append(ca[p] * e[1][p] - magnetic_coeff * (dz_x - minus_x(hz)))
        new[2].append(ca[p] * e[2][p] - magnetic_coeff * (minus_x(hy) - minus_y(hx)))
    return new


def scaled(cb, e):
    return [[cb[p] * e[c][p] for p in range(len(cb))] for c in range(3)]


def joined(ref, index, spans):
    return jnp.concatenate([ref[*index, lo:hi] for lo, hi in spans], axis=0)


def prepared(e, h, labels, tables):
    ca = [looked_up(m, tables[0]) for m in labels]
    cb = [looked_up(m, tables[1]) for m in labels]
    return e, h, ca, cb


def raw(seeds, material, spans):
    depth = seeds.shape[1]
    e = [[joined(seeds, (c, p), spans) for p in range(depth)] for c in range(3)]
    h = [[joined(seeds, (3 + c, p), spans) for p in range(depth)] for c in range(3)]
    return e, h, [joined(material, (p,), spans) for p in range(depth)]


def table_entries(table):
    count = table.shape[0] // 2
    rows = [table[m : m + 1] for m in range(2 * count)]
    return rows[:count], rows[count:]


def loaded(seeds, material, table, spans):
    return prepared(*raw(seeds, material, spans), table_entries(table))


NONE = (None, None)


def send_halos(sub, fields, near, far, packed=lambda planes: planes):
    odd = lax.rem(lax.axis_index(sub), 2) == 1
    e, h, ca, cb = fields
    v1 = scaled(cb, e)
    h1 = update_h(h, v1, NONE)
    e1 = update_e(e, ca, h1, NONE)
    v2 = scaled(cb, e1)
    h2 = update_h(h1, v2, NONE)
    up = (h1[0][-1], h1[1][-1], h2[0][-1], h2[1][-1], cb[-1])
    down = (v1[0][0], v1[1][0], v2[0][0], v2[1][0], cb[0])
    up, down = packed(jnp.stack(up)), packed(jnp.stack(down))
    near[...] = jnp.where(odd, down, up)
    far[...] = jnp.where(odd, up, down)


def halo_kernel(spans, sub, table, seeds, material, near, far):
    send_halos(sub, loaded(seeds, material, table, spans), near, far)


def ramp(position, count):
    position = position.astype(jnp.float32) + 0.5
    return jnp.where(
        position < BAND,
        position / BAND,
        jnp.where(position > count - BAND, (count - position) / BAND, 1.0),
    )


def final_fields(fields, near, far, sub, sub_size, unpacked=lambda planes: planes):
    e, h, ca, cb = fields
    index = lax.axis_index(sub)
    odd = lax.rem(index, 2) == 1
    below, above = index > 0, index < sub_size - 1
    a, b = near[...], far[...]
    from_below = unpacked(jnp.where(odd, a, b))
    from_above = unpacked(jnp.where(above, jnp.where(odd, b, a), 0.0))
    part_h1x, part_h1y, part_h2x, part_h2y, cb_low = from_below
    v1x_up, v1y_up, part_v2x, part_v2y, cb_up = from_above

    v1 = scaled(cb, e)
    h1 = update_h(h, v1, (v1x_up, v1y_up))
    dh1x, dh1y = -v1[1][0], v1[0][0]
    h1_low = (jnp.where(below, part_h1x + dh1x, 0.0), jnp.where(below, part_h1y + dh1y, 0.0))
    e1 = update_e(e, ca, h1, h1_low)
    v2 = scaled(cb, e1)
    v2_up = (
        part_v2x - cb_up * (magnetic_coeff * h1[1][-1]),
        part_v2y + cb_up * (magnetic_coeff * h1[0][-1]),
    )
    h2 = update_h(h1, v2, v2_up)
    dv2x = cb_low * (magnetic_coeff * dh1y)
    dv2y = cb_low * (-magnetic_coeff * dh1x)
    dv2z = cb_low * (-magnetic_coeff * (minus_x(dh1y) - minus_y(dh1x)))
    h2x_low = part_h2x + (dh1x + (plus_y(dv2z) - (v2[1][0] - dv2y)))
    h2y_low = part_h2y + (dh1y + ((v2[0][0] - dv2x) - plus_x(dv2z)))
    h2_low = (jnp.where(below, h2x_low, 0.0), jnp.where(below, h2y_low, 0.0))
    e2 = update_e(e1, ca, h2, h2_low)
    return e2 + h2


def middle_out(block):
    return rolled(block, block.shape[-1] // 2)


def y_packed(first, second):
    lane = lane_of(first.shape)
    middle = (lane >= BAND) & (lane < first.shape[-1] - BAND)
    return jnp.where(middle, middle_out(second), first)


def inner_lanes(shape):
    lane = lane_of(shape)
    return (lane >= BAND) & (lane < shape[-1] - BAND)


def y_unpacked(block):
    a, b = rolled(block, BAND), rolled(block, -BAND)
    middle = inner_lanes(block.shape)
    below = lane_of(block.shape) < BAND
    first = jnp.where(middle, 0.0, jnp.where(below, a, b))
    second = jnp.where(middle, 0.0, jnp.where(below, b, a))
    return first, second


def strip_packed(strip):
    half = strip.shape[1] // 2
    first, second = strip[:, :half], strip[:, half:]
    return jnp.where(inner_lanes(first.shape), second, middle_out(first))


def strip_of(corners, block):
    middle = inner_lanes(block.shape)
    first = jnp.where(middle, middle_out(block), corners[0])
    second = jnp.where(middle, block, corners[1])
    return jnp.concatenate([first, second], axis=1)


def low_rows(shape):
    return row_of(shape) < 4


def bands_packed(block):
    rows, lanes = block.shape[1:]
    count, width, high = rows // 2 + 4, REACH * (rows // 8), lanes - BAND
    shape = (block.shape[0], 8, lanes)
    lane = lane_of(shape)
    low = low_rows(shape)
    side = jnp.zeros(shape, block.dtype)
    for g in range(rows // 8):
        at = BAND + REACH * (g + 1)
        piece = rolled(block[:, 8 * g : 8 * g + 8], REACH * (g + 1))
        here = ((lane >= at) & (lane < at + REACH)) | (
            (lane >= at + high - BAND - REACH) & (lane < at + high - BAND)
        )
        side = jnp.where(here, piece, side)
    other = rolled(pltpu.roll(side, 4, 1), width + REACH)
    own = ((lane >= BAND) & (lane < BAND + REACH + width)) | ((lane >= high) & (lane < high + width))
    side = jnp.where(own, side, other)
    middle = (lane >= BAND) & (lane < high)
    packed = y_packed(block[:, :count], block[:, rows - count :])
    first = jnp.where(low & middle, side, packed[:, :8])
    last = jnp.where(low | middle, packed[:, count - 8 :], side)
    return jnp.concatenate([first, packed[:, 8 : count - 8], last], axis=1)


def bands_unpacked(packed):
    count, lanes = packed.shape[1:]
    rows = 2 * count - 8
    width, high = REACH * (rows // 8), lanes - BAND
    first, last = packed[:, :8], packed[:, count - 8 :]
    low = low_rows(first.shape)
    lane = lane_of(first.shape)
    middle = (lane >= BAND) & (lane < high)
    side = jnp.where(low, first, last)
    other = rolled(pltpu.roll(side, 4, 1), -width - REACH)
    side = jnp.where(low == middle, side, other)
    beside = ((lane >= BAND) & (lane < BAND + REACH)) | ((lane >= high - REACH) & (lane < high))
    moved = [rolled(packed[:, at : at + 8], lanes // 2) for at in range(0, count, 8)]
    pieces = [packed[:, at : at + 8] for at in range(0, count - 8, 8)]
    pieces += [jnp.where(low, last, moved[0])] + moved[1:]
    result = []
    for g, piece in enumerate(pieces):
        result.append(jnp.where(middle, jnp.where(beside, rolled(side, -REACH * (g + 1)), 0.0), piece))
    return jnp.concatenate(result, axis=1)


def first_kernel(span, skip, decay, coupling, seeds, material, shared, held, labels, table, entries, sems):
    size_x = held.shape[2]
    copies = []

    def fetch(source, target):
        copies.append(pltpu.make_async_copy(source, target, sems.at[len(copies)]))
        copies[-1].start()

    def fetch_rows(lo, hi):
        rows = pl.ds(lo, hi - lo)
        fetch(material.at[0, :, rows], labels.at[:, rows])
        for c in range(0, 6, 2):
            some = pl.ds(c, 2)
            fetch(seeds.at[0, some, :, rows], held.at[some, :, rows])

    fetch_rows(*span)
    early = len(copies)
    fetch(decay, entries.at[0])
    fetch(coupling, entries.at[1])
    fetch_rows(0, span[0])
    fetch_rows(span[1], size_x)
    rows = slice(span[0] + skip, span[1] - skip)
    for copy in copies[:early]:
        copy.wait()
    planes = [held[c, :, rows] for c in range(6)] + [labels[:, rows].astype(jnp.float32)]
    shared[...] = bands_packed(jnp.concatenate(planes, axis=0))
    for copy in copies[early : early + 2]:
        copy.wait()
    count = entries.shape[1]
    for k in range(2):
        for m in range(count):
            table[k * count + m : k * count + m + 1] = jnp.full((1, table.shape[1]), entries[k, m], jnp.float32)
    for copy in copies[early + 2 :]:
        copy.wait()


def halo_pair_kernel(edges, inner, sub, table, seeds, material, near_edge, far_edge, near, far):
    send_halos(sub, loaded(seeds, material, table, edges), near_edge, far_edge)
    send_halos(sub, loaded(seeds, material, table, inner), near, far)


def shared_fields(table, shared):
    depth = shared.shape[0] // 7
    planes = bands_unpacked(shared[...])
    f = [planes[depth * c : depth * (c + 1)] for c in range(7)]
    return prepared(f[:3], f[3:6], f[6], table_entries(table))


def shared_halo_kernel(sub, table, shared, near, far, done):
    done[...] = jnp.zeros(done.shape, done.dtype)
    send_halos(sub, shared_fields(table, shared), near, far, bands_packed)


def weighted_planes(seeds, material, table, near, far, spans, keeps, sub, sub_size):
    planes = final_fields(loaded(seeds, material, table, spans), near, far, sub, sub_size)
    return weighted(planes, spans, keeps, *seeds.shape[2:])


def weighted(planes, spans, keeps, size_x, size_y):
    at, results = 0, []
    for (lo, hi), (start, stop) in zip(spans, keeps):
        shape = (stop - start, size_y)
        weight = ramp(row_of(shape) + start, size_x) * ramp(lane_of(shape), size_y)
        first = at + start - lo
        results.append(jnp.stack([plane[first : first + stop - start] * weight for part in planes for plane in part]))
        at += hi - lo
    return results


def edge_kernel(spans, sub, sub_size, tile, table, seeds, material, near, far, edge, corner, strip):
    size_x = seeds.shape[2]
    keeps = ((0, BAND), (size_x - BAND, size_x))
    low, high = weighted_planes(seeds, material, table, near, far, spans, keeps, sub, sub_size)
    odd = lax.rem(lax.axis_index(tile), 2) == 1
    edge[:, :BAND] = low
    edge[:, BAND:] = high
    corner[...] = y_packed(low, high)
    strip[...] = strip_packed(jnp.where(odd, high, low))


def middle_kernel(spans, sub, sub_size, tile, table, seeds, material, near, far, edge, _, mid, bands, beside):
    size_x = seeds.shape[2]
    keep = (BAND, size_x - BAND)
    odd = lax.rem(lax.axis_index(tile), 2) == 1
    beside[...] = strip_packed(jnp.where(odd, edge[:, :BAND], edge[:, BAND:]))
    planes, = weighted_planes(seeds, material, table, near, far, spans, (keep,), sub, sub_size)
    half = bands.shape[1]
    mid[...] = planes
    bands[...] = y_packed(planes[:, :half], planes[:, -half:])


def whole_kernel(spans, sub, sub_size, table, seeds, material, near, far, out):
    planes, = weighted_planes(seeds, material, table, near, far, spans, spans, sub, sub_size)
    out[...] = planes


def y_swapped(block):
    below = lane_of(block.shape) < BAND
    return jnp.where(inner_lanes(block.shape), 0.0, jnp.where(below, rolled(block, BAND), rolled(block, -BAND)))


def shared_kernel(span, size_x, sub, sub_size, table, shared, near, far, part):
    planes = final_fields(shared_fields(table, shared), near, far, sub, sub_size, bands_unpacked)
    found, = weighted(planes, (span,), (span,), size_x, part.shape[2])
    part[...] = y_swapped(found)


def corner_kernel(tile, edge, corner, summed, send):
    odd = lax.rem(lax.axis_index(tile), 2) == 1
    half = BAND // 2
    first, second = y_unpacked(corner[...])
    low = edge[:, :BAND] + first
    high = edge[:, BAND:] + second
    summed[:, :BAND] = low
    summed[:, BAND:] = high
    by, away = jnp.where(odd, low, high), jnp.where(odd, high, low)
    send[:, :half] = y_packed(by[:, :half], by[:, half:])
    send[:, half:] = y_packed(away[:, :half], away[:, half:])


def early_kernel(mid, part, out, whole, sem):
    size_x = out.shape[3]
    skip = HALO // 2
    count = part.shape[1] - 2 * skip
    start = (size_x - count) // 2
    found = mid[:, start - BAND : start - BAND + count] + part[:, skip : skip + count]
    whole[...] = found.reshape(whole.shape)
    copy = pltpu.make_async_copy(whole, out.at[0, :, :, pl.ds(start, count)], sem)
    copy.start()
    copy.wait()


def late_kernel(tile, mid, bands, summed, strip, beside, low, high):
    odd = lax.rem(lax.axis_index(tile), 2) == 1
    half = bands.shape[1]
    first, second = y_unpacked(bands[...])
    nothing = (jnp.zeros(strip.shape, jnp.float32),) * 2
    by, away = strip_of(nothing, beside[...]), strip_of(nothing, strip[...])

    def by_component(rows):
        return rows.reshape(*low.shape[:2], *rows.shape[1:])

    low[:, :, BAND:] = by_component(mid[:, :half] + first)
    high[:, :, :half] = by_component(mid[:, -half:] + second)
    low[:, :, :BAND] = by_component(summed[:, :BAND] + jnp.where(odd, by, away))
    high[:, :, half:] = by_component(summed[:, BAND:] + jnp.where(odd, away, by))


def last_kernel(tile, low, high, got, _, out, edges, sems):
    odd = lax.rem(lax.axis_index(tile), 2) == 1
    size_x, count = out.shape[3], low.shape[2]
    half, quarter = count - BAND, BAND // 2
    copies = []

    def write(source, start, rows):
        target = out.at[0, :, :, pl.ds(start, rows)]
        copies.append(pltpu.make_async_copy(source, target, sems.at[len(copies)]))
        copies[-1].start()

    write(low.at[:, :, pl.ds(BAND, half)], BAND, half)
    write(high.at[:, :, pl.ds(0, half)], size_x - count, half)
    straight = got[:, :quarter]
    middle = inner_lanes(straight.shape)
    by = jnp.where(middle, 0.0, straight), jnp.where(middle, 0.0, middle_out(straight))
    by = jnp.concatenate(by, axis=1)
    away = jnp.concatenate(y_unpacked(got[:, quarter:]), axis=1)
    shape = edges.shape[1:]
    edges[0] = low[:, :, :BAND] + jnp.where(odd, by, away).reshape(shape)
    write(edges.at[0], 0, BAND)
    edges[1] = high[:, :, half:] + jnp.where(odd, away, by).reshape(shape)
    write(edges.at[1], size_x - BAND, BAND)
    for copy in copies:
        copy.wait()


HBM = pl.BlockSpec(memory_space=pltpu.HBM)
VMEM = pl.BlockSpec(memory_space=pltpu.VMEM)
PARAMS = pltpu.CompilerParams(vmem_limit_bytes=32 * 1024 * 1024)


def cost(flops):
    return pl.CostEstimate(flops=flops, bytes_accessed=0, transcendentals=0)


def called(kernel, shapes, *operands, flops=0):
    outs = [jax.ShapeDtypeStruct(shape, jnp.float32) for shape in shapes]
    return pl.pallas_call(
        kernel,
        out_shape=outs,
        in_specs=[VMEM] * len(operands),
        out_specs=[VMEM] * len(outs),
        compiler_params=PARAMS,
        cost_estimate=cost(flops),
    )(*operands)


def after(first, *values):
    return lax.optimization_barrier((first, *values))


def near_exchange(near, sub_size):
    return lax.ppermute(near, "sub", [(i, i ^ 1) for i in range(sub_size)])


def far_exchange(far, sub_size, tile_size):
    pairs = []
    for t in range(tile_size):
        for i in range(sub_size):
            j = ((i + 1) ^ 1) - 1
            other = (t, j) if 0 <= j < sub_size else (t ^ 1, i)
            pairs.append((t * sub_size + i, other[0] * sub_size + other[1]))
    return lax.ppermute(far, ("tile", "sub"), pairs)


def swapped(value, bits, tile_size):
    return lax.ppermute(value, "tile", [(t, t ^ bits) for t in range(tile_size)])


def from_behind(value, steps, count):
    return lax.ppermute(value, "tile", [(t, (t + steps) % count) for t in range(count)])


def table_rows(decay, coupling, size_y):
    entries = jnp.concatenate([decay, coupling])
    return jnp.broadcast_to(entries[:, None], (entries.shape[0], size_y))


def two_by_two(seeds, material, decay, coupling, sub_size, tile_size):
    depth, size_x, size_y = seeds.shape[2:]
    planes = 6 * depth
    edges = ((0, BAND + HALO), (size_x - BAND - HALO, size_x))
    inner = ((BAND - HALO, size_x - BAND + HALO),)
    keep = ((size_x - SHARED) // 2, (size_x + SHARED) // 2)
    span = (keep[0] - HALO // 2, keep[1] + HALO // 2)
    fetched = (keep[0] - HALO, keep[1] + HALO)
    rows = size_x - 2 * BAND
    edge_rows, inner_rows = 2 * (BAND + HALO), rows + 2 * HALO
    packed_rows = (SHARED + HALO) // 2 + 4
    whole = jax.ShapeDtypeStruct(seeds.shape, jnp.float32)

    shared, seeds, material, table = pl.pallas_call(
        functools.partial(first_kernel, fetched, HALO // 2),
        out_shape=[
            jax.ShapeDtypeStruct((7 * depth, packed_rows, size_y), jnp.float32),
            jax.ShapeDtypeStruct(seeds.shape[1:], jnp.float32),
            jax.ShapeDtypeStruct(material.shape[1:], jnp.int32),
            jax.ShapeDtypeStruct((2 * decay.shape[0], size_y), jnp.float32),
        ],
        in_specs=[HBM] * 4,
        out_specs=[VMEM] * 4,
        scratch_shapes=[pltpu.SMEM((2, *decay.shape), jnp.float32), pltpu.SemaphoreType.DMA((14,))],
        compiler_params=PARAMS,
        cost_estimate=cost(0),
    )(*(pltpu.with_memory_space_constraint(x, pltpu.HBM) for x in (decay, coupling, seeds, material)))
    shared = swapped(shared, 2, tile_size)
    edge_near, edge_far, inner_near, inner_far = called(
        functools.partial(halo_pair_kernel, edges, inner, "sub"),
        [(PLANES, edge_rows, size_y)] * 2 + [(PLANES, inner_rows, size_y)] * 2, table, seeds, material,
    )
    edge_near, inner_near = near_exchange(edge_near, sub_size), near_exchange(inner_near, sub_size)
    edge_far = far_exchange(edge_far, sub_size, tile_size)
    inner_far = far_exchange(inner_far, sub_size, tile_size)

    edge, corner, strip = called(
        functools.partial(edge_kernel, edges, "sub", sub_size, "tile"),
        [(planes, 2 * BAND, size_y), (planes, BAND, size_y), (planes, BAND // 2, size_y)],
        table, seeds, material, edge_near, edge_far,
    )
    corner = swapped(corner, 2, tile_size)
    strip = swapped(strip, 3, tile_size)

    shape = (PLANES, packed_rows, size_y)
    shared_near, shared_far, done = called(
        functools.partial(shared_halo_kernel, "sub"), [shape, shape, (8, size_y)], table, shared, flops=LARGE
    )
    shared_near = near_exchange(shared_near, sub_size)
    shared_far = far_exchange(shared_far, sub_size, tile_size)

    mid, bands, beside = called(
        functools.partial(middle_kernel, inner, "sub", sub_size, "tile"),
        [(planes, rows, size_y), (planes, (rows - SHARED) // 2, size_y), (planes, BAND // 2, size_y)],
        table, seeds, material, inner_near, inner_far, edge, done,
    )
    bands = swapped(bands, 2, tile_size)
    beside = swapped(beside, 1, tile_size)

    corner, strip, mid = after(corner, strip, mid)
    summed, send = called(
        functools.partial(corner_kernel, "tile"), [(planes, 2 * BAND, size_y), (planes, BAND, size_y)],
        edge, corner, flops=SMALL,
    )
    got = swapped(send, 1, tile_size)
    beside, shared_near = after(beside, shared_near)
    part, = called(
        functools.partial(shared_kernel, span, size_x, "sub", sub_size),
        [(planes, SHARED + HALO, size_y)], table, shared, shared_near, shared_far, flops=MEDIUM,
    )
    early = pl.pallas_call(
        early_kernel,
        out_shape=whole,
        in_specs=[VMEM] * 2,
        out_specs=HBM,
        scratch_shapes=[pltpu.VMEM((6, depth, SHARED, size_y), jnp.float32), pltpu.SemaphoreType.DMA],
        compiler_params=PARAMS,
        cost_estimate=cost(0),
    )(mid, part)
    low, high = called(
        functools.partial(late_kernel, "tile"), [(6, depth, (size_x - SHARED) // 2, size_y)] * 2,
        mid, bands, summed, strip, beside,
    )
    return pl.pallas_call(
        functools.partial(last_kernel, "tile"),
        out_shape=whole,
        in_specs=[VMEM] * 3 + [HBM],
        out_specs=HBM,
        scratch_shapes=[pltpu.VMEM((2, 6, depth, BAND, size_y), jnp.float32), pltpu.SemaphoreType.DMA((4,))],
        input_output_aliases={3: 0},
        compiler_params=PARAMS,
        cost_estimate=cost(0),
    )(low, high, got, early)


def any_lattice(seeds, material, decay, coupling, sub_size, tile_size):
    depth, size_x, size_y = seeds.shape[2:]
    seeds, material = seeds[0], material[0]
    spans = ((0, size_x),)
    table = table_rows(decay, coupling, size_y)
    shape = (PLANES, size_x, size_y)
    near, far = called(functools.partial(halo_kernel, spans, "sub"), [shape, shape], table, seeds, material)
    near = near_exchange(near, sub_size)
    far = far_exchange(far, sub_size, tile_size)
    weighted, = called(
        functools.partial(whole_kernel, spans, "sub", sub_size), [(6 * depth, size_x, size_y)],
        table, seeds, material, near, far,
    )
    weighted = weighted.reshape(6, depth, size_x, size_y)
    side = math.isqrt(tile_size)
    prev_band = from_behind(weighted[:, :, size_x - BAND :, :], 1, tile_size)
    next_band = from_behind(weighted[:, :, :BAND, :], -1, tile_size)
    combined = weighted.at[:, :, :BAND, :].add(prev_band)
    combined = combined.at[:, :, size_x - BAND :, :].add(next_band)
    flat = (6, depth, size_x * BAND // size_y, size_y)
    thin = (6, depth, size_x, BAND)
    top_slab = combined[..., size_y - BAND :].reshape(flat)
    bottom_slab = combined[..., :BAND].reshape(flat)
    result = combined.at[..., :BAND].add(from_behind(top_slab, side, tile_size).reshape(thin))
    result = result.at[..., size_y - BAND :].add(from_behind(bottom_slab, -side, tile_size).reshape(thin))
    return result[None]


def solution(mesh):
    sub_size, tile_size = mesh.shape["sub"], mesh.shape["tile"]
    body = two_by_two if tile_size == 4 else any_lattice

    def on_device(seeds, material, decay, coupling):
        return body(seeds, material, decay, coupling, sub_size, tile_size)

    placed = (P("tile", None, "sub", None, None), P("tile", "sub", None, None), P(), P())
    return jax.shard_map(
        on_device,
        mesh=mesh,
        in_specs=placed,
        out_specs=P("tile", None, "sub", None, None),
        check_vma=False,
    )
```
